32 devices in a mesh: zone: 2 (over core), gx: 4 (over y, x), yz: 4 (over z).
Axes of the slice: x: 2, y: 2, z: 4, core: 2. Of those that a mesh axis runs over, the one named last changes fastest.
Arguments:
- adjoint: float32 [2, 27, 32, 16, 512], P('zone', None, 'gx', None, 'yz'), may hold values from -6 to 6
- saved: float32 [2, 2, 27, 32, 16, 512], P(None, 'zone', None, 'gx', None, 'yz')
- solid: int32 [2, 32, 16, 512], P('zone', 'gx', None, 'yz'), may hold values 0 or 1
- band_device: int32 [2, 16, 512, 2], P('zone', None, 'yz'), may hold values from 0 to 3, as said below
- band_cell: int32 [2, 16, 512, 2], P('zone', None, 'yz'), may hold values from 0 to 127
- band_weight: float32 [2, 16, 512, 2], P('zone', None, 'yz'), may hold values from 0.1 to 0.9
Outputs:
- adjoint_out: float32 [2, 27, 32, 16, 512], P('zone', None, 'gx', None, 'yz')
The draws below stay inside these ranges and needn't reach their ends.
Inputs may be any that keep to these rules, and one draw needn't show every extreme that they name: band_device and band_cell name, for each band cell and partner, a cell of the other zone's interface plane in the same radial row; within a radial row, the target of cell z and partner k is (z + s + d + k) mod 512 for one shift s of that row and a jitter d from -2 to 2.
All inputs are finite; a program needn't handle non-finite values. No bound on the sum of `solid` on one device may be relied on, other than what follows from the above.
Results may differ from the reference program's by a relative error of at most 0.0001.
Values sent between devices are 32-bit elements; how exact they have to be, the bound alone decides.
No kernel may reach another device: no remote copies, remote signals or barrier semaphores. Data moves between devices by JAX's collectives and lax.ppermute only.
A program may use at most 64 MiB of HBM per device.

```python
import jax
import jax.numpy as jnp
import numpy as np
from jax import lax

Q = 27
TAPS = 2
STEPS = 2
NY = 16
BZ = 128
NX = 32
NZ = 512


def band_targets(key):
    shifts = jax.random.randint(jax.random.fold_in(key, 11), (2, NY, 1, 1), 0, NZ)
    jitter = jax.random.randint(jax.random.fold_in(key, 12), (2, NY, NZ, 1), -2, 3)
    cells = jnp.arange(NZ, dtype=jnp.int32)[None, None, :, None]
    partners = jnp.arange(TAPS, dtype=jnp.int32)[None, None, None, :]
    return (cells + shifts + jitter + partners + 2 * NZ) % NZ


def draw_band_device(key, part):
    targets = band_targets(key)
    return (targets // BZ).astype(jnp.int32)


def draw_band_cell(key, part):
    targets = band_targets(key)
    return (targets % BZ).astype(jnp.int32)


def draw_saved(key, part):
    key = jax.random.fold_in(key, 3)
    counts = jnp.array([3, 2, 3, 2, 1, 2, 3, 2, 3, 2, 1, 2, 1, 0, 1, 2, 1, 2, 3, 2, 3, 2, 1, 2, 3, 2, 3])
    weights = jnp.array([8.0 / 27.0, 2.0 / 27.0, 1.0 / 54.0, 1.0 / 216.0], dtype=jnp.float32)[counts]
    lower, upper = (0.5, 1.5)
    ratios = jax.random.uniform(key, (STEPS, 2, Q, NX, NY, NZ), jnp.float32, lower, upper)
    return weights[None, None, :, None, None, None] * ratios


def place_ends(values, stream_key, least, top_value):
    longest = values.shape.index(max(values.shape))
    spots = []
    for shift in (0, 1):
        where = [jax.random.randint(jax.random.fold_in(stream_key, axis), (), 0, length) for axis, length in enumerate(values.shape)]
        where[longest] = (where[longest] + shift) % values.shape[longest]
        spots.append(tuple(where))
    return values.at[spots[0]].set(least).at[spots[1]].set(top_value)


def steps_of(rng, shape, cuts, smallest, high):
    gain = 1.0
    for axis_at, shards_of in cuts:
        heights = jax.random.uniform(jax.random.fold_in(jax.random.fold_in(rng, 6), axis_at), (shards_of,), jnp.float32, smallest / len(cuts), high / len(cuts))
        gain = gain * jnp.repeat(jnp.exp(heights), shape[axis_at] // shards_of).reshape((-1,) + (1,) * (len(shape) - 1 - axis_at))
    return gain


def scatter_about(rng, shape, spread, reach, shards=(), kind=jnp.bfloat16):
    factor_of = steps_of(rng, shape, shards, -0.22, 0.18) if shards else 1.0
    drawn = jax.random.normal(rng, shape, jnp.float32) * spread * factor_of
    return jnp.minimum(jnp.maximum(drawn, -reach), reach).astype(kind)


def setup_inputs(seed: int = 0) -> dict:
    splits = jax.random.split(jax.random.key(seed), 7)
    return {
        "adjoint": scatter_about(splits[0], (2, Q, NX, NY, NZ), 1.0, 6.0, ((0, 2), (2, 4), (4, 4)), jnp.float32),
        "saved": draw_saved(jax.random.fold_in(splits[6], 71), 0),
        "solid": place_ends((jax.random.randint(splits[2], (2, NX, NY, NZ), 0, 8) < 1).astype(jnp.int32), jax.random.fold_in(splits[2], 1), 0, 1),
        "band_device": draw_band_device(jax.random.fold_in(splits[6], 71), 0),
        "band_cell": draw_band_cell(jax.random.fold_in(splits[6], 71), 0),
        "band_weight": jnp.clip(0.1 + 0.79999997 * jax.random.uniform(splits[5], (2, NY, NZ, TAPS), jnp.float32) ** steps_of(splits[5], (2, NY, NZ, TAPS), ((0, 2), (2, 4)), -0.2, 0.2), 0.1, 0.9),
    }


OMEGA = 1.6


def lattice_vectors():
    velocities = np.array([[along_x, along_y, along_z] for along_x in (-1, 0, 1) for along_y in (-1, 0, 1) for along_z in (-1, 0, 1)])
    lookup = np.array([8.0 / 27.0, 2.0 / 27.0, 1.0 / 54.0, 1.0 / 216.0])
    weights = lookup[np.sum(np.abs(velocities), axis=1)]
    return velocities, weights


def moment_table():
    velocities, weights = lattice_vectors()
    speeds = velocities * 1.0
    table_rows = [weights, weights * speeds[:, 0], weights * speeds[:, 1], weights * speeds[:, 2],
                  weights * speeds[:, 0] * speeds[:, 0], weights * speeds[:, 1] * speeds[:, 1],
                  weights * speeds[:, 2] * speeds[:, 2], weights * speeds[:, 0] * speeds[:, 1],
                  weights * speeds[:, 0] * speeds[:, 2], weights * speeds[:, 1] * speeds[:, 2]]
    return np.stack(table_rows)


def finish_collision(pulled, moments, velocity, solid_now):
    speeds = jnp.asarray(lattice_vectors()[0], dtype=jnp.float32)
    vel_x, vel_y, vel_z = velocity[0], velocity[1], velocity[2]
    zeroth = moments[0]
    quadratic = (vel_x * vel_x * moments[4] + vel_y * vel_y * moments[5] + vel_z * vel_z * moments[6]
                 + 2.0 * (vel_x * vel_y * moments[7] + vel_x * vel_z * moments[8] + vel_y * vel_z * moments[9]))
    squared = vel_x * vel_x + vel_y * vel_y + vel_z * vel_z
    scalar_part = zeroth * (1.0 + 1.5 * squared) - 4.5 * quadratic
    vector_x = 3.0 * moments[1] + 9.0 * (moments[4] * vel_x + moments[7] * vel_y + moments[8] * vel_z) - 3.0 * vel_x * zeroth
    vector_y = 3.0 * moments[2] + 9.0 * (moments[7] * vel_x + moments[5] * vel_y + moments[9] * vel_z) - 3.0 * vel_y * zeroth
    vector_z = 3.0 * moments[3] + 9.0 * (moments[8] * vel_x + moments[9] * vel_y + moments[6] * vel_z) - 3.0 * vel_z * zeroth
    projected = (scalar_part[None] + speeds[:, 0, None, None, None] * vector_x[None]
                 + speeds[:, 1, None, None, None] * vector_y[None] + speeds[:, 2, None, None, None] * vector_z[None])
    relaxed = (1.0 - OMEGA) * pulled + OMEGA * projected
    bounced = pulled[::-1]
    return jnp.where(solid_now[None] == 1, bounced, relaxed)


def collide_adjoint(pulled, saved_now, solid_now):
    speeds = jnp.asarray(lattice_vectors()[0], dtype=jnp.float32)
    moment_rows = jnp.asarray(moment_table(), dtype=jnp.float32)
    density = jnp.sum(saved_now, axis=0)
    momentum = jnp.einsum("qa,qxyz->axyz", speeds, saved_now, precision=lax.Precision.HIGHEST)
    velocity = momentum / density[None]
    moments = jnp.einsum("mq,qxyz->mxyz", moment_rows, pulled, precision=lax.Precision.HIGHEST)
    return finish_collision(pulled, moments, velocity, solid_now)


def stream_pull(padded, extent_x, extent_y, extent_z):
    velocities = lattice_vectors()[0]
    pieces = []
    for direction in range(27):
        shift_x = 1 + int(velocities[direction, 0])
        shift_y = 1 + int(velocities[direction, 1])
        shift_z = 1 + int(velocities[direction, 2])
        pieces.append(padded[direction, shift_x:shift_x + extent_x, shift_y:shift_y + extent_y, shift_z:shift_z + extent_z])
    return jnp.stack(pieces)


def band_ghost(band_values):
    velocities = lattice_vectors()[0]
    extent_y = band_values.shape[1]
    padded = jnp.pad(band_values, ((0, 0), (1, 1), (0, 0)))
    ghosts = []
    for direction in range(9):
        shift_y = 1 + int(velocities[18 + direction, 1])
        ghosts.append(padded[direction, shift_y:shift_y + extent_y])
    zeros_part = jnp.zeros((18,) + band_values.shape[1:], band_values.dtype)
    return jnp.concatenate([zeros_part, jnp.stack(ghosts)], axis=0)


def reference(adjoint, saved, solid, band_device, band_cell, band_weight):
    extent_x = adjoint.shape[2]
    extent_y = adjoint.shape[3]
    extent_z = adjoint.shape[4]
    taps = band_weight.shape[3]
    current = adjoint
    for backward in (1, 0):
        results = []
        for zone_index in (0, 1):
            field_now = current[zone_index]
            partner_plane = current[1 - zone_index, 0:9, extent_x - 1]
            target = (band_device[zone_index] * BZ + band_cell[zone_index]).astype(jnp.int32)
            target = jnp.broadcast_to(target.reshape(1, extent_y, extent_z * taps), (9, extent_y, extent_z * taps))
            picked = jnp.take_along_axis(partner_plane, target, axis=2).reshape(9, extent_y, extent_z, taps)
            band_values = jnp.sum(picked * band_weight[zone_index][None], axis=-1)
            padded = jnp.pad(field_now, ((0, 0), (1, 1), (1, 1), (1, 1)))
            pulled = stream_pull(padded, extent_x, extent_y, extent_z)
            pulled = pulled.at[:, extent_x - 1].add(band_ghost(band_values))
            results.append(collide_adjoint(pulled, saved[backward, zone_index], solid[zone_index]))
        current = jnp.stack(results)
    return current
```

```python
import jax
import jax.numpy as jnp
import numpy as np
from jax import lax
from jax.experimental import pallas as pl
from jax.experimental.pallas import tpu as pltpu
from jax.sharding import PartitionSpec as P

OMEGA = 1.6
VMEM_LIMIT = 48 * 1024 * 1024
SIGNS = (-1, 0, 1)


def number(cx, cy, cz):
    return 9 * (cx + 1) + 3 * (cy + 1) + (cz + 1)


def lanes():
    return lax.broadcasted_iota(jnp.int32, (16, 128), 1)


def shift_y(tile, cy):
    if cy == 0:
        return tile
    row = lax.broadcasted_iota(jnp.int32, tile.shape, 0)
    if cy == 1:
        return jnp.where(row == 15, 0.0, pltpu.roll(tile, 15, 0))
    return jnp.where(row == 0, 0.0, pltpu.roll(tile, 1, 0))


def pack_columns(planes, x, low, high):
    lane = lanes()
    for slot in range(9):
        place = (x + 1) * 9 + slot
        here = lane == place
        low = jnp.where(here, pltpu.roll(planes(3 * slot + 2), place, 1), low)
        high = jnp.where(here, pltpu.roll(planes(3 * slot), place + 1, 1), high)
    return low, high


def pack_kernel(adj, low_out, high_out, top_out, bottom_out):
    extent_x = adj.shape[1]

    def one(x, carry):
        return pack_columns(lambda i: adj[i, x], x, *carry)

    zero = jnp.zeros((16, 128), jnp.float32)
    low, high = lax.fori_loop(0, extent_x, one, (zero, zero))
    low_out[...] = low
    high_out[...] = high
    for j in range(9):
        top_out[j] = adj[j, extent_x - 1]
        bottom_out[j] = adj[18 + j, 0]


def band_tiles(blocks, device, cell, weight, count):
    me = lax.axis_index("yz")
    hops = [lax.rem(me - device[k] + count, count) for k in range(2)]
    values = []
    for j in range(9):
        halves = []
        for r in (0, 8):
            total = jnp.zeros((8, 128), jnp.float32)
            for k in range(2):
                spot = cell[k, r : r + 8]
                picked = jnp.zeros((8, 128), jnp.float32)
                for m in range(count):
                    got = jnp.take_along_axis(blocks[m][j, r : r + 8], spot, axis=1)
                    picked = jnp.where(hops[k][r : r + 8] == m, got, picked)
                total = total + picked * weight[k, r : r + 8]
            halves.append(total)
        values.append(jnp.concatenate(halves, axis=0))
    return values


def velocity_of(saved):
    totals, along_y, along_z = [], [], []
    for cx in SIGNS:
        sums, diffs = [], []
        for cy in SIGNS:
            lo, mid, hi = [saved(number(cx, cy, cz)) for cz in SIGNS]
            sums.append(lo + mid + hi)
            diffs.append(hi - lo)
        totals.append(sums[0] + sums[1] + sums[2])
        along_y.append(sums[2] - sums[0])
        along_z.append(diffs[0] + diffs[1] + diffs[2])
    density = totals[0] + totals[1] + totals[2]
    momentum = (
        totals[2] - totals[0],
        along_y[0] + along_y[1] + along_y[2],
        along_z[0] + along_z[1] + along_z[2],
    )
    return [part / density for part in momentum]


def moments_of(pull):
    rows = []
    for cx in SIGNS:
        plain, first, second = [], [], []
        for cy in SIGNS:
            lo, mid, hi = [pull(cx, cy, cz) for cz in SIGNS]
            both = lo + hi
            plain.append(mid + 0.25 * both)
            first.append(hi - lo)
            second.append(both)
        pair = plain[0] + plain[2]
        rows.append(
            (
                plain[1] + 0.25 * pair,
                plain[2] - plain[0],
                pair,
                first[1] + 0.25 * (first[0] + first[2]),
                first[2] - first[0],
                second[1] + 0.25 * (second[0] + second[2]),
            )
        )
    even = [rows[1][n] + 0.25 * (rows[0][n] + rows[2][n]) for n in range(6)]
    zero = (8.0 / 27.0) * even[0]
    along = (
        (2.0 / 27.0) * (rows[2][0] - rows[0][0]),
        (2.0 / 27.0) * even[1],
        (2.0 / 27.0) * even[3],
    )
    square = (
        (2.0 / 27.0) * (rows[2][0] + rows[0][0]),
        (2.0 / 27.0) * even[2],
        (2.0 / 27.0) * even[5],
    )
    mixed = (
        (1.0 / 54.0) * (rows[2][1] - rows[0][1]),
        (1.0 / 54.0) * (rows[2][3] - rows[0][3]),
        (1.0 / 54.0) * even[4],
    )
    return zero, along, square, mixed


def collide(pull, velocity, solid, store):
    zero, along, square, mixed = moments_of(lambda cx, cy, cz: pull(number(cx, cy, cz)))
    ux, uy, uz = velocity
    xy, xz, yz = mixed
    quadratic = (
        ux * ux * square[0]
        + uy * uy * square[1]
        + uz * uz * square[2]
        + 2.0 * (ux * uy * xy + ux * uz * xz + uy * uz * yz)
    )
    speed = ux * ux + uy * uy + uz * uz
    scalar = OMEGA * (zero * (1.0 + 1.5 * speed) - 4.5 * quadratic)
    vec_x = OMEGA * (3.0 * along[0] + 9.0 * (square[0] * ux + xy * uy + xz * uz) - 3.0 * ux * zero)
    vec_y = OMEGA * (3.0 * along[1] + 9.0 * (xy * ux + square[1] * uy + yz * uz) - 3.0 * uy * zero)
    vec_z = OMEGA * (3.0 * along[2] + 9.0 * (xz * ux + yz * uy + square[2] * uz) - 3.0 * uz * zero)
    wall = solid == 1
    for cx in SIGNS:
        base = scalar if cx == 0 else (scalar + vec_x if cx > 0 else scalar - vec_x)
        for cy in SIGNS:
            inner = base if cy == 0 else (base + vec_y if cy > 0 else base - vec_y)
            for cz in SIGNS:
                full = inner if cz == 0 else (inner + vec_z if cz > 0 else inner - vec_z)
                i = number(cx, cy, cz)
                store(i, jnp.where(wall, pull(26 - i), (1.0 - OMEGA) * pull(i) + full))


def step_kernel(count, backward, last, *refs):
    refs = list(refs)
    adj, saved, solid, from_low, from_high, edge_low, edge_high = refs[:7]
    blocks = refs[7 : 7 + count]
    device, cell, weight = refs[7 + count : 10 + count]
    rest = refs[10 + count :]
    if last:
        out = rest.pop(0)
    else:
        out, low_out, high_out, top_out, bottom_out = rest[:5]
        rest = rest[5:]
    ext, kept, made, pulled, band, adj_sem, ghost_sem, saved_sem, out_sem = rest
    extent_x = made.shape[1]

    def load(x):
        return pltpu.make_async_copy(saved.at[backward, 0, :, x], kept.at[:, x], saved_sem.at[x])

    def save(x):
        return pltpu.make_async_copy(made.at[:, x], out.at[:, x], out_sem.at[x])

    whole = pltpu.make_async_copy(adj, ext.at[:, pl.ds(1, extent_x)], adj_sem)
    low_copy = pltpu.make_async_copy(from_low.at[pl.ds(0, 9)], ext.at[pl.ds(0, 9), 0], ghost_sem.at[0])
    high_copy = pltpu.make_async_copy(
        from_high.at[pl.ds(0, 9)], ext.at[pl.ds(18, 9), extent_x + 1], ghost_sem.at[1]
    )
    whole.start()
    low_copy.start()
    high_copy.start()
    for x in range(extent_x):
        load(x).start()

    for j, tile in enumerate(band_tiles(blocks, device, cell, weight, count)):
        band[j] = tile
    lane = lanes()
    span = 9 * extent_x
    joined = []
    for side, edge in ((0, edge_low), (1, edge_high)):
        tile = jnp.where(lane < 9, pltpu.roll(from_low[9 + side], 128 - span, 1), edge[...])
        beyond = (lane >= span + 9) & (lane < span + 18)
        joined.append(jnp.where(beyond, pltpu.roll(from_high[9 + side], span, 1), tile))
    low_edge, high_edge = joined
    whole.wait()
    low_copy.wait()
    high_copy.wait()

    def plane(x, final):
        load(x).wait()
        for cx in SIGNS:
            for cy in SIGNS:
                slot = 3 * (cx + 1) + cy + 1
                place = (x + 1 + cx) * 9 + slot
                for cz in SIGNS:
                    i = number(cx, cy, cz)
                    tile = ext[i, x + 1 + cx]
                    if cz == -1:
                        edge = pltpu.roll(low_edge, 128 - place, 1)
                        tile = jnp.where(lane == 0, edge, pltpu.roll(tile, 1, 1))
                    elif cz == 1:
                        edge = pltpu.roll(high_edge, 127 - place, 1)
                        tile = jnp.where(lane == 127, edge, pltpu.roll(tile, 127, 1))
                    if final and cx == 1:
                        tile = tile + band[i - 18]
                    pulled[i] = shift_y(tile, cy)
        velocity = velocity_of(lambda i: kept[i, x])

        def store(i, tile):
            made[i, x] = tile

        collide(lambda i: pulled[i], velocity, solid[0, x], store)
        save(x).start()

    lax.fori_loop(0, extent_x - 1, lambda x, c: (plane(x, False), c)[1], 0)
    plane(extent_x - 1, True)
    if not last:
        zero = jnp.zeros((16, 128), jnp.float32)
        low, high = lax.fori_loop(
            0, extent_x, lambda x, c: pack_columns(lambda i: made[i, x], x, *c), (zero, zero)
        )
        low_out[...] = low
        high_out[...] = high
        for j in range(9):
            top_out[j] = made[j, extent_x - 1]
            bottom_out[j] = made[18 + j, 0]
    for x in range(extent_x):
        save(x).wait()


def tile_shape(*lead):
    return jax.ShapeDtypeStruct(lead + (16, 128), jnp.float32)


def in_vmem(n):
    return [pl.BlockSpec(memory_space=pltpu.VMEM)] * n


def in_any(n):
    return [pl.BlockSpec(memory_space=pl.ANY)] * n


def body(sizes, adjoint, saved, solid, band_device, band_cell, band_weight):
    zones, widths, count = sizes
    field = adjoint[0]
    extent_x = field.shape[1]
    axes = ("zone", "gx", "yz")
    device = jnp.moveaxis(band_device[0], -1, 0)
    cell = jnp.moveaxis(band_cell[0], -1, 0)
    weight = jnp.moveaxis(band_weight[0], -1, 0)
    params = pltpu.CompilerParams(vmem_limit_bytes=VMEM_LIMIT)

    def flat(zone, gx, yz):
        return (zone * widths + gx) * count + yz

    def shifted(values, axis, step):
        size = widths if axis == "gx" else count
        pairs = [(i, i + step) for i in range(size) if 0 <= i + step < size]
        return lax.ppermute(values, axis, pairs)

    def crossed(values, hop):
        pairs = [
            (flat(zone, widths - 1, z), flat(1 - zone, widths - 1, (z + hop) % count))
            for zone in range(zones)
            for z in range(count)
        ]
        return lax.ppermute(values, axes, pairs)

    edges = (tile_shape(), tile_shape(), tile_shape(9), tile_shape(9))
    low, high, top, bottom = pl.pallas_call(
        pack_kernel,
        out_shape=edges,
        in_specs=in_vmem(1),
        out_specs=tuple(in_vmem(4)),
        compiler_params=params,
    )(field)
    for backward in (1, 0):
        last = backward == 0
        edge_low = shifted(high, "yz", 1)
        edge_high = shifted(low, "yz", -1)
        blocks = [crossed(top, hop) for hop in range(count)]
        seams = jnp.stack([edge_low, edge_high])
        from_low = shifted(jnp.concatenate([top, seams]), "gx", 1)
        from_high = shifted(jnp.concatenate([bottom, seams]), "gx", -1)
        result = pl.pallas_call(
            lambda *refs, backward=backward, last=last: step_kernel(count, backward, last, *refs),
            out_shape=(tile_shape(27, extent_x),) + (() if last else edges),
            in_specs=in_any(2) + in_vmem(5 + count + 3),
            out_specs=tuple(in_any(1) + ([] if last else in_vmem(4))),
            scratch_shapes=[
                pltpu.VMEM((27, extent_x + 2, 16, 128), jnp.float32),
                pltpu.VMEM((27, extent_x, 16, 128), jnp.float32),
                pltpu.VMEM((27, extent_x, 16, 128), jnp.float32),
                pltpu.VMEM((27, 16, 128), jnp.float32),
                pltpu.VMEM((9, 16, 128), jnp.float32),
                pltpu.SemaphoreType.DMA(()),
                pltpu.SemaphoreType.DMA((2,)),
                pltpu.SemaphoreType.DMA((extent_x,)),
                pltpu.SemaphoreType.DMA((extent_x,)),
            ],
            compiler_params=params,
        )(field, saved, solid, from_low, from_high, edge_low, edge_high, *blocks, device, cell, weight)
        if last:
            field = result[0]
        else:
            field, low, high, top, bottom = result
    return field[None]


def solution(mesh):
    sizes = tuple(mesh.shape[axis] for axis in ("zone", "gx", "yz"))
    in_specs = (
        P("zone", None, "gx", None, "yz"),
        P(None, "zone", None, "gx", None, "yz"),
        P("zone", "gx", None, "yz"),
        P("zone", None, "yz", None),
        P("zone", None, "yz", None),
        P("zone", None, "yz", None),
    )
    out_specs = P("zone", None, "gx", None, "yz")
    return jax.shard_map(
        lambda *args: body(sizes, *args),
        mesh=mesh,
        in_specs=in_specs,
        out_specs=out_specs,
        check_vma=False,
    )
```

```python
import jax
import jax.numpy as jnp
import numpy as np
from jax import lax
from jax.experimental import pallas as pl
from jax.experimental.pallas import tpu as pltpu
from jax.sharding import PartitionSpec as P

OMEGA = 1.6
VMEM_LIMIT = 48 * 1024 * 1024
SIGNS = (-1, 0, 1)


def number(cx, cy, cz):
    return 9 * (cx + 1) + 3 * (cy + 1) + (cz + 1)


def lanes():
    return lax.broadcasted_iota(jnp.int32, (16, 128), 1)


def shift_y(tile, cy):
    if cy == 0:
        return tile
    row = lax.broadcasted_iota(jnp.int32, tile.shape, 0)
    if cy == 1:
        return jnp.where(row == 15, 0.0, pltpu.roll(tile, 15, 0))
    return jnp.where(row == 0, 0.0, pltpu.roll(tile, 1, 0))


def pack_columns(planes, x, low, high):
    lane = lanes()
    for slot in range(9):
        place = (x + 1) * 9 + slot
        here = lane == place
        low = jnp.where(here, pltpu.roll(planes(3 * slot + 2), place, 1), low)
        high = jnp.where(here, pltpu.roll(planes(3 * slot), place + 1, 1), high)
    return low, high


def pack_kernel(adj, low_out, high_out, top_out, bottom_out):
    extent_x = adj.shape[1]

    def one(x, carry):
        return pack_columns(lambda i: adj[i, x], x, *carry)

    zero = jnp.zeros((16, 128), jnp.float32)
    low, high = lax.fori_loop(0, extent_x, one, (zero, zero))
    low_out[...] = low
    high_out[...] = high
    for j in range(9):
        top_out[j] = adj[j, extent_x - 1]
        bottom_out[j] = adj[18 + j, 0]


def band_tiles(blocks, device, cell, weight, count):
    values = []
    for j in range(9):
        halves = []
        for r in (0, 8):
            total = jnp.zeros((8, 128), jnp.float32)
            for k in range(2):
                spot = cell[k, r : r + 8]
                picked = jnp.zeros((8, 128), jnp.float32)
                for m in range(count):
                    got = jnp.take_along_axis(blocks[m, j, r : r + 8], spot, axis=1)
                    picked = jnp.where(device[k, r : r + 8] == m, got, picked)
                total = total + picked * weight[k, r : r + 8]
            halves.append(total)
        values.append(jnp.concatenate(halves, axis=0))
    return values


def velocity_of(saved):
    totals, along_y, along_z = [], [], []
    for cx in SIGNS:
        sums, diffs = [], []
        for cy in SIGNS:
            lo, mid, hi = [saved(number(cx, cy, cz)) for cz in SIGNS]
            sums.append(lo + mid + hi)
            diffs.append(hi - lo)
        totals.append(sums[0] + sums[1] + sums[2])
        along_y.append(sums[2] - sums[0])
        along_z.append(diffs[0] + diffs[1] + diffs[2])
    density = totals[0] + totals[1] + totals[2]
    momentum = (
        totals[2] - totals[0],
        along_y[0] + along_y[1] + along_y[2],
        along_z[0] + along_z[1] + along_z[2],
    )
    return [part / density for part in momentum]


def moments_of(pull):
    rows = []
    for cx in SIGNS:
        plain, first, second = [], [], []
        for cy in SIGNS:
            lo, mid, hi = [pull(cx, cy, cz) for cz in SIGNS]
            both = lo + hi
            plain.append(mid + 0.25 * both)
            first.append(hi - lo)
            second.append(both)
        pair = plain[0] + plain[2]
        rows.append(
            (
                plain[1] + 0.25 * pair,
                plain[2] - plain[0],
                pair,
                first[1] + 0.25 * (first[0] + first[2]),
                first[2] - first[0],
                second[1] + 0.25 * (second[0] + second[2]),
            )
        )
    even = [rows[1][n] + 0.25 * (rows[0][n] + rows[2][n]) for n in range(6)]
    zero = (8.0 / 27.0) * even[0]
    along = (
        (2.0 / 27.0) * (rows[2][0] - rows[0][0]),
        (2.0 / 27.0) * even[1],
        (2.0 / 27.0) * even[3],
    )
    square = (
        (2.0 / 27.0) * (rows[2][0] + rows[0][0]),
        (2.0 / 27.0) * even[2],
        (2.0 / 27.0) * even[5],
    )
    mixed = (
        (1.0 / 54.0) * (rows[2][1] - rows[0][1]),
        (1.0 / 54.0) * (rows[2][3] - rows[0][3]),
        (1.0 / 54.0) * even[4],
    )
    return zero, along, square, mixed


def collide(pull, velocity, solid, store):
    zero, along, square, mixed = moments_of(lambda cx, cy, cz: pull(number(cx, cy, cz)))
    ux, uy, uz = velocity
    xy, xz, yz = mixed
    quadratic = (
        ux * ux * square[0]
        + uy * uy * square[1]
        + uz * uz * square[2]
        + 2.0 * (ux * uy * xy + ux * uz * xz + uy * uz * yz)
    )
    speed = ux * ux + uy * uy + uz * uz
    scalar = OMEGA * (zero * (1.0 + 1.5 * speed) - 4.5 * quadratic)
    vec_x = OMEGA * (3.0 * along[0] + 9.0 * (square[0] * ux + xy * uy + xz * uz) - 3.0 * ux * zero)
    vec_y = OMEGA * (3.0 * along[1] + 9.0 * (xy * ux + square[1] * uy + yz * uz) - 3.0 * uy * zero)
    vec_z = OMEGA * (3.0 * along[2] + 9.0 * (xz * ux + yz * uy + square[2] * uz) - 3.0 * uz * zero)
    wall = solid == 1
    for cx in SIGNS:
        base = scalar if cx == 0 else (scalar + vec_x if cx > 0 else scalar - vec_x)
        for cy in SIGNS:
            inner = base if cy == 0 else (base + vec_y if cy > 0 else base - vec_y)
            for cz in SIGNS:
                full = inner if cz == 0 else (inner + vec_z if cz > 0 else inner - vec_z)
                i = number(cx, cy, cz)
                store(i, jnp.where(wall, pull(26 - i), (1.0 - OMEGA) * pull(i) + full))


def step_kernel(count, backward, last, *refs):
    refs = list(refs)
    adj, saved, solid, from_low, from_high, edge_low, edge_high = refs[:7]
    blocks, device, cell, weight = refs[7:11]
    rest = refs[11:]
    if last:
        out = rest.pop(0)
    else:
        out, low_out, high_out, top_out, bottom_out = rest[:5]
        rest = rest[5:]
    ext, kept, made, pulled, band, adj_sem, ghost_sem, saved_sem, out_sem = rest
    extent_x = made.shape[1]

    def load(x):
        return pltpu.make_async_copy(saved.at[backward, 0, :, x], kept.at[:, x], saved_sem.at[x])

    def save(x):
        return pltpu.make_async_copy(made.at[:, x], out.at[:, x], out_sem.at[x])

    whole = pltpu.make_async_copy(adj, ext.at[:, pl.ds(1, extent_x)], adj_sem)
    low_copy = pltpu.make_async_copy(from_low.at[pl.ds(0, 9)], ext.at[pl.ds(0, 9), 0], ghost_sem.at[0])
    high_copy = pltpu.make_async_copy(
        from_high.at[pl.ds(0, 9)], ext.at[pl.ds(18, 9), extent_x + 1], ghost_sem.at[1]
    )
    whole.start()
    low_copy.start()
    high_copy.start()
    for x in range(extent_x):
        load(x).start()

    for j, tile in enumerate(band_tiles(blocks, device, cell, weight, count)):
        band[j] = tile
    lane = lanes()
    span = 9 * extent_x
    joined = []
    for side, edge in ((0, edge_low), (1, edge_high)):
        tile = jnp.where(lane < 9, pltpu.roll(from_low[9 + side], 128 - span, 1), edge[...])
        beyond = (lane >= span + 9) & (lane < span + 18)
        joined.append(jnp.where(beyond, pltpu.roll(from_high[9 + side], span, 1), tile))
    low_edge, high_edge = joined
    whole.wait()
    low_copy.wait()
    high_copy.wait()

    def plane(x, final):
        load(x).wait()
        for cx in SIGNS:
            for cy in SIGNS:
                slot = 3 * (cx + 1) + cy + 1
                place = (x + 1 + cx) * 9 + slot
                for cz in SIGNS:
                    i = number(cx, cy, cz)
                    tile = ext[i, x + 1 + cx]
                    if cz == -1:
                        edge = pltpu.roll(low_edge, 128 - place, 1)
                        tile = jnp.where(lane == 0, edge, pltpu.roll(tile, 1, 1))
                    elif cz == 1:
                        edge = pltpu.roll(high_edge, 127 - place, 1)
                        tile = jnp.where(lane == 127, edge, pltpu.roll(tile, 127, 1))
                    if final and cx == 1:
                        tile = tile + band[i - 18]
                    pulled[i] = shift_y(tile, cy)
        velocity = velocity_of(lambda i: kept[i, x])

        def store(i, tile):
            made[i, x] = tile

        collide(lambda i: pulled[i], velocity, solid[0, x], store)
        save(x).start()

    lax.fori_loop(0, extent_x - 1, lambda x, c: (plane(x, False), c)[1], 0)
    plane(extent_x - 1, True)
    if not last:
        zero = jnp.zeros((16, 128), jnp.float32)
        low, high = lax.fori_loop(
            0, extent_x, lambda x, c: pack_columns(lambda i: made[i, x], x, *c), (zero, zero)
        )
        low_out[...] = low
        high_out[...] = high
        for j in range(9):
            top_out[j] = made[j, extent_x - 1]
            bottom_out[j] = made[18 + j, 0]
    for x in range(extent_x):
        save(x).wait()


def tile_shape(*lead):
    return jax.ShapeDtypeStruct(lead + (16, 128), jnp.float32)


def in_vmem(n):
    return [pl.BlockSpec(memory_space=pltpu.VMEM)] * n


def in_any(n):
    return [pl.BlockSpec(memory_space=pl.ANY)] * n


def body(sizes, adjoint, saved, solid, band_device, band_cell, band_weight):
    zones, widths, count = sizes
    field = adjoint[0]
    extent_x = field.shape[1]
    axes = ("zone", "gx", "yz")
    device = jnp.moveaxis(band_device[0], -1, 0)
    cell = jnp.moveaxis(band_cell[0], -1, 0)
    weight = jnp.moveaxis(band_weight[0], -1, 0)
    params = pltpu.CompilerParams(vmem_limit_bytes=VMEM_LIMIT)

    def flat(zone, gx, yz):
        return (zone * widths + gx) * count + yz

    def shifted(values, axis, step):
        size = widths if axis == "gx" else count
        pairs = [(i, i + step) for i in range(size) if 0 <= i + step < size]
        return lax.ppermute(values, axis, pairs)

    def crossed(values):
        pairs = [
            (flat(zone, widths - 1, z), flat(1 - zone, widths - 1, z))
            for zone in range(zones)
            for z in range(count)
        ]
        partner = lax.ppermute(values, axes, pairs)
        slots = jnp.broadcast_to(partner[None], (count,) + partner.shape)
        return lax.all_to_all(slots, "yz", 0, 0)

    edges = (tile_shape(), tile_shape(), tile_shape(9), tile_shape(9))
    low, high, top, bottom = pl.pallas_call(
        pack_kernel,
        out_shape=edges,
        in_specs=in_vmem(1),
        out_specs=tuple(in_vmem(4)),
        compiler_params=params,
    )(field)
    for backward in (1, 0):
        last = backward == 0
        edge_low = shifted(high, "yz", 1)
        edge_high = shifted(low, "yz", -1)
        blocks = crossed(top)
        seams = jnp.stack([edge_low, edge_high])
        from_low = shifted(jnp.concatenate([top, seams]), "gx", 1)
        from_high = shifted(jnp.concatenate([bottom, seams]), "gx", -1)
        result = pl.pallas_call(
            lambda *refs, backward=backward, last=last: step_kernel(count, backward, last, *refs),
            out_shape=(tile_shape(27, extent_x),) + (() if last else edges),
            in_specs=in_any(2) + in_vmem(9),
            out_specs=tuple(in_any(1) + ([] if last else in_vmem(4))),
            scratch_shapes=[
                pltpu.VMEM((27, extent_x + 2, 16, 128), jnp.float32),
                pltpu.VMEM((27, extent_x, 16, 128), jnp.float32),
                pltpu.VMEM((27, extent_x, 16, 128), jnp.float32),
                pltpu.VMEM((27, 16, 128), jnp.float32),
                pltpu.VMEM((9, 16, 128), jnp.float32),
                pltpu.SemaphoreType.DMA(()),
                pltpu.SemaphoreType.DMA((2,)),
                pltpu.SemaphoreType.DMA((extent_x,)),
                pltpu.SemaphoreType.DMA((extent_x,)),
            ],
            compiler_params=params,
        )(field, saved, solid, from_low, from_high, edge_low, edge_high, blocks, device, cell, weight)
        if last:
            field = result[0]
        else:
            field, low, high, top, bottom = result
    return field[None]


def solution(mesh):
    sizes = tuple(mesh.shape[axis] for axis in ("zone", "gx", "yz"))
    in_specs = (
        P("zone", None, "gx", None, "yz"),
        P(None, "zone", None, "gx", None, "yz"),
        P("zone", "gx", None, "yz"),
        P("zone", None, "yz", None),
        P("zone", None, "yz", None),
        P("zone", None, "yz", None),
    )
    out_specs = P("zone", None, "gx", None, "yz")
    return jax.shard_map(
        lambda *args: body(sizes, *args),
        mesh=mesh,
        in_specs=in_specs,
        out_specs=out_specs,
        check_vma=False,
    )
```

```python
import jax
import jax.numpy as jnp
import numpy as np
from jax import lax
from jax.experimental import pallas as pl
from jax.experimental.pallas import tpu as pltpu
from jax.sharding import PartitionSpec as P

OMEGA = 1.6
VMEM_LIMIT = 20 * 1024 * 1024
SIGNS = (-1, 0, 1)


def number(cx, cy, cz):
    return 9 * (cx + 1) + 3 * (cy + 1) + (cz + 1)


def lanes():
    return lax.broadcasted_iota(jnp.int32, (16, 128), 1)


def shift_y(tile, cy):
    if cy == 0:
        return tile
    row = lax.broadcasted_iota(jnp.int32, tile.shape, 0)
    if cy == 1:
        return jnp.where(row == 15, 0.0, pltpu.roll(tile, 15, 0))
    return jnp.where(row == 0, 0.0, pltpu.roll(tile, 1, 0))


def pack_columns(planes, x, low, high):
    lane = lanes()
    for slot in range(9):
        place = (x + 1) * 9 + slot
        here = lane == place
        low = jnp.where(here, pltpu.roll(planes(3 * slot + 2), place, 1), low)
        high = jnp.where(here, pltpu.roll(planes(3 * slot), place + 1, 1), high)
    return low, high


def is_even(axis):
    return lax.rem(lax.axis_index(axis), 2) == 0


def write_messages(top, low, high, first, second):
    even = is_even("yz")
    for j in range(9):
        tile = top(j)
        first[j] = tile
        second[j] = tile
    first[9] = jnp.where(even, high, low)
    second[9] = jnp.where(even, low, high)


def edges_from(first, second):
    even = is_even("yz")
    me, count = lax.axis_index("yz"), lax.axis_size("yz")
    low = jnp.where(me == 0, 0.0, jnp.where(even, second[9], first[9]))
    high = jnp.where(me == count - 1, 0.0, jnp.where(even, first[9], second[9]))
    return low, high


def pack_kernel(adj, first_out, second_out):
    extent_x = adj.shape[1]
    zero = jnp.zeros((16, 128), jnp.float32)
    low, high = lax.fori_loop(
        0, extent_x, lambda x, c: pack_columns(lambda i: adj[i, x], x, *c), (zero, zero)
    )
    write_messages(lambda j: adj[j, extent_x - 1], low, high, first_out, second_out)


def velocity_kernel(saved, out, kept, sems):
    steps, _, _, extent_x = saved.shape[:4]

    def load(n):
        step, x = n // extent_x, lax.rem(n, extent_x)
        return pltpu.make_async_copy(saved.at[step, 0, :, x], kept.at[n], sems.at[n])

    total = steps * extent_x
    lax.fori_loop(0, total, lambda n, c: (load(n).start(), c)[1], 0)

    def one(n, carry):
        load(n).wait()
        for a, tile in enumerate(velocity_of(lambda i: kept[n, i])):
            out[n // extent_x, a, lax.rem(n, extent_x)] = tile
        return carry

    lax.fori_loop(0, total, one, 0)


def side_kernel(adj, first, second, out):
    extent_x = adj.shape[1]
    even = is_even("gx")
    for j in range(9):
        out[j] = jnp.where(even, adj[j, extent_x - 1], adj[18 + j, 0])
    out[9], out[10] = edges_from(first, second)


def cross_kernel(count, *refs):
    adj, own, first, second = refs[:4]
    others = refs[4 : 4 + count - 3]
    info, out = refs[4 + count - 3 :]
    extent_x = adj.shape[1]
    interface = lax.axis_index("gx") == lax.axis_size("gx") - 1
    out[9], out[10] = edges_from(first, second)

    @pl.when(jnp.logical_not(interface))
    def _():
        even = is_even("gx")
        for j in range(9):
            out[j] = jnp.where(even, adj[18 + j, 0], adj[j, extent_x - 1])

    @pl.when(interface)
    def _():
        me = lax.axis_index("yz")
        even = is_even("yz")
        rows = (0, 8)
        spots, picks = {}, {}
        for r in rows:
            for k in range(2):
                code = info[k, r : r + 8].astype(jnp.int32)
                ahead = lax.rem(code // 128 - me + count, count)
                spots[r, k] = lax.rem(code, 128)
                turned = jnp.where(even, ahead, lax.rem(count - ahead, count))
                masks = [turned == 1, turned == count - 1]
                masks += [ahead == count - hop for hop in range(2, count - 1)]
                picks[r, k] = masks
        for j in range(9):
            halves = []
            for r in rows:
                total = jnp.zeros((8, 128), jnp.float32)
                for k in range(2):
                    tiles = [ref[j, r : r + 8] for ref in (own, first, second, *others)]
                    got = [jnp.take_along_axis(tile, spots[r, k], axis=1) for tile in tiles]
                    picked = got[0]
                    for mask, value in zip(picks[r, k], got[1:]):
                        picked = jnp.where(mask, value, picked)
                    total = total + picked * info[2 + k, r : r + 8]
                halves.append(total)
            out[j] = jnp.concatenate(halves, axis=0)


def velocity_of(saved):
    totals, along_y, along_z = [], [], []
    for cx in SIGNS:
        sums, diffs = [], []
        for cy in SIGNS:
            lo, mid, hi = [saved(number(cx, cy, cz)) for cz in SIGNS]
            sums.append(lo + mid + hi)
            diffs.append(hi - lo)
        totals.append(sums[0] + sums[1] + sums[2])
        along_y.append(sums[2] - sums[0])
        along_z.append(diffs[0] + diffs[1] + diffs[2])
    density = totals[0] + totals[1] + totals[2]
    momentum = (
        totals[2] - totals[0],
        along_y[0] + along_y[1] + along_y[2],
        along_z[0] + along_z[1] + along_z[2],
    )
    return [part / density for part in momentum]


def moments_of(pull):
    rows = []
    for cx in SIGNS:
        plain, first, second = [], [], []
        for cy in SIGNS:
            lo, mid, hi = [pull(cx, cy, cz) for cz in SIGNS]
            both = lo + hi
            plain.append(mid + 0.25 * both)
            first.append(hi - lo)
            second.append(both)
        pair = plain[0] + plain[2]
        rows.append(
            (
                plain[1] + 0.25 * pair,
                plain[2] - plain[0],
                pair,
                first[1] + 0.25 * (first[0] + first[2]),
                first[2] - first[0],
                second[1] + 0.25 * (second[0] + second[2]),
            )
        )
    even = [rows[1][n] + 0.25 * (rows[0][n] + rows[2][n]) for n in range(6)]
    zero = (8.0 / 27.0) * even[0]
    along = (
        (2.0 / 27.0) * (rows[2][0] - rows[0][0]),
        (2.0 / 27.0) * even[1],
        (2.0 / 27.0) * even[3],
    )
    square = (
        (2.0 / 27.0) * (rows[2][0] + rows[0][0]),
        (2.0 / 27.0) * even[2],
        (2.0 / 27.0) * even[5],
    )
    mixed = (
        (1.0 / 54.0) * (rows[2][1] - rows[0][1]),
        (1.0 / 54.0) * (rows[2][3] - rows[0][3]),
        (1.0 / 54.0) * even[4],
    )
    return zero, along, square, mixed


def collide(pull, velocity, solid, store):
    zero, along, square, mixed = moments_of(lambda cx, cy, cz: pull(number(cx, cy, cz)))
    ux, uy, uz = velocity
    xy, xz, yz = mixed
    quadratic = (
        ux * ux * square[0]
        + uy * uy * square[1]
        + uz * uz * square[2]
        + 2.0 * (ux * uy * xy + ux * uz * xz + uy * uz * yz)
    )
    speed = ux * ux + uy * uy + uz * uz
    scalar = OMEGA * (zero * (1.0 + 1.5 * speed) - 4.5 * quadratic)
    vec_x = OMEGA * (3.0 * along[0] + 9.0 * (square[0] * ux + xy * uy + xz * uz) - 3.0 * ux * zero)
    vec_y = OMEGA * (3.0 * along[1] + 9.0 * (xy * ux + square[1] * uy + yz * uz) - 3.0 * uy * zero)
    vec_z = OMEGA * (3.0 * along[2] + 9.0 * (xz * ux + yz * uy + square[2] * uz) - 3.0 * uz * zero)
    wall = solid == 1
    for cx in SIGNS:
        base = scalar if cx == 0 else (scalar + vec_x if cx > 0 else scalar - vec_x)
        for cy in SIGNS:
            inner = base if cy == 0 else (base + vec_y if cy > 0 else base - vec_y)
            for cz in SIGNS:
                full = inner if cz == 0 else (inner + vec_z if cz > 0 else inner - vec_z)
                i = number(cx, cy, cz)
                store(i, jnp.where(wall, pull(26 - i), (1.0 - OMEGA) * pull(i) + full))


def pull_plane(tile_of, edges_of, pulled, raw=None):
    lane = lanes()
    for cx in SIGNS:
        low_edge, high_edge, start = edges_of(cx)
        for cy in SIGNS:
            place = start + 3 * (cx + 1) + cy + 1
            for cz in SIGNS:
                i = number(cx, cy, cz)
                source = tile_of(i, cx)
                tile = source
                if cz == -1:
                    edge = pltpu.roll(low_edge, 128 - place, 1)
                    tile = jnp.where(lane == 0, edge, pltpu.roll(source, 1, 1))
                elif cz == 1:
                    edge = pltpu.roll(high_edge, 127 - place, 1)
                    tile = jnp.where(lane == 127, edge, pltpu.roll(source, 127, 1))
                if raw is not None and cx == 1:
                    tile = jnp.where(raw, source, tile)
                pulled[i] = shift_y(tile, cy)


def inner_kernel(step, last, adj, vel, solid, first, second, *rest):
    if last:
        out, made, pulled, sems = rest
    else:
        out, low_out, high_out, made, pulled, sems = rest
    extent_x = adj.shape[1]
    low_edge, high_edge = edges_from(first, second)

    def save(x):
        return pltpu.make_async_copy(made.at[x - 1], out.at[:, x], sems.at[x - 1])

    def plane(x, carry):
        pull_plane(
            lambda i, cx: adj[i, x + cx],
            lambda cx: (low_edge, high_edge, (x + 1 + cx) * 9),
            pulled,
        )

        def store(i, tile):
            made[x - 1, i] = tile

        velocity = [vel[step, a, x] for a in range(3)]
        collide(lambda i: pulled[i], velocity, solid[0, x], store)
        save(x).start()
        if last:
            return carry
        return pack_columns(lambda i: made[x - 1, i], x, *carry)

    zero = jnp.zeros((16, 128), jnp.float32)
    carry = lax.fori_loop(1, extent_x - 1, plane, 0 if last else (zero, zero))
    if not last:
        low_out[...], high_out[...] = carry
    lax.fori_loop(1, extent_x - 1, lambda x, c: (save(x).wait(), c)[1], 0)


def outer_kernel(step, last, adj, vel, solid, first, second, side, cross, *rest):
    if last:
        _, out, made, pulled, sems = rest
    else:
        _, low_in, high_in, out, first_out, second_out, made, pulled, sems = rest
    extent_x = adj.shape[1]
    low_edge, high_edge = edges_from(first, second)
    even = is_even("gx")
    interface = lax.axis_index("gx") == lax.axis_size("gx") - 1
    below = lambda j: jnp.where(even, cross[j], side[j])
    above = lambda j: jnp.where(even, side[j], cross[j])

    def plane(n, x, tile_of, edges_of, raw):
        pull_plane(tile_of, edges_of, pulled, raw)

        def store(i, tile):
            made[n, i] = tile

        velocity = [vel[step, a, x] for a in range(3)]
        collide(lambda i: pulled[i], velocity, solid[0, x], store)
        save = pltpu.make_async_copy(made.at[n], out.at[:, x], sems.at[n])
        save.start()
        return save

    final = extent_x - 1
    saves = [
        plane(
            0,
            0,
            lambda i, cx: below(i) if cx == -1 else adj[i, cx],
            lambda cx: (
                (below(9), below(10), extent_x * 9)
                if cx == -1
                else (low_edge, high_edge, (1 + cx) * 9)
            ),
            None,
        ),
        plane(
            1,
            final,
            lambda i, cx: above(i - 18) if cx == 1 else adj[i, final + cx],
            lambda cx: (
                (above(9), above(10), 9)
                if cx == 1
                else (low_edge, high_edge, (final + 1 + cx) * 9)
            ),
            interface,
        ),
    ]
    if not last:
        low, high = low_in[...], high_in[...]
        low, high = pack_columns(lambda i: made[0, i], 0, low, high)
        low, high = pack_columns(lambda i: made[1, i], final, low, high)
        write_messages(lambda j: made[1, j], low, high, first_out, second_out)
    for save in saves:
        save.wait()


def tile_shape(*lead):
    return jax.ShapeDtypeStruct(lead + (16, 128), jnp.float32)


def in_vmem(n):
    return [pl.BlockSpec(memory_space=pltpu.VMEM)] * n


def in_any(n):
    return [pl.BlockSpec(memory_space=pl.ANY)] * n


def body(sizes, adjoint, saved, solid, band_device, band_cell, band_weight):
    zones, widths, count = sizes
    field = adjoint[0]
    extent_x = field.shape[1]
    axes = ("zone", "gx", "yz")
    params = pltpu.CompilerParams(vmem_limit_bytes=VMEM_LIMIT)

    def send(values, target):
        flat = lambda zone, gx, yz: (zone * widths + gx) * count + yz
        pairs = []
        for zone in range(zones):
            for gx in range(widths):
                for yz in range(count):
                    to = target(zone, gx, yz)
                    if to is not None:
                        pairs.append((flat(zone, gx, yz), flat(*to)))
        return lax.ppermute(values, axes, pairs)

    def partner_of(place, shift):
        return place + 1 if (place + shift) % 2 == 0 else place - 1

    def along_z(shift):
        return lambda zone, gx, yz: (zone, gx, partner_of(yz, shift) % count)

    def hop_z(hop):
        return lambda zone, gx, yz: (zone, gx, (yz + hop) % count) if gx == widths - 1 else None

    def flip(zone, gx, yz):
        return (1 - zone, gx, yz) if gx == widths - 1 else None

    def along_x(zone, gx, yz):
        return (zone, partner_of(gx, 0), yz)

    def along_x_or_flip(zone, gx, yz):
        if gx == widths - 1:
            return (1 - zone, gx, yz)
        return None if gx == 0 else (zone, partner_of(gx, 1), yz)

    code = band_device[0] * 128 + band_cell[0]
    info = jnp.concatenate(
        [jnp.moveaxis(code.astype(jnp.float32), -1, 0), jnp.moveaxis(band_weight[0], -1, 0)]
    )
    info = send(info, flip)
    first, second = pl.pallas_call(
        pack_kernel,
        out_shape=(tile_shape(10),) * 2,
        in_specs=in_vmem(1),
        out_specs=tuple(in_vmem(2)),
        compiler_params=params,
    )(field)
    vel = pl.pallas_call(
        velocity_kernel,
        out_shape=tile_shape(2, 3, extent_x),
        in_specs=in_any(1),
        out_specs=in_vmem(1)[0],
        scratch_shapes=[
            pltpu.VMEM((2 * extent_x, 27, 16, 128), jnp.float32),
            pltpu.SemaphoreType.DMA((2 * extent_x,)),
        ],
        compiler_params=params,
    )(saved)
    for step in (1, 0):
        last = step == 0
        own = first
        first = send(own, along_z(0))
        second = send(second, along_z(1))
        others = [send(own, hop_z(hop)) for hop in range(2, count - 1)]
        side = pl.pallas_call(
            side_kernel,
            out_shape=tile_shape(11),
            in_specs=in_vmem(3),
            out_specs=in_vmem(1)[0],
            compiler_params=params,
        )(field, first, second)
        side = send(side, along_x)
        cross = pl.pallas_call(
            lambda *refs: cross_kernel(count, *refs),
            out_shape=tile_shape(11),
            in_specs=in_vmem(2 + count),
            out_specs=in_vmem(1)[0],
            compiler_params=params,
        )(field, own, first, second, *others, info)
        cross = send(cross, along_x_or_flip)
        columns = () if last else (tile_shape(),) * 2
        inner = pl.pallas_call(
            lambda *refs, step=step, last=last: inner_kernel(step, last, *refs),
            out_shape=(tile_shape(27, extent_x), *columns),
            in_specs=in_vmem(5),
            out_specs=tuple(in_any(1) + in_vmem(len(columns))),
            scratch_shapes=[
                pltpu.VMEM((extent_x - 2, 27, 16, 128), jnp.float32),
                pltpu.VMEM((27, 16, 128), jnp.float32),
                pltpu.SemaphoreType.DMA((extent_x - 2,)),
            ],
            compiler_params=params,
        )(field, vel, solid, first, second)
        messages = () if last else (tile_shape(10),) * 2
        outer = pl.pallas_call(
            lambda *refs, step=step, last=last: outer_kernel(step, last, *refs),
            out_shape=(tile_shape(27, extent_x), *messages),
            in_specs=in_vmem(7) + in_any(1) + in_vmem(len(columns)),
            out_specs=tuple(in_any(1) + in_vmem(len(messages))),
            scratch_shapes=[
                pltpu.VMEM((2, 27, 16, 128), jnp.float32),
                pltpu.VMEM((27, 16, 128), jnp.float32),
                pltpu.SemaphoreType.DMA((2,)),
            ],
            input_output_aliases={7: 0},
            compiler_params=params,
        )(field, vel, solid, first, second, side, cross, *inner)
        if last:
            field = outer[0]
        else:
            field, first, second = outer
    return field[None]


def solution(mesh):
    sizes = tuple(mesh.shape[axis] for axis in ("zone", "gx", "yz"))
    in_specs = (
        P("zone", None, "gx", None, "yz"),
        P(None, "zone", None, "gx", None, "yz"),
        P("zone", "gx", None, "yz"),
        P("zone", None, "yz", None),
        P("zone", None, "yz", None),
        P("zone", None, "yz", None),
    )
    out_specs = P("zone", None, "gx", None, "yz")
    return jax.shard_map(
        lambda *args: body(sizes, *args),
        mesh=mesh,
        in_specs=in_specs,
        out_specs=out_specs,
        check_vma=False,
    )
```

```python
import jax
import jax.numpy as jnp
import numpy as np
from jax import lax
from jax.experimental import pallas as pl
from jax.experimental.pallas import tpu as pltpu
from jax.sharding import PartitionSpec as P

OMEGA = 1.6
VMEM_LIMIT = 20 * 1024 * 1024
SIGNS = (-1, 0, 1)


def number(cx, cy, cz):
    return 9 * (cx + 1) + 3 * (cy + 1) + (cz + 1)


def lanes():
    return lax.broadcasted_iota(jnp.int32, (16, 128), 1)


def shift_y(tile, cy):
    if cy == 0:
        return tile
    row = lax.broadcasted_iota(jnp.int32, tile.shape, 0)
    if cy == 1:
        return jnp.where(row == 15, 0.0, pltpu.roll(tile, 15, 0))
    return jnp.where(row == 0, 0.0, pltpu.roll(tile, 1, 0))


def pack_columns(planes, x, low, high):
    lane = lanes()
    for slot in range(9):
        place = (x + 1) * 9 + slot
        here = lane == place
        low = jnp.where(here, pltpu.roll(planes(3 * slot + 2), place, 1), low)
        high = jnp.where(here, pltpu.roll(planes(3 * slot), place + 1, 1), high)
    return low, high


def is_even(axis):
    return lax.rem(lax.axis_index(axis), 2) == 0


def write_edges(low, high, first, second):
    even = is_even("yz")
    first[...] = jnp.where(even, high, low)
    second[...] = jnp.where(even, low, high)


def edges_from(first, second):
    even = is_even("yz")
    me, count = lax.axis_index("yz"), lax.axis_size("yz")
    low = jnp.where(me == 0, 0.0, jnp.where(even, second[...], first[...]))
    high = jnp.where(me == count - 1, 0.0, jnp.where(even, first[...], second[...]))
    return low, high


def top_kernel(adj, out, sem):
    copy = pltpu.make_async_copy(adj.at[pl.ds(0, 9), adj.shape[1] - 1], out, sem)
    copy.start()
    copy.wait()


def pack_kernel(adj, first_out, second_out):
    zero = jnp.zeros((16, 128), jnp.float32)
    low, high = lax.fori_loop(
        0, adj.shape[1], lambda x, c: pack_columns(lambda i: adj[i, x], x, *c), (zero, zero)
    )
    write_edges(low, high, first_out, second_out)


def velocity_kernel(saved, out, kept, sems):
    steps, _, _, extent_x = saved.shape[:4]

    def load(n):
        step, x = n // extent_x, lax.rem(n, extent_x)
        return pltpu.make_async_copy(saved.at[step, 0, :, x], kept.at[n], sems.at[n])

    total = steps * extent_x
    lax.fori_loop(0, total, lambda n, c: (load(n).start(), c)[1], 0)

    def one(n, carry):
        load(n).wait()
        for a, tile in enumerate(velocity_of(lambda i: kept[n, i])):
            out[n // extent_x, a, lax.rem(n, extent_x)] = tile
        return carry

    lax.fori_loop(0, total, one, 0)


def side_kernel(adj, first, second, out):
    extent_x = adj.shape[1]
    even = is_even("gx")
    for j in range(9):
        out[j] = jnp.where(even, adj[j, extent_x - 1], adj[18 + j, 0])
    out[9], out[10] = edges_from(first, second)


def cross_kernel(count, *refs):
    adj, low_side, high_side, own = refs[:4]
    blocks = refs[3 : 3 + count]
    info, _, out = refs[3 + count :]
    extent_x = adj.shape[1]
    interface = lax.axis_index("gx") == lax.axis_size("gx") - 1
    out[9], out[10] = edges_from(low_side, high_side)

    @pl.when(jnp.logical_not(interface))
    def _():
        even = is_even("gx")
        for j in range(9):
            out[j] = jnp.where(even, adj[18 + j, 0], adj[j, extent_x - 1])

    @pl.when(interface)
    def _():
        me = lax.axis_index("yz")
        even = is_even("yz")
        rows = (0, 8)
        spots, picks = {}, {}
        for r in rows:
            for k in range(2):
                code = info[k, r : r + 8].astype(jnp.int32)
                ahead = lax.rem(code // 128 - me + count, count)
                spots[r, k] = lax.rem(code, 128)
                turned = jnp.where(even, ahead, lax.rem(count - ahead, count))
                masks = [turned == 1, turned == count - 1]
                masks += [ahead == count - hop for hop in range(2, count - 1)]
                picks[r, k] = masks
        for j in range(9):
            halves = []
            for r in rows:
                total = jnp.zeros((8, 128), jnp.float32)
                for k in range(2):
                    tiles = [ref[j, r : r + 8] for ref in blocks]
                    got = [jnp.take_along_axis(tile, spots[r, k], axis=1) for tile in tiles]
                    picked = got[0]
                    for mask, value in zip(picks[r, k], got[1:]):
                        picked = jnp.where(mask, value, picked)
                    total = total + picked * info[2 + k, r : r + 8]
                halves.append(total)
            out[j] = jnp.concatenate(halves, axis=0)


def velocity_of(saved):
    totals, along_y, along_z = [], [], []
    for cx in SIGNS:
        sums, diffs = [], []
        for cy in SIGNS:
            lo, mid, hi = [saved(number(cx, cy, cz)) for cz in SIGNS]
            sums.append(lo + mid + hi)
            diffs.append(hi - lo)
        totals.append(sums[0] + sums[1] + sums[2])
        along_y.append(sums[2] - sums[0])
        along_z.append(diffs[0] + diffs[1] + diffs[2])
    density = totals[0] + totals[1] + totals[2]
    momentum = (
        totals[2] - totals[0],
        along_y[0] + along_y[1] + along_y[2],
        along_z[0] + along_z[1] + along_z[2],
    )
    return [part / density for part in momentum]


def moments_of(pull):
    rows = []
    for cx in SIGNS:
        plain, first, second = [], [], []
        for cy in SIGNS:
            lo, mid, hi = [pull(cx, cy, cz) for cz in SIGNS]
            both = lo + hi
            plain.append(mid + 0.25 * both)
            first.append(hi - lo)
            second.append(both)
        pair = plain[0] + plain[2]
        rows.append(
            (
                plain[1] + 0.25 * pair,
                plain[2] - plain[0],
                pair,
                first[1] + 0.25 * (first[0] + first[2]),
                first[2] - first[0],
                second[1] + 0.25 * (second[0] + second[2]),
            )
        )
    even = [rows[1][n] + 0.25 * (rows[0][n] + rows[2][n]) for n in range(6)]
    zero = (8.0 / 27.0) * even[0]
    along = (
        (2.0 / 27.0) * (rows[2][0] - rows[0][0]),
        (2.0 / 27.0) * even[1],
        (2.0 / 27.0) * even[3],
    )
    square = (
        (2.0 / 27.0) * (rows[2][0] + rows[0][0]),
        (2.0 / 27.0) * even[2],
        (2.0 / 27.0) * even[5],
    )
    mixed = (
        (1.0 / 54.0) * (rows[2][1] - rows[0][1]),
        (1.0 / 54.0) * (rows[2][3] - rows[0][3]),
        (1.0 / 54.0) * even[4],
    )
    return zero, along, square, mixed


def collide(pull, velocity, solid, store):
    zero, along, square, mixed = moments_of(lambda cx, cy, cz: pull(number(cx, cy, cz)))
    ux, uy, uz = velocity
    xy, xz, yz = mixed
    quadratic = (
        ux * ux * square[0]
        + uy * uy * square[1]
        + uz * uz * square[2]
        + 2.0 * (ux * uy * xy + ux * uz * xz + uy * uz * yz)
    )
    speed = ux * ux + uy * uy + uz * uz
    scalar = OMEGA * (zero * (1.0 + 1.5 * speed) - 4.5 * quadratic)
    vec_x = OMEGA * (3.0 * along[0] + 9.0 * (square[0] * ux + xy * uy + xz * uz) - 3.0 * ux * zero)
    vec_y = OMEGA * (3.0 * along[1] + 9.0 * (xy * ux + square[1] * uy + yz * uz) - 3.0 * uy * zero)
    vec_z = OMEGA * (3.0 * along[2] + 9.0 * (xz * ux + yz * uy + square[2] * uz) - 3.0 * uz * zero)
    wall = solid == 1
    for cx in SIGNS:
        base = scalar if cx == 0 else (scalar + vec_x if cx > 0 else scalar - vec_x)
        for cy in SIGNS:
            inner = base if cy == 0 else (base + vec_y if cy > 0 else base - vec_y)
            for cz in SIGNS:
                full = inner if cz == 0 else (inner + vec_z if cz > 0 else inner - vec_z)
                i = number(cx, cy, cz)
                store(i, jnp.where(wall, pull(26 - i), (1.0 - OMEGA) * pull(i) + full))


def pull_plane(tile_of, edges_of, pulled, raw=None):
    lane = lanes()
    for cx in SIGNS:
        low_edge, high_edge, start = edges_of(cx)
        for cy in SIGNS:
            place = start + 3 * (cx + 1) + cy + 1
            for cz in SIGNS:
                i = number(cx, cy, cz)
                source = tile_of(i, cx)
                tile = source
                if cz == -1:
                    edge = pltpu.roll(low_edge, 128 - place, 1)
                    tile = jnp.where(lane == 0, edge, pltpu.roll(source, 1, 1))
                elif cz == 1:
                    edge = pltpu.roll(high_edge, 127 - place, 1)
                    tile = jnp.where(lane == 127, edge, pltpu.roll(source, 127, 1))
                if raw is not None and cx == 1:
                    tile = jnp.where(raw, source, tile)
                pulled[i] = shift_y(tile, cy)


def inner_kernel(step, last, adj, vel, solid, first, second, _, *rest):
    if last:
        out, made, pulled, sems = rest
    else:
        out, low_out, high_out, made, pulled, sems = rest
    extent_x = adj.shape[1]
    low_edge, high_edge = edges_from(first, second)

    def save(x):
        return pltpu.make_async_copy(made.at[x - 1], out.at[:, x], sems.at[x - 1])

    def plane(x, carry):
        pull_plane(
            lambda i, cx: adj[i, x + cx],
            lambda cx: (low_edge, high_edge, (x + 1 + cx) * 9),
            pulled,
        )

        def store(i, tile):
            made[x - 1, i] = tile

        velocity = [vel[step, a, x] for a in range(3)]
        collide(lambda i: pulled[i], velocity, solid[0, x], store)
        save(x).start()
        if last:
            return carry
        return pack_columns(lambda i: made[x - 1, i], x, *carry)

    zero = jnp.zeros((16, 128), jnp.float32)
    carry = lax.fori_loop(1, extent_x - 1, plane, 0 if last else (zero, zero))
    if not last:
        low_out[...], high_out[...] = carry
    lax.fori_loop(1, extent_x - 1, lambda x, c: (save(x).wait(), c)[1], 0)


def outer_plane(n, x, step, adj, vel, solid, edges, side, cross, out, made, pulled, sems):
    extent_x = adj.shape[1]
    even = is_even("gx")
    if x == 0:
        ghost, start, raw = -1, extent_x * 9, None
        beyond = lambda j: jnp.where(even, cross[j], side[j])
    else:
        ghost, start = 1, 9
        raw = lax.axis_index("gx") == lax.axis_size("gx") - 1
        beyond = lambda j: jnp.where(even, side[j], cross[j])
    pull_plane(
        lambda i, cx: beyond(i % 9) if cx == ghost else adj[i, x + cx],
        lambda cx: (beyond(9), beyond(10), start) if cx == ghost else (*edges, (x + 1 + cx) * 9),
        pulled,
        raw,
    )

    def store(i, tile):
        made[n, i] = tile

    velocity = [vel[step, a, x] for a in range(3)]
    collide(lambda i: pulled[i], velocity, solid[0, x], store)
    save = pltpu.make_async_copy(made.at[n], out.at[:, x], sems.at[n])
    save.start()
    return save


def top_plane_kernel(step, adj, vel, solid, first, second, side, cross, low_in, high_in, _, *rest):
    out, top_out, low_out, high_out, made, pulled, sems = rest
    final = adj.shape[1] - 1
    edges = edges_from(first, second)
    save = outer_plane(0, final, step, adj, vel, solid, edges, side, cross, out, made, pulled, sems)
    for j in range(9):
        top_out[j] = made[0, j]
    low_out[...], high_out[...] = pack_columns(lambda i: made[0, i], final, low_in[...], high_in[...])
    save.wait()


def bottom_plane_kernel(step, adj, vel, solid, first, second, side, cross, low_in, high_in, _, *rest):
    out, first_out, second_out, made, pulled, sems = rest
    edges = edges_from(first, second)
    save = outer_plane(0, 0, step, adj, vel, solid, edges, side, cross, out, made, pulled, sems)
    low, high = pack_columns(lambda i: made[0, i], 0, low_in[...], high_in[...])
    write_edges(low, high, first_out, second_out)
    save.wait()


def last_planes_kernel(step, adj, vel, solid, first, second, side, cross, _, *rest):
    out, made, pulled, sems = rest
    edges = edges_from(first, second)
    saves = [
        outer_plane(n, x, step, adj, vel, solid, edges, side, cross, out, made, pulled, sems)
        for n, x in enumerate((0, adj.shape[1] - 1))
    ]
    for save in saves:
        save.wait()


def tile_shape(*lead):
    return jax.ShapeDtypeStruct(lead + (16, 128), jnp.float32)


def in_vmem(n):
    return [pl.BlockSpec(memory_space=pltpu.VMEM)] * n


def in_any(n):
    return [pl.BlockSpec(memory_space=pl.ANY)] * n


def body(sizes, adjoint, saved, solid, band_device, band_cell, band_weight):
    zones, widths, count = sizes
    field = adjoint[0]
    extent_x = field.shape[1]
    axes = ("zone", "gx", "yz")
    params = pltpu.CompilerParams(vmem_limit_bytes=VMEM_LIMIT)

    def send(values, target):
        flat = lambda zone, gx, yz: (zone * widths + gx) * count + yz
        pairs = []
        for zone in range(zones):
            for gx in range(widths):
                for yz in range(count):
                    to = target(zone, gx, yz)
                    if to is not None:
                        pairs.append((flat(zone, gx, yz), flat(*to)))
        return lax.ppermute(values, axes, pairs)

    def partner_of(place, shift):
        return place + 1 if (place + shift) % 2 == 0 else place - 1

    def along_z(shift):
        return lambda zone, gx, yz: (zone, gx, partner_of(yz, shift) % count)

    def at_interface(target):
        return lambda zone, gx, yz: target(zone, gx, yz) if gx == widths - 1 else None

    def hop_z(hop):
        return lambda zone, gx, yz: (zone, gx, (yz + hop) % count)

    def flip(zone, gx, yz):
        return (1 - zone, gx, yz)

    def along_x(zone, gx, yz):
        return (zone, partner_of(gx, 0), yz)

    def along_x_or_flip(zone, gx, yz):
        if gx == widths - 1:
            return (1 - zone, gx, yz)
        return None if gx == 0 else (zone, partner_of(gx, 1), yz)

    code = band_device[0] * 128 + band_cell[0]
    info = jnp.concatenate(
        [jnp.moveaxis(code.astype(jnp.float32), -1, 0), jnp.moveaxis(band_weight[0], -1, 0)]
    )
    info = send(info, at_interface(flip))
    top = pl.pallas_call(
        top_kernel,
        out_shape=tile_shape(9),
        in_specs=[pl.BlockSpec(memory_space=pltpu.HBM)],
        out_specs=in_vmem(1)[0],
        scratch_shapes=[pltpu.SemaphoreType.DMA(())],
        compiler_params=params,
    )(field)
    first, second = pl.pallas_call(
        pack_kernel,
        out_shape=(tile_shape(),) * 2,
        in_specs=in_vmem(1),
        out_specs=tuple(in_vmem(2)),
        compiler_params=params,
    )(field)
    vel = pl.pallas_call(
        velocity_kernel,
        out_shape=tile_shape(2, 3, extent_x),
        in_specs=in_any(1),
        out_specs=in_vmem(1)[0],
        scratch_shapes=[
            pltpu.VMEM((2 * extent_x, 27, 16, 128), jnp.float32),
            pltpu.SemaphoreType.DMA((2 * extent_x,)),
        ],
        compiler_params=params,
    )(saved)
    for step in (1, 0):
        last = step == 0
        blocks = [send(top, at_interface(hop_z(hop))) for hop in range(2, count - 1)]
        blocks = [send(top, at_interface(along_z(shift))) for shift in (0, 1)] + blocks
        first = send(first, along_z(0))
        second = send(second, along_z(1))
        side_out = pl.pallas_call(
            side_kernel,
            out_shape=tile_shape(11),
            in_specs=in_vmem(3),
            out_specs=in_vmem(1)[0],
            compiler_params=params,
        )(field, first, second)
        side = send(side_out, along_x)

        def make_inner(after):
            columns = () if last else (tile_shape(),) * 2
            return pl.pallas_call(
                lambda *refs: inner_kernel(step, last, *refs),
                out_shape=(tile_shape(27, extent_x), *columns),
                in_specs=in_vmem(5) + in_any(1),
                out_specs=tuple(in_any(1) + in_vmem(len(columns))),
                scratch_shapes=[
                    pltpu.VMEM((extent_x - 2, 27, 16, 128), jnp.float32),
                    pltpu.VMEM((27, 16, 128), jnp.float32),
                    pltpu.SemaphoreType.DMA((extent_x - 2,)),
                ],
                compiler_params=params,
            )(field, vel, solid, first, second, after)

        def make_cross(after):
            return pl.pallas_call(
                lambda *refs: cross_kernel(count, *refs),
                out_shape=tile_shape(11),
                in_specs=in_vmem(4 + count) + in_any(1),
                out_specs=in_vmem(1)[0],
                compiler_params=params,
            )(field, first, second, top, *blocks, info, after)

        def make_outer(kernel, planes, given, extra):
            return pl.pallas_call(
                lambda *refs: kernel(step, *refs),
                out_shape=(tile_shape(27, extent_x), *extra),
                in_specs=in_vmem(7 + len(given) - 1) + in_any(1),
                out_specs=tuple(in_any(1) + in_vmem(len(extra))),
                scratch_shapes=[
                    pltpu.VMEM((planes, 27, 16, 128), jnp.float32),
                    pltpu.VMEM((27, 16, 128), jnp.float32),
                    pltpu.SemaphoreType.DMA((planes,)),
                ],
                input_output_aliases={7 + len(given) - 1: 0},
                compiler_params=params,
            )(field, vel, solid, first, second, side, cross, *given)

        if last:
            cross_out = make_cross(side_out)
            cross = send(cross_out, along_x_or_flip)
            (new,) = make_inner(cross_out)
            (field,) = make_outer(last_planes_kernel, 2, (new,), ())
        else:
            new, low, high = make_inner(side_out)
            cross = send(make_cross(low), along_x_or_flip)
            tile = tile_shape()
            new, top, low, high = make_outer(
                top_plane_kernel, 1, (low, high, new), (tile_shape(9), tile, tile)
            )
            field, first, second = make_outer(bottom_plane_kernel, 1, (low, high, new), (tile, tile))
    return field[None]


def solution(mesh):
    sizes = tuple(mesh.shape[axis] for axis in ("zone", "gx", "yz"))
    in_specs = (
        P("zone", None, "gx", None, "yz"),
        P(None, "zone", None, "gx", None, "yz"),
        P("zone", "gx", None, "yz"),
        P("zone", None, "yz", None),
        P("zone", None, "yz", None),
        P("zone", None, "yz", None),
    )
    out_specs = P("zone", None, "gx", None, "yz")
    return jax.shard_map(
        lambda *args: body(sizes, *args),
        mesh=mesh,
        in_specs=in_specs,
        out_specs=out_specs,
        check_vma=False,
    )
```

```python
import jax
import jax.numpy as jnp
import numpy as np
from jax import lax
from jax.experimental import pallas as pl
from jax.experimental.pallas import tpu as pltpu
from jax.sharding import PartitionSpec as P

OMEGA = 1.6
VMEM_LIMIT = 20 * 1024 * 1024
SIGNS = (-1, 0, 1)


def number(cx, cy, cz):
    return 9 * (cx + 1) + 3 * (cy + 1) + (cz + 1)


def lanes():
    return lax.broadcasted_iota(jnp.int32, (16, 128), 1)


def shift_y(tile, cy):
    if cy == 0:
        return tile
    row = lax.broadcasted_iota(jnp.int32, tile.shape, 0)
    if cy == 1:
        return jnp.where(row == 15, 0.0, pltpu.roll(tile, 15, 0))
    return jnp.where(row == 0, 0.0, pltpu.roll(tile, 1, 0))


def pack_columns(planes, x, low, high):
    lane = lanes()
    for slot in range(9):
        place = (x + 1) * 9 + slot
        here = lane == place
        low = jnp.where(here, pltpu.roll(planes(3 * slot + 2), place, 1), low)
        high = jnp.where(here, pltpu.roll(planes(3 * slot), place + 1, 1), high)
    return low, high


def is_even(axis):
    return lax.rem(lax.axis_index(axis), 2) == 0


def write_messages(top, low, high, first, second):
    even = is_even("yz")
    for j in range(9):
        tile = top(j)
        first[j] = tile
        second[j] = tile
    first[9] = jnp.where(even, high, low)
    second[9] = jnp.where(even, low, high)


def edges_from(first, second):
    even = is_even("yz")
    me, count = lax.axis_index("yz"), lax.axis_size("yz")
    low = jnp.where(me == 0, 0.0, jnp.where(even, second[9], first[9]))
    high = jnp.where(me == count - 1, 0.0, jnp.where(even, first[9], second[9]))
    return low, high


def top_kernel(adj, out, sem):
    copy = pltpu.make_async_copy(adj.at[pl.ds(0, 9), adj.shape[1] - 1], out, sem)
    copy.start()
    copy.wait()


def pack_kernel(adj, first_out, second_out):
    zero = jnp.zeros((16, 128), jnp.float32)
    low, high = lax.fori_loop(
        0, adj.shape[1], lambda x, c: pack_columns(lambda i: adj[i, x], x, *c), (zero, zero)
    )
    write_messages(lambda j: adj[j, adj.shape[1] - 1], low, high, first_out, second_out)


def velocity_kernel(saved, out, kept, sems):
    steps, _, _, extent_x = saved.shape[:4]

    def load(n):
        step, x = n // extent_x, lax.rem(n, extent_x)
        return pltpu.make_async_copy(saved.at[step, 0, :, x], kept.at[n], sems.at[n])

    total = steps * extent_x
    lax.fori_loop(0, total, lambda n, c: (load(n).start(), c)[1], 0)

    def one(n, carry):
        load(n).wait()
        for a, tile in enumerate(velocity_of(lambda i: kept[n, i])):
            out[n // extent_x, a, lax.rem(n, extent_x)] = tile
        return carry

    lax.fori_loop(0, total, one, 0)


def side_kernel(adj, first, second, out):
    extent_x = adj.shape[1]
    even = is_even("gx")
    for j in range(9):
        out[j] = jnp.where(even, adj[j, extent_x - 1], adj[18 + j, 0])
    out[9], out[10] = edges_from(first, second)


def cross_kernel(count, *refs):
    adj, own, first, second = refs[:4]
    blocks = refs[1 : 1 + count]
    info, out = refs[1 + count :]
    extent_x = adj.shape[1]
    interface = lax.axis_index("gx") == lax.axis_size("gx") - 1
    out[9], out[10] = edges_from(first, second)

    @pl.when(jnp.logical_not(interface))
    def _():
        even = is_even("gx")
        for j in range(9):
            out[j] = jnp.where(even, adj[18 + j, 0], adj[j, extent_x - 1])

    @pl.when(interface)
    def _():
        me = lax.axis_index("yz")
        even = is_even("yz")
        rows = (0, 8)
        spots, picks = {}, {}
        for r in rows:
            for k in range(2):
                code = info[k, r : r + 8].astype(jnp.int32)
                ahead = lax.rem(code // 128 - me + count, count)
                spots[r, k] = lax.rem(code, 128)
                turned = jnp.where(even, ahead, lax.rem(count - ahead, count))
                masks = [turned == 1, turned == count - 1]
                masks += [ahead == count - hop for hop in range(2, count - 1)]
                picks[r, k] = masks
        for j in range(9):
            halves = []
            for r in rows:
                total = jnp.zeros((8, 128), jnp.float32)
                for k in range(2):
                    tiles = [ref[j, r : r + 8] for ref in blocks]
                    got = [jnp.take_along_axis(tile, spots[r, k], axis=1) for tile in tiles]
                    picked = got[0]
                    for mask, value in zip(picks[r, k], got[1:]):
                        picked = jnp.where(mask, value, picked)
                    total = total + picked * info[2 + k, r : r + 8]
                halves.append(total)
            out[j] = jnp.concatenate(halves, axis=0)


def velocity_of(saved):
    totals, along_y, along_z = [], [], []
    for cx in SIGNS:
        sums, diffs = [], []
        for cy in SIGNS:
            lo, mid, hi = [saved(number(cx, cy, cz)) for cz in SIGNS]
            sums.append(lo + mid + hi)
            diffs.append(hi - lo)
        totals.append(sums[0] + sums[1] + sums[2])
        along_y.append(sums[2] - sums[0])
        along_z.append(diffs[0] + diffs[1] + diffs[2])
    density = totals[0] + totals[1] + totals[2]
    momentum = (
        totals[2] - totals[0],
        along_y[0] + along_y[1] + along_y[2],
        along_z[0] + along_z[1] + along_z[2],
    )
    return [part / density for part in momentum]


def moments_of(pull):
    rows = []
    for cx in SIGNS:
        plain, first, second = [], [], []
        for cy in SIGNS:
            lo, mid, hi = [pull(cx, cy, cz) for cz in SIGNS]
            both = lo + hi
            plain.append(mid + 0.25 * both)
            first.append(hi - lo)
            second.append(both)
        pair = plain[0] + plain[2]
        rows.append(
            (
                plain[1] + 0.25 * pair,
                plain[2] - plain[0],
                pair,
                first[1] + 0.25 * (first[0] + first[2]),
                first[2] - first[0],
                second[1] + 0.25 * (second[0] + second[2]),
            )
        )
    even = [rows[1][n] + 0.25 * (rows[0][n] + rows[2][n]) for n in range(6)]
    zero = (8.0 / 27.0) * even[0]
    along = (
        (2.0 / 27.0) * (rows[2][0] - rows[0][0]),
        (2.0 / 27.0) * even[1],
        (2.0 / 27.0) * even[3],
    )
    square = (
        (2.0 / 27.0) * (rows[2][0] + rows[0][0]),
        (2.0 / 27.0) * even[2],
        (2.0 / 27.0) * even[5],
    )
    mixed = (
        (1.0 / 54.0) * (rows[2][1] - rows[0][1]),
        (1.0 / 54.0) * (rows[2][3] - rows[0][3]),
        (1.0 / 54.0) * even[4],
    )
    return zero, along, square, mixed


def collide(pull, velocity, solid, store):
    zero, along, square, mixed = moments_of(lambda cx, cy, cz: pull(number(cx, cy, cz)))
    ux, uy, uz = velocity
    xy, xz, yz = mixed
    quadratic = (
        ux * ux * square[0]
        + uy * uy * square[1]
        + uz * uz * square[2]
        + 2.0 * (ux * uy * xy + ux * uz * xz + uy * uz * yz)
    )
    speed = ux * ux + uy * uy + uz * uz
    scalar = OMEGA * (zero * (1.0 + 1.5 * speed) - 4.5 * quadratic)
    vec_x = OMEGA * (3.0 * along[0] + 9.0 * (square[0] * ux + xy * uy + xz * uz) - 3.0 * ux * zero)
    vec_y = OMEGA * (3.0 * along[1] + 9.0 * (xy * ux + square[1] * uy + yz * uz) - 3.0 * uy * zero)
    vec_z = OMEGA * (3.0 * along[2] + 9.0 * (xz * ux + yz * uy + square[2] * uz) - 3.0 * uz * zero)
    wall = solid == 1
    for cx in SIGNS:
        base = scalar if cx == 0 else (scalar + vec_x if cx > 0 else scalar - vec_x)
        for cy in SIGNS:
            inner = base if cy == 0 else (base + vec_y if cy > 0 else base - vec_y)
            for cz in SIGNS:
                full = inner if cz == 0 else (inner + vec_z if cz > 0 else inner - vec_z)
                i = number(cx, cy, cz)
                store(i, jnp.where(wall, pull(26 - i), (1.0 - OMEGA) * pull(i) + full))


def pull_plane(tile_of, edges_of, pulled, raw=None):
    lane = lanes()
    for cx in SIGNS:
        low_edge, high_edge, start = edges_of(cx)
        for cy in SIGNS:
            place = start + 3 * (cx + 1) + cy + 1
            for cz in SIGNS:
                i = number(cx, cy, cz)
                source = tile_of(i, cx)
                tile = source
                if cz == -1:
                    edge = pltpu.roll(low_edge, 128 - place, 1)
                    tile = jnp.where(lane == 0, edge, pltpu.roll(source, 1, 1))
                elif cz == 1:
                    edge = pltpu.roll(high_edge, 127 - place, 1)
                    tile = jnp.where(lane == 127, edge, pltpu.roll(source, 127, 1))
                if raw is not None and cx == 1:
                    tile = jnp.where(raw, source, tile)
                pulled[i] = shift_y(tile, cy)


def inner_kernel(step, last, adj, vel, solid, first, second, *rest):
    if last:
        out, made, pulled, sems = rest
    else:
        low_in, high_in, _, out, low_out, high_out, made, pulled, sems = rest
    extent_x = adj.shape[1]
    low_edge, high_edge = edges_from(first, second)

    def save(x):
        return pltpu.make_async_copy(made.at[x - 1], out.at[:, x], sems.at[x - 1])

    def plane(x, carry):
        pull_plane(
            lambda i, cx: adj[i, x + cx],
            lambda cx: (low_edge, high_edge, (x + 1 + cx) * 9),
            pulled,
        )

        def store(i, tile):
            made[x - 1, i] = tile

        velocity = [vel[step, a, x] for a in range(3)]
        collide(lambda i: pulled[i], velocity, solid[0, x], store)
        save(x).start()
        if last:
            return carry
        return pack_columns(lambda i: made[x - 1, i], x, *carry)

    carry = 0 if last else (low_in[...], high_in[...])
    carry = lax.fori_loop(1, extent_x - 1, plane, carry)
    if not last:
        low_out[...], high_out[...] = carry
    lax.fori_loop(1, extent_x - 1, lambda x, c: (save(x).wait(), c)[1], 0)


def outer_plane(n, x, step, adj, vel, solid, edges, side, cross, out, made, pulled, sems):
    extent_x = adj.shape[1]
    even = is_even("gx")
    if x == 0:
        ghost, start, raw = -1, extent_x * 9, None
        beyond = lambda j: jnp.where(even, cross[j], side[j])
    else:
        ghost, start = 1, 9
        raw = lax.axis_index("gx") == lax.axis_size("gx") - 1
        beyond = lambda j: jnp.where(even, side[j], cross[j])
    pull_plane(
        lambda i, cx: beyond(i % 9) if cx == ghost else adj[i, x + cx],
        lambda cx: (beyond(9), beyond(10), start) if cx == ghost else (*edges, (x + 1 + cx) * 9),
        pulled,
        raw,
    )

    def store(i, tile):
        made[n, i] = tile

    velocity = [vel[step, a, x] for a in range(3)]
    collide(lambda i: pulled[i], velocity, solid[0, x], store)
    save = pltpu.make_async_copy(made.at[n], out.at[:, x], sems.at[n])
    save.start()
    return save


def top_plane_kernel(step, adj, vel, solid, first, second, side, cross, *rest):
    out, top_out, low_out, high_out, made, pulled, sems = rest
    final = adj.shape[1] - 1
    edges = edges_from(first, second)
    save = outer_plane(0, final, step, adj, vel, solid, edges, side, cross, out, made, pulled, sems)
    for j in range(9):
        top_out[j] = made[0, j]
    zero = jnp.zeros((16, 128), jnp.float32)
    low_out[...], high_out[...] = pack_columns(lambda i: made[0, i], final, zero, zero)
    save.wait()


def bottom_plane_kernel(step, adj, vel, solid, first, second, side, cross, *rest):
    low_in, high_in, top, *_, out, first_out, second_out, made, pulled, sems = rest
    edges = edges_from(first, second)
    save = outer_plane(0, 0, step, adj, vel, solid, edges, side, cross, out, made, pulled, sems)
    low, high = pack_columns(lambda i: made[0, i], 0, low_in[...], high_in[...])
    write_messages(lambda j: top[j], low, high, first_out, second_out)
    save.wait()


def last_planes_kernel(step, adj, vel, solid, first, second, side, cross, _, *rest):
    out, made, pulled, sems = rest
    edges = edges_from(first, second)
    saves = [
        outer_plane(n, x, step, adj, vel, solid, edges, side, cross, out, made, pulled, sems)
        for n, x in enumerate((0, adj.shape[1] - 1))
    ]
    for save in saves:
        save.wait()


def tile_shape(*lead):
    return jax.ShapeDtypeStruct(lead + (16, 128), jnp.float32)


def in_vmem(n):
    return [pl.BlockSpec(memory_space=pltpu.VMEM)] * n


def in_any(n):
    return [pl.BlockSpec(memory_space=pl.ANY)] * n


def body(sizes, adjoint, saved, solid, band_device, band_cell, band_weight):
    zones, widths, count = sizes
    field = adjoint[0]
    extent_x = field.shape[1]
    axes = ("zone", "gx", "yz")
    params = pltpu.CompilerParams(vmem_limit_bytes=VMEM_LIMIT)

    def send(values, target):
        flat = lambda zone, gx, yz: (zone * widths + gx) * count + yz
        pairs = []
        for zone in range(zones):
            for gx in range(widths):
                for yz in range(count):
                    to = target(zone, gx, yz)
                    if to is not None:
                        pairs.append((flat(zone, gx, yz), flat(*to)))
        return lax.ppermute(values, axes, pairs)

    def partner_of(place, shift):
        return place + 1 if (place + shift) % 2 == 0 else place - 1

    def along_z(shift):
        return lambda zone, gx, yz: (zone, gx, partner_of(yz, shift) % count)

    def at_interface(target):
        return lambda zone, gx, yz: target(zone, gx, yz) if gx == widths - 1 else None

    def hop_z(hop):
        return lambda zone, gx, yz: (zone, gx, (yz + hop) % count)

    def flip(zone, gx, yz):
        return (1 - zone, gx, yz)

    def along_x(zone, gx, yz):
        return (zone, partner_of(gx, 0), yz)

    def along_x_or_flip(zone, gx, yz):
        if gx == widths - 1:
            return (1 - zone, gx, yz)
        return None if gx == 0 else (zone, partner_of(gx, 1), yz)

    def far_blocks(plane):
        return [send(plane, at_interface(hop_z(hop))) for hop in range(2, count - 1)]

    code = band_device[0] * 128 + band_cell[0]
    info = jnp.concatenate(
        [jnp.moveaxis(code.astype(jnp.float32), -1, 0), jnp.moveaxis(band_weight[0], -1, 0)]
    )
    info = send(info, at_interface(flip))
    top = pl.pallas_call(
        top_kernel,
        out_shape=tile_shape(9),
        in_specs=[pl.BlockSpec(memory_space=pltpu.HBM)],
        out_specs=in_vmem(1)[0],
        scratch_shapes=[pltpu.SemaphoreType.DMA(())],
        compiler_params=params,
    )(field)
    first, second = pl.pallas_call(
        pack_kernel,
        out_shape=(tile_shape(10),) * 2,
        in_specs=in_vmem(1),
        out_specs=tuple(in_vmem(2)),
        compiler_params=params,
    )(field)
    vel = pl.pallas_call(
        velocity_kernel,
        out_shape=tile_shape(2, 3, extent_x),
        in_specs=in_any(1),
        out_specs=in_vmem(1)[0],
        scratch_shapes=[
            pltpu.VMEM((2 * extent_x, 27, 16, 128), jnp.float32),
            pltpu.SemaphoreType.DMA((2 * extent_x,)),
        ],
        compiler_params=params,
    )(saved)
    others = far_blocks(top)
    for step in (1, 0):
        last = step == 0
        first = send(first, along_z(0))
        second = send(second, along_z(1))
        side = pl.pallas_call(
            side_kernel,
            out_shape=tile_shape(11),
            in_specs=in_vmem(3),
            out_specs=in_vmem(1)[0],
            compiler_params=params,
        )(field, first, second)
        side = send(side, along_x)
        cross = pl.pallas_call(
            lambda *refs: cross_kernel(count, *refs),
            out_shape=tile_shape(11),
            in_specs=in_vmem(2 + count),
            out_specs=in_vmem(1)[0],
            compiler_params=params,
        )(field, top, first, second, *others, info)
        cross = send(cross, along_x_or_flip)

        def make_planes(kernel, planes, given, new, extra, after=()):
            operands = (field, vel, solid, *given)
            return pl.pallas_call(
                lambda *refs: kernel(step, *refs),
                out_shape=(tile_shape(27, extent_x), *extra),
                in_specs=in_vmem(len(operands)) + in_any(len(after) + len(new)),
                out_specs=tuple(in_any(1) + in_vmem(len(extra))),
                scratch_shapes=[
                    pltpu.VMEM((planes, 27, 16, 128), jnp.float32),
                    pltpu.VMEM((27, 16, 128), jnp.float32),
                    pltpu.SemaphoreType.DMA((planes,)),
                ],
                input_output_aliases={len(operands) + len(after): 0} if new else {},
                compiler_params=params,
            )(*operands, *after, *new)

        def inner(step, *refs):
            inner_kernel(step, last, *refs)

        ghosts = (first, second, side, cross)
        tile = tile_shape()
        if last:
            new = make_planes(inner, extent_x - 2, ghosts[:2], (), ())
            (field,) = make_planes(last_planes_kernel, 2, ghosts, new, ())
        else:
            pair = (tile, tile)
            new, top, *columns = make_planes(top_plane_kernel, 1, ghosts, (), (tile_shape(9), *pair))
            new, *columns = make_planes(
                inner, extent_x - 2, (*ghosts[:2], *columns), (new,), pair
            )
            others = far_blocks(top)
            messages = (tile_shape(10),) * 2
            field, first, second = make_planes(
                bottom_plane_kernel, 1, (*ghosts, *columns, top), (new,), messages, others
            )
    return field[None]


def solution(mesh):
    sizes = tuple(mesh.shape[axis] for axis in ("zone", "gx", "yz"))
    in_specs = (
        P("zone", None, "gx", None, "yz"),
        P(None, "zone", None, "gx", None, "yz"),
        P("zone", "gx", None, "yz"),
        P("zone", None, "yz", None),
        P("zone", None, "yz", None),
        P("zone", None, "yz", None),
    )
    out_specs = P("zone", None, "gx", None, "yz")
    return jax.shard_map(
        lambda *args: body(sizes, *args),
        mesh=mesh,
        in_specs=in_specs,
        out_specs=out_specs,
        check_vma=False,
    )
```

```python
import jax
import jax.numpy as jnp
import numpy as np
from jax import lax
from jax.experimental import pallas as pl
from jax.experimental.pallas import tpu as pltpu
from jax.sharding import PartitionSpec as P

OMEGA = 1.6
VMEM_LIMIT = 20 * 1024 * 1024
SIGNS = (-1, 0, 1)


def number(cx, cy, cz):
    return 9 * (cx + 1) + 3 * (cy + 1) + (cz + 1)


def lanes():
    return lax.broadcasted_iota(jnp.int32, (16, 128), 1)


def shift_y(tile, cy):
    if cy == 0:
        return tile
    row = lax.broadcasted_iota(jnp.int32, tile.shape, 0)
    if cy == 1:
        return jnp.where(row == 15, 0.0, pltpu.roll(tile, 15, 0))
    return jnp.where(row == 0, 0.0, pltpu.roll(tile, 1, 0))


def pack_columns(planes, x, low, high):
    lane = lanes()
    for slot in range(9):
        place = (x + 1) * 9 + slot
        here = lane == place
        low = jnp.where(here, pltpu.roll(planes(3 * slot + 2), place, 1), low)
        high = jnp.where(here, pltpu.roll(planes(3 * slot), place + 1, 1), high)
    return low, high


def is_even(axis):
    return lax.rem(lax.axis_index(axis), 2) == 0


def write_messages(top, low, high, first, second):
    even = is_even("yz")
    for j in range(9):
        tile = top(j)
        first[j] = tile
        second[j] = tile
    first[9] = jnp.where(even, high, low)
    second[9] = jnp.where(even, low, high)


def edges_from(first, second):
    even = is_even("yz")
    me, count = lax.axis_index("yz"), lax.axis_size("yz")
    low = jnp.where(me == 0, 0.0, jnp.where(even, second[9], first[9]))
    high = jnp.where(me == count - 1, 0.0, jnp.where(even, first[9], second[9]))
    return low, high


def pack_kernel(adj, first_out, second_out):
    extent_x = adj.shape[1]
    zero = jnp.zeros((16, 128), jnp.float32)
    low, high = lax.fori_loop(
        0, extent_x, lambda x, c: pack_columns(lambda i: adj[i, x], x, *c), (zero, zero)
    )
    write_messages(lambda j: adj[j, extent_x - 1], low, high, first_out, second_out)


def velocity_kernel(saved, out, kept, sems):
    steps, _, _, extent_x = saved.shape[:4]

    def load(n):
        step, x = n // extent_x, lax.rem(n, extent_x)
        return pltpu.make_async_copy(saved.at[step, 0, :, x], kept.at[n], sems.at[n])

    total = steps * extent_x
    lax.fori_loop(0, total, lambda n, c: (load(n).start(), c)[1], 0)

    def one(n, carry):
        load(n).wait()
        for a, tile in enumerate(velocity_of(lambda i: kept[n, i])):
            out[n // extent_x, a, lax.rem(n, extent_x)] = tile
        return carry

    lax.fori_loop(0, total, one, 0)


def side_kernel(adj, first, second, one_out, two_out):
    extent_x = adj.shape[1]
    even = is_even("gx")
    for j in range(9):
        top, bottom = adj[j, extent_x - 1], adj[18 + j, 0]
        one_out[j] = jnp.where(even, top, bottom)
        two_out[j] = jnp.where(even, bottom, top)
    low, high = edges_from(first, second)
    one_out[9], one_out[10] = low, high
    two_out[9], two_out[10] = low, high


def cross_kernel(count, *refs):
    own, first, second = refs[:3]
    blocks = refs[:count]
    info, _, out = refs[count:]
    interface = lax.axis_index("gx") == lax.axis_size("gx") - 1

    @pl.when(interface)
    def _():
        me = lax.axis_index("yz")
        even = is_even("yz")
        rows = (0, 8)
        spots, picks = {}, {}
        for r in rows:
            for k in range(2):
                code = info[k, r : r + 8].astype(jnp.int32)
                ahead = lax.rem(code // 128 - me + count, count)
                spots[r, k] = lax.rem(code, 128)
                turned = jnp.where(even, ahead, lax.rem(count - ahead, count))
                masks = [turned == 1, turned == count - 1]
                masks += [ahead == count - hop for hop in range(2, count - 1)]
                picks[r, k] = masks
        for j in range(9):
            halves = []
            for r in rows:
                total = jnp.zeros((8, 128), jnp.float32)
                for k in range(2):
                    tiles = [ref[j, r : r + 8] for ref in blocks]
                    got = [jnp.take_along_axis(tile, spots[r, k], axis=1) for tile in tiles]
                    picked = got[0]
                    for mask, value in zip(picks[r, k], got[1:]):
                        picked = jnp.where(mask, value, picked)
                    total = total + picked * info[2 + k, r : r + 8]
                halves.append(total)
            out[j] = jnp.concatenate(halves, axis=0)


def velocity_of(saved):
    totals, along_y, along_z = [], [], []
    for cx in SIGNS:
        sums, diffs = [], []
        for cy in SIGNS:
            lo, mid, hi = [saved(number(cx, cy, cz)) for cz in SIGNS]
            sums.append(lo + mid + hi)
            diffs.append(hi - lo)
        totals.append(sums[0] + sums[1] + sums[2])
        along_y.append(sums[2] - sums[0])
        along_z.append(diffs[0] + diffs[1] + diffs[2])
    density = totals[0] + totals[1] + totals[2]
    momentum = (
        totals[2] - totals[0],
        along_y[0] + along_y[1] + along_y[2],
        along_z[0] + along_z[1] + along_z[2],
    )
    return [part / density for part in momentum]


def moments_of(pull):
    rows = []
    for cx in SIGNS:
        plain, first, second = [], [], []
        for cy in SIGNS:
            lo, mid, hi = [pull(cx, cy, cz) for cz in SIGNS]
            both = lo + hi
            plain.append(mid + 0.25 * both)
            first.append(hi - lo)
            second.append(both)
        pair = plain[0] + plain[2]
        rows.append(
            (
                plain[1] + 0.25 * pair,
                plain[2] - plain[0],
                pair,
                first[1] + 0.25 * (first[0] + first[2]),
                first[2] - first[0],
                second[1] + 0.25 * (second[0] + second[2]),
            )
        )
    even = [rows[1][n] + 0.25 * (rows[0][n] + rows[2][n]) for n in range(6)]
    zero = (8.0 / 27.0) * even[0]
    along = (
        (2.0 / 27.0) * (rows[2][0] - rows[0][0]),
        (2.0 / 27.0) * even[1],
        (2.0 / 27.0) * even[3],
    )
    square = (
        (2.0 / 27.0) * (rows[2][0] + rows[0][0]),
        (2.0 / 27.0) * even[2],
        (2.0 / 27.0) * even[5],
    )
    mixed = (
        (1.0 / 54.0) * (rows[2][1] - rows[0][1]),
        (1.0 / 54.0) * (rows[2][3] - rows[0][3]),
        (1.0 / 54.0) * even[4],
    )
    return zero, along, square, mixed


def collide(pull, velocity, solid, store):
    zero, along, square, mixed = moments_of(lambda cx, cy, cz: pull(number(cx, cy, cz)))
    ux, uy, uz = velocity
    xy, xz, yz = mixed
    quadratic = (
        ux * ux * square[0]
        + uy * uy * square[1]
        + uz * uz * square[2]
        + 2.0 * (ux * uy * xy + ux * uz * xz + uy * uz * yz)
    )
    speed = ux * ux + uy * uy + uz * uz
    scalar = OMEGA * (zero * (1.0 + 1.5 * speed) - 4.5 * quadratic)
    vec_x = OMEGA * (3.0 * along[0] + 9.0 * (square[0] * ux + xy * uy + xz * uz) - 3.0 * ux * zero)
    vec_y = OMEGA * (3.0 * along[1] + 9.0 * (xy * ux + square[1] * uy + yz * uz) - 3.0 * uy * zero)
    vec_z = OMEGA * (3.0 * along[2] + 9.0 * (xz * ux + yz * uy + square[2] * uz) - 3.0 * uz * zero)
    wall = solid == 1
    for cx in SIGNS:
        base = scalar if cx == 0 else (scalar + vec_x if cx > 0 else scalar - vec_x)
        for cy in SIGNS:
            inner = base if cy == 0 else (base + vec_y if cy > 0 else base - vec_y)
            for cz in SIGNS:
                full = inner if cz == 0 else (inner + vec_z if cz > 0 else inner - vec_z)
                i = number(cx, cy, cz)
                store(i, jnp.where(wall, pull(26 - i), (1.0 - OMEGA) * pull(i) + full))


def pull_plane(tile_of, edges_of, pulled, raw=None):
    lane = lanes()
    for cx in SIGNS:
        low_edge, high_edge, start = edges_of(cx)
        for cy in SIGNS:
            place = start + 3 * (cx + 1) + cy + 1
            for cz in SIGNS:
                i = number(cx, cy, cz)
                source = tile_of(i, cx)
                tile = source
                if cz == -1:
                    edge = pltpu.roll(low_edge, 128 - place, 1)
                    tile = jnp.where(lane == 0, edge, pltpu.roll(source, 1, 1))
                elif cz == 1:
                    edge = pltpu.roll(high_edge, 127 - place, 1)
                    tile = jnp.where(lane == 127, edge, pltpu.roll(source, 127, 1))
                if raw is not None and cx == 1:
                    tile = jnp.where(raw, source, tile)
                pulled[i] = shift_y(tile, cy)


def inner_kernel(step, last, adj, vel, solid, first, second, *rest):
    out, low_out, high_out, made, pulled, sems = rest
    extent_x = adj.shape[1]
    low_edge, high_edge = edges_from(first, second)

    def save(x):
        return pltpu.make_async_copy(made.at[x - 1], out.at[:, x], sems.at[x - 1])

    def plane(x, carry):
        pull_plane(
            lambda i, cx: adj[i, x + cx],
            lambda cx: (low_edge, high_edge, (x + 1 + cx) * 9),
            pulled,
        )

        def store(i, tile):
            made[x - 1, i] = tile

        velocity = [vel[step, a, x] for a in range(3)]
        collide(lambda i: pulled[i], velocity, solid[0, x], store)
        save(x).start()
        if last:
            return carry
        return pack_columns(lambda i: made[x - 1, i], x, *carry)

    zero = jnp.zeros((16, 128), jnp.float32)
    low_out[...], high_out[...] = lax.fori_loop(1, extent_x - 1, plane, (zero, zero))
    lax.fori_loop(1, extent_x - 1, lambda x, c: (save(x).wait(), c)[1], 0)


def outer_kernel(step, adj, vel, solid, first, second, one, two, cross, *rest):
    *rest, made, pulled, sems = rest
    low_in, high_in, _, out, *messages = rest
    extent_x = adj.shape[1]
    edges = edges_from(first, second)
    even = is_even("gx")
    interface = lax.axis_index("gx") == lax.axis_size("gx") - 1

    def below(j):
        return jnp.where(even, two[j], one[j])

    def above(j):
        tile = jnp.where(even, one[j], two[j])
        return jnp.where(interface, cross[j], tile) if j < 9 else tile

    def plane(n, x, ghost, beyond, start, raw):
        pull_plane(
            lambda i, cx: beyond(i % 9) if cx == ghost else adj[i, x + cx],
            lambda cx: (
                (beyond(9), beyond(10), start) if cx == ghost else (*edges, (x + 1 + cx) * 9)
            ),
            pulled,
            raw,
        )

        def store(i, tile):
            made[n, i] = tile

        velocity = [vel[step, a, x] for a in range(3)]
        collide(lambda i: pulled[i], velocity, solid[0, x], store)
        save = pltpu.make_async_copy(made.at[n], out.at[:, x], sems.at[n])
        save.start()
        return save

    final = extent_x - 1
    saves = [plane(0, 0, -1, below, extent_x * 9, None), plane(1, final, 1, above, 9, interface)]
    if messages:
        low, high = low_in[...], high_in[...]
        low, high = pack_columns(lambda i: made[0, i], 0, low, high)
        low, high = pack_columns(lambda i: made[1, i], final, low, high)
        write_messages(lambda j: made[1, j], low, high, *messages)
    for save in saves:
        save.wait()


def tile_shape(*lead):
    return jax.ShapeDtypeStruct(lead + (16, 128), jnp.float32)


def in_vmem(n):
    return [pl.BlockSpec(memory_space=pltpu.VMEM)] * n


def in_any(n):
    return [pl.BlockSpec(memory_space=pl.ANY)] * n


def body(sizes, adjoint, saved, solid, band_device, band_cell, band_weight):
    zones, widths, count = sizes
    field = adjoint[0]
    extent_x = field.shape[1]
    axes = ("zone", "gx", "yz")
    params = pltpu.CompilerParams(vmem_limit_bytes=VMEM_LIMIT)

    def send(values, target):
        flat = lambda zone, gx, yz: (zone * widths + gx) * count + yz
        pairs = []
        for zone in range(zones):
            for gx in range(widths):
                for yz in range(count):
                    to = target(zone, gx, yz)
                    if to is not None:
                        pairs.append((flat(zone, gx, yz), flat(*to)))
        return lax.ppermute(values, axes, pairs)

    def partner_of(place, shift):
        return place + 1 if (place + shift) % 2 == 0 else place - 1

    def along_z(shift):
        return lambda zone, gx, yz: (zone, gx, partner_of(yz, shift) % count)

    def at_interface(target):
        return lambda zone, gx, yz: target(zone, gx, yz) if gx == widths - 1 else None

    def hop_z(hop):
        return lambda zone, gx, yz: (zone, gx, (yz + hop) % count)

    def flip(zone, gx, yz):
        return (1 - zone, gx, yz)

    def along_x(shift):
        def target(zone, gx, yz):
            to = partner_of(gx, shift)
            return (zone, to, yz) if 0 <= to < widths else None

        return target

    code = band_device[0] * 128 + band_cell[0]
    info = jnp.concatenate(
        [jnp.moveaxis(code.astype(jnp.float32), -1, 0), jnp.moveaxis(band_weight[0], -1, 0)]
    )
    info = send(info, at_interface(flip))
    first, second = pl.pallas_call(
        pack_kernel,
        out_shape=(tile_shape(10),) * 2,
        in_specs=in_vmem(1),
        out_specs=tuple(in_vmem(2)),
        compiler_params=params,
    )(field)
    vel = pl.pallas_call(
        velocity_kernel,
        out_shape=tile_shape(2, 3, extent_x),
        in_specs=in_any(1),
        out_specs=in_vmem(1)[0],
        scratch_shapes=[
            pltpu.VMEM((2 * extent_x, 27, 16, 128), jnp.float32),
            pltpu.SemaphoreType.DMA((2 * extent_x,)),
        ],
        compiler_params=params,
    )(saved)
    for step in (1, 0):
        last = step == 0
        own = first
        first = send(own, along_z(0))
        second = send(second, along_z(1))
        others = [send(own, at_interface(hop_z(hop))) for hop in range(2, count - 1)]
        one, two = pl.pallas_call(
            side_kernel,
            out_shape=(tile_shape(11),) * 2,
            in_specs=in_vmem(3),
            out_specs=tuple(in_vmem(2)),
            compiler_params=params,
        )(field, first, second)
        two = send(two, along_x(1))
        one = send(one, along_x(0))

        def make_planes(kernel, planes, given, new, extra):
            operands = (field, vel, solid, first, second, *given)
            return pl.pallas_call(
                lambda *refs: kernel(step, *refs),
                out_shape=(tile_shape(27, extent_x), *extra),
                in_specs=in_vmem(len(operands)) + in_any(len(new)),
                out_specs=tuple(in_any(1) + in_vmem(len(extra))),
                scratch_shapes=[
                    pltpu.VMEM((planes, 27, 16, 128), jnp.float32),
                    pltpu.VMEM((27, 16, 128), jnp.float32),
                    pltpu.SemaphoreType.DMA((planes,)),
                ],
                input_output_aliases={len(operands): 0} if new else {},
                compiler_params=params,
            )(*operands, *new)

        messages = () if last else (tile_shape(10),) * 2
        new, *columns = make_planes(
            lambda step, *refs: inner_kernel(step, last, *refs), extent_x - 2, (), (), (tile_shape(),) * 2
        )
        cross = pl.pallas_call(
            lambda *refs: cross_kernel(count, *refs),
            out_shape=tile_shape(9),
            in_specs=in_vmem(count + 1) + in_any(1),
            out_specs=in_vmem(1)[0],
            compiler_params=params,
        )(own, first, second, *others, info, columns[0])
        cross = send(cross, at_interface(flip))
        field, *messages = make_planes(
            outer_kernel, 2, (one, two, cross, *columns), (new,), messages
        )
        if not last:
            first, second = messages
    return field[None]


def solution(mesh):
    sizes = tuple(mesh.shape[axis] for axis in ("zone", "gx", "yz"))
    in_specs = (
        P("zone", None, "gx", None, "yz"),
        P(None, "zone", None, "gx", None, "yz"),
        P("zone", "gx", None, "yz"),
        P("zone", None, "yz", None),
        P("zone", None, "yz", None),
        P("zone", None, "yz", None),
    )
    out_specs = P("zone", None, "gx", None, "yz")
    return jax.shard_map(
        lambda *args: body(sizes, *args),
        mesh=mesh,
        in_specs=in_specs,
        out_specs=out_specs,
        check_vma=False,
    )
```

```python
import jax
import jax.numpy as jnp
import numpy as np
from jax import lax
from jax.experimental import pallas as pl
from jax.experimental.pallas import tpu as pltpu
from jax.sharding import PartitionSpec as P

OMEGA = 1.6
VMEM_LIMIT = 20 * 1024 * 1024
SIGNS = (-1, 0, 1)


def number(cx, cy, cz):
    return 9 * (cx + 1) + 3 * (cy + 1) + (cz + 1)


def lanes():
    return lax.broadcasted_iota(jnp.int32, (16, 128), 1)


def shift_y(tile, cy):
    if cy == 0:
        return tile
    row = lax.broadcasted_iota(jnp.int32, tile.shape, 0)
    if cy == 1:
        return jnp.where(row == 15, 0.0, pltpu.roll(tile, 15, 0))
    return jnp.where(row == 0, 0.0, pltpu.roll(tile, 1, 0))


def pack_columns(planes, x, low, high):
    lane = lanes()
    for slot in range(9):
        place = (x + 1) * 9 + slot
        here = lane == place
        low = jnp.where(here, pltpu.roll(planes(3 * slot + 2), place, 1), low)
        high = jnp.where(here, pltpu.roll(planes(3 * slot), place + 1, 1), high)
    return low, high


def is_even(axis):
    return lax.rem(lax.axis_index(axis), 2) == 0


def write_messages(top, low, high, first, second):
    even = is_even("yz")
    for j in range(9):
        tile = top(j)
        first[j] = tile
        second[j] = tile
    first[9] = jnp.where(even, high, low)
    second[9] = jnp.where(even, low, high)


def edges_from(first, second):
    even = is_even("yz")
    me, count = lax.axis_index("yz"), lax.axis_size("yz")
    low = jnp.where(me == 0, 0.0, jnp.where(even, second[9], first[9]))
    high = jnp.where(me == count - 1, 0.0, jnp.where(even, first[9], second[9]))
    return low, high


def pack_kernel(adj, first_out, second_out):
    extent_x = adj.shape[1]
    zero = jnp.zeros((16, 128), jnp.float32)
    low, high = lax.fori_loop(
        0, extent_x, lambda x, c: pack_columns(lambda i: adj[i, x], x, *c), (zero, zero)
    )
    write_messages(lambda j: adj[j, extent_x - 1], low, high, first_out, second_out)


def info_kernel(device, cell, weight, out):
    for k in range(2):
        out[k] = (device[:, k] * 128 + cell[:, k]).astype(jnp.float32)
        out[2 + k] = weight[:, k]


def velocity_kernel(saved, out, kept, sems):
    steps, _, _, extent_x = saved.shape[:4]

    def load(n):
        step, x = n // extent_x, lax.rem(n, extent_x)
        return pltpu.make_async_copy(saved.at[step, 0, :, x], kept.at[n], sems.at[n])

    total = steps * extent_x
    lax.fori_loop(0, total, lambda n, c: (load(n).start(), c)[1], 0)

    def one(n, carry):
        load(n).wait()
        for a, tile in enumerate(velocity_of(lambda i: kept[n, i])):
            out[n // extent_x, a, lax.rem(n, extent_x)] = tile
        return carry

    lax.fori_loop(0, total, one, 0)


def side_kernel(adj, first, second, _, two_out, one_out):
    extent_x = adj.shape[1]
    even = is_even("gx")
    for j in range(9):
        top, bottom = adj[j, extent_x - 1], adj[18 + j, 0]
        one_out[j] = jnp.where(even, top, bottom)
        two_out[j] = jnp.where(even, bottom, top)
    low, high = edges_from(first, second)
    one_out[9], one_out[10] = low, high
    two_out[9], two_out[10] = low, high


def cross_kernel(count, *refs):
    own, first, second = refs[:3]
    blocks = refs[:count]
    info, _, out = refs[count:]
    interface = lax.axis_index("gx") == lax.axis_size("gx") - 1

    @pl.when(interface)
    def _():
        me = lax.axis_index("yz")
        even = is_even("yz")
        rows = (0, 8)
        spots, picks = {}, {}
        for r in rows:
            for k in range(2):
                code = info[k, r : r + 8].astype(jnp.int32)
                ahead = lax.rem(code // 128 - me + count, count)
                spots[r, k] = lax.rem(code, 128)
                turned = jnp.where(even, ahead, lax.rem(count - ahead, count))
                masks = [turned == 1, turned == count - 1]
                masks += [ahead == count - hop for hop in range(2, count - 1)]
                picks[r, k] = masks
        for j in range(9):
            halves = []
            for r in rows:
                total = jnp.zeros((8, 128), jnp.float32)
                for k in range(2):
                    tiles = [ref[j, r : r + 8] for ref in blocks]
                    got = [jnp.take_along_axis(tile, spots[r, k], axis=1) for tile in tiles]
                    picked = got[0]
                    for mask, value in zip(picks[r, k], got[1:]):
                        picked = jnp.where(mask, value, picked)
                    total = total + picked * info[2 + k, r : r + 8]
                halves.append(total)
            out[j] = jnp.concatenate(halves, axis=0)


def velocity_of(saved):
    totals, along_y, along_z = [], [], []
    for cx in SIGNS:
        sums, diffs = [], []
        for cy in SIGNS:
            lo, mid, hi = [saved(number(cx, cy, cz)) for cz in SIGNS]
            sums.append(lo + mid + hi)
            diffs.append(hi - lo)
        totals.append(sums[0] + sums[1] + sums[2])
        along_y.append(sums[2] - sums[0])
        along_z.append(diffs[0] + diffs[1] + diffs[2])
    density = totals[0] + totals[1] + totals[2]
    momentum = (
        totals[2] - totals[0],
        along_y[0] + along_y[1] + along_y[2],
        along_z[0] + along_z[1] + along_z[2],
    )
    return [part / density for part in momentum]


def moments_of(pull):
    rows = []
    for cx in SIGNS:
        plain, first, second = [], [], []
        for cy in SIGNS:
            lo, mid, hi = [pull(cx, cy, cz) for cz in SIGNS]
            both = lo + hi
            plain.append(mid + 0.25 * both)
            first.append(hi - lo)
            second.append(both)
        pair = plain[0] + plain[2]
        rows.append(
            (
                plain[1] + 0.25 * pair,
                plain[2] - plain[0],
                pair,
                first[1] + 0.25 * (first[0] + first[2]),
                first[2] - first[0],
                second[1] + 0.25 * (second[0] + second[2]),
            )
        )
    even = [rows[1][n] + 0.25 * (rows[0][n] + rows[2][n]) for n in range(6)]
    zero = (8.0 / 27.0) * even[0]
    along = (
        (2.0 / 27.0) * (rows[2][0] - rows[0][0]),
        (2.0 / 27.0) * even[1],
        (2.0 / 27.0) * even[3],
    )
    square = (
        (2.0 / 27.0) * (rows[2][0] + rows[0][0]),
        (2.0 / 27.0) * even[2],
        (2.0 / 27.0) * even[5],
    )
    mixed = (
        (1.0 / 54.0) * (rows[2][1] - rows[0][1]),
        (1.0 / 54.0) * (rows[2][3] - rows[0][3]),
        (1.0 / 54.0) * even[4],
    )
    return zero, along, square, mixed


def collide(pull, velocity, solid, store):
    zero, along, square, mixed = moments_of(lambda cx, cy, cz: pull(number(cx, cy, cz)))
    ux, uy, uz = velocity
    xy, xz, yz = mixed
    quadratic = (
        ux * ux * square[0]
        + uy * uy * square[1]
        + uz * uz * square[2]
        + 2.0 * (ux * uy * xy + ux * uz * xz + uy * uz * yz)
    )
    speed = ux * ux + uy * uy + uz * uz
    scalar = OMEGA * (zero * (1.0 + 1.5 * speed) - 4.5 * quadratic)
    vec_x = OMEGA * (3.0 * along[0] + 9.0 * (square[0] * ux + xy * uy + xz * uz) - 3.0 * ux * zero)
    vec_y = OMEGA * (3.0 * along[1] + 9.0 * (xy * ux + square[1] * uy + yz * uz) - 3.0 * uy * zero)
    vec_z = OMEGA * (3.0 * along[2] + 9.0 * (xz * ux + yz * uy + square[2] * uz) - 3.0 * uz * zero)
    wall = solid == 1
    for cx in SIGNS:
        base = scalar if cx == 0 else (scalar + vec_x if cx > 0 else scalar - vec_x)
        for cy in SIGNS:
            inner = base if cy == 0 else (base + vec_y if cy > 0 else base - vec_y)
            for cz in SIGNS:
                full = inner if cz == 0 else (inner + vec_z if cz > 0 else inner - vec_z)
                i = number(cx, cy, cz)
                store(i, jnp.where(wall, pull(26 - i), (1.0 - OMEGA) * pull(i) + full))


def pull_plane(tile_of, edges_of, pulled, raw=None):
    lane = lanes()
    for cx in SIGNS:
        low_edge, high_edge, start = edges_of(cx)
        for cy in SIGNS:
            place = start + 3 * (cx + 1) + cy + 1
            for cz in SIGNS:
                i = number(cx, cy, cz)
                source = tile_of(i, cx)
                tile = source
                if cz == -1:
                    edge = pltpu.roll(low_edge, 128 - place, 1)
                    tile = jnp.where(lane == 0, edge, pltpu.roll(source, 1, 1))
                elif cz == 1:
                    edge = pltpu.roll(high_edge, 127 - place, 1)
                    tile = jnp.where(lane == 127, edge, pltpu.roll(source, 127, 1))
                if raw is not None and cx == 1:
                    tile = jnp.where(raw, source, tile)
                pulled[i] = shift_y(tile, cy)


def inner_kernel(step, last, adj, vel, solid, first, second, *rest):
    out, low_out, high_out, made, pulled, sems = rest
    extent_x = adj.shape[1]
    low_edge, high_edge = edges_from(first, second)

    def save(x):
        return pltpu.make_async_copy(made.at[x - 1], out.at[:, x], sems.at[x - 1])

    def plane(x, carry):
        pull_plane(
            lambda i, cx: adj[i, x + cx],
            lambda cx: (low_edge, high_edge, (x + 1 + cx) * 9),
            pulled,
        )

        def store(i, tile):
            made[x - 1, i] = tile

        velocity = [vel[step, a, x] for a in range(3)]
        collide(lambda i: pulled[i], velocity, solid[0, x], store)
        save(x).start()
        if last:
            return carry
        return pack_columns(lambda i: made[x - 1, i], x, *carry)

    zero = jnp.zeros((16, 128), jnp.float32)
    low_out[...], high_out[...] = lax.fori_loop(1, extent_x - 1, plane, (zero, zero))
    lax.fori_loop(1, extent_x - 1, lambda x, c: (save(x).wait(), c)[1], 0)


def outer_kernel(step, adj, vel, solid, first, second, two, one, cross, *rest):
    *rest, made, pulled, sems = rest
    low_in, high_in, _, out, *messages = rest
    extent_x = adj.shape[1]
    edges = edges_from(first, second)
    even = is_even("gx")
    interface = lax.axis_index("gx") == lax.axis_size("gx") - 1

    def below(j):
        return jnp.where(even, two[j], one[j])

    def above(j):
        tile = jnp.where(even, one[j], two[j])
        return jnp.where(interface, cross[j], tile) if j < 9 else tile

    def plane(n, x, ghost, beyond, start, raw):
        pull_plane(
            lambda i, cx: beyond(i % 9) if cx == ghost else adj[i, x + cx],
            lambda cx: (
                (beyond(9), beyond(10), start) if cx == ghost else (*edges, (x + 1 + cx) * 9)
            ),
            pulled,
            raw,
        )

        def store(i, tile):
            made[n, i] = tile

        velocity = [vel[step, a, x] for a in range(3)]
        collide(lambda i: pulled[i], velocity, solid[0, x], store)
        save = pltpu.make_async_copy(made.at[n], out.at[:, x], sems.at[n])
        save.start()
        return save

    final = extent_x - 1
    saves = [plane(0, 0, -1, below, extent_x * 9, None), plane(1, final, 1, above, 9, interface)]
    if messages:
        low, high = low_in[...], high_in[...]
        low, high = pack_columns(lambda i: made[0, i], 0, low, high)
        low, high = pack_columns(lambda i: made[1, i], final, low, high)
        write_messages(lambda j: made[1, j], low, high, *messages)
    for save in saves:
        save.wait()


def tile_shape(*lead):
    return jax.ShapeDtypeStruct(lead + (16, 128), jnp.float32)


def in_vmem(n):
    return [pl.BlockSpec(memory_space=pltpu.VMEM)] * n


def in_any(n):
    return [pl.BlockSpec(memory_space=pl.ANY)] * n


def body(sizes, adjoint, saved, solid, band_device, band_cell, band_weight):
    zones, widths, count = sizes
    field = adjoint[0]
    extent_x = field.shape[1]
    axes = ("zone", "gx", "yz")
    params = pltpu.CompilerParams(vmem_limit_bytes=VMEM_LIMIT)

    def send(values, target):
        flat = lambda zone, gx, yz: (zone * widths + gx) * count + yz
        pairs = []
        for zone in range(zones):
            for gx in range(widths):
                for yz in range(count):
                    to = target(zone, gx, yz)
                    if to is not None:
                        pairs.append((flat(zone, gx, yz), flat(*to)))
        return lax.ppermute(values, axes, pairs)

    def partner_of(place, shift):
        return place + 1 if (place + shift) % 2 == 0 else place - 1

    def along_z(shift):
        return lambda zone, gx, yz: (zone, gx, partner_of(yz, shift) % count)

    def at_interface(target):
        return lambda zone, gx, yz: target(zone, gx, yz) if gx == widths - 1 else None

    def hop_z(hop):
        return lambda zone, gx, yz: (zone, gx, (yz + hop) % count)

    def flip(zone, gx, yz):
        return (1 - zone, gx, yz)

    def along_x(shift):
        def target(zone, gx, yz):
            to = partner_of(gx, shift)
            return (zone, to, yz) if 0 <= to < widths else None

        return target

    info = pl.pallas_call(
        info_kernel,
        out_shape=tile_shape(4),
        in_specs=in_vmem(3),
        out_specs=in_vmem(1)[0],
        compiler_params=params,
    )(*[jnp.swapaxes(array[0], 1, 2) for array in (band_device, band_cell, band_weight)])
    info = send(info, at_interface(flip))
    first, second = pl.pallas_call(
        pack_kernel,
        out_shape=(tile_shape(10),) * 2,
        in_specs=in_vmem(1),
        out_specs=tuple(in_vmem(2)),
        compiler_params=params,
    )(field)
    vel = pl.pallas_call(
        velocity_kernel,
        out_shape=tile_shape(2, 3, extent_x),
        in_specs=in_any(1),
        out_specs=in_vmem(1)[0],
        scratch_shapes=[
            pltpu.VMEM((2 * extent_x, 27, 16, 128), jnp.float32),
            pltpu.SemaphoreType.DMA((2 * extent_x,)),
        ],
        compiler_params=params,
    )(saved)
    for step in (1, 0):
        last = step == 0
        own = first
        first = send(own, along_z(0))
        second = send(second, along_z(1))
        others = [send(own, at_interface(hop_z(hop))) for hop in range(2, count - 1)]
        two, one = pl.pallas_call(
            side_kernel,
            out_shape=(tile_shape(11),) * 2,
            in_specs=in_vmem(3) + in_any(1),
            out_specs=tuple(in_vmem(2)),
            compiler_params=params,
        )(field, first, second, vel)
        two = send(two, along_x(1))
        one = send(one, along_x(0))

        def make_planes(kernel, planes, given, new, extra):
            operands = (field, vel, solid, first, second, *given)
            return pl.pallas_call(
                lambda *refs: kernel(step, *refs),
                out_shape=(tile_shape(27, extent_x), *extra),
                in_specs=in_vmem(len(operands)) + in_any(len(new)),
                out_specs=tuple(in_any(1) + in_vmem(len(extra))),
                scratch_shapes=[
                    pltpu.VMEM((planes, 27, 16, 128), jnp.float32),
                    pltpu.VMEM((27, 16, 128), jnp.float32),
                    pltpu.SemaphoreType.DMA((planes,)),
                ],
                input_output_aliases={len(operands): 0} if new else {},
                compiler_params=params,
            )(*operands, *new)

        messages = () if last else (tile_shape(10),) * 2
        def make_inner():
            kernel = lambda step, *refs: inner_kernel(step, last, *refs)
            return make_planes(kernel, extent_x - 2, (), (), (tile_shape(),) * 2)

        def make_cross(after):
            return pl.pallas_call(
                lambda *refs: cross_kernel(count, *refs),
                out_shape=tile_shape(9),
                in_specs=in_vmem(count + 1) + in_any(1),
                out_specs=in_vmem(1)[0],
                compiler_params=params,
            )(own, first, second, *others, info, after)

        if last:
            new, *columns = make_inner()
            cross = make_cross(columns[0])
        else:
            cross = make_cross(vel)
            new, *columns = make_inner()
        cross = send(cross, at_interface(flip))
        field, *messages = make_planes(
            outer_kernel, 2, (two, one, cross, *columns), (new,), messages
        )
        if not last:
            first, second = messages
    return field[None]


def solution(mesh):
    sizes = tuple(mesh.shape[axis] for axis in ("zone", "gx", "yz"))
    in_specs = (
        P("zone", None, "gx", None, "yz"),
        P(None, "zone", None, "gx", None, "yz"),
        P("zone", "gx", None, "yz"),
        P("zone", None, "yz", None),
        P("zone", None, "yz", None),
        P("zone", None, "yz", None),
    )
    out_specs = P("zone", None, "gx", None, "yz")
    return jax.shard_map(
        lambda *args: body(sizes, *args),
        mesh=mesh,
        in_specs=in_specs,
        out_specs=out_specs,
        check_vma=False,
    )
```

```python
import itertools

import jax
import jax.numpy as jnp
import numpy as np
from jax import lax
from jax.experimental import pallas as pl
from jax.experimental.pallas import tpu as pltpu
from jax.sharding import PartitionSpec as P

OMEGA = 1.6
VMEM_LIMIT = 20 * 1024 * 1024
SIGNS = (-1, 0, 1)


def number(cx, cy, cz):
    return 9 * (cx + 1) + 3 * (cy + 1) + (cz + 1)


def lanes():
    return lax.broadcasted_iota(jnp.int32, (16, 128), 1)


def shift_y(tile, cy):
    if cy == 0:
        return tile
    row = lax.broadcasted_iota(jnp.int32, tile.shape, 0)
    if cy == 1:
        return jnp.where(row == 15, 0.0, pltpu.roll(tile, 15, 0))
    return jnp.where(row == 0, 0.0, pltpu.roll(tile, 1, 0))


def pack_columns(planes, x, low, high):
    lane = lanes()
    for slot in range(9):
        place = (x + 1) * 9 + slot
        here = lane == place
        low = jnp.where(here, pltpu.roll(planes(3 * slot + 2), place, 1), low)
        high = jnp.where(here, pltpu.roll(planes(3 * slot), place + 1, 1), high)
    return low, high


def is_even(axis):
    return lax.rem(lax.axis_index(axis), 2) == 0


def write_messages(top, low, high, first, second):
    even = is_even("yz")
    for j in range(9):
        tile = top(j)
        first[j] = tile
        second[j] = tile
    first[9] = jnp.where(even, high, low)
    second[9] = jnp.where(even, low, high)


def edges_from(first, second):
    even = is_even("yz")
    me, count = lax.axis_index("yz"), lax.axis_size("yz")
    low = jnp.where(me == 0, 0.0, jnp.where(even, second[9], first[9]))
    high = jnp.where(me == count - 1, 0.0, jnp.where(even, first[9], second[9]))
    return low, high


def pack_kernel(adj, first_out, second_out, kept, sems):
    extent_x = adj.shape[1]

    def load(x):
        return pltpu.make_async_copy(adj.at[:, x], kept.at[x], sems.at[x])

    for x in range(extent_x):
        load(x).start()

    def one(x, carry):
        load(x).wait()
        return pack_columns(lambda i: kept[x, i], x, *carry)

    zero = jnp.zeros((16, 128), jnp.float32)
    low, high = lax.fori_loop(0, extent_x, one, (zero, zero))
    write_messages(lambda j: kept[extent_x - 1, j], low, high, first_out, second_out)


def info_kernel(device, cell, weight, out):
    for k in range(2):
        out[k] = (device[:, k] * 128 + cell[:, k]).astype(jnp.float32)
        out[2 + k] = weight[:, k]


def velocity_kernel(step, saved, out, kept, sems):
    extent_x = out.shape[1]

    def load(x):
        return pltpu.make_async_copy(saved.at[step, 0, :, x], kept.at[x], sems.at[x])

    lax.fori_loop(0, extent_x, lambda x, c: (load(x).start(), c)[1], 0)

    def one(x, carry):
        load(x).wait()
        for a, tile in enumerate(velocity_of(lambda i: kept[x, i])):
            out[a, x] = tile
        return carry

    lax.fori_loop(0, extent_x, one, 0)


def side_kernel(adj, first, second, _, two_out, one_out):
    extent_x = adj.shape[1]
    even = is_even("gx")
    for j in range(9):
        top, bottom = adj[j, extent_x - 1], adj[18 + j, 0]
        one_out[j] = jnp.where(even, top, bottom)
        two_out[j] = jnp.where(even, bottom, top)
    low, high = edges_from(first, second)
    one_out[9], one_out[10] = low, high
    two_out[9], two_out[10] = low, high


def cross_kernel(count, *refs):
    own, first, second = refs[:3]
    blocks = refs[:count]
    info, _, out = refs[count:]
    interface = lax.axis_index("gx") == lax.axis_size("gx") - 1

    @pl.when(interface)
    def _():
        me = lax.axis_index("yz")
        even = is_even("yz")
        rows = (0, 8)
        spots, picks = {}, {}
        for r in rows:
            for k in range(2):
                code = info[k, r : r + 8].astype(jnp.int32)
                ahead = lax.rem(code // 128 - me + count, count)
                spots[r, k] = lax.rem(code, 128)
                turned = jnp.where(even, ahead, lax.rem(count - ahead, count))
                masks = [turned == 1, turned == count - 1]
                masks += [ahead == count - hop for hop in range(2, count - 1)]
                picks[r, k] = masks
        for j in range(9):
            halves = []
            for r in rows:
                total = jnp.zeros((8, 128), jnp.float32)
                for k in range(2):
                    tiles = [ref[j, r : r + 8] for ref in blocks]
                    got = [jnp.take_along_axis(tile, spots[r, k], axis=1) for tile in tiles]
                    picked = got[0]
                    for mask, value in zip(picks[r, k], got[1:]):
                        picked = jnp.where(mask, value, picked)
                    total = total + picked * info[2 + k, r : r + 8]
                halves.append(total)
            out[j] = jnp.concatenate(halves, axis=0)


def velocity_of(saved):
    totals, along_y, along_z = [], [], []
    for cx in SIGNS:
        sums, diffs = [], []
        for cy in SIGNS:
            lo, mid, hi = [saved(number(cx, cy, cz)) for cz in SIGNS]
            sums.append(lo + mid + hi)
            diffs.append(hi - lo)
        totals.append(sums[0] + sums[1] + sums[2])
        along_y.append(sums[2] - sums[0])
        along_z.append(diffs[0] + diffs[1] + diffs[2])
    density = totals[0] + totals[1] + totals[2]
    momentum = (
        totals[2] - totals[0],
        along_y[0] + along_y[1] + along_y[2],
        along_z[0] + along_z[1] + along_z[2],
    )
    return [part / density for part in momentum]


def moments_of(pull):
    rows = []
    for cx in SIGNS:
        plain, first, second = [], [], []
        for cy in SIGNS:
            lo, mid, hi = [pull(cx, cy, cz) for cz in SIGNS]
            both = lo + hi
            plain.append(mid + 0.25 * both)
            first.append(hi - lo)
            second.append(both)
        pair = plain[0] + plain[2]
        rows.append(
            (
                plain[1] + 0.25 * pair,
                plain[2] - plain[0],
                pair,
                first[1] + 0.25 * (first[0] + first[2]),
                first[2] - first[0],
                second[1] + 0.25 * (second[0] + second[2]),
            )
        )
    even = [rows[1][n] + 0.25 * (rows[0][n] + rows[2][n]) for n in range(6)]
    zero = (8.0 / 27.0) * even[0]
    along = (
        (2.0 / 27.0) * (rows[2][0] - rows[0][0]),
        (2.0 / 27.0) * even[1],
        (2.0 / 27.0) * even[3],
    )
    square = (
        (2.0 / 27.0) * (rows[2][0] + rows[0][0]),
        (2.0 / 27.0) * even[2],
        (2.0 / 27.0) * even[5],
    )
    mixed = (
        (1.0 / 54.0) * (rows[2][1] - rows[0][1]),
        (1.0 / 54.0) * (rows[2][3] - rows[0][3]),
        (1.0 / 54.0) * even[4],
    )
    return zero, along, square, mixed


def collide(pull, velocity, solid, store):
    zero, along, square, mixed = moments_of(lambda cx, cy, cz: pull(number(cx, cy, cz)))
    ux, uy, uz = velocity
    xy, xz, yz = mixed
    quadratic = (
        ux * ux * square[0]
        + uy * uy * square[1]
        + uz * uz * square[2]
        + 2.0 * (ux * uy * xy + ux * uz * xz + uy * uz * yz)
    )
    speed = ux * ux + uy * uy + uz * uz
    scalar = OMEGA * (zero * (1.0 + 1.5 * speed) - 4.5 * quadratic)
    vec_x = OMEGA * (3.0 * along[0] + 9.0 * (square[0] * ux + xy * uy + xz * uz) - 3.0 * ux * zero)
    vec_y = OMEGA * (3.0 * along[1] + 9.0 * (xy * ux + square[1] * uy + yz * uz) - 3.0 * uy * zero)
    vec_z = OMEGA * (3.0 * along[2] + 9.0 * (xz * ux + yz * uy + square[2] * uz) - 3.0 * uz * zero)
    wall = solid == 1
    for cx in SIGNS:
        base = scalar if cx == 0 else (scalar + vec_x if cx > 0 else scalar - vec_x)
        for cy in SIGNS:
            inner = base if cy == 0 else (base + vec_y if cy > 0 else base - vec_y)
            for cz in SIGNS:
                full = inner if cz == 0 else (inner + vec_z if cz > 0 else inner - vec_z)
                i = number(cx, cy, cz)
                store(i, jnp.where(wall, pull(26 - i), (1.0 - OMEGA) * pull(i) + full))


def pull_plane(tile_of, edges_of, pulled, raw=None):
    lane = lanes()
    for cx in SIGNS:
        low_edge, high_edge, start = edges_of(cx)
        for cy in SIGNS:
            place = start + 3 * (cx + 1) + cy + 1
            for cz in SIGNS:
                i = number(cx, cy, cz)
                source = tile_of(i, cx)
                tile = source
                if cz == -1:
                    edge = pltpu.roll(low_edge, 128 - place, 1)
                    tile = jnp.where(lane == 0, edge, pltpu.roll(source, 1, 1))
                elif cz == 1:
                    edge = pltpu.roll(high_edge, 127 - place, 1)
                    tile = jnp.where(lane == 127, edge, pltpu.roll(source, 127, 1))
                if raw is not None and cx == 1:
                    tile = jnp.where(raw, source, tile)
                pulled[i] = shift_y(tile, cy)


def inner_kernel(step, last, adj, vel, solid, first, second, *rest):
    out, low_out, high_out, made, pulled, sems = rest
    extent_x = adj.shape[1]
    low_edge, high_edge = edges_from(first, second)

    def save(x):
        return pltpu.make_async_copy(made.at[x - 1], out.at[:, x], sems.at[x - 1])

    def plane(x, carry):
        pull_plane(
            lambda i, cx: adj[i, x + cx],
            lambda cx: (low_edge, high_edge, (x + 1 + cx) * 9),
            pulled,
        )

        def store(i, tile):
            made[x - 1, i] = tile

        velocity = [vel[a, x] for a in range(3)]
        collide(lambda i: pulled[i], velocity, solid[0, x], store)
        save(x).start()
        if last:
            return carry
        return pack_columns(lambda i: made[x - 1, i], x, *carry)

    zero = jnp.zeros((16, 128), jnp.float32)
    low_out[...], high_out[...] = lax.fori_loop(1, extent_x - 1, plane, (zero, zero))
    lax.fori_loop(1, extent_x - 1, lambda x, c: (save(x).wait(), c)[1], 0)


def outer_kernel(step, adj, vel, solid, first, second, two, one, cross, *rest):
    *rest, made, pulled, sems = rest
    low_in, high_in, _, out, *messages = rest
    extent_x = adj.shape[1]
    edges = edges_from(first, second)
    even = is_even("gx")
    interface = lax.axis_index("gx") == lax.axis_size("gx") - 1

    bottom = lax.axis_index("gx") == 0

    def below(j):
        return jnp.where(bottom, 0.0, jnp.where(even, two[j], one[j]))

    def above(j):
        tile = jnp.where(even, one[j], two[j])
        return jnp.where(interface, cross[j], tile) if j < 9 else tile

    def plane(n, x, ghost, beyond, start, raw):
        pull_plane(
            lambda i, cx: beyond(i % 9) if cx == ghost else adj[i, x + cx],
            lambda cx: (
                (beyond(9), beyond(10), start) if cx == ghost else (*edges, (x + 1 + cx) * 9)
            ),
            pulled,
            raw,
        )

        def store(i, tile):
            made[n, i] = tile

        velocity = [vel[a, x] for a in range(3)]
        collide(lambda i: pulled[i], velocity, solid[0, x], store)
        save = pltpu.make_async_copy(made.at[n], out.at[:, x], sems.at[n])
        save.start()
        return save

    final = extent_x - 1
    saves = [plane(0, 0, -1, below, extent_x * 9, None), plane(1, final, 1, above, 9, interface)]
    if messages:
        low, high = low_in[...], high_in[...]
        low, high = pack_columns(lambda i: made[0, i], 0, low, high)
        low, high = pack_columns(lambda i: made[1, i], final, low, high)
        write_messages(lambda j: made[1, j], low, high, *messages)
    for save in saves:
        save.wait()


def tile_shape(*lead):
    return jax.ShapeDtypeStruct(lead + (16, 128), jnp.float32)


def in_vmem(n):
    return [pl.BlockSpec(memory_space=pltpu.VMEM)] * n


def in_any(n):
    return [pl.BlockSpec(memory_space=pl.ANY)] * n


def body(sizes, adjoint, saved, solid, band_device, band_cell, band_weight):
    zones, widths, count = sizes
    field = adjoint[0]
    extent_x = field.shape[1]
    axes = ("zone", "gx", "yz")
    params = pltpu.CompilerParams(vmem_limit_bytes=VMEM_LIMIT)

    def send(values, target):
        flat = lambda zone, gx, yz: (zone * widths + gx) * count + yz
        places = itertools.product(range(zones), range(widths), range(count))
        return lax.ppermute(values, axes, [(flat(*here), flat(*target(*here))) for here in places])

    def partner_of(place, shift):
        return place + 1 if (place + shift) % 2 == 0 else place - 1

    def flip(zone, gx, yz):
        return (1 - zone, gx, yz)

    def along_z(shift):
        def target(zone, gx, yz):
            to = partner_of(yz, shift)
            if gx == widths - 1 or 0 <= to < count:
                return (zone, gx, to % count)
            return flip(zone, gx, yz)

        return target

    def hop_z(hop):
        def target(zone, gx, yz):
            if gx == widths - 1:
                return (zone, gx, (yz + hop) % count)
            return flip(zone, gx, yz)

        return target

    def along_x(shift):
        def target(zone, gx, yz):
            to = partner_of(gx, shift)
            return (zone, to, yz) if 0 <= to < widths else flip(zone, gx, yz)

        return target

    info = pl.pallas_call(
        info_kernel,
        out_shape=tile_shape(4),
        in_specs=in_vmem(3),
        out_specs=in_vmem(1)[0],
        compiler_params=params,
    )(*[jnp.swapaxes(array[0], 1, 2) for array in (band_device, band_cell, band_weight)])
    info = send(info, flip)
    first, second = pl.pallas_call(
        pack_kernel,
        out_shape=(tile_shape(10),) * 2,
        in_specs=[pl.BlockSpec(memory_space=pltpu.HBM)],
        out_specs=tuple(in_vmem(2)),
        scratch_shapes=[
            pltpu.VMEM((extent_x, 27, 16, 128), jnp.float32),
            pltpu.SemaphoreType.DMA((extent_x,)),
        ],
        compiler_params=params,
    )(pltpu.with_memory_space_constraint(field, pltpu.HBM))
    saved = pltpu.with_memory_space_constraint(saved, pltpu.HBM)
    for step in (1, 0):
        last = step == 0
        own = first
        first = send(own, along_z(0))
        second = send(second, along_z(1))
        others = [send(own, hop_z(hop)) for hop in range(2, count - 1)]
        vel = pl.pallas_call(
            lambda *refs: velocity_kernel(step, *refs),
            out_shape=tile_shape(3, extent_x),
            in_specs=[pl.BlockSpec(memory_space=pltpu.HBM)],
            out_specs=in_vmem(1)[0],
            scratch_shapes=[
                pltpu.VMEM((extent_x, 27, 16, 128), jnp.float32),
                pltpu.SemaphoreType.DMA((extent_x,)),
            ],
            compiler_params=params,
        )(saved)
        two, one = pl.pallas_call(
            side_kernel,
            out_shape=(tile_shape(11),) * 2,
            in_specs=in_vmem(3) + in_any(1),
            out_specs=tuple(in_vmem(2)),
            compiler_params=params,
        )(field, first, second, vel)
        two = send(two, along_x(1))
        one = send(one, along_x(0))

        def make_planes(kernel, planes, given, new, extra):
            operands = (field, vel, solid, first, second, *given)
            return pl.pallas_call(
                lambda *refs: kernel(step, *refs),
                out_shape=(tile_shape(27, extent_x), *extra),
                in_specs=in_vmem(len(operands)) + in_any(len(new)),
                out_specs=tuple(in_any(1) + in_vmem(len(extra))),
                scratch_shapes=[
                    pltpu.VMEM((planes, 27, 16, 128), jnp.float32),
                    pltpu.VMEM((27, 16, 128), jnp.float32),
                    pltpu.SemaphoreType.DMA((planes,)),
                ],
                input_output_aliases={len(operands): 0} if new else {},
                compiler_params=params,
            )(*operands, *new)

        messages = () if last else (tile_shape(10),) * 2
        def make_inner():
            kernel = lambda step, *refs: inner_kernel(step, last, *refs)
            return make_planes(kernel, extent_x - 2, (), (), (tile_shape(),) * 2)

        def make_cross(after):
            return pl.pallas_call(
                lambda *refs: cross_kernel(count, *refs),
                out_shape=tile_shape(9),
                in_specs=in_vmem(count + 1) + in_any(1),
                out_specs=in_vmem(1)[0],
                compiler_params=params,
            )(own, first, second, *others, info, after)

        if last:
            new, *columns = make_inner()
            cross = make_cross(columns[0])
        else:
            cross = make_cross(vel)
            new, *columns = make_inner()
        cross = send(cross, flip)
        field, *messages = make_planes(
            outer_kernel, 2, (two, one, cross, *columns), (new,), messages
        )
        if not last:
            first, second = messages
    return field[None]


def solution(mesh):
    sizes = tuple(mesh.shape[axis] for axis in ("zone", "gx", "yz"))
    in_specs = (
        P("zone", None, "gx", None, "yz"),
        P(None, "zone", None, "gx", None, "yz"),
        P("zone", "gx", None, "yz"),
        P("zone", None, "yz", None),
        P("zone", None, "yz", None),
        P("zone", None, "yz", None),
    )
    out_specs = P("zone", None, "gx", None, "yz")
    return jax.shard_map(
        lambda *args: body(sizes, *args),
        mesh=mesh,
        in_specs=in_specs,
        out_specs=out_specs,
        check_vma=False,
    )
```

```python
import itertools

import jax
import jax.numpy as jnp
import numpy as np
from jax import lax
from jax.experimental import pallas as pl
from jax.experimental.pallas import tpu as pltpu
from jax.sharding import PartitionSpec as P

OMEGA = 1.6
VMEM_LIMIT = 20 * 1024 * 1024
SIGNS = (-1, 0, 1)


def number(cx, cy, cz):
    return 9 * (cx + 1) + 3 * (cy + 1) + (cz + 1)


def lanes():
    return lax.broadcasted_iota(jnp.int32, (16, 128), 1)


def shift_y(tile, cy):
    if cy == 0:
        return tile
    row = lax.broadcasted_iota(jnp.int32, tile.shape, 0)
    if cy == 1:
        return jnp.where(row == 15, 0.0, pltpu.roll(tile, 15, 0))
    return jnp.where(row == 0, 0.0, pltpu.roll(tile, 1, 0))


def pack_columns(planes, x, low, high):
    lane = lanes()
    for slot in range(9):
        place = (x + 1) * 9 + slot
        here = lane == place
        low = jnp.where(here, pltpu.roll(planes(3 * slot + 2), place, 1), low)
        high = jnp.where(here, pltpu.roll(planes(3 * slot), place + 1, 1), high)
    return low, high


def is_even(axis):
    return lax.rem(lax.axis_index(axis), 2) == 0


def write_messages(top, low, high, first, second):
    even = is_even("yz")
    for j in range(9):
        tile = top(j)
        first[j] = tile
        second[j] = tile
    first[9] = jnp.where(even, high, low)
    second[9] = jnp.where(even, low, high)


def edges_from(first, second):
    even = is_even("yz")
    me, count = lax.axis_index("yz"), lax.axis_size("yz")
    low = jnp.where(me == 0, 0.0, jnp.where(even, second[9], first[9]))
    high = jnp.where(me == count - 1, 0.0, jnp.where(even, first[9], second[9]))
    return low, high


def pack_kernel(adj, first_out, second_out, kept, top, sems):
    extent_x = adj.shape[2]
    copies = [
        pltpu.make_async_copy(adj.at[:, 2 * side, x], kept.at[side, x], sems.at[side, x])
        for x in range(extent_x)
        for side in range(2)
    ]
    copies.append(pltpu.make_async_copy(adj.at[pl.ds(0, 3), :, extent_x - 1], top, sems.at[2, 0]))
    for copy in copies:
        copy.start()
    edges = jnp.zeros((16, 128), jnp.float32), jnp.zeros((16, 128), jnp.float32)
    for x in range(extent_x):
        for copy in copies[2 * x : 2 * x + 2]:
            copy.wait()
        edges = pack_columns(lambda i: kept[(i % 3) // 2, x, i // 3], x, *edges)
    copies[-1].wait()
    write_messages(lambda j: top[j // 3, j % 3], *edges, first_out, second_out)


def info_kernel(device, cell, weight, out):
    for k in range(2):
        out[k] = (device[:, k] * 128 + cell[:, k]).astype(jnp.float32)
        out[2 + k] = weight[:, k]


def velocity_kernel(step, saved, out, kept, sems):
    extent_x = out.shape[1]

    def load(x):
        return pltpu.make_async_copy(saved.at[step, 0, :, x], kept.at[x], sems.at[x])

    lax.fori_loop(0, extent_x, lambda x, c: (load(x).start(), c)[1], 0)

    def one(x, carry):
        load(x).wait()
        for a, tile in enumerate(velocity_of(lambda i: kept[x, i])):
            out[a, x] = tile
        return carry

    lax.fori_loop(0, extent_x, one, 0)


def side_kernel(adj, first, second, _, two_out, one_out):
    extent_x = adj.shape[1]
    even = is_even("gx")
    interface = lax.axis_index("gx") == lax.axis_size("gx") - 1
    for j in range(9):
        top, bottom = adj[j, extent_x - 1], adj[18 + j, 0]
        one_out[j] = jnp.where(even, top, bottom)
        two_out[j] = jnp.where(even | interface, jnp.where(interface, top, bottom), top)
    lane = lanes()
    low, high = edges_from(first, second)
    top, bottom = [
        jnp.where(lane < 64, pltpu.roll(low, 128 - start, 1), pltpu.roll(high, 192 - start, 1))
        for start in (9 * extent_x, 9)
    ]
    one_out[9] = jnp.where(even, top, bottom)
    two_out[9] = jnp.where(even, bottom, top)


def cross_kernel(count, *refs):
    own, first, second, ends = refs[:4]
    others = refs[4 : 1 + count]
    info, _, out = refs[1 + count :]
    interface = lax.axis_index("gx") == lax.axis_size("gx") - 1

    @pl.when(interface)
    def _():
        me = lax.axis_index("yz")
        even = is_even("yz")
        at_end = (me == 0) | (me == count - 1)
        rows = (0, 8)
        spots, picks = {}, {}
        for r in rows:
            for k in range(2):
                code = info[k, r : r + 8].astype(jnp.int32)
                ahead = lax.rem(code // 128 - me + count, count)
                spots[r, k] = lax.rem(code, 128)
                turned = jnp.where(even, ahead, lax.rem(count - ahead, count))
                masks = [turned == 1, turned == count - 1]
                masks += [ahead == count - hop for hop in range(2, count - 1)]
                picks[r, k] = masks
        for j in range(9):
            halves = []
            for r in rows:
                total = jnp.zeros((8, 128), jnp.float32)
                for k in range(2):
                    tiles = [ref[j, r : r + 8] for ref in (own, first, second, *others)]
                    tiles[2] = jnp.where(at_end, ends[j, r : r + 8], tiles[2])
                    got = [jnp.take_along_axis(tile, spots[r, k], axis=1) for tile in tiles]
                    picked = got[0]
                    for mask, value in zip(picks[r, k], got[1:]):
                        picked = jnp.where(mask, value, picked)
                    total = total + picked * info[2 + k, r : r + 8]
                halves.append(total)
            out[j] = jnp.concatenate(halves, axis=0)


def velocity_of(saved):
    totals, along_y, along_z = [], [], []
    for cx in SIGNS:
        sums, diffs = [], []
        for cy in SIGNS:
            lo, mid, hi = [saved(number(cx, cy, cz)) for cz in SIGNS]
            sums.append(lo + mid + hi)
            diffs.append(hi - lo)
        totals.append(sums[0] + sums[1] + sums[2])
        along_y.append(sums[2] - sums[0])
        along_z.append(diffs[0] + diffs[1] + diffs[2])
    density = totals[0] + totals[1] + totals[2]
    momentum = (
        totals[2] - totals[0],
        along_y[0] + along_y[1] + along_y[2],
        along_z[0] + along_z[1] + along_z[2],
    )
    return [part / density for part in momentum]


def moments_of(pull):
    rows = []
    for cx in SIGNS:
        plain, first, second = [], [], []
        for cy in SIGNS:
            lo, mid, hi = [pull(cx, cy, cz) for cz in SIGNS]
            both = lo + hi
            plain.append(mid + 0.25 * both)
            first.append(hi - lo)
            second.append(both)
        pair = plain[0] + plain[2]
        rows.append(
            (
                plain[1] + 0.25 * pair,
                plain[2] - plain[0],
                pair,
                first[1] + 0.25 * (first[0] + first[2]),
                first[2] - first[0],
                second[1] + 0.25 * (second[0] + second[2]),
            )
        )
    even = [rows[1][n] + 0.25 * (rows[0][n] + rows[2][n]) for n in range(6)]
    zero = (8.0 / 27.0) * even[0]
    along = (
        (2.0 / 27.0) * (rows[2][0] - rows[0][0]),
        (2.0 / 27.0) * even[1],
        (2.0 / 27.0) * even[3],
    )
    square = (
        (2.0 / 27.0) * (rows[2][0] + rows[0][0]),
        (2.0 / 27.0) * even[2],
        (2.0 / 27.0) * even[5],
    )
    mixed = (
        (1.0 / 54.0) * (rows[2][1] - rows[0][1]),
        (1.0 / 54.0) * (rows[2][3] - rows[0][3]),
        (1.0 / 54.0) * even[4],
    )
    return zero, along, square, mixed


def collide(pull, velocity, solid, store):
    zero, along, square, mixed = moments_of(lambda cx, cy, cz: pull(number(cx, cy, cz)))
    ux, uy, uz = velocity
    xy, xz, yz = mixed
    quadratic = (
        ux * ux * square[0]
        + uy * uy * square[1]
        + uz * uz * square[2]
        + 2.0 * (ux * uy * xy + ux * uz * xz + uy * uz * yz)
    )
    speed = ux * ux + uy * uy + uz * uz
    scalar = OMEGA * (zero * (1.0 + 1.5 * speed) - 4.5 * quadratic)
    vec_x = OMEGA * (3.0 * along[0] + 9.0 * (square[0] * ux + xy * uy + xz * uz) - 3.0 * ux * zero)
    vec_y = OMEGA * (3.0 * along[1] + 9.0 * (xy * ux + square[1] * uy + yz * uz) - 3.0 * uy * zero)
    vec_z = OMEGA * (3.0 * along[2] + 9.0 * (xz * ux + yz * uy + square[2] * uz) - 3.0 * uz * zero)
    wall = solid == 1
    for cx in SIGNS:
        base = scalar if cx == 0 else (scalar + vec_x if cx > 0 else scalar - vec_x)
        for cy in SIGNS:
            inner = base if cy == 0 else (base + vec_y if cy > 0 else base - vec_y)
            for cz in SIGNS:
                full = inner if cz == 0 else (inner + vec_z if cz > 0 else inner - vec_z)
                i = number(cx, cy, cz)
                store(i, jnp.where(wall, pull(26 - i), (1.0 - OMEGA) * pull(i) + full))


def pull_plane(tile_of, edges_of, pulled, raw=None):
    lane = lanes()
    for cx in SIGNS:
        low_edge, high_edge, start = edges_of(cx)
        for cy in SIGNS:
            place = start + 3 * (cx + 1) + cy + 1
            for cz in SIGNS:
                i = number(cx, cy, cz)
                source = tile_of(i, cx)
                tile = source
                if cz == -1:
                    edge = pltpu.roll(low_edge, 128 - place, 1)
                    tile = jnp.where(lane == 0, edge, pltpu.roll(source, 1, 1))
                elif cz == 1:
                    edge = pltpu.roll(high_edge, 127 - place, 1)
                    tile = jnp.where(lane == 127, edge, pltpu.roll(source, 127, 1))
                if raw is not None and cx == 1:
                    tile = jnp.where(raw, source, tile)
                pulled[i] = shift_y(tile, cy)


def inner_kernel(step, last, adj, vel, solid, first, second, *rest):
    out, low_out, high_out, made, pulled, sems = rest
    extent_x = adj.shape[1]
    low_edge, high_edge = edges_from(first, second)

    def save(x):
        return pltpu.make_async_copy(made.at[x - 1], out.at[:, x], sems.at[x - 1])

    def plane(x, carry):
        here = pulled.at[lax.rem(x, 2)]
        pull_plane(
            lambda i, cx: adj[i, x + cx],
            lambda cx: (low_edge, high_edge, (x + 1 + cx) * 9),
            here,
        )

        def store(i, tile):
            made[x - 1, i] = tile

        velocity = [vel[a, x] for a in range(3)]
        collide(lambda i: here[i], velocity, solid[0, x], store)
        save(x).start()
        if last:
            return carry
        return pack_columns(lambda i: made[x - 1, i], x, *carry)

    zero = jnp.zeros((16, 128), jnp.float32)
    low_out[...], high_out[...] = lax.fori_loop(1, extent_x - 1, plane, (zero, zero), unroll=2)
    lax.fori_loop(1, extent_x - 1, lambda x, c: (save(x).wait(), c)[1], 0)


def outer_kernel(step, adj, vel, solid, first, second, two, one, cross, *rest):
    *rest, made, pulled, sems = rest
    low_in, high_in, _, out, *messages = rest
    extent_x = adj.shape[1]
    edges = edges_from(first, second)
    even = is_even("gx")
    interface = lax.axis_index("gx") == lax.axis_size("gx") - 1

    bottom = lax.axis_index("gx") == 0

    def below(j):
        return jnp.where(bottom, 0.0, jnp.where(even, two[j], one[j]))

    def above(j):
        tile = jnp.where(even, one[j], two[j])
        return jnp.where(interface, cross[j], tile) if j < 9 else tile

    def plane(n, x, ghost, beyond, raw):
        pull_plane(
            lambda i, cx: beyond(i % 9) if cx == ghost else adj[i, x + cx],
            lambda cx: (
                (beyond(9), pltpu.roll(beyond(9), 64, 1), 0)
                if cx == ghost
                else (*edges, (x + 1 + cx) * 9)
            ),
            pulled.at[n],
            raw,
        )

        def store(i, tile):
            made[n, i] = tile

        velocity = [vel[a, x] for a in range(3)]
        collide(lambda i: pulled[n, i], velocity, solid[0, x], store)
        save = pltpu.make_async_copy(made.at[n], out.at[:, x], sems.at[n])
        save.start()
        return save

    final = extent_x - 1
    saves = [plane(0, 0, -1, below, None), plane(1, final, 1, above, interface)]
    if messages:
        low, high = low_in[...], high_in[...]
        low, high = pack_columns(lambda i: made[0, i], 0, low, high)
        low, high = pack_columns(lambda i: made[1, i], final, low, high)
        write_messages(lambda j: made[1, j], low, high, *messages)
    for save in saves:
        save.wait()


def tile_shape(*lead):
    return jax.ShapeDtypeStruct(lead + (16, 128), jnp.float32)


def in_vmem(n):
    return [pl.BlockSpec(memory_space=pltpu.VMEM)] * n


def in_any(n):
    return [pl.BlockSpec(memory_space=pl.ANY)] * n


def body(sizes, adjoint, saved, solid, band_device, band_cell, band_weight):
    zones, widths, count = sizes
    field = adjoint[0]
    extent_x = field.shape[1]
    axes = ("zone", "gx", "yz")
    params = pltpu.CompilerParams(vmem_limit_bytes=VMEM_LIMIT)

    def send(values, target):
        flat = lambda zone, gx, yz: (zone * widths + gx) * count + yz
        places = itertools.product(range(zones), range(widths), range(count))
        return lax.ppermute(values, axes, [(flat(*here), flat(*target(*here))) for here in places])

    def partner_of(place, shift):
        return place + 1 if (place + shift) % 2 == 0 else place - 1

    def flip(zone, gx, yz):
        return (1 - zone, gx, yz)

    def along_z(shift):
        def target(zone, gx, yz):
            to = partner_of(yz, shift)
            return (zone, gx, to) if 0 <= to < count else flip(zone, gx, yz)

        return target

    def hop_z(hop):
        def target(zone, gx, yz):
            if gx == widths - 1:
                return (zone, gx, (yz + hop) % count)
            return flip(zone, gx, yz)

        return target

    def along_x(shift):
        def target(zone, gx, yz):
            to = partner_of(gx, shift)
            if gx == widths - 1 and shift == 1 and yz in (0, count - 1):
                return (zone, gx, count - 1 - yz)
            return (zone, to, yz) if 0 <= to < widths else flip(zone, gx, yz)

        return target

    info = pl.pallas_call(
        info_kernel,
        out_shape=tile_shape(4),
        in_specs=in_vmem(3),
        out_specs=in_vmem(1)[0],
        compiler_params=params,
    )(*[jnp.swapaxes(array[0], 1, 2) for array in (band_device, band_cell, band_weight)])
    info = send(info, flip)
    first, second = pl.pallas_call(
        pack_kernel,
        out_shape=(tile_shape(10),) * 2,
        in_specs=[pl.BlockSpec(memory_space=pltpu.HBM)],
        out_specs=tuple(in_vmem(2)),
        scratch_shapes=[
            pltpu.VMEM((2, extent_x, 9, 16, 128), jnp.float32),
            pltpu.VMEM((3, 3, 16, 128), jnp.float32),
            pltpu.SemaphoreType.DMA((3, extent_x)),
        ],
        compiler_params=params,
    )(pltpu.with_memory_space_constraint(field.reshape(9, 3, extent_x, 16, 128), pltpu.HBM))
    saved = pltpu.with_memory_space_constraint(saved, pltpu.HBM)
    for step in (1, 0):
        last = step == 0
        own = first
        first = send(own, along_z(0))
        second = send(second, along_z(1))
        others = [send(own, hop_z(hop)) for hop in range(2, count - 1)]
        vel = pl.pallas_call(
            lambda *refs: velocity_kernel(step, *refs),
            out_shape=tile_shape(3, extent_x),
            in_specs=[pl.BlockSpec(memory_space=pltpu.HBM)],
            out_specs=in_vmem(1)[0],
            scratch_shapes=[
                pltpu.VMEM((extent_x, 27, 16, 128), jnp.float32),
                pltpu.SemaphoreType.DMA((extent_x,)),
            ],
            compiler_params=params,
        )(saved)
        two, one = pl.pallas_call(
            side_kernel,
            out_shape=(tile_shape(10),) * 2,
            in_specs=in_vmem(3) + in_any(1),
            out_specs=tuple(in_vmem(2)),
            compiler_params=params,
        )(field, first, second, vel)
        two = send(two, along_x(1))
        one = send(one, along_x(0))

        def make_planes(kernel, planes, given, new, extra):
            operands = (field, vel, solid, first, second, *given)
            return pl.pallas_call(
                lambda *refs: kernel(step, *refs),
                out_shape=(tile_shape(27, extent_x), *extra),
                in_specs=in_vmem(len(operands)) + in_any(len(new)),
                out_specs=tuple(in_any(1) + in_vmem(len(extra))),
                scratch_shapes=[
                    pltpu.VMEM((planes, 27, 16, 128), jnp.float32),
                    pltpu.VMEM((2, 27, 16, 128), jnp.float32),
                    pltpu.SemaphoreType.DMA((planes,)),
                ],
                input_output_aliases={len(operands): 0} if new else {},
                compiler_params=params,
            )(*operands, *new)

        messages = () if last else (tile_shape(10),) * 2
        kernel = lambda step, *refs: inner_kernel(step, last, *refs)
        new, *columns = make_planes(kernel, extent_x - 2, (), (), (tile_shape(),) * 2)
        cross = pl.pallas_call(
            lambda *refs: cross_kernel(count, *refs),
            out_shape=tile_shape(9),
            in_specs=in_vmem(count + 2) + in_any(1),
            out_specs=in_vmem(1)[0],
            compiler_params=params,
        )(own, first, second, two, *others, info, columns[0])
        cross = send(cross, flip)
        field, *messages = make_planes(
            outer_kernel, 2, (two, one, cross, *columns), (new,), messages
        )
        if not last:
            first, second = messages
    return field[None]


def solution(mesh):
    sizes = tuple(mesh.shape[axis] for axis in ("zone", "gx", "yz"))
    in_specs = (
        P("zone", None, "gx", None, "yz"),
        P(None, "zone", None, "gx", None, "yz"),
        P("zone", "gx", None, "yz"),
        P("zone", None, "yz", None),
        P("zone", None, "yz", None),
        P("zone", None, "yz", None),
    )
    out_specs = P("zone", None, "gx", None, "yz")
    return jax.shard_map(
        lambda *args: body(sizes, *args),
        mesh=mesh,
        in_specs=in_specs,
        out_specs=out_specs,
        check_vma=False,
    )
```

```python
import itertools

import jax
import jax.numpy as jnp
import numpy as np
from jax import lax
from jax.experimental import pallas as pl
from jax.experimental.pallas import tpu as pltpu
from jax.sharding import PartitionSpec as P

OMEGA = 1.6
VMEM_LIMIT = 20 * 1024 * 1024
SIGNS = (-1, 0, 1)


def number(cx, cy, cz):
    return 9 * (cx + 1) + 3 * (cy + 1) + (cz + 1)


def lanes():
    return lax.broadcasted_iota(jnp.int32, (16, 128), 1)


def shift_y(tile, cy):
    if cy == 0:
        return tile
    row = lax.broadcasted_iota(jnp.int32, tile.shape, 0)
    if cy == 1:
        return jnp.where(row == 15, 0.0, pltpu.roll(tile, 15, 0))
    return jnp.where(row == 0, 0.0, pltpu.roll(tile, 1, 0))


def pack_columns(planes, x, low, high):
    lane = lanes()
    for slot in range(9):
        place = (x + 1) * 9 + slot
        here = lane == place
        low = jnp.where(here, pltpu.roll(planes(3 * slot + 2), place, 1), low)
        high = jnp.where(here, pltpu.roll(planes(3 * slot), place + 1, 1), high)
    return low, high


def is_even(axis):
    return lax.rem(lax.axis_index(axis), 2) == 0


def write_messages(top, low, high, first, second):
    even = is_even("yz")
    for j in range(9):
        tile = top(j)
        first[j] = tile
        second[j] = tile
    first[9] = jnp.where(even, high, low)
    second[9] = jnp.where(even, low, high)


def edges_from(first, second):
    even = is_even("yz")
    me, count = lax.axis_index("yz"), lax.axis_size("yz")
    low = jnp.where(me == 0, 0.0, jnp.where(even, second[9], first[9]))
    high = jnp.where(me == count - 1, 0.0, jnp.where(even, first[9], second[9]))
    return low, high


def pack_kernel(adj, first_out, second_out, kept, top, sems):
    extent_x = adj.shape[2]
    copies = [
        pltpu.make_async_copy(adj.at[:, 2 * side, x], kept.at[side, x], sems.at[side, x])
        for x in range(extent_x)
        for side in range(2)
    ]
    copies.append(pltpu.make_async_copy(adj.at[pl.ds(0, 3), :, extent_x - 1], top, sems.at[2, 0]))
    for copy in copies:
        copy.start()
    edges = jnp.zeros((16, 128), jnp.float32), jnp.zeros((16, 128), jnp.float32)
    for x in range(extent_x):
        for copy in copies[2 * x : 2 * x + 2]:
            copy.wait()
        edges = pack_columns(lambda i: kept[(i % 3) // 2, x, i // 3], x, *edges)
    copies[-1].wait()
    write_messages(lambda j: top[j // 3, j % 3], *edges, first_out, second_out)


def info_kernel(device, cell, weight, out):
    for k in range(2):
        out[k] = (device[:, k] * 128 + cell[:, k]).astype(jnp.float32)
        out[2 + k] = weight[:, k]


def velocity_kernel(step, saved, out, kept, sems):
    extent_x = out.shape[1]

    def load(x):
        return pltpu.make_async_copy(saved.at[step, 0, :, x], kept.at[x], sems.at[x])

    lax.fori_loop(0, extent_x, lambda x, c: (load(x).start(), c)[1], 0)

    def one(x, carry):
        load(x).wait()
        for a, tile in enumerate(velocity_of(lambda i: kept[x, i])):
            out[a, x] = tile
        return carry

    lax.fori_loop(0, extent_x, one, 0)


def side_kernel(adj, first, second, _, two_out, one_out):
    extent_x = adj.shape[1]
    even = is_even("gx")
    for j in range(9):
        top, bottom = adj[j, extent_x - 1], adj[18 + j, 0]
        one_out[j] = jnp.where(even, top, bottom)
        two_out[j] = jnp.where(even, bottom, top)
    lane = lanes()
    low, high = edges_from(first, second)
    top, bottom = [
        jnp.where(lane < 64, pltpu.roll(low, 128 - start, 1), pltpu.roll(high, 192 - start, 1))
        for start in (9 * extent_x, 9)
    ]
    one_out[9] = jnp.where(even, top, bottom)
    two_out[9] = jnp.where(even, bottom, top)


def cross_kernel(count, *refs):
    own, first, second, ends = refs[:4]
    others = refs[4 : 1 + count]
    info, _, out = refs[1 + count :]
    interface = lax.axis_index("gx") == lax.axis_size("gx") - 1

    @pl.when(interface)
    def _():
        me = lax.axis_index("yz")
        even = is_even("yz")
        at_end = (me == 0) | (me == count - 1)
        rows = (0, 8)
        spots, picks = {}, {}
        for r in rows:
            for k in range(2):
                code = info[k, r : r + 8].astype(jnp.int32)
                ahead = lax.rem(code // 128 - me + count, count)
                spots[r, k] = lax.rem(code, 128)
                turned = jnp.where(even, ahead, lax.rem(count - ahead, count))
                masks = [turned == 1, turned == count - 1]
                masks += [ahead == count - hop for hop in range(2, count - 1)]
                picks[r, k] = masks
        for j in range(9):
            halves = []
            for r in rows:
                total = jnp.zeros((8, 128), jnp.float32)
                for k in range(2):
                    tiles = [ref[j, r : r + 8] for ref in (own, first, second, *others)]
                    tiles[2] = jnp.where(at_end, ends[j, r : r + 8], tiles[2])
                    got = [jnp.take_along_axis(tile, spots[r, k], axis=1) for tile in tiles]
                    picked = got[0]
                    for mask, value in zip(picks[r, k], got[1:]):
                        picked = jnp.where(mask, value, picked)
                    total = total + picked * info[2 + k, r : r + 8]
                halves.append(total)
            out[j] = jnp.concatenate(halves, axis=0)


def velocity_of(saved):
    totals, along_y, along_z = [], [], []
    for cx in SIGNS:
        sums, diffs = [], []
        for cy in SIGNS:
            lo, mid, hi = [saved(number(cx, cy, cz)) for cz in SIGNS]
            sums.append(lo + mid + hi)
            diffs.append(hi - lo)
        totals.append(sums[0] + sums[1] + sums[2])
        along_y.append(sums[2] - sums[0])
        along_z.append(diffs[0] + diffs[1] + diffs[2])
    density = totals[0] + totals[1] + totals[2]
    momentum = (
        totals[2] - totals[0],
        along_y[0] + along_y[1] + along_y[2],
        along_z[0] + along_z[1] + along_z[2],
    )
    return [part / density for part in momentum]


def moments_of(pull):
    rows = []
    for cx in SIGNS:
        plain, first, second = [], [], []
        for cy in SIGNS:
            lo, mid, hi = [pull(cx, cy, cz) for cz in SIGNS]
            both = lo + hi
            plain.append(mid + 0.25 * both)
            first.append(hi - lo)
            second.append(both)
        pair = plain[0] + plain[2]
        rows.append(
            (
                plain[1] + 0.25 * pair,
                plain[2] - plain[0],
                pair,
                first[1] + 0.25 * (first[0] + first[2]),
                first[2] - first[0],
                second[1] + 0.25 * (second[0] + second[2]),
            )
        )
    even = [rows[1][n] + 0.25 * (rows[0][n] + rows[2][n]) for n in range(6)]
    zero = (8.0 / 27.0) * even[0]
    along = (
        (2.0 / 27.0) * (rows[2][0] - rows[0][0]),
        (2.0 / 27.0) * even[1],
        (2.0 / 27.0) * even[3],
    )
    square = (
        (2.0 / 27.0) * (rows[2][0] + rows[0][0]),
        (2.0 / 27.0) * even[2],
        (2.0 / 27.0) * even[5],
    )
    mixed = (
        (1.0 / 54.0) * (rows[2][1] - rows[0][1]),
        (1.0 / 54.0) * (rows[2][3] - rows[0][3]),
        (1.0 / 54.0) * even[4],
    )
    return zero, along, square, mixed


def collide(pull, velocity, solid, store):
    zero, along, square, mixed = moments_of(lambda cx, cy, cz: pull(number(cx, cy, cz)))
    ux, uy, uz = velocity
    xy, xz, yz = mixed
    quadratic = (
        ux * ux * square[0]
        + uy * uy * square[1]
        + uz * uz * square[2]
        + 2.0 * (ux * uy * xy + ux * uz * xz + uy * uz * yz)
    )
    speed = ux * ux + uy * uy + uz * uz
    scalar = OMEGA * (zero * (1.0 + 1.5 * speed) - 4.5 * quadratic)
    vec_x = OMEGA * (3.0 * along[0] + 9.0 * (square[0] * ux + xy * uy + xz * uz) - 3.0 * ux * zero)
    vec_y = OMEGA * (3.0 * along[1] + 9.0 * (xy * ux + square[1] * uy + yz * uz) - 3.0 * uy * zero)
    vec_z = OMEGA * (3.0 * along[2] + 9.0 * (xz * ux + yz * uy + square[2] * uz) - 3.0 * uz * zero)
    wall = solid == 1
    for cx in SIGNS:
        base = scalar if cx == 0 else (scalar + vec_x if cx > 0 else scalar - vec_x)
        for cy in SIGNS:
            inner = base if cy == 0 else (base + vec_y if cy > 0 else base - vec_y)
            for cz in SIGNS:
                full = inner if cz == 0 else (inner + vec_z if cz > 0 else inner - vec_z)
                i = number(cx, cy, cz)
                store(i, jnp.where(wall, pull(26 - i), (1.0 - OMEGA) * pull(i) + full))


def pull_plane(tile_of, edges_of, pulled, raw=None):
    lane = lanes()
    for cx in SIGNS:
        low_edge, high_edge, start = edges_of(cx)
        for cy in SIGNS:
            place = start + 3 * (cx + 1) + cy + 1
            for cz in SIGNS:
                i = number(cx, cy, cz)
                source = tile_of(i, cx)
                tile = source
                if cz == -1:
                    edge = pltpu.roll(low_edge, 128 - place, 1)
                    tile = jnp.where(lane == 0, edge, pltpu.roll(source, 1, 1))
                elif cz == 1:
                    edge = pltpu.roll(high_edge, 127 - place, 1)
                    tile = jnp.where(lane == 127, edge, pltpu.roll(source, 127, 1))
                if raw is not None and cx == 1:
                    tile = jnp.where(raw, source, tile)
                pulled[i] = shift_y(tile, cy)


def inner_kernel(step, last, adj, vel, solid, first, second, *rest):
    out, low_out, high_out, made, pulled, sems = rest
    extent_x = adj.shape[1]
    low_edge, high_edge = edges_from(first, second)

    def save(x):
        return pltpu.make_async_copy(made.at[x - 1], out.at[:, x], sems.at[x - 1])

    def plane(x, carry):
        here = pulled.at[lax.rem(x, 2)]
        pull_plane(
            lambda i, cx: adj[i, x + cx],
            lambda cx: (low_edge, high_edge, (x + 1 + cx) * 9),
            here,
        )

        def store(i, tile):
            made[x - 1, i] = tile

        velocity = [vel[a, x] for a in range(3)]
        collide(lambda i: here[i], velocity, solid[0, x], store)
        save(x).start()
        if last:
            return carry
        return pack_columns(lambda i: made[x - 1, i], x, *carry)

    zero = jnp.zeros((16, 128), jnp.float32)
    low_out[...], high_out[...] = lax.fori_loop(1, extent_x - 1, plane, (zero, zero), unroll=2)
    lax.fori_loop(1, extent_x - 1, lambda x, c: (save(x).wait(), c)[1], 0)


def outer_kernel(step, adj, vel, solid, first, second, two, one, cross, *rest):
    *rest, made, pulled, sems = rest
    low_in, high_in, _, out, *messages = rest
    extent_x = adj.shape[1]
    edges = edges_from(first, second)
    even = is_even("gx")
    interface = lax.axis_index("gx") == lax.axis_size("gx") - 1

    bottom = lax.axis_index("gx") == 0

    def below(j):
        return jnp.where(bottom, 0.0, jnp.where(even, two[j], one[j]))

    def above(j):
        tile = jnp.where(even, one[j], two[j])
        return jnp.where(interface, cross[j], tile) if j < 9 else tile

    def plane(n, x, ghost, beyond, raw):
        pull_plane(
            lambda i, cx: beyond(i % 9) if cx == ghost else adj[i, x + cx],
            lambda cx: (
                (beyond(9), pltpu.roll(beyond(9), 64, 1), 0)
                if cx == ghost
                else (*edges, (x + 1 + cx) * 9)
            ),
            pulled.at[n],
            raw,
        )

        def store(i, tile):
            made[n, i] = tile

        velocity = [vel[a, x] for a in range(3)]
        collide(lambda i: pulled[n, i], velocity, solid[0, x], store)
        save = pltpu.make_async_copy(made.at[n], out.at[:, x], sems.at[n])
        save.start()
        return save

    final = extent_x - 1
    saves = [plane(0, 0, -1, below, None), plane(1, final, 1, above, interface)]
    if messages:
        low, high = low_in[...], high_in[...]
        low, high = pack_columns(lambda i: made[0, i], 0, low, high)
        low, high = pack_columns(lambda i: made[1, i], final, low, high)
        write_messages(lambda j: made[1, j], low, high, *messages)
    for save in saves:
        save.wait()


def tile_shape(*lead):
    return jax.ShapeDtypeStruct(lead + (16, 128), jnp.float32)


def in_vmem(n):
    return [pl.BlockSpec(memory_space=pltpu.VMEM)] * n


def in_any(n):
    return [pl.BlockSpec(memory_space=pl.ANY)] * n


def body(sizes, adjoint, saved, solid, band_device, band_cell, band_weight):
    zones, widths, count = sizes
    field = adjoint[0]
    extent_x = field.shape[1]
    axes = ("zone", "gx", "yz")
    params = pltpu.CompilerParams(vmem_limit_bytes=VMEM_LIMIT)

    def send(values, target):
        flat = lambda zone, gx, yz: (zone * widths + gx) * count + yz
        places = itertools.product(range(zones), range(widths), range(count))
        return lax.ppermute(values, axes, [(flat(*here), flat(*target(*here))) for here in places])

    def partner_of(place, shift):
        return place + 1 if (place + shift) % 2 == 0 else place - 1

    def flip(zone, gx, yz):
        return (1 - zone, gx, yz)

    def along_z(shift):
        def target(zone, gx, yz):
            to = partner_of(yz, shift)
            return (zone, gx, to) if 0 <= to < count else flip(zone, gx, yz)

        return target

    def hop_z(hop):
        def target(zone, gx, yz):
            if gx == widths - 1:
                return (zone, gx, (yz + hop) % count)
            return flip(zone, gx, yz)

        return target

    def ends_z(zone, gx, yz):
        if gx == widths - 1 and yz in (0, count - 1):
            return (zone, gx, count - 1 - yz)
        return flip(zone, gx, yz)

    def along_x(shift):
        def target(zone, gx, yz):
            to = partner_of(gx, shift)
            return (zone, to, yz) if 0 <= to < widths else flip(zone, gx, yz)

        return target

    info = pl.pallas_call(
        info_kernel,
        out_shape=tile_shape(4),
        in_specs=in_vmem(3),
        out_specs=in_vmem(1)[0],
        compiler_params=params,
    )(*[jnp.swapaxes(array[0], 1, 2) for array in (band_device, band_cell, band_weight)])
    info = send(info, flip)
    first, second = pl.pallas_call(
        pack_kernel,
        out_shape=(tile_shape(10),) * 2,
        in_specs=[pl.BlockSpec(memory_space=pltpu.HBM)],
        out_specs=tuple(in_vmem(2)),
        scratch_shapes=[
            pltpu.VMEM((2, extent_x, 9, 16, 128), jnp.float32),
            pltpu.VMEM((3, 3, 16, 128), jnp.float32),
            pltpu.SemaphoreType.DMA((3, extent_x)),
        ],
        compiler_params=params,
    )(pltpu.with_memory_space_constraint(field.reshape(9, 3, extent_x, 16, 128), pltpu.HBM))
    saved = pltpu.with_memory_space_constraint(saved, pltpu.HBM)
    for step in (1, 0):
        last = step == 0
        own = first
        first = send(own, along_z(0))
        second = send(second, along_z(1))
        others = [send(own, target) for target in (ends_z, *map(hop_z, range(2, count - 1)))]
        vel = pl.pallas_call(
            lambda *refs: velocity_kernel(step, *refs),
            out_shape=tile_shape(3, extent_x),
            in_specs=[pl.BlockSpec(memory_space=pltpu.HBM)],
            out_specs=in_vmem(1)[0],
            scratch_shapes=[
                pltpu.VMEM((extent_x, 27, 16, 128), jnp.float32),
                pltpu.SemaphoreType.DMA((extent_x,)),
            ],
            compiler_params=params,
        )(saved)
        two, one = pl.pallas_call(
            side_kernel,
            out_shape=(tile_shape(10),) * 2,
            in_specs=in_vmem(3) + in_any(1),
            out_specs=tuple(in_vmem(2)),
            compiler_params=params,
        )(field, first, second, vel)
        two = send(two, along_x(1))
        one = send(one, along_x(0))

        def make_planes(kernel, planes, given, new, extra):
            operands = (field, vel, solid, first, second, *given)
            return pl.pallas_call(
                lambda *refs: kernel(step, *refs),
                out_shape=(tile_shape(27, extent_x), *extra),
                in_specs=in_vmem(len(operands)) + in_any(len(new)),
                out_specs=tuple(in_any(1) + in_vmem(len(extra))),
                scratch_shapes=[
                    pltpu.VMEM((planes, 27, 16, 128), jnp.float32),
                    pltpu.VMEM((2, 27, 16, 128), jnp.float32),
                    pltpu.SemaphoreType.DMA((planes,)),
                ],
                input_output_aliases={len(operands): 0} if new else {},
                compiler_params=params,
            )(*operands, *new)

        messages = () if last else (tile_shape(10),) * 2
        kernel = lambda step, *refs: inner_kernel(step, last, *refs)
        new, *columns = make_planes(kernel, extent_x - 2, (), (), (tile_shape(),) * 2)
        cross = pl.pallas_call(
            lambda *refs: cross_kernel(count, *refs),
            out_shape=tile_shape(9),
            in_specs=in_vmem(count + 2) + in_any(1),
            out_specs=in_vmem(1)[0],
            compiler_params=params,
        )(own, first, second, *others, info, columns[0])
        cross = send(cross, flip)
        field, *messages = make_planes(
            outer_kernel, 2, (two, one, cross, *columns), (new,), messages
        )
        if not last:
            first, second = messages
    return field[None]


def solution(mesh):
    sizes = tuple(mesh.shape[axis] for axis in ("zone", "gx", "yz"))
    in_specs = (
        P("zone", None, "gx", None, "yz"),
        P(None, "zone", None, "gx", None, "yz"),
        P("zone", "gx", None, "yz"),
        P("zone", None, "yz", None),
        P("zone", None, "yz", None),
        P("zone", None, "yz", None),
    )
    out_specs = P("zone", None, "gx", None, "yz")
    return jax.shard_map(
        lambda *args: body(sizes, *args),
        mesh=mesh,
        in_specs=in_specs,
        out_specs=out_specs,
        check_vma=False,
    )
```

```python
import itertools

import jax
import jax.numpy as jnp
import numpy as np
from jax import lax
from jax.experimental import pallas as pl
from jax.experimental.pallas import tpu as pltpu
from jax.sharding import PartitionSpec as P

OMEGA = 1.6
VMEM_LIMIT = 20 * 1024 * 1024
SIGNS = (-1, 0, 1)


def number(cx, cy, cz):
    return 9 * (cx + 1) + 3 * (cy + 1) + (cz + 1)


def lanes():
    return lax.broadcasted_iota(jnp.int32, (16, 128), 1)


def shift_y(tile, cy):
    if cy == 0:
        return tile
    row = lax.broadcasted_iota(jnp.int32, tile.shape, 0)
    if cy == 1:
        return jnp.where(row == 15, 0.0, pltpu.roll(tile, 15, 0))
    return jnp.where(row == 0, 0.0, pltpu.roll(tile, 1, 0))


def pack_columns(planes, x, low, high):
    lane = lanes()
    for slot in range(9):
        place = (x + 1) * 9 + slot
        here = lane == place
        low = jnp.where(here, pltpu.roll(planes(3 * slot + 2), place, 1), low)
        high = jnp.where(here, pltpu.roll(planes(3 * slot), place + 1, 1), high)
    return low, high


def is_even(axis):
    return lax.rem(lax.axis_index(axis), 2) == 0


def write_messages(top, low, high, first, second):
    even = is_even("yz")
    for j in range(9):
        tile = top(j)
        first[j] = tile
        second[j] = tile
    first[9] = jnp.where(even, high, low)
    second[9] = jnp.where(even, low, high)


def edges_from(first, second):
    even = is_even("yz")
    me, count = lax.axis_index("yz"), lax.axis_size("yz")
    low = jnp.where(me == 0, 0.0, jnp.where(even, second[9], first[9]))
    high = jnp.where(me == count - 1, 0.0, jnp.where(even, first[9], second[9]))
    return low, high


def pack_kernel(adj, top_out, first_out, second_out, kept, sems):
    extent_x = adj.shape[1]
    sides = [i for i in range(27) if i % 3 != 1]
    pairs = [(adj.at[i], kept.at[n]) for n, i in enumerate(sides)]
    pairs.append((adj.at[pl.ds(0, 9), extent_x - 1], top_out))
    copies = [pltpu.make_async_copy(*pair, sems.at[n]) for n, pair in enumerate(pairs)]
    for copy in copies:
        copy.start()
    for copy in copies:
        copy.wait()
    edges = jnp.zeros((16, 128), jnp.float32), jnp.zeros((16, 128), jnp.float32)
    for x in range(extent_x):
        edges = pack_columns(lambda i: kept[sides.index(i), x], x, *edges)
    write_messages(lambda j: top_out[j], *edges, first_out, second_out)


def info_kernel(device, cell, weight, out):
    for k in range(2):
        out[k] = (device[:, k] * 128 + cell[:, k]).astype(jnp.float32)
        out[2 + k] = weight[:, k]


def velocity_kernel(step, saved, out, kept, sems):
    extent_x = out.shape[1]

    def load(x):
        return pltpu.make_async_copy(saved.at[step, 0, :, x], kept.at[x], sems.at[x])

    lax.fori_loop(0, extent_x, lambda x, c: (load(x).start(), c)[1], 0)

    def one(x, carry):
        load(x).wait()
        for a, tile in enumerate(velocity_of(lambda i: kept[x, i])):
            out[a, x] = tile
        return carry

    lax.fori_loop(0, extent_x, one, 0)


def side_kernel(adj, second, first, _, two_out, one_out):
    extent_x = adj.shape[1]
    even = is_even("gx")
    for j in range(9):
        top, bottom = adj[j, extent_x - 1], adj[18 + j, 0]
        one_out[j] = jnp.where(even, top, bottom)
        two_out[j] = jnp.where(even, bottom, top)
    lane = lanes()
    low, high = edges_from(first, second)
    top, bottom = [
        jnp.where(lane < 64, pltpu.roll(low, 128 - start, 1), pltpu.roll(high, 192 - start, 1))
        for start in (9 * extent_x, 9)
    ]
    one_out[9] = jnp.where(even, top, bottom)
    two_out[9] = jnp.where(even, bottom, top)


def cross_kernel(count, *refs):
    own, first, second, ends = refs[:4]
    others = refs[4 : 1 + count]
    info, _, out = refs[1 + count :]
    interface = lax.axis_index("gx") == lax.axis_size("gx") - 1

    @pl.when(interface)
    def _():
        me = lax.axis_index("yz")
        even = is_even("yz")
        at_end = (me == 0) | (me == count - 1)
        rows = (0, 8)
        spots, picks = {}, {}
        for r in rows:
            for k in range(2):
                code = info[k, r : r + 8].astype(jnp.int32)
                ahead = lax.rem(code // 128 - me + count, count)
                spots[r, k] = lax.rem(code, 128)
                turned = jnp.where(even, ahead, lax.rem(count - ahead, count))
                masks = [turned == 1, turned == count - 1]
                masks += [ahead == count - hop for hop in range(2, count - 1)]
                picks[r, k] = masks
        for j in range(9):
            halves = []
            for r in rows:
                total = jnp.zeros((8, 128), jnp.float32)
                for k in range(2):
                    tiles = [ref[j, r : r + 8] for ref in (own, first, second, *others)]
                    tiles[2] = jnp.where(at_end, ends[j, r : r + 8], tiles[2])
                    got = [jnp.take_along_axis(tile, spots[r, k], axis=1) for tile in tiles]
                    picked = got[0]
                    for mask, value in zip(picks[r, k], got[1:]):
                        picked = jnp.where(mask, value, picked)
                    total = total + picked * info[2 + k, r : r + 8]
                halves.append(total)
            out[j] = jnp.concatenate(halves, axis=0)


def velocity_of(saved):
    totals, along_y, along_z = [], [], []
    for cx in SIGNS:
        sums, diffs = [], []
        for cy in SIGNS:
            lo, mid, hi = [saved(number(cx, cy, cz)) for cz in SIGNS]
            sums.append(lo + mid + hi)
            diffs.append(hi - lo)
        totals.append(sums[0] + sums[1] + sums[2])
        along_y.append(sums[2] - sums[0])
        along_z.append(diffs[0] + diffs[1] + diffs[2])
    density = totals[0] + totals[1] + totals[2]
    momentum = (
        totals[2] - totals[0],
        along_y[0] + along_y[1] + along_y[2],
        along_z[0] + along_z[1] + along_z[2],
    )
    return [part / density for part in momentum]


def moments_of(pull):
    rows = []
    for cx in SIGNS:
        plain, first, second = [], [], []
        for cy in SIGNS:
            lo, mid, hi = [pull(cx, cy, cz) for cz in SIGNS]
            both = lo + hi
            plain.append(mid + 0.25 * both)
            first.append(hi - lo)
            second.append(both)
        pair = plain[0] + plain[2]
        rows.append(
            (
                plain[1] + 0.25 * pair,
                plain[2] - plain[0],
                pair,
                first[1] + 0.25 * (first[0] + first[2]),
                first[2] - first[0],
                second[1] + 0.25 * (second[0] + second[2]),
            )
        )
    even = [rows[1][n] + 0.25 * (rows[0][n] + rows[2][n]) for n in range(6)]
    zero = (8.0 / 27.0) * even[0]
    along = (
        (2.0 / 27.0) * (rows[2][0] - rows[0][0]),
        (2.0 / 27.0) * even[1],
        (2.0 / 27.0) * even[3],
    )
    square = (
        (2.0 / 27.0) * (rows[2][0] + rows[0][0]),
        (2.0 / 27.0) * even[2],
        (2.0 / 27.0) * even[5],
    )
    mixed = (
        (1.0 / 54.0) * (rows[2][1] - rows[0][1]),
        (1.0 / 54.0) * (rows[2][3] - rows[0][3]),
        (1.0 / 54.0) * even[4],
    )
    return zero, along, square, mixed


def collide(pull, velocity, solid, store):
    zero, along, square, mixed = moments_of(lambda cx, cy, cz: pull(number(cx, cy, cz)))
    ux, uy, uz = velocity
    xy, xz, yz = mixed
    quadratic = (
        ux * ux * square[0]
        + uy * uy * square[1]
        + uz * uz * square[2]
        + 2.0 * (ux * uy * xy + ux * uz * xz + uy * uz * yz)
    )
    speed = ux * ux + uy * uy + uz * uz
    scalar = OMEGA * (zero * (1.0 + 1.5 * speed) - 4.5 * quadratic)
    vec_x = OMEGA * (3.0 * along[0] + 9.0 * (square[0] * ux + xy * uy + xz * uz) - 3.0 * ux * zero)
    vec_y = OMEGA * (3.0 * along[1] + 9.0 * (xy * ux + square[1] * uy + yz * uz) - 3.0 * uy * zero)
    vec_z = OMEGA * (3.0 * along[2] + 9.0 * (xz * ux + yz * uy + square[2] * uz) - 3.0 * uz * zero)
    wall = solid == 1
    for cx in SIGNS:
        base = scalar if cx == 0 else (scalar + vec_x if cx > 0 else scalar - vec_x)
        for cy in SIGNS:
            inner = base if cy == 0 else (base + vec_y if cy > 0 else base - vec_y)
            for cz in SIGNS:
                full = inner if cz == 0 else (inner + vec_z if cz > 0 else inner - vec_z)
                i = number(cx, cy, cz)
                store(i, jnp.where(wall, pull(26 - i), (1.0 - OMEGA) * pull(i) + full))


def pull_plane(tile_of, edges_of, pulled, raw=None):
    lane = lanes()
    for cx in SIGNS:
        low_edge, high_edge, start = edges_of(cx)
        for cy in SIGNS:
            place = start + 3 * (cx + 1) + cy + 1
            for cz in SIGNS:
                i = number(cx, cy, cz)
                source = tile_of(i, cx)
                tile = source
                if cz == -1:
                    edge = pltpu.roll(low_edge, 128 - place, 1)
                    tile = jnp.where(lane == 0, edge, pltpu.roll(source, 1, 1))
                elif cz == 1:
                    edge = pltpu.roll(high_edge, 127 - place, 1)
                    tile = jnp.where(lane == 127, edge, pltpu.roll(source, 127, 1))
                if raw is not None and cx == 1:
                    tile = jnp.where(raw, source, tile)
                pulled[i] = shift_y(tile, cy)


def inner_kernel(step, last, adj, vel, solid, first, second, *rest):
    out, low_out, high_out, made, pulled, sems = rest
    extent_x = adj.shape[1]
    low_edge, high_edge = edges_from(first, second)

    def save(x):
        return pltpu.make_async_copy(made.at[x - 1], out.at[:, x], sems.at[x - 1])

    def plane(x, carry):
        here = pulled.at[lax.rem(x, 2)]
        pull_plane(
            lambda i, cx: adj[i, x + cx],
            lambda cx: (low_edge, high_edge, (x + 1 + cx) * 9),
            here,
        )

        def store(i, tile):
            made[x - 1, i] = tile

        velocity = [vel[a, x] for a in range(3)]
        collide(lambda i: here[i], velocity, solid[0, x], store)
        save(x).start()
        if last:
            return carry
        return pack_columns(lambda i: made[x - 1, i], x, *carry)

    zero = jnp.zeros((16, 128), jnp.float32)
    low_out[...], high_out[...] = lax.fori_loop(1, extent_x - 1, plane, (zero, zero), unroll=2)
    lax.fori_loop(1, extent_x - 1, lambda x, c: (save(x).wait(), c)[1], 0)


def outer_kernel(x, step, adj, vel, solid, first, second, two, one, *rest):
    if x == 0:
        low_in, high_in, _, out, low_out, high_out, made, pulled, sems = rest
    else:
        cross, low_in, high_in, _, out, *messages, made, pulled, sems = rest
    extent_x = adj.shape[1]
    edges = edges_from(first, second)
    even = is_even("gx")
    interface = lax.axis_index("gx") == lax.axis_size("gx") - 1

    bottom = lax.axis_index("gx") == 0

    def below(j):
        return jnp.where(bottom, 0.0, jnp.where(even, two[j], one[j]))

    def above(j):
        tile = jnp.where(even, one[j], two[j])
        return jnp.where(interface, cross[j], tile) if j < 9 else tile

    ghost, beyond, raw = (-1, below, None) if x == 0 else (1, above, interface)
    pull_plane(
        lambda i, cx: beyond(i % 9) if cx == ghost else adj[i, x + cx],
        lambda cx: (
            (beyond(9), pltpu.roll(beyond(9), 64, 1), 0)
            if cx == ghost
            else (*edges, (x + 1 + cx) * 9)
        ),
        pulled.at[0],
        raw,
    )

    def store(i, tile):
        made[0, i] = tile

    velocity = [vel[a, x] for a in range(3)]
    collide(lambda i: pulled[0, i], velocity, solid[0, x], store)
    save = pltpu.make_async_copy(made.at[0], out.at[:, x], sems.at[0])
    save.start()
    if x == 0:
        low_out[...], high_out[...] = pack_columns(
            lambda i: made[0, i], x, low_in[...], high_in[...]
        )
    elif messages:
        low, high = pack_columns(lambda i: made[0, i], x, low_in[...], high_in[...])
        top_out, *messages = messages
        write_messages(lambda j: made[0, j], low, high, *messages)
        for j in range(9):
            top_out[j] = made[0, j]
    save.wait()


def tile_shape(*lead):
    return jax.ShapeDtypeStruct(lead + (16, 128), jnp.float32)


def in_vmem(n):
    return [pl.BlockSpec(memory_space=pltpu.VMEM)] * n


def in_any(n):
    return [pl.BlockSpec(memory_space=pl.ANY)] * n


def body(sizes, adjoint, saved, solid, band_device, band_cell, band_weight):
    zones, widths, count = sizes
    field = adjoint[0]
    extent_x = field.shape[1]
    axes = ("zone", "gx", "yz")
    params = pltpu.CompilerParams(vmem_limit_bytes=VMEM_LIMIT)

    def send(values, target):
        flat = lambda zone, gx, yz: (zone * widths + gx) * count + yz
        places = itertools.product(range(zones), range(widths), range(count))
        return lax.ppermute(values, axes, [(flat(*here), flat(*target(*here))) for here in places])

    def partner_of(place, shift):
        return place + 1 if (place + shift) % 2 == 0 else place - 1

    def flip(zone, gx, yz):
        return (1 - zone, gx, yz)

    def along_z(shift):
        def target(zone, gx, yz):
            to = partner_of(yz, shift)
            return (zone, gx, to) if 0 <= to < count else flip(zone, gx, yz)

        return target

    def hop_z(hop):
        def target(zone, gx, yz):
            if gx == widths - 1:
                return (zone, gx, (yz + hop) % count)
            return flip(zone, gx, yz)

        return target

    def ends_z(zone, gx, yz):
        if gx == widths - 1 and yz in (0, count - 1):
            return (zone, gx, count - 1 - yz)
        return flip(zone, gx, yz)

    def along_x(shift):
        def target(zone, gx, yz):
            to = partner_of(gx, shift)
            return (zone, to, yz) if 0 <= to < widths else flip(zone, gx, yz)

        return target

    info = pl.pallas_call(
        info_kernel,
        out_shape=tile_shape(4),
        in_specs=in_vmem(3),
        out_specs=in_vmem(1)[0],
        compiler_params=params,
    )(*[jnp.swapaxes(array[0], 1, 2) for array in (band_device, band_cell, band_weight)])
    info = send(info, flip)
    resident = pltpu.with_memory_space_constraint(field, pltpu.HBM)
    messages = (tile_shape(9), tile_shape(10), tile_shape(10))
    own, first, second = pl.pallas_call(
        pack_kernel,
        out_shape=messages,
        in_specs=[pl.BlockSpec(memory_space=pltpu.HBM)],
        out_specs=tuple(in_vmem(3)),
        scratch_shapes=[
            pltpu.VMEM((18, extent_x, 16, 128), jnp.float32),
            pltpu.SemaphoreType.DMA((19,)),
        ],
        compiler_params=params,
    )(resident)
    saved = pltpu.with_memory_space_constraint(saved, pltpu.HBM)
    for step in (1, 0):
        last = step == 0
        others = [send(own, target) for target in (ends_z, *map(hop_z, range(2, count - 1)))]
        first = send(first, along_z(0))
        second = send(second, along_z(1))
        vel = pl.pallas_call(
            lambda *refs: velocity_kernel(step, *refs),
            out_shape=tile_shape(3, extent_x),
            in_specs=[pl.BlockSpec(memory_space=pltpu.HBM)],
            out_specs=in_vmem(1)[0],
            scratch_shapes=[
                pltpu.VMEM((extent_x, 27, 16, 128), jnp.float32),
                pltpu.SemaphoreType.DMA((extent_x,)),
            ],
            compiler_params=params,
        )(saved)
        two, one = pl.pallas_call(
            side_kernel,
            out_shape=(tile_shape(10),) * 2,
            in_specs=in_vmem(3) + in_any(1),
            out_specs=tuple(in_vmem(2)),
            compiler_params=params,
        )(field, second, first, vel)
        two = send(two, along_x(1))
        one = send(one, along_x(0))

        def make_planes(kernel, planes, given, new, extra):
            operands = (field, vel, solid, first, second, *given)
            return pl.pallas_call(
                lambda *refs: kernel(step, *refs),
                out_shape=(tile_shape(27, extent_x), *extra),
                in_specs=in_vmem(len(operands)) + in_any(len(new)),
                out_specs=tuple(in_any(1) + in_vmem(len(extra))),
                scratch_shapes=[
                    pltpu.VMEM((planes, 27, 16, 128), jnp.float32),
                    pltpu.VMEM((2, 27, 16, 128), jnp.float32),
                    pltpu.SemaphoreType.DMA((planes,)),
                ],
                input_output_aliases={len(operands): 0} if new else {},
                compiler_params=params,
            )(*operands, *new)

        kernel = lambda step, *refs: inner_kernel(step, last, *refs)
        new, *columns = make_planes(kernel, extent_x - 2, (), (), (tile_shape(),) * 2)
        cross = pl.pallas_call(
            lambda *refs: cross_kernel(count, *refs),
            out_shape=tile_shape(9),
            in_specs=in_vmem(count + 2) + in_any(1),
            out_specs=in_vmem(1)[0],
            compiler_params=params,
        )(own, first, second, *others, info, columns[0])
        cross = send(cross, flip)
        ghosts = (two, one)
        new, *columns = make_planes(
            lambda *refs: outer_kernel(0, *refs), 1, (*ghosts, *columns), (new,), (tile_shape(),) * 2
        )
        field, *results = make_planes(
            lambda *refs: outer_kernel(extent_x - 1, *refs),
            1,
            (*ghosts, cross, *columns),
            (new,),
            () if last else messages,
        )
        if not last:
            own, first, second = results
    return field[None]


def solution(mesh):
    sizes = tuple(mesh.shape[axis] for axis in ("zone", "gx", "yz"))
    in_specs = (
        P("zone", None, "gx", None, "yz"),
        P(None, "zone", None, "gx", None, "yz"),
        P("zone", "gx", None, "yz"),
        P("zone", None, "yz", None),
        P("zone", None, "yz", None),
        P("zone", None, "yz", None),
    )
    out_specs = P("zone", None, "gx", None, "yz")
    return jax.shard_map(
        lambda *args: body(sizes, *args),
        mesh=mesh,
        in_specs=in_specs,
        out_specs=out_specs,
        check_vma=False,
    )
```

```python
import itertools

import jax
import jax.numpy as jnp
import numpy as np
from jax import lax
from jax.experimental import pallas as pl
from jax.experimental.pallas import tpu as pltpu
from jax.sharding import PartitionSpec as P

OMEGA = 1.6
VMEM_LIMIT = 20 * 1024 * 1024
SIGNS = (-1, 0, 1)


def number(cx, cy, cz):
    return 9 * (cx + 1) + 3 * (cy + 1) + (cz + 1)


def lanes():
    return lax.broadcasted_iota(jnp.int32, (16, 128), 1)


def shift_y(tile, cy):
    if cy == 0:
        return tile
    row = lax.broadcasted_iota(jnp.int32, tile.shape, 0)
    if cy == 1:
        return jnp.where(row == 15, 0.0, pltpu.roll(tile, 15, 0))
    return jnp.where(row == 0, 0.0, pltpu.roll(tile, 1, 0))


def pack_columns(planes, x, low, high):
    lane = lanes()
    for slot in range(9):
        place = (x + 1) * 9 + slot
        here = lane == place
        low = jnp.where(here, pltpu.roll(planes(3 * slot + 2), place, 1), low)
        high = jnp.where(here, pltpu.roll(planes(3 * slot), place + 1, 1), high)
    return low, high


def is_even(axis):
    return lax.rem(lax.axis_index(axis), 2) == 0


def write_messages(top, low, high, own, first, second):
    even = is_even("yz")
    for j in range(9):
        tile = top(j)
        own[j] = tile
        first[j] = tile
        second[j] = tile
    first[9] = jnp.where(even, low, high)
    second[9] = jnp.where(even, high, low)


def edges_from(first, second):
    even = is_even("yz")
    me, count = lax.axis_index("yz"), lax.axis_size("yz")
    low = jnp.where(me == 0, 0.0, jnp.where(even, first[9], second[9]))
    high = jnp.where(me == count - 1, 0.0, jnp.where(even, second[9], first[9]))
    return low, high


def pack_kernel(adj, own_out, first_out, second_out, kept, top, sems):
    extent_x = adj.shape[2]
    copies = [
        pltpu.make_async_copy(adj.at[:, 2 * side, x], kept.at[side, x], sems.at[side, x])
        for x in range(extent_x)
        for side in range(2)
    ]
    copies.append(pltpu.make_async_copy(adj.at[pl.ds(0, 3), :, extent_x - 1], top, sems.at[2, 0]))
    for copy in copies:
        copy.start()
    edges = jnp.zeros((16, 128), jnp.float32), jnp.zeros((16, 128), jnp.float32)
    for x in range(extent_x):
        for copy in copies[2 * x : 2 * x + 2]:
            copy.wait()
        edges = pack_columns(lambda i: kept[(i % 3) // 2, x, i // 3], x, *edges)
    copies[-1].wait()
    write_messages(lambda j: top[j // 3, j % 3], *edges, own_out, first_out, second_out)


def info_kernel(device, cell, weight, out):
    for k in range(2):
        out[k] = (device[:, k] * 128 + cell[:, k]).astype(jnp.float32)
        out[2 + k] = weight[:, k]


def velocity_kernel(step, saved, out, kept, sems):
    extent_x = out.shape[1]

    def load(x):
        return pltpu.make_async_copy(saved.at[step, 0, :, x], kept.at[x], sems.at[x])

    lax.fori_loop(0, extent_x, lambda x, c: (load(x).start(), c)[1], 0)

    def one(x, carry):
        load(x).wait()
        for a, tile in enumerate(velocity_of(lambda i: kept[x, i])):
            out[a, x] = tile
        return carry

    lax.fori_loop(0, extent_x, one, 0)


def side_kernel(adj, first, second, _, two_out, one_out):
    extent_x = adj.shape[1]
    even = is_even("gx")
    for j in range(9):
        top, bottom = adj[j, extent_x - 1], adj[18 + j, 0]
        one_out[j] = jnp.where(even, top, bottom)
        two_out[j] = jnp.where(even, bottom, top)
    lane = lanes()
    low, high = edges_from(first, second)
    top, bottom = [
        jnp.where(lane < 64, pltpu.roll(low, 128 - start, 1), pltpu.roll(high, 192 - start, 1))
        for start in (9 * extent_x, 9)
    ]
    one_out[9] = jnp.where(even, top, bottom)
    two_out[9] = jnp.where(even, bottom, top)


def cross_kernel(count, *refs):
    own, first, second, ends = refs[:4]
    others = refs[4 : 1 + count]
    info, _, out = refs[1 + count :]
    interface = lax.axis_index("gx") == lax.axis_size("gx") - 1

    @pl.when(interface)
    def _():
        me = lax.axis_index("yz")
        even = is_even("yz")
        at_end = (me == 0) | (me == count - 1)
        rows = (0, 8)
        spots, picks = {}, {}
        for r in rows:
            for k in range(2):
                code = info[k, r : r + 8].astype(jnp.int32)
                ahead = lax.rem(code // 128 - me + count, count)
                spots[r, k] = lax.rem(code, 128)
                turned = jnp.where(even, lax.rem(count - ahead, count), ahead)
                masks = [turned == 1, turned == count - 1]
                masks += [ahead == count - hop for hop in range(2, count - 1)]
                picks[r, k] = masks
        for j in range(9):
            halves = []
            for r in rows:
                total = jnp.zeros((8, 128), jnp.float32)
                for k in range(2):
                    tiles = [ref[j, r : r + 8] for ref in (own, first, second, *others)]
                    tiles[1] = jnp.where(at_end, ends[j, r : r + 8], tiles[1])
                    got = [jnp.take_along_axis(tile, spots[r, k], axis=1) for tile in tiles]
                    picked = got[0]
                    for mask, value in zip(picks[r, k], got[1:]):
                        picked = jnp.where(mask, value, picked)
                    total = total + picked * info[2 + k, r : r + 8]
                halves.append(total)
            out[j] = jnp.concatenate(halves, axis=0)


def velocity_of(saved):
    totals, along_y, along_z = [], [], []
    for cx in SIGNS:
        sums, diffs = [], []
        for cy in SIGNS:
            lo, mid, hi = [saved(number(cx, cy, cz)) for cz in SIGNS]
            sums.append(lo + mid + hi)
            diffs.append(hi - lo)
        totals.append(sums[0] + sums[1] + sums[2])
        along_y.append(sums[2] - sums[0])
        along_z.append(diffs[0] + diffs[1] + diffs[2])
    density = totals[0] + totals[1] + totals[2]
    momentum = (
        totals[2] - totals[0],
        along_y[0] + along_y[1] + along_y[2],
        along_z[0] + along_z[1] + along_z[2],
    )
    return [part / density for part in momentum]


def moments_of(pull):
    rows = []
    for cx in SIGNS:
        plain, first, second = [], [], []
        for cy in SIGNS:
            lo, mid, hi = [pull(cx, cy, cz) for cz in SIGNS]
            both = lo + hi
            plain.append(mid + 0.25 * both)
            first.append(hi - lo)
            second.append(both)
        pair = plain[0] + plain[2]
        rows.append(
            (
                plain[1] + 0.25 * pair,
                plain[2] - plain[0],
                pair,
                first[1] + 0.25 * (first[0] + first[2]),
                first[2] - first[0],
                second[1] + 0.25 * (second[0] + second[2]),
            )
        )
    even = [rows[1][n] + 0.25 * (rows[0][n] + rows[2][n]) for n in range(6)]
    zero = (8.0 / 27.0) * even[0]
    along = (
        (2.0 / 27.0) * (rows[2][0] - rows[0][0]),
        (2.0 / 27.0) * even[1],
        (2.0 / 27.0) * even[3],
    )
    square = (
        (2.0 / 27.0) * (rows[2][0] + rows[0][0]),
        (2.0 / 27.0) * even[2],
        (2.0 / 27.0) * even[5],
    )
    mixed = (
        (1.0 / 54.0) * (rows[2][1] - rows[0][1]),
        (1.0 / 54.0) * (rows[2][3] - rows[0][3]),
        (1.0 / 54.0) * even[4],
    )
    return zero, along, square, mixed


def collide(pull, velocity, solid, store):
    zero, along, square, mixed = moments_of(lambda cx, cy, cz: pull(number(cx, cy, cz)))
    ux, uy, uz = velocity
    xy, xz, yz = mixed
    quadratic = (
        ux * ux * square[0]
        + uy * uy * square[1]
        + uz * uz * square[2]
        + 2.0 * (ux * uy * xy + ux * uz * xz + uy * uz * yz)
    )
    speed = ux * ux + uy * uy + uz * uz
    scalar = OMEGA * (zero * (1.0 + 1.5 * speed) - 4.5 * quadratic)
    vec_x = OMEGA * (3.0 * along[0] + 9.0 * (square[0] * ux + xy * uy + xz * uz) - 3.0 * ux * zero)
    vec_y = OMEGA * (3.0 * along[1] + 9.0 * (xy * ux + square[1] * uy + yz * uz) - 3.0 * uy * zero)
    vec_z = OMEGA * (3.0 * along[2] + 9.0 * (xz * ux + yz * uy + square[2] * uz) - 3.0 * uz * zero)
    wall = solid == 1
    for cx in SIGNS:
        base = scalar if cx == 0 else (scalar + vec_x if cx > 0 else scalar - vec_x)
        for cy in SIGNS:
            inner = base if cy == 0 else (base + vec_y if cy > 0 else base - vec_y)
            for cz in SIGNS:
                full = inner if cz == 0 else (inner + vec_z if cz > 0 else inner - vec_z)
                i = number(cx, cy, cz)
                store(i, jnp.where(wall, pull(26 - i), (1.0 - OMEGA) * pull(i) + full))


def pull_plane(tile_of, edges_of, pulled, raw=None):
    lane = lanes()
    for cx in SIGNS:
        low_edge, high_edge, start = edges_of(cx)
        for cy in SIGNS:
            place = start + 3 * (cx + 1) + cy + 1
            for cz in SIGNS:
                i = number(cx, cy, cz)
                source = tile_of(i, cx)
                tile = source
                if cz == -1:
                    edge = pltpu.roll(low_edge, 128 - place, 1)
                    tile = jnp.where(lane == 0, edge, pltpu.roll(source, 1, 1))
                elif cz == 1:
                    edge = pltpu.roll(high_edge, 127 - place, 1)
                    tile = jnp.where(lane == 127, edge, pltpu.roll(source, 127, 1))
                if raw is not None and cx == 1:
                    tile = jnp.where(raw, source, tile)
                pulled[i] = shift_y(tile, cy)


def inner_kernel(step, last, adj, vel, solid, first, second, *rest):
    out, low_out, high_out, made, pulled, sems = rest
    extent_x = adj.shape[1]
    low_edge, high_edge = edges_from(first, second)

    def save(x):
        return pltpu.make_async_copy(made.at[x - 1], out.at[:, x], sems.at[x - 1])

    def plane(x, carry):
        here = pulled.at[lax.rem(x, 2)]
        pull_plane(
            lambda i, cx: adj[i, x + cx],
            lambda cx: (low_edge, high_edge, (x + 1 + cx) * 9),
            here,
        )

        def store(i, tile):
            made[x - 1, i] = tile

        velocity = [vel[a, x] for a in range(3)]
        collide(lambda i: here[i], velocity, solid[0, x], store)
        save(x).start()
        if last:
            return carry
        return pack_columns(lambda i: made[x - 1, i], x, *carry)

    zero = jnp.zeros((16, 128), jnp.float32)
    low_out[...], high_out[...] = lax.fori_loop(1, extent_x - 1, plane, (zero, zero), unroll=2)
    lax.fori_loop(1, extent_x - 1, lambda x, c: (save(x).wait(), c)[1], 0)


def outer_kernel(step, adj, vel, solid, first, second, two, one, cross, *rest):
    *rest, made, pulled, sems = rest
    low_in, high_in, _, out, *messages = rest
    extent_x = adj.shape[1]
    edges = edges_from(first, second)
    even = is_even("gx")
    interface = lax.axis_index("gx") == lax.axis_size("gx") - 1

    bottom = lax.axis_index("gx") == 0

    def below(j):
        return jnp.where(bottom, 0.0, jnp.where(even, two[j], one[j]))

    def above(j):
        tile = jnp.where(even, one[j], two[j])
        return jnp.where(interface, cross[j], tile) if j < 9 else tile

    def plane(n, x, ghost, beyond, raw):
        pull_plane(
            lambda i, cx: beyond(i % 9) if cx == ghost else adj[i, x + cx],
            lambda cx: (
                (beyond(9), pltpu.roll(beyond(9), 64, 1), 0)
                if cx == ghost
                else (*edges, (x + 1 + cx) * 9)
            ),
            pulled.at[n],
            raw,
        )

        def store(i, tile):
            made[n, i] = tile

        velocity = [vel[a, x] for a in range(3)]
        collide(lambda i: pulled[n, i], velocity, solid[0, x], store)
        save = pltpu.make_async_copy(made.at[n], out.at[:, x], sems.at[n])
        save.start()
        return save

    final = extent_x - 1
    saves = [plane(0, 0, -1, below, None), plane(1, final, 1, above, interface)]
    if messages:
        low, high = low_in[...], high_in[...]
        low, high = pack_columns(lambda i: made[0, i], 0, low, high)
        low, high = pack_columns(lambda i: made[1, i], final, low, high)
        write_messages(lambda j: made[1, j], low, high, *messages)
    for save in saves:
        save.wait()


def tile_shape(*lead):
    return jax.ShapeDtypeStruct(lead + (16, 128), jnp.float32)


def in_vmem(n):
    return [pl.BlockSpec(memory_space=pltpu.VMEM)] * n


def in_any(n):
    return [pl.BlockSpec(memory_space=pl.ANY)] * n


def body(sizes, adjoint, saved, solid, band_device, band_cell, band_weight):
    zones, widths, count = sizes
    field = adjoint[0]
    extent_x = field.shape[1]
    axes = ("zone", "gx", "yz")
    params = pltpu.CompilerParams(vmem_limit_bytes=VMEM_LIMIT)

    def send(values, target):
        flat = lambda zone, gx, yz: (zone * widths + gx) * count + yz
        places = itertools.product(range(zones), range(widths), range(count))
        return lax.ppermute(values, axes, [(flat(*here), flat(*target(*here))) for here in places])

    def partner_of(place, shift):
        return place + 1 if (place + shift) % 2 == 0 else place - 1

    def flip(zone, gx, yz):
        return (1 - zone, gx, yz)

    def along_z(shift):
        def target(zone, gx, yz):
            to = partner_of(yz, shift)
            return (zone, gx, to) if 0 <= to < count else flip(zone, gx, yz)

        return target

    def hop_z(hop):
        def target(zone, gx, yz):
            if gx == widths - 1:
                return (zone, gx, (yz + hop) % count)
            return flip(zone, gx, yz)

        return target

    def ends_z(zone, gx, yz):
        if gx == widths - 1 and yz in (0, count - 1):
            return (zone, gx, count - 1 - yz)
        return flip(zone, gx, yz)

    def along_x(shift):
        def target(zone, gx, yz):
            to = partner_of(gx, shift)
            return (zone, to, yz) if 0 <= to < widths else flip(zone, gx, yz)

        return target

    info = pl.pallas_call(
        info_kernel,
        out_shape=tile_shape(4),
        in_specs=in_vmem(3),
        out_specs=in_vmem(1)[0],
        compiler_params=params,
    )(*[jnp.swapaxes(array[0], 1, 2) for array in (band_device, band_cell, band_weight)])
    info = send(info, flip)
    messages = (tile_shape(9), tile_shape(10), tile_shape(10))
    own, first, second = pl.pallas_call(
        pack_kernel,
        out_shape=messages,
        in_specs=[pl.BlockSpec(memory_space=pltpu.HBM)],
        out_specs=tuple(in_vmem(3)),
        scratch_shapes=[
            pltpu.VMEM((2, extent_x, 9, 16, 128), jnp.float32),
            pltpu.VMEM((3, 3, 16, 128), jnp.float32),
            pltpu.SemaphoreType.DMA((3, extent_x)),
        ],
        compiler_params=params,
    )(pltpu.with_memory_space_constraint(field.reshape(9, 3, extent_x, 16, 128), pltpu.HBM))
    saved = pltpu.with_memory_space_constraint(saved, pltpu.HBM)
    for step in (1, 0):
        last = step == 0
        first = send(first, along_z(1))
        second = send(second, along_z(0))
        others = [send(own, target) for target in (ends_z, *map(hop_z, range(2, count - 1)))]
        vel = pl.pallas_call(
            lambda *refs: velocity_kernel(step, *refs),
            out_shape=tile_shape(3, extent_x),
            in_specs=[pl.BlockSpec(memory_space=pltpu.HBM)],
            out_specs=in_vmem(1)[0],
            scratch_shapes=[
                pltpu.VMEM((extent_x, 27, 16, 128), jnp.float32),
                pltpu.SemaphoreType.DMA((extent_x,)),
            ],
            compiler_params=params,
        )(saved)
        two, one = pl.pallas_call(
            side_kernel,
            out_shape=(tile_shape(10),) * 2,
            in_specs=in_vmem(3) + in_any(1),
            out_specs=tuple(in_vmem(2)),
            compiler_params=params,
        )(field, first, second, vel)
        two = send(two, along_x(1))
        one = send(one, along_x(0))

        def make_planes(kernel, planes, given, new, extra):
            operands = (field, vel, solid, first, second, *given)
            return pl.pallas_call(
                lambda *refs: kernel(step, *refs),
                out_shape=(tile_shape(27, extent_x), *extra),
                in_specs=in_vmem(len(operands)) + in_any(len(new)),
                out_specs=tuple(in_any(1) + in_vmem(len(extra))),
                scratch_shapes=[
                    pltpu.VMEM((planes, 27, 16, 128), jnp.float32),
                    pltpu.VMEM((2, 27, 16, 128), jnp.float32),
                    pltpu.SemaphoreType.DMA((planes,)),
                ],
                input_output_aliases={len(operands): 0} if new else {},
                compiler_params=params,
            )(*operands, *new)

        kernel = lambda step, *refs: inner_kernel(step, last, *refs)
        new, *columns = make_planes(kernel, extent_x - 2, (), (), (tile_shape(),) * 2)
        cross = pl.pallas_call(
            lambda *refs: cross_kernel(count, *refs),
            out_shape=tile_shape(9),
            in_specs=in_vmem(count + 2) + in_any(1),
            out_specs=in_vmem(1)[0],
            compiler_params=params,
        )(own, first, second, *others, info, columns[0])
        cross = send(cross, flip)
        field, *results = make_planes(
            outer_kernel, 2, (two, one, cross, *columns), (new,), () if last else messages
        )
        if not last:
            own, first, second = results
    return field[None]


def solution(mesh):
    sizes = tuple(mesh.shape[axis] for axis in ("zone", "gx", "yz"))
    in_specs = (
        P("zone", None, "gx", None, "yz"),
        P(None, "zone", None, "gx", None, "yz"),
        P("zone", "gx", None, "yz"),
        P("zone", None, "yz", None),
        P("zone", None, "yz", None),
        P("zone", None, "yz", None),
    )
    out_specs = P("zone", None, "gx", None, "yz")
    return jax.shard_map(
        lambda *args: body(sizes, *args),
        mesh=mesh,
        in_specs=in_specs,
        out_specs=out_specs,
        check_vma=False,
    )
```

```python
import itertools

import jax
import jax.numpy as jnp
import numpy as np
from jax import lax
from jax.experimental import pallas as pl
from jax.experimental.pallas import tpu as pltpu
from jax.sharding import PartitionSpec as P

OMEGA = 1.6
VMEM_LIMIT = 20 * 1024 * 1024
SIGNS = (-1, 0, 1)


def number(cx, cy, cz):
    return 9 * (cx + 1) + 3 * (cy + 1) + (cz + 1)


def lanes():
    return lax.broadcasted_iota(jnp.int32, (16, 128), 1)


def shift_y(tile, cy):
    if cy == 0:
        return tile
    row = lax.broadcasted_iota(jnp.int32, tile.shape, 0)
    if cy == 1:
        return jnp.where(row == 15, 0.0, pltpu.roll(tile, 15, 0))
    return jnp.where(row == 0, 0.0, pltpu.roll(tile, 1, 0))


def pack_columns(planes, x, low, high):
    lane = lanes()
    for slot in range(9):
        place = (x + 1) * 9 + slot
        here = lane == place
        low = jnp.where(here, pltpu.roll(planes(3 * slot + 2), place, 1), low)
        high = jnp.where(here, pltpu.roll(planes(3 * slot), place + 1, 1), high)
    return low, high


def is_even(axis):
    return lax.rem(lax.axis_index(axis), 2) == 0


def write_messages(top, low, high, own, first, second):
    even = is_even("yz")
    for j in range(9):
        tile = top(j)
        own[j] = tile
        first[j] = tile
        second[j] = tile
    first[9] = jnp.where(even, low, high)
    second[9] = jnp.where(even, high, low)


def edges_from(first, second):
    even = is_even("yz")
    me, count = lax.axis_index("yz"), lax.axis_size("yz")
    low = jnp.where(me == 0, 0.0, jnp.where(even, first[9], second[9]))
    high = jnp.where(me == count - 1, 0.0, jnp.where(even, second[9], first[9]))
    return low, high


def pack_kernel(adj, field_out, own_out, first_out, second_out, sems):
    extent_x = adj.shape[1]
    copies = [
        pltpu.make_async_copy(adj.at[:, x], field_out.at[:, x], sems.at[x]) for x in range(extent_x)
    ]
    for copy in copies:
        copy.start()
    edges = jnp.zeros((16, 128), jnp.float32), jnp.zeros((16, 128), jnp.float32)
    for x in range(extent_x):
        copies[x].wait()
        edges = pack_columns(lambda i: field_out[i, x], x, *edges)
    write_messages(
        lambda j: field_out[j, extent_x - 1], *edges, own_out, first_out, second_out
    )


def info_kernel(device, cell, weight, out):
    for k in range(2):
        out[k] = (device[:, k] * 128 + cell[:, k]).astype(jnp.float32)
        out[2 + k] = weight[:, k]


def velocity_kernel(step, saved, *rest):
    *carried, out, kept, sems = rest
    extent_x = out.shape[1]
    copies = []
    if carried:
        copies.append(pltpu.make_async_copy(carried[0], carried[1], sems.at[extent_x]))
        copies[0].start()

    def load(x):
        return pltpu.make_async_copy(saved.at[step, 0, :, x], kept.at[x], sems.at[x])

    lax.fori_loop(0, extent_x, lambda x, c: (load(x).start(), c)[1], 0)

    def one(x, carry):
        load(x).wait()
        for a, tile in enumerate(velocity_of(lambda i: kept[x, i])):
            out[a, x] = tile
        return carry

    lax.fori_loop(0, extent_x, one, 0)
    for copy in copies:
        copy.wait()


def side_kernel(adj, first, second, _, two_out, one_out):
    extent_x = adj.shape[1]
    even = is_even("gx")
    for j in range(9):
        top, bottom = adj[j, extent_x - 1], adj[18 + j, 0]
        one_out[j] = jnp.where(even, top, bottom)
        two_out[j] = jnp.where(even, bottom, top)
    lane = lanes()
    low, high = edges_from(first, second)
    top, bottom = [
        jnp.where(lane < 64, pltpu.roll(low, 128 - start, 1), pltpu.roll(high, 192 - start, 1))
        for start in (9 * extent_x, 9)
    ]
    one_out[9] = jnp.where(even, top, bottom)
    two_out[9] = jnp.where(even, bottom, top)


def cross_kernel(count, *refs):
    own, first, second, ends = refs[:4]
    others = refs[4 : 1 + count]
    info, _, out = refs[1 + count :]
    interface = lax.axis_index("gx") == lax.axis_size("gx") - 1

    @pl.when(interface)
    def _():
        me = lax.axis_index("yz")
        even = is_even("yz")
        at_end = (me == 0) | (me == count - 1)
        rows = (0, 8)
        spots, picks = {}, {}
        for r in rows:
            for k in range(2):
                code = info[k, r : r + 8].astype(jnp.int32)
                ahead = lax.rem(code // 128 - me + count, count)
                spots[r, k] = lax.rem(code, 128)
                turned = jnp.where(even, lax.rem(count - ahead, count), ahead)
                masks = [turned == 1, turned == count - 1]
                masks += [ahead == count - hop for hop in range(2, count - 1)]
                picks[r, k] = masks
        for j in range(9):
            halves = []
            for r in rows:
                total = jnp.zeros((8, 128), jnp.float32)
                for k in range(2):
                    tiles = [ref[j, r : r + 8] for ref in (own, first, second, *others)]
                    tiles[1] = jnp.where(at_end, ends[j, r : r + 8], tiles[1])
                    got = [jnp.take_along_axis(tile, spots[r, k], axis=1) for tile in tiles]
                    picked = got[0]
                    for mask, value in zip(picks[r, k], got[1:]):
                        picked = jnp.where(mask, value, picked)
                    total = total + picked * info[2 + k, r : r + 8]
                halves.append(total)
            out[j] = jnp.concatenate(halves, axis=0)


def velocity_of(saved):
    totals, along_y, along_z = [], [], []
    for cx in SIGNS:
        sums, diffs = [], []
        for cy in SIGNS:
            lo, mid, hi = [saved(number(cx, cy, cz)) for cz in SIGNS]
            sums.append(lo + mid + hi)
            diffs.append(hi - lo)
        totals.append(sums[0] + sums[1] + sums[2])
        along_y.append(sums[2] - sums[0])
        along_z.append(diffs[0] + diffs[1] + diffs[2])
    density = totals[0] + totals[1] + totals[2]
    momentum = (
        totals[2] - totals[0],
        along_y[0] + along_y[1] + along_y[2],
        along_z[0] + along_z[1] + along_z[2],
    )
    return [part / density for part in momentum]


def moments_of(pull):
    rows = []
    for cx in SIGNS:
        plain, first, second = [], [], []
        for cy in SIGNS:
            lo, mid, hi = [pull(cx, cy, cz) for cz in SIGNS]
            both = lo + hi
            plain.append(mid + 0.25 * both)
            first.append(hi - lo)
            second.append(both)
        pair = plain[0] + plain[2]
        rows.append(
            (
                plain[1] + 0.25 * pair,
                plain[2] - plain[0],
                pair,
                first[1] + 0.25 * (first[0] + first[2]),
                first[2] - first[0],
                second[1] + 0.25 * (second[0] + second[2]),
            )
        )
    even = [rows[1][n] + 0.25 * (rows[0][n] + rows[2][n]) for n in range(6)]
    zero = (8.0 / 27.0) * even[0]
    along = (
        (2.0 / 27.0) * (rows[2][0] - rows[0][0]),
        (2.0 / 27.0) * even[1],
        (2.0 / 27.0) * even[3],
    )
    square = (
        (2.0 / 27.0) * (rows[2][0] + rows[0][0]),
        (2.0 / 27.0) * even[2],
        (2.0 / 27.0) * even[5],
    )
    mixed = (
        (1.0 / 54.0) * (rows[2][1] - rows[0][1]),
        (1.0 / 54.0) * (rows[2][3] - rows[0][3]),
        (1.0 / 54.0) * even[4],
    )
    return zero, along, square, mixed


def collide(pull, velocity, solid, store):
    zero, along, square, mixed = moments_of(lambda cx, cy, cz: pull(number(cx, cy, cz)))
    ux, uy, uz = velocity
    xy, xz, yz = mixed
    quadratic = (
        ux * ux * square[0]
        + uy * uy * square[1]
        + uz * uz * square[2]
        + 2.0 * (ux * uy * xy + ux * uz * xz + uy * uz * yz)
    )
    speed = ux * ux + uy * uy + uz * uz
    scalar = OMEGA * (zero * (1.0 + 1.5 * speed) - 4.5 * quadratic)
    vec_x = OMEGA * (3.0 * along[0] + 9.0 * (square[0] * ux + xy * uy + xz * uz) - 3.0 * ux * zero)
    vec_y = OMEGA * (3.0 * along[1] + 9.0 * (xy * ux + square[1] * uy + yz * uz) - 3.0 * uy * zero)
    vec_z = OMEGA * (3.0 * along[2] + 9.0 * (xz * ux + yz * uy + square[2] * uz) - 3.0 * uz * zero)
    wall = solid == 1
    for cx in SIGNS:
        base = scalar if cx == 0 else (scalar + vec_x if cx > 0 else scalar - vec_x)
        for cy in SIGNS:
            inner = base if cy == 0 else (base + vec_y if cy > 0 else base - vec_y)
            for cz in SIGNS:
                full = inner if cz == 0 else (inner + vec_z if cz > 0 else inner - vec_z)
                i = number(cx, cy, cz)
                store(i, jnp.where(wall, pull(26 - i), (1.0 - OMEGA) * pull(i) + full))


def pull_plane(tile_of, edges_of, pulled, raw=None):
    lane = lanes()
    for cx in SIGNS:
        low_edge, high_edge, start = edges_of(cx)
        for cy in SIGNS:
            place = start + 3 * (cx + 1) + cy + 1
            for cz in SIGNS:
                i = number(cx, cy, cz)
                source = tile_of(i, cx)
                tile = source
                if cz == -1:
                    edge = pltpu.roll(low_edge, 128 - place, 1)
                    tile = jnp.where(lane == 0, edge, pltpu.roll(source, 1, 1))
                elif cz == 1:
                    edge = pltpu.roll(high_edge, 127 - place, 1)
                    tile = jnp.where(lane == 127, edge, pltpu.roll(source, 127, 1))
                if raw is not None and cx == 1:
                    tile = jnp.where(raw, source, tile)
                pulled[i] = shift_y(tile, cy)


def inner_kernel(step, last, adj, vel, solid, first, second, *rest):
    out, low_out, high_out, made, pulled, sems = rest
    extent_x = adj.shape[1]
    low_edge, high_edge = edges_from(first, second)

    def save(x):
        return pltpu.make_async_copy(made.at[x - 1], out.at[:, x], sems.at[x - 1, 0])

    def plane(x, carry):
        here = pulled.at[lax.rem(x, 2)]
        pull_plane(
            lambda i, cx: adj[i, x + cx],
            lambda cx: (low_edge, high_edge, (x + 1 + cx) * 9),
            here,
        )

        def store(i, tile):
            made[x - 1, i] = tile

        velocity = [vel[a, x] for a in range(3)]
        collide(lambda i: here[i], velocity, solid[0, x], store)
        save(x).start()
        if last:
            return carry
        return pack_columns(lambda i: made[x - 1, i], x, *carry)

    zero = jnp.zeros((16, 128), jnp.float32)
    low_out[...], high_out[...] = lax.fori_loop(1, extent_x - 1, plane, (zero, zero), unroll=2)
    lax.fori_loop(1, extent_x - 1, lambda x, c: (save(x).wait(), c)[1], 0)


def outer_kernel(step, adj, vel, solid, first, second, two, one, cross, *rest):
    *rest, made, pulled, sems = rest
    low_in, high_in, _, out, *messages = rest
    extent_x = adj.shape[1]
    edges = edges_from(first, second)
    even = is_even("gx")
    interface = lax.axis_index("gx") == lax.axis_size("gx") - 1

    bottom = lax.axis_index("gx") == 0

    def below(j):
        return jnp.where(bottom, 0.0, jnp.where(even, two[j], one[j]))

    def above(j):
        tile = jnp.where(even, one[j], two[j])
        return jnp.where(interface, cross[j], tile) if j < 9 else tile

    def plane(n, x, ghost, beyond, raw):
        pull_plane(
            lambda i, cx: beyond(i % 9) if cx == ghost else adj[i, x + cx],
            lambda cx: (
                (beyond(9), pltpu.roll(beyond(9), 64, 1), 0)
                if cx == ghost
                else (*edges, (x + 1 + cx) * 9)
            ),
            pulled.at[n],
            raw,
        )

        def store(i, tile):
            made[n, i] = tile
            if i % 9 == 8:
                save(i // 9).start()

        def save(third):
            rows = pl.ds(9 * third, 9)
            return pltpu.make_async_copy(made.at[n, rows], out.at[rows, x], sems.at[n, third])

        velocity = [vel[a, x] for a in range(3)]
        collide(lambda i: pulled[n, i], velocity, solid[0, x], store)
        return [save(third) for third in range(3)]

    final = extent_x - 1
    saves = [plane(0, 0, -1, below, None), plane(1, final, 1, above, interface)]
    if messages:
        low, high = low_in[...], high_in[...]
        low, high = pack_columns(lambda i: made[0, i], 0, low, high)
        low, high = pack_columns(lambda i: made[1, i], final, low, high)
        write_messages(lambda j: made[1, j], low, high, *messages)
    for save in itertools.chain(*saves):
        save.wait()


def tile_shape(*lead):
    return jax.ShapeDtypeStruct(lead + (16, 128), jnp.float32)


def in_vmem(n):
    return [pl.BlockSpec(memory_space=pltpu.VMEM)] * n


def in_any(n):
    return [pl.BlockSpec(memory_space=pl.ANY)] * n


def body(sizes, adjoint, saved, solid, band_device, band_cell, band_weight):
    zones, widths, count = sizes
    field = adjoint[0]
    extent_x = field.shape[1]
    axes = ("zone", "gx", "yz")
    params = pltpu.CompilerParams(vmem_limit_bytes=VMEM_LIMIT)

    def send(values, target):
        flat = lambda zone, gx, yz: (zone * widths + gx) * count + yz
        places = itertools.product(range(zones), range(widths), range(count))
        return lax.ppermute(values, axes, [(flat(*here), flat(*target(*here))) for here in places])

    def partner_of(place, shift):
        return place + 1 if (place + shift) % 2 == 0 else place - 1

    def flip(zone, gx, yz):
        return (1 - zone, gx, yz)

    def along_z(shift):
        def target(zone, gx, yz):
            to = partner_of(yz, shift)
            return (zone, gx, to) if 0 <= to < count else flip(zone, gx, yz)

        return target

    def hop_z(hop):
        def target(zone, gx, yz):
            if gx == widths - 1:
                return (zone, gx, (yz + hop) % count)
            return flip(zone, gx, yz)

        return target

    def ends_z(zone, gx, yz):
        if gx == widths - 1 and yz in (0, count - 1):
            return (zone, gx, count - 1 - yz)
        return flip(zone, gx, yz)

    def along_x(shift):
        def target(zone, gx, yz):
            to = partner_of(gx, shift)
            return (zone, to, yz) if 0 <= to < widths else flip(zone, gx, yz)

        return target

    info = pl.pallas_call(
        info_kernel,
        out_shape=tile_shape(4),
        in_specs=in_vmem(3),
        out_specs=in_vmem(1)[0],
        compiler_params=params,
    )(*[jnp.swapaxes(array[0], 1, 2) for array in (band_device, band_cell, band_weight)])
    messages = (tile_shape(9), tile_shape(10), tile_shape(10))
    field, own, first, second = pl.pallas_call(
        pack_kernel,
        out_shape=(tile_shape(27, extent_x), *messages),
        in_specs=[pl.BlockSpec(memory_space=pltpu.HBM)],
        out_specs=tuple(in_vmem(4)),
        scratch_shapes=[pltpu.SemaphoreType.DMA((extent_x,))],
        compiler_params=params,
    )(pltpu.with_memory_space_constraint(field, pltpu.HBM))
    saved = pltpu.with_memory_space_constraint(saved, pltpu.HBM)
    info = send(info, flip)
    for step in (1, 0):
        last = step == 0
        first = send(first, along_z(1))
        second = send(second, along_z(0))
        others = [send(own, target) for target in (ends_z, *map(hop_z, range(2, count - 1)))]
        carried = () if last else (pltpu.with_memory_space_constraint(solid, pltpu.HBM),)
        *copied, vel = pl.pallas_call(
            lambda *refs: velocity_kernel(step, *refs),
            out_shape=(
                *(jax.ShapeDtypeStruct(array.shape, array.dtype) for array in carried),
                tile_shape(3, extent_x),
            ),
            in_specs=[pl.BlockSpec(memory_space=pltpu.HBM)] * (1 + len(carried)),
            out_specs=tuple(in_vmem(1 + len(carried))),
            scratch_shapes=[
                pltpu.VMEM((extent_x, 27, 16, 128), jnp.float32),
                pltpu.SemaphoreType.DMA((extent_x + 1,)),
            ],
            compiler_params=params,
        )(saved, *carried)
        solid = copied[0] if copied else solid
        two, one = pl.pallas_call(
            side_kernel,
            out_shape=(tile_shape(10),) * 2,
            in_specs=in_vmem(3) + in_any(1),
            out_specs=tuple(in_vmem(2)),
            compiler_params=params,
        )(field, first, second, vel)
        two = send(two, along_x(1))
        one = send(one, along_x(0))

        def make_planes(kernel, planes, given, new, extra):
            operands = (field, vel, solid, first, second, *given)
            return pl.pallas_call(
                lambda *refs: kernel(step, *refs),
                out_shape=(tile_shape(27, extent_x), *extra),
                in_specs=in_vmem(len(operands)) + in_any(len(new)),
                out_specs=tuple(in_any(1) + in_vmem(len(extra))),
                scratch_shapes=[
                    pltpu.VMEM((planes, 27, 16, 128), jnp.float32),
                    pltpu.VMEM((2, 27, 16, 128), jnp.float32),
                    pltpu.SemaphoreType.DMA((planes, 3)),
                ],
                input_output_aliases={len(operands): 0} if new else {},
                compiler_params=params,
            )(*operands, *new)

        kernel = lambda step, *refs: inner_kernel(step, last, *refs)
        new, *columns = make_planes(kernel, extent_x - 2, (), (), (tile_shape(),) * 2)
        cross = pl.pallas_call(
            lambda *refs: cross_kernel(count, *refs),
            out_shape=tile_shape(9),
            in_specs=in_vmem(count + 2) + in_any(1),
            out_specs=in_vmem(1)[0],
            compiler_params=params,
        )(own, first, second, *others, info, columns[0])
        cross = send(cross, flip)
        field, *results = make_planes(
            outer_kernel, 2, (two, one, cross, *columns), (new,), () if last else messages
        )
        if not last:
            own, first, second = results
    return field[None]


def solution(mesh):
    sizes = tuple(mesh.shape[axis] for axis in ("zone", "gx", "yz"))
    in_specs = (
        P("zone", None, "gx", None, "yz"),
        P(None, "zone", None, "gx", None, "yz"),
        P("zone", "gx", None, "yz"),
        P("zone", None, "yz", None),
        P("zone", None, "yz", None),
        P("zone", None, "yz", None),
    )
    out_specs = P("zone", None, "gx", None, "yz")
    return jax.shard_map(
        lambda *args: body(sizes, *args),
        mesh=mesh,
        in_specs=in_specs,
        out_specs=out_specs,
        check_vma=False,
    )
```

```python
import itertools

import jax
import jax.numpy as jnp
import numpy as np
from jax import lax
from jax.experimental import pallas as pl
from jax.experimental.pallas import tpu as pltpu
from jax.sharding import PartitionSpec as P

OMEGA = 1.6
VMEM_LIMIT = 20 * 1024 * 1024
SIGNS = (-1, 0, 1)


def number(cx, cy, cz):
    return 9 * (cx + 1) + 3 * (cy + 1) + (cz + 1)


def lanes():
    return lax.broadcasted_iota(jnp.int32, (16, 128), 1)


def shift_y(tile, cy):
    if cy == 0:
        return tile
    row = lax.broadcasted_iota(jnp.int32, tile.shape, 0)
    if cy == 1:
        return jnp.where(row == 15, 0.0, pltpu.roll(tile, 15, 0))
    return jnp.where(row == 0, 0.0, pltpu.roll(tile, 1, 0))


def pack_columns(planes, x, low, high):
    lane = lanes()
    for slot in range(9):
        place = (x + 1) * 9 + slot
        here = lane == place
        low = jnp.where(here, pltpu.roll(planes(3 * slot + 2), place, 1), low)
        high = jnp.where(here, pltpu.roll(planes(3 * slot), place + 1, 1), high)
    return low, high


def is_even(axis):
    return lax.rem(lax.axis_index(axis), 2) == 0


def write_messages(top, low, high, own, first, second):
    even = is_even("yz")
    for j in range(9):
        tile = top(j)
        own[j] = tile
        first[j] = tile
        second[j] = tile
    first[9] = jnp.where(even, low, high)
    second[9] = jnp.where(even, high, low)


def edges_from(first, second):
    even = is_even("yz")
    me, count = lax.axis_index("yz"), lax.axis_size("yz")
    low = jnp.where(me == 0, 0.0, jnp.where(even, first[9], second[9]))
    high = jnp.where(me == count - 1, 0.0, jnp.where(even, second[9], first[9]))
    return low, high


def pack_kernel(adj, field_out, own_out, first_out, second_out, sems):
    extent_x = adj.shape[1]
    copies = [
        pltpu.make_async_copy(adj.at[:, x], field_out.at[:, x], sems.at[x]) for x in range(extent_x)
    ]
    for copy in copies:
        copy.start()
    edges = jnp.zeros((16, 128), jnp.float32), jnp.zeros((16, 128), jnp.float32)
    for x in range(extent_x):
        copies[x].wait()
        edges = pack_columns(lambda i: field_out[i, x], x, *edges)
    write_messages(
        lambda j: field_out[j, extent_x - 1], *edges, own_out, first_out, second_out
    )


def info_kernel(device, cell, weight, out):
    for k in range(2):
        out[k] = (device[:, k] * 128 + cell[:, k]).astype(jnp.float32)
        out[2 + k] = weight[:, k]


def velocity_kernel(step, saved, *rest):
    *carried, out, kept, sems = rest
    extent_x = out.shape[1]
    copies = []
    if carried:
        copies.append(pltpu.make_async_copy(carried[0], carried[1], sems.at[extent_x]))
        copies[0].start()

    def load(x):
        return pltpu.make_async_copy(saved.at[step, 0, :, x], kept.at[x], sems.at[x])

    lax.fori_loop(0, extent_x, lambda x, c: (load(x).start(), c)[1], 0)

    def one(x, carry):
        load(x).wait()
        for a, tile in enumerate(velocity_of(lambda i: kept[x, i])):
            out[a, x] = tile
        return carry

    lax.fori_loop(0, extent_x, one, 0)
    for copy in copies:
        copy.wait()


def side_kernel(adj, first, second, _, two_out, one_out):
    extent_x = adj.shape[1]
    even = is_even("gx")
    for j in range(9):
        top, bottom = adj[j, extent_x - 1], adj[18 + j, 0]
        one_out[j] = jnp.where(even, top, bottom)
        two_out[j] = jnp.where(even, bottom, top)
    lane = lanes()
    low, high = edges_from(first, second)
    top, bottom = [
        jnp.where(lane < 64, pltpu.roll(low, 128 - start, 1), pltpu.roll(high, 192 - start, 1))
        for start in (9 * extent_x, 9)
    ]
    one_out[9] = jnp.where(even, top, bottom)
    two_out[9] = jnp.where(even, bottom, top)


def cross_kernel(count, *refs):
    own, first, second = refs[:3]
    *others, ends = refs[3 : 1 + count]
    info, _, out = refs[1 + count :]
    interface = lax.axis_index("gx") == lax.axis_size("gx") - 1

    @pl.when(interface)
    def _():
        me = lax.axis_index("yz")
        even = is_even("yz")
        at_end = (me == 0) | (me == count - 1)
        rows = (0, 8)
        spots, picks = {}, {}
        for r in rows:
            for k in range(2):
                code = info[k, r : r + 8].astype(jnp.int32)
                ahead = lax.rem(code // 128 - me + count, count)
                spots[r, k] = lax.rem(code, 128)
                turned = jnp.where(even, lax.rem(count - ahead, count), ahead)
                masks = [turned == 1, turned == count - 1]
                masks += [ahead == count - hop for hop in range(2, count - 1)]
                picks[r, k] = masks
        for j in range(9):
            halves = []
            for r in rows:
                total = jnp.zeros((8, 128), jnp.float32)
                for k in range(2):
                    tiles = [ref[j, r : r + 8] for ref in (own, first, second, *others)]
                    tiles[1] = jnp.where(at_end, ends[j, r : r + 8], tiles[1])
                    got = [jnp.take_along_axis(tile, spots[r, k], axis=1) for tile in tiles]
                    picked = got[0]
                    for mask, value in zip(picks[r, k], got[1:]):
                        picked = jnp.where(mask, value, picked)
                    total = total + picked * info[2 + k, r : r + 8]
                halves.append(total)
            out[j] = jnp.concatenate(halves, axis=0)


def velocity_of(saved):
    totals, along_y, along_z = [], [], []
    for cx in SIGNS:
        sums, diffs = [], []
        for cy in SIGNS:
            lo, mid, hi = [saved(number(cx, cy, cz)) for cz in SIGNS]
            sums.append(lo + mid + hi)
            diffs.append(hi - lo)
        totals.append(sums[0] + sums[1] + sums[2])
        along_y.append(sums[2] - sums[0])
        along_z.append(diffs[0] + diffs[1] + diffs[2])
    density = totals[0] + totals[1] + totals[2]
    momentum = (
        totals[2] - totals[0],
        along_y[0] + along_y[1] + along_y[2],
        along_z[0] + along_z[1] + along_z[2],
    )
    return [part / density for part in momentum]


def moments_of(pull):
    rows = []
    for cx in SIGNS:
        plain, first, second = [], [], []
        for cy in SIGNS:
            lo, mid, hi = [pull(cx, cy, cz) for cz in SIGNS]
            both = lo + hi
            plain.append(mid + 0.25 * both)
            first.append(hi - lo)
            second.append(both)
        pair = plain[0] + plain[2]
        rows.append(
            (
                plain[1] + 0.25 * pair,
                plain[2] - plain[0],
                pair,
                first[1] + 0.25 * (first[0] + first[2]),
                first[2] - first[0],
                second[1] + 0.25 * (second[0] + second[2]),
            )
        )
    even = [rows[1][n] + 0.25 * (rows[0][n] + rows[2][n]) for n in range(6)]
    zero = (8.0 / 27.0) * even[0]
    along = (
        (2.0 / 27.0) * (rows[2][0] - rows[0][0]),
        (2.0 / 27.0) * even[1],
        (2.0 / 27.0) * even[3],
    )
    square = (
        (2.0 / 27.0) * (rows[2][0] + rows[0][0]),
        (2.0 / 27.0) * even[2],
        (2.0 / 27.0) * even[5],
    )
    mixed = (
        (1.0 / 54.0) * (rows[2][1] - rows[0][1]),
        (1.0 / 54.0) * (rows[2][3] - rows[0][3]),
        (1.0 / 54.0) * even[4],
    )
    return zero, along, square, mixed


def collide(pull, velocity, solid, store):
    zero, along, square, mixed = moments_of(lambda cx, cy, cz: pull(number(cx, cy, cz)))
    ux, uy, uz = velocity
    xy, xz, yz = mixed
    quadratic = (
        ux * ux * square[0]
        + uy * uy * square[1]
        + uz * uz * square[2]
        + 2.0 * (ux * uy * xy + ux * uz * xz + uy * uz * yz)
    )
    speed = ux * ux + uy * uy + uz * uz
    scalar = OMEGA * (zero * (1.0 + 1.5 * speed) - 4.5 * quadratic)
    vec_x = OMEGA * (3.0 * along[0] + 9.0 * (square[0] * ux + xy * uy + xz * uz) - 3.0 * ux * zero)
    vec_y = OMEGA * (3.0 * along[1] + 9.0 * (xy * ux + square[1] * uy + yz * uz) - 3.0 * uy * zero)
    vec_z = OMEGA * (3.0 * along[2] + 9.0 * (xz * ux + yz * uy + square[2] * uz) - 3.0 * uz * zero)
    wall = solid == 1
    for cx in SIGNS:
        base = scalar if cx == 0 else (scalar + vec_x if cx > 0 else scalar - vec_x)
        for cy in SIGNS:
            inner = base if cy == 0 else (base + vec_y if cy > 0 else base - vec_y)
            for cz in SIGNS:
                full = inner if cz == 0 else (inner + vec_z if cz > 0 else inner - vec_z)
                i = number(cx, cy, cz)
                store(i, jnp.where(wall, pull(26 - i), (1.0 - OMEGA) * pull(i) + full))


def pull_plane(tile_of, edges_of, pulled, raw=None):
    lane = lanes()
    for cx in SIGNS:
        low_edge, high_edge, start = edges_of(cx)
        for cy in SIGNS:
            place = start + 3 * (cx + 1) + cy + 1
            for cz in SIGNS:
                i = number(cx, cy, cz)
                source = tile_of(i, cx)
                tile = source
                if cz == -1:
                    edge = pltpu.roll(low_edge, 128 - place, 1)
                    tile = jnp.where(lane == 0, edge, pltpu.roll(source, 1, 1))
                elif cz == 1:
                    edge = pltpu.roll(high_edge, 127 - place, 1)
                    tile = jnp.where(lane == 127, edge, pltpu.roll(source, 127, 1))
                if raw is not None and cx == 1:
                    tile = jnp.where(raw, source, tile)
                pulled[i] = shift_y(tile, cy)


def inner_kernel(step, last, adj, vel, solid, first, second, *rest):
    out, low_out, high_out, made, pulled, sems = rest
    extent_x = adj.shape[1]
    low_edge, high_edge = edges_from(first, second)

    def save(x):
        return pltpu.make_async_copy(made.at[x - 1], out.at[:, x], sems.at[x - 1])

    def plane(x, carry):
        here = pulled.at[lax.rem(x, 2)]
        pull_plane(
            lambda i, cx: adj[i, x + cx],
            lambda cx: (low_edge, high_edge, (x + 1 + cx) * 9),
            here,
        )

        def store(i, tile):
            made[x - 1, i] = tile

        velocity = [vel[a, x] for a in range(3)]
        collide(lambda i: here[i], velocity, solid[0, x], store)
        save(x).start()
        if last:
            return carry
        return pack_columns(lambda i: made[x - 1, i], x, *carry)

    zero = jnp.zeros((16, 128), jnp.float32)
    low_out[...], high_out[...] = lax.fori_loop(1, extent_x - 1, plane, (zero, zero), unroll=2)
    lax.fori_loop(1, extent_x - 1, lambda x, c: (save(x).wait(), c)[1], 0)


def outer_kernel(step, adj, vel, solid, first, second, two, one, cross, *rest):
    *rest, made, pulled, sems = rest
    low_in, high_in, _, out, *messages = rest
    extent_x = adj.shape[1]
    edges = edges_from(first, second)
    even = is_even("gx")
    interface = lax.axis_index("gx") == lax.axis_size("gx") - 1

    bottom = lax.axis_index("gx") == 0

    def below(j):
        return jnp.where(bottom, 0.0, jnp.where(even, two[j], one[j]))

    def above(j):
        tile = jnp.where(even, one[j], two[j])
        return jnp.where(interface, cross[j], tile) if j < 9 else tile

    def plane(n, x, ghost, beyond, raw):
        pull_plane(
            lambda i, cx: beyond(i % 9) if cx == ghost else adj[i, x + cx],
            lambda cx: (
                (beyond(9), pltpu.roll(beyond(9), 64, 1), 0)
                if cx == ghost
                else (*edges, (x + 1 + cx) * 9)
            ),
            pulled.at[n],
            raw,
        )

        def store(i, tile):
            made[n, i] = tile

        velocity = [vel[a, x] for a in range(3)]
        collide(lambda i: pulled[n, i], velocity, solid[0, x], store)
        save = pltpu.make_async_copy(made.at[n], out.at[:, x], sems.at[n])
        save.start()
        return save

    final = extent_x - 1
    saves = [plane(0, 0, -1, below, None), plane(1, final, 1, above, interface)]
    if messages:
        low, high = low_in[...], high_in[...]
        low, high = pack_columns(lambda i: made[0, i], 0, low, high)
        low, high = pack_columns(lambda i: made[1, i], final, low, high)
        write_messages(lambda j: made[1, j], low, high, *messages)
    for save in saves:
        save.wait()


def tile_shape(*lead):
    return jax.ShapeDtypeStruct(lead + (16, 128), jnp.float32)


def in_vmem(n):
    return [pl.BlockSpec(memory_space=pltpu.VMEM)] * n


def in_any(n):
    return [pl.BlockSpec(memory_space=pl.ANY)] * n


def body(sizes, adjoint, saved, solid, band_device, band_cell, band_weight):
    zones, widths, count = sizes
    field = adjoint[0]
    extent_x = field.shape[1]
    axes = ("zone", "gx", "yz")
    params = pltpu.CompilerParams(vmem_limit_bytes=VMEM_LIMIT)

    def send(values, target):
        flat = lambda zone, gx, yz: (zone * widths + gx) * count + yz
        places = itertools.product(range(zones), range(widths), range(count))
        return lax.ppermute(values, axes, [(flat(*here), flat(*target(*here))) for here in places])

    def partner_of(place, shift):
        return place + 1 if (place + shift) % 2 == 0 else place - 1

    def flip(zone, gx, yz):
        return (1 - zone, gx, yz)

    def along_z(shift):
        def target(zone, gx, yz):
            to = partner_of(yz, shift)
            return (zone, gx, to) if 0 <= to < count else flip(zone, gx, yz)

        return target

    def hop_z(hop):
        def target(zone, gx, yz):
            if gx == widths - 1:
                return (zone, gx, (yz + hop) % count)
            return flip(zone, gx, yz)

        return target

    def ends_z(zone, gx, yz):
        if gx == widths - 1 and yz in (0, count - 1):
            return (zone, gx, count - 1 - yz)
        return flip(zone, gx, yz)

    def along_x(shift):
        def target(zone, gx, yz):
            to = partner_of(gx, shift)
            return (zone, to, yz) if 0 <= to < widths else flip(zone, gx, yz)

        return target

    info = pl.pallas_call(
        info_kernel,
        out_shape=tile_shape(4),
        in_specs=in_vmem(3),
        out_specs=in_vmem(1)[0],
        compiler_params=params,
    )(*[jnp.swapaxes(array[0], 1, 2) for array in (band_device, band_cell, band_weight)])
    messages = (tile_shape(9), tile_shape(10), tile_shape(10))
    field, own, first, second = pl.pallas_call(
        pack_kernel,
        out_shape=(tile_shape(27, extent_x), *messages),
        in_specs=[pl.BlockSpec(memory_space=pltpu.HBM)],
        out_specs=tuple(in_vmem(4)),
        scratch_shapes=[pltpu.SemaphoreType.DMA((extent_x,))],
        compiler_params=params,
    )(pltpu.with_memory_space_constraint(field, pltpu.HBM))
    saved = pltpu.with_memory_space_constraint(saved, pltpu.HBM)
    info = send(info, flip)
    for step in (1, 0):
        last = step == 0
        first = send(first, along_z(1))
        second = send(second, along_z(0))
        others = [send(own, target) for target in (*map(hop_z, range(2, count - 1)), ends_z)]
        carried = () if last else (pltpu.with_memory_space_constraint(solid, pltpu.HBM),)
        *copied, vel = pl.pallas_call(
            lambda *refs: velocity_kernel(step, *refs),
            out_shape=(
                *(jax.ShapeDtypeStruct(array.shape, array.dtype) for array in carried),
                tile_shape(3, extent_x),
            ),
            in_specs=[pl.BlockSpec(memory_space=pltpu.HBM)] * (1 + len(carried)),
            out_specs=tuple(in_vmem(1 + len(carried))),
            scratch_shapes=[
                pltpu.VMEM((extent_x, 27, 16, 128), jnp.float32),
                pltpu.SemaphoreType.DMA((extent_x + 1,)),
            ],
            compiler_params=params,
        )(saved, *carried)
        solid = copied[0] if copied else solid
        two, one = pl.pallas_call(
            side_kernel,
            out_shape=(tile_shape(10),) * 2,
            in_specs=in_vmem(3) + in_any(1),
            out_specs=tuple(in_vmem(2)),
            compiler_params=params,
        )(field, first, second, vel)
        two = send(two, along_x(1))
        one = send(one, along_x(0))

        def make_planes(kernel, planes, given, new, extra):
            operands = (field, vel, solid, first, second, *given)
            return pl.pallas_call(
                lambda *refs: kernel(step, *refs),
                out_shape=(tile_shape(27, extent_x), *extra),
                in_specs=in_vmem(len(operands)) + in_any(len(new)),
                out_specs=tuple(in_any(1) + in_vmem(len(extra))),
                scratch_shapes=[
                    pltpu.VMEM((planes, 27, 16, 128), jnp.float32),
                    pltpu.VMEM((2, 27, 16, 128), jnp.float32),
                    pltpu.SemaphoreType.DMA((planes,)),
                ],
                input_output_aliases={len(operands): 0} if new else {},
                compiler_params=params,
            )(*operands, *new)

        kernel = lambda step, *refs: inner_kernel(step, last, *refs)
        new, *columns = make_planes(kernel, extent_x - 2, (), (), (tile_shape(),) * 2)
        cross = pl.pallas_call(
            lambda *refs: cross_kernel(count, *refs),
            out_shape=tile_shape(9),
            in_specs=in_vmem(count + 2) + in_any(1),
            out_specs=in_vmem(1)[0],
            compiler_params=params,
        )(own, first, second, *others, info, columns[0])
        cross = send(cross, flip)
        field, *results = make_planes(
            outer_kernel, 2, (two, one, cross, *columns), (new,), () if last else messages
        )
        if not last:
            own, first, second = results
    return field[None]


def solution(mesh):
    sizes = tuple(mesh.shape[axis] for axis in ("zone", "gx", "yz"))
    in_specs = (
        P("zone", None, "gx", None, "yz"),
        P(None, "zone", None, "gx", None, "yz"),
        P("zone", "gx", None, "yz"),
        P("zone", None, "yz", None),
        P("zone", None, "yz", None),
        P("zone", None, "yz", None),
    )
    out_specs = P("zone", None, "gx", None, "yz")
    return jax.shard_map(
        lambda *args: body(sizes, *args),
        mesh=mesh,
        in_specs=in_specs,
        out_specs=out_specs,
        check_vma=False,
    )
```

```python
import itertools

import jax
import jax.numpy as jnp
import numpy as np
from jax import lax
from jax.experimental import pallas as pl
from jax.experimental.pallas import tpu as pltpu
from jax.sharding import PartitionSpec as P

OMEGA = 1.6
VMEM_LIMIT = 20 * 1024 * 1024
SIGNS = (-1, 0, 1)


def number(cx, cy, cz):
    return 9 * (cx + 1) + 3 * (cy + 1) + (cz + 1)


def lanes():
    return lax.broadcasted_iota(jnp.int32, (16, 128), 1)


def shift_y(tile, cy):
    if cy == 0:
        return tile
    row = lax.broadcasted_iota(jnp.int32, tile.shape, 0)
    if cy == 1:
        return jnp.where(row == 15, 0.0, pltpu.roll(tile, 15, 0))
    return jnp.where(row == 0, 0.0, pltpu.roll(tile, 1, 0))


def pack_columns(planes, x, low, high):
    lane = lanes()
    for slot in range(9):
        place = (x + 1) * 9 + slot
        here = lane == place
        low = jnp.where(here, pltpu.roll(planes(3 * slot + 2), place, 1), low)
        high = jnp.where(here, pltpu.roll(planes(3 * slot), place + 1, 1), high)
    return low, high


def is_even(axis):
    return lax.rem(lax.axis_index(axis), 2) == 0


def write_messages(top, low, high, own, first, second):
    even = is_even("yz")
    for j in range(9):
        tile = top(j)
        own[j] = tile
        first[j] = tile
        second[j] = tile
    first[9] = jnp.where(even, low, high)
    second[9] = jnp.where(even, high, low)


def edges_from(first, second):
    even = is_even("yz")
    me, count = lax.axis_index("yz"), lax.axis_size("yz")
    low = jnp.where(me == 0, 0.0, jnp.where(even, first[9], second[9]))
    high = jnp.where(me == count - 1, 0.0, jnp.where(even, second[9], first[9]))
    return low, high


def pack_kernel(adj, field_out, own_out, first_out, second_out, sems):
    extent_x = adj.shape[1]
    copies = [
        pltpu.make_async_copy(adj.at[:, x], field_out.at[:, x], sems.at[x]) for x in range(extent_x)
    ]
    for copy in copies:
        copy.start()
    edges = jnp.zeros((16, 128), jnp.float32), jnp.zeros((16, 128), jnp.float32)
    for x in range(extent_x):
        copies[x].wait()
        edges = pack_columns(lambda i: field_out[i, x], x, *edges)
    write_messages(
        lambda j: field_out[j, extent_x - 1], *edges, own_out, first_out, second_out
    )


def info_kernel(device, cell, weight, out):
    for k in range(2):
        out[k] = (device[:, k] * 128 + cell[:, k]).astype(jnp.float32)
        out[2 + k] = weight[:, k]


def velocity_kernel(step, saved, *rest):
    *carried, out, kept, sems = rest
    extent_x = out.shape[1]
    copies = []
    if carried:
        copies.append(pltpu.make_async_copy(carried[0], carried[1], sems.at[extent_x]))
        copies[0].start()

    def load(x):
        return pltpu.make_async_copy(saved.at[step, 0, :, x], kept.at[x], sems.at[x])

    lax.fori_loop(0, extent_x, lambda x, c: (load(x).start(), c)[1], 0)

    def one(x, carry):
        load(x).wait()
        for a, tile in enumerate(velocity_of(lambda i: kept[x, i])):
            out[a, x] = tile
        return carry

    lax.fori_loop(0, extent_x, one, 0)
    for copy in copies:
        copy.wait()


def side_kernel(adj, first, second, _, two_out, one_out):
    extent_x = adj.shape[1]
    even = is_even("gx")
    for j in range(9):
        top, bottom = adj[j, extent_x - 1], adj[18 + j, 0]
        one_out[j] = jnp.where(even, top, bottom)
        two_out[j] = jnp.where(even, bottom, top)
    lane = lanes()
    low, high = edges_from(first, second)
    top, bottom = [
        jnp.where(lane < 64, pltpu.roll(low, 128 - start, 1), pltpu.roll(high, 192 - start, 1))
        for start in (9 * extent_x, 9)
    ]
    one_out[9] = jnp.where(even, top, bottom)
    two_out[9] = jnp.where(even, bottom, top)


def cross_kernel(count, *refs):
    own, first, second = refs[:3]
    *others, ends = refs[3 : 1 + count]
    info, _, out = refs[1 + count :]
    interface = lax.axis_index("gx") == lax.axis_size("gx") - 1

    @pl.when(interface)
    def _():
        me = lax.axis_index("yz")
        even = is_even("yz")
        at_end = (me == 0) | (me == count - 1)
        rows = (0, 8)
        spots, picks = {}, {}
        for r in rows:
            for k in range(2):
                code = info[k, r : r + 8].astype(jnp.int32)
                ahead = lax.rem(code // 128 - me + count, count)
                spots[r, k] = lax.rem(code, 128)
                turned = jnp.where(even, lax.rem(count - ahead, count), ahead)
                masks = [turned == 1, turned == count - 1]
                masks += [ahead == count - hop for hop in range(2, count - 1)]
                picks[r, k] = masks
        for j in range(9):
            halves = []
            for r in rows:
                total = jnp.zeros((8, 128), jnp.float32)
                for k in range(2):
                    tiles = [ref[j, r : r + 8] for ref in (own, first, second, *others)]
                    tiles[1] = jnp.where(at_end, ends[j, r : r + 8], tiles[1])
                    got = [jnp.take_along_axis(tile, spots[r, k], axis=1) for tile in tiles]
                    picked = got[0]
                    for mask, value in zip(picks[r, k], got[1:]):
                        picked = jnp.where(mask, value, picked)
                    total = total + picked * info[2 + k, r : r + 8]
                halves.append(total)
            out[j] = jnp.concatenate(halves, axis=0)


def velocity_of(saved):
    totals, along_y, along_z = [], [], []
    for cx in SIGNS:
        sums, diffs = [], []
        for cy in SIGNS:
            lo, mid, hi = [saved(number(cx, cy, cz)) for cz in SIGNS]
            sums.append(lo + mid + hi)
            diffs.append(hi - lo)
        totals.append(sums[0] + sums[1] + sums[2])
        along_y.append(sums[2] - sums[0])
        along_z.append(diffs[0] + diffs[1] + diffs[2])
    density = totals[0] + totals[1] + totals[2]
    momentum = (
        totals[2] - totals[0],
        along_y[0] + along_y[1] + along_y[2],
        along_z[0] + along_z[1] + along_z[2],
    )
    return [part / density for part in momentum]


def moments_of(pull):
    rows = []
    for cx in SIGNS:
        plain, first, second = [], [], []
        for cy in SIGNS:
            lo, mid, hi = [pull(cx, cy, cz) for cz in SIGNS]
            both = lo + hi
            plain.append(mid + 0.25 * both)
            first.append(hi - lo)
            second.append(both)
        pair = plain[0] + plain[2]
        rows.append(
            (
                plain[1] + 0.25 * pair,
                plain[2] - plain[0],
                pair,
                first[1] + 0.25 * (first[0] + first[2]),
                first[2] - first[0],
                second[1] + 0.25 * (second[0] + second[2]),
            )
        )
    even = [rows[1][n] + 0.25 * (rows[0][n] + rows[2][n]) for n in range(6)]
    zero = (8.0 / 27.0) * even[0]
    along = (
        (2.0 / 27.0) * (rows[2][0] - rows[0][0]),
        (2.0 / 27.0) * even[1],
        (2.0 / 27.0) * even[3],
    )
    square = (
        (2.0 / 27.0) * (rows[2][0] + rows[0][0]),
        (2.0 / 27.0) * even[2],
        (2.0 / 27.0) * even[5],
    )
    mixed = (
        (1.0 / 54.0) * (rows[2][1] - rows[0][1]),
        (1.0 / 54.0) * (rows[2][3] - rows[0][3]),
        (1.0 / 54.0) * even[4],
    )
    return zero, along, square, mixed


def collide(pull, velocity, solid, store):
    zero, along, square, mixed = moments_of(lambda cx, cy, cz: pull(number(cx, cy, cz)))
    ux, uy, uz = velocity
    xy, xz, yz = mixed
    quadratic = (
        ux * ux * square[0]
        + uy * uy * square[1]
        + uz * uz * square[2]
        + 2.0 * (ux * uy * xy + ux * uz * xz + uy * uz * yz)
    )
    speed = ux * ux + uy * uy + uz * uz
    scalar = OMEGA * (zero * (1.0 + 1.5 * speed) - 4.5 * quadratic)
    vec_x = OMEGA * (3.0 * along[0] + 9.0 * (square[0] * ux + xy * uy + xz * uz) - 3.0 * ux * zero)
    vec_y = OMEGA * (3.0 * along[1] + 9.0 * (xy * ux + square[1] * uy + yz * uz) - 3.0 * uy * zero)
    vec_z = OMEGA * (3.0 * along[2] + 9.0 * (xz * ux + yz * uy + square[2] * uz) - 3.0 * uz * zero)
    wall = solid == 1
    for cx in SIGNS:
        base = scalar if cx == 0 else (scalar + vec_x if cx > 0 else scalar - vec_x)
        for cy in SIGNS:
            inner = base if cy == 0 else (base + vec_y if cy > 0 else base - vec_y)
            for cz in SIGNS:
                full = inner if cz == 0 else (inner + vec_z if cz > 0 else inner - vec_z)
                i = number(cx, cy, cz)
                store(i, jnp.where(wall, pull(26 - i), (1.0 - OMEGA) * pull(i) + full))


def pull_plane(tile_of, edges_of, pulled, raw=None):
    lane = lanes()
    for cx in SIGNS:
        low_edge, high_edge, start = edges_of(cx)
        for cy in SIGNS:
            place = start + 3 * (cx + 1) + cy + 1
            for cz in SIGNS:
                i = number(cx, cy, cz)
                source = tile_of(i, cx)
                tile = source
                if cz == -1:
                    edge = pltpu.roll(low_edge, 128 - place, 1)
                    tile = jnp.where(lane == 0, edge, pltpu.roll(source, 1, 1))
                elif cz == 1:
                    edge = pltpu.roll(high_edge, 127 - place, 1)
                    tile = jnp.where(lane == 127, edge, pltpu.roll(source, 127, 1))
                if raw is not None and cx == 1:
                    tile = jnp.where(raw, source, tile)
                pulled[i] = shift_y(tile, cy)


def inner_kernel(step, last, adj, vel, solid, first, second, *rest):
    out, low_out, high_out, made, pulled, sems = rest
    extent_x = adj.shape[1]
    low_edge, high_edge = edges_from(first, second)

    def save(x):
        return pltpu.make_async_copy(made.at[x - 1], out.at[:, x], sems.at[x - 1])

    def plane(x, carry):
        here = pulled.at[lax.rem(x, 2)]
        pull_plane(
            lambda i, cx: adj[i, x + cx],
            lambda cx: (low_edge, high_edge, (x + 1 + cx) * 9),
            here,
        )

        def store(i, tile):
            made[x - 1, i] = tile

        velocity = [vel[a, x] for a in range(3)]
        collide(lambda i: here[i], velocity, solid[0, x], store)
        save(x).start()
        if last:
            return carry
        return pack_columns(lambda i: made[x - 1, i], x, *carry)

    zero = jnp.zeros((16, 128), jnp.float32)
    low_out[...], high_out[...] = lax.fori_loop(1, extent_x - 1, plane, (zero, zero), unroll=2)
    lax.fori_loop(1, extent_x - 1, lambda x, c: (save(x).wait(), c)[1], 0)


def outer_kernel(swapped, step, adj, vel, solid, first, second, two, one, cross, *rest):
    *rest, made, pulled, sems = rest
    low_in, high_in, _, out, *messages = rest
    two, one = (one, two) if swapped else (two, one)
    extent_x = adj.shape[1]
    edges = edges_from(first, second)
    even = is_even("gx")
    interface = lax.axis_index("gx") == lax.axis_size("gx") - 1

    bottom = lax.axis_index("gx") == 0

    def below(j):
        return jnp.where(bottom, 0.0, jnp.where(even, two[j], one[j]))

    def above(j):
        tile = jnp.where(even, one[j], two[j])
        return jnp.where(interface, cross[j], tile) if j < 9 else tile

    def plane(n, x, ghost, beyond, raw):
        pull_plane(
            lambda i, cx: beyond(i % 9) if cx == ghost else adj[i, x + cx],
            lambda cx: (
                (beyond(9), pltpu.roll(beyond(9), 64, 1), 0)
                if cx == ghost
                else (*edges, (x + 1 + cx) * 9)
            ),
            pulled.at[n],
            raw,
        )

        def store(i, tile):
            made[n, i] = tile

        velocity = [vel[a, x] for a in range(3)]
        collide(lambda i: pulled[n, i], velocity, solid[0, x], store)
        save = pltpu.make_async_copy(made.at[n], out.at[:, x], sems.at[n])
        save.start()
        return save

    final = extent_x - 1
    saves = [plane(0, 0, -1, below, None), plane(1, final, 1, above, interface)]
    if messages:
        low, high = low_in[...], high_in[...]
        low, high = pack_columns(lambda i: made[0, i], 0, low, high)
        low, high = pack_columns(lambda i: made[1, i], final, low, high)
        write_messages(lambda j: made[1, j], low, high, *messages)
    for save in saves:
        save.wait()


def tile_shape(*lead):
    return jax.ShapeDtypeStruct(lead + (16, 128), jnp.float32)


def in_vmem(n):
    return [pl.BlockSpec(memory_space=pltpu.VMEM)] * n


def in_any(n):
    return [pl.BlockSpec(memory_space=pl.ANY)] * n


def body(sizes, adjoint, saved, solid, band_device, band_cell, band_weight):
    zones, widths, count = sizes
    field = adjoint[0]
    extent_x = field.shape[1]
    axes = ("zone", "gx", "yz")
    params = pltpu.CompilerParams(vmem_limit_bytes=VMEM_LIMIT)

    def send(values, target):
        flat = lambda zone, gx, yz: (zone * widths + gx) * count + yz
        places = itertools.product(range(zones), range(widths), range(count))
        return lax.ppermute(values, axes, [(flat(*here), flat(*target(*here))) for here in places])

    def partner_of(place, shift):
        return place + 1 if (place + shift) % 2 == 0 else place - 1

    def flip(zone, gx, yz):
        return (1 - zone, gx, yz)

    def along_z(shift):
        def target(zone, gx, yz):
            to = partner_of(yz, shift)
            return (zone, gx, to) if 0 <= to < count else flip(zone, gx, yz)

        return target

    def hop_z(hop):
        def target(zone, gx, yz):
            if gx == widths - 1:
                return (zone, gx, (yz + hop) % count)
            return flip(zone, gx, yz)

        return target

    def ends_z(zone, gx, yz):
        if gx == widths - 1 and yz in (0, count - 1):
            return (zone, gx, count - 1 - yz)
        return flip(zone, gx, yz)

    def along_x(shift):
        def target(zone, gx, yz):
            to = partner_of(gx, shift)
            return (zone, to, yz) if 0 <= to < widths else flip(zone, gx, yz)

        return target

    info = pl.pallas_call(
        info_kernel,
        out_shape=tile_shape(4),
        in_specs=in_vmem(3),
        out_specs=in_vmem(1)[0],
        compiler_params=params,
    )(*[jnp.swapaxes(array[0], 1, 2) for array in (band_device, band_cell, band_weight)])
    messages = (tile_shape(9), tile_shape(10), tile_shape(10))
    field, own, first, second = pl.pallas_call(
        pack_kernel,
        out_shape=(tile_shape(27, extent_x), *messages),
        in_specs=[pl.BlockSpec(memory_space=pltpu.HBM)],
        out_specs=tuple(in_vmem(4)),
        scratch_shapes=[pltpu.SemaphoreType.DMA((extent_x,))],
        compiler_params=params,
    )(pltpu.with_memory_space_constraint(field, pltpu.HBM))
    saved = pltpu.with_memory_space_constraint(saved, pltpu.HBM)
    info = send(info, flip)
    for step in (1, 0):
        last = step == 0
        first = send(first, along_z(1))
        second = send(second, along_z(0))
        others = [send(own, target) for target in (*map(hop_z, range(2, count - 1)), ends_z)]
        carried = () if last else (pltpu.with_memory_space_constraint(solid, pltpu.HBM),)
        *copied, vel = pl.pallas_call(
            lambda *refs: velocity_kernel(step, *refs),
            out_shape=(
                *(jax.ShapeDtypeStruct(array.shape, array.dtype) for array in carried),
                tile_shape(3, extent_x),
            ),
            in_specs=[pl.BlockSpec(memory_space=pltpu.HBM)] * (1 + len(carried)),
            out_specs=tuple(in_vmem(1 + len(carried))),
            scratch_shapes=[
                pltpu.VMEM((extent_x, 27, 16, 128), jnp.float32),
                pltpu.SemaphoreType.DMA((extent_x + 1,)),
            ],
            compiler_params=params,
        )(saved, *carried)
        solid = copied[0] if copied else solid
        two, one = pl.pallas_call(
            side_kernel,
            out_shape=(tile_shape(10),) * 2,
            in_specs=in_vmem(3) + in_any(1),
            out_specs=tuple(in_vmem(2)),
            compiler_params=params,
        )(field, first, second, vel)
        two = send(two, along_x(1))
        one = send(one, along_x(0))

        def make_planes(kernel, planes, given, new, extra):
            operands = (field, vel, solid, first, second, *given)
            return pl.pallas_call(
                lambda *refs: kernel(step, *refs),
                out_shape=(tile_shape(27, extent_x), *extra),
                in_specs=in_vmem(len(operands)) + in_any(len(new)),
                out_specs=tuple(in_any(1) + in_vmem(len(extra))),
                scratch_shapes=[
                    pltpu.VMEM((planes, 27, 16, 128), jnp.float32),
                    pltpu.VMEM((2, 27, 16, 128), jnp.float32),
                    pltpu.SemaphoreType.DMA((planes,)),
                ],
                input_output_aliases={len(operands): 0} if new else {},
                compiler_params=params,
            )(*operands, *new)

        kernel = lambda step, *refs: inner_kernel(step, last, *refs)
        new, *columns = make_planes(kernel, extent_x - 2, (), (), (tile_shape(),) * 2)
        cross = pl.pallas_call(
            lambda *refs: cross_kernel(count, *refs),
            out_shape=tile_shape(9),
            in_specs=in_vmem(count + 2) + in_any(1),
            out_specs=in_vmem(1)[0],
            compiler_params=params,
        )(own, first, second, *others, info, columns[0])
        cross = send(cross, flip)
        ghosts = (one, two) if last else (two, one)
        kernel = lambda step, *refs: outer_kernel(last, step, *refs)
        field, *results = make_planes(
            kernel, 2, (*ghosts, cross, *columns), (new,), () if last else messages
        )
        if not last:
            own, first, second = results
    return field[None]


def solution(mesh):
    sizes = tuple(mesh.shape[axis] for axis in ("zone", "gx", "yz"))
    in_specs = (
        P("zone", None, "gx", None, "yz"),
        P(None, "zone", None, "gx", None, "yz"),
        P("zone", "gx", None, "yz"),
        P("zone", None, "yz", None),
        P("zone", None, "yz", None),
        P("zone", None, "yz", None),
    )
    out_specs = P("zone", None, "gx", None, "yz")
    return jax.shard_map(
        lambda *args: body(sizes, *args),
        mesh=mesh,
        in_specs=in_specs,
        out_specs=out_specs,
        check_vma=False,
    )
```

```python
import itertools

import jax
import jax.numpy as jnp
import numpy as np
from jax import lax
from jax.experimental import pallas as pl
from jax.experimental.pallas import tpu as pltpu
from jax.sharding import PartitionSpec as P

OMEGA = 1.6
VMEM_LIMIT = 20 * 1024 * 1024
SIGNS = (-1, 0, 1)


def number(cx, cy, cz):
    return 9 * (cx + 1) + 3 * (cy + 1) + (cz + 1)


def lanes():
    return lax.broadcasted_iota(jnp.int32, (16, 128), 1)


def shift_y(tile, cy):
    if cy == 0:
        return tile
    row = lax.broadcasted_iota(jnp.int32, tile.shape, 0)
    if cy == 1:
        return jnp.where(row == 15, 0.0, pltpu.roll(tile, 15, 0))
    return jnp.where(row == 0, 0.0, pltpu.roll(tile, 1, 0))


def pack_columns(planes, x, low, high):
    lane = lanes()
    for slot in range(9):
        place = (x + 1) * 9 + slot
        here = lane == place
        low = jnp.where(here, pltpu.roll(planes(3 * slot + 2), place, 1), low)
        high = jnp.where(here, pltpu.roll(planes(3 * slot), place + 1, 1), high)
    return low, high


def is_even(axis):
    return lax.rem(lax.axis_index(axis), 2) == 0


def write_messages(top, low, high, own, first, second):
    even = is_even("yz")
    for j in range(9):
        tile = top(j)
        own[j] = tile
        first[j] = tile
        second[j] = tile
    first[9] = jnp.where(even, low, high)
    second[9] = jnp.where(even, high, low)


def edges_from(first, second):
    even = is_even("yz")
    me, count = lax.axis_index("yz"), lax.axis_size("yz")
    low = jnp.where(me == 0, 0.0, jnp.where(even, first[9], second[9]))
    high = jnp.where(me == count - 1, 0.0, jnp.where(even, second[9], first[9]))
    return low, high


def pack_kernel(adj, field_out, own_out, first_out, second_out, sems):
    extent_x = adj.shape[1]
    copies = [
        pltpu.make_async_copy(adj.at[:, x], field_out.at[:, x], sems.at[x]) for x in range(extent_x)
    ]
    for copy in copies:
        copy.start()
    edges = jnp.zeros((16, 128), jnp.float32), jnp.zeros((16, 128), jnp.float32)
    for x in range(extent_x):
        copies[x].wait()
        edges = pack_columns(lambda i: field_out[i, x], x, *edges)
    write_messages(
        lambda j: field_out[j, extent_x - 1], *edges, own_out, first_out, second_out
    )


def info_kernel(device, cell, weight, out):
    for k in range(2):
        out[k] = (device[:, k] * 128 + cell[:, k]).astype(jnp.float32)
        out[2 + k] = weight[:, k]


def velocity_kernel(step, saved, *rest):
    *carried, out, kept, sems = rest
    extent_x = out.shape[1]
    copies = []
    if carried:
        copies.append(pltpu.make_async_copy(carried[0], carried[1], sems.at[extent_x]))
        copies[0].start()

    def load(x):
        return pltpu.make_async_copy(saved.at[step, 0, :, x], kept.at[x], sems.at[x])

    lax.fori_loop(0, extent_x, lambda x, c: (load(x).start(), c)[1], 0)

    def one(x, carry):
        load(x).wait()
        for a, tile in enumerate(velocity_of(lambda i: kept[x, i])):
            out[a, x] = tile
        return carry

    lax.fori_loop(0, extent_x, one, 0)
    for copy in copies:
        copy.wait()


def side_kernel(adj, first, second, _, two_out, one_out):
    extent_x = adj.shape[1]
    even = is_even("gx")
    for j in range(9):
        top, bottom = adj[j, extent_x - 1], adj[18 + j, 0]
        one_out[j] = jnp.where(even, top, bottom)
        two_out[j] = jnp.where(even, bottom, top)
    lane = lanes()
    low, high = edges_from(first, second)
    top, bottom = [
        jnp.where(lane < 64, pltpu.roll(low, 128 - start, 1), pltpu.roll(high, 192 - start, 1))
        for start in (9 * extent_x, 9)
    ]
    one_out[9] = jnp.where(even, top, bottom)
    two_out[9] = jnp.where(even, bottom, top)


def cross_kernel(count, *refs):
    own, first, second = refs[:3]
    *others, ends = refs[3 : 1 + count]
    info, _, out = refs[1 + count :]
    interface = lax.axis_index("gx") == lax.axis_size("gx") - 1

    @pl.when(interface)
    def _():
        me = lax.axis_index("yz")
        even = is_even("yz")
        at_end = (me == 0) | (me == count - 1)
        rows = (0, 8)
        spots, picks = {}, {}
        for r in rows:
            for k in range(2):
                code = info[k, r : r + 8].astype(jnp.int32)
                ahead = lax.rem(code // 128 - me + count, count)
                spots[r, k] = lax.rem(code, 128)
                turned = jnp.where(even, lax.rem(count - ahead, count), ahead)
                masks = [turned == 1, turned == count - 1]
                masks += [ahead == count - hop for hop in range(2, count - 1)]
                picks[r, k] = masks
        for j in range(9):
            halves = []
            for r in rows:
                total = jnp.zeros((8, 128), jnp.float32)
                for k in range(2):
                    tiles = [ref[j, r : r + 8] for ref in (own, first, second, *others)]
                    tiles[1] = jnp.where(at_end, ends[j, r : r + 8], tiles[1])
                    got = [jnp.take_along_axis(tile, spots[r, k], axis=1) for tile in tiles]
                    picked = got[0]
                    for mask, value in zip(picks[r, k], got[1:]):
                        picked = jnp.where(mask, value, picked)
                    total = total + picked * info[2 + k, r : r + 8]
                halves.append(total)
            out[j] = jnp.concatenate(halves, axis=0)


def velocity_of(saved):
    totals, along_y, along_z = [], [], []
    for cx in SIGNS:
        sums, diffs = [], []
        for cy in SIGNS:
            lo, mid, hi = [saved(number(cx, cy, cz)) for cz in SIGNS]
            sums.append(lo + mid + hi)
            diffs.append(hi - lo)
        totals.append(sums[0] + sums[1] + sums[2])
        along_y.append(sums[2] - sums[0])
        along_z.append(diffs[0] + diffs[1] + diffs[2])
    density = totals[0] + totals[1] + totals[2]
    momentum = (
        totals[2] - totals[0],
        along_y[0] + along_y[1] + along_y[2],
        along_z[0] + along_z[1] + along_z[2],
    )
    return [part / density for part in momentum]


def moments_of(pull):
    rows = []
    for cx in SIGNS:
        plain, first, second = [], [], []
        for cy in SIGNS:
            lo, mid, hi = [pull(cx, cy, cz) for cz in SIGNS]
            both = lo + hi
            plain.append(mid + 0.25 * both)
            first.append(hi - lo)
            second.append(both)
        pair = plain[0] + plain[2]
        rows.append(
            (
                plain[1] + 0.25 * pair,
                plain[2] - plain[0],
                pair,
                first[1] + 0.25 * (first[0] + first[2]),
                first[2] - first[0],
                second[1] + 0.25 * (second[0] + second[2]),
            )
        )
    even = [rows[1][n] + 0.25 * (rows[0][n] + rows[2][n]) for n in range(6)]
    zero = (8.0 / 27.0) * even[0]
    along = (
        (2.0 / 27.0) * (rows[2][0] - rows[0][0]),
        (2.0 / 27.0) * even[1],
        (2.0 / 27.0) * even[3],
    )
    square = (
        (2.0 / 27.0) * (rows[2][0] + rows[0][0]),
        (2.0 / 27.0) * even[2],
        (2.0 / 27.0) * even[5],
    )
    mixed = (
        (1.0 / 54.0) * (rows[2][1] - rows[0][1]),
        (1.0 / 54.0) * (rows[2][3] - rows[0][3]),
        (1.0 / 54.0) * even[4],
    )
    return zero, along, square, mixed


def collide(pull, velocity, solid, store):
    zero, along, square, mixed = moments_of(lambda cx, cy, cz: pull(number(cx, cy, cz)))
    ux, uy, uz = velocity
    xy, xz, yz = mixed
    quadratic = (
        ux * ux * square[0]
        + uy * uy * square[1]
        + uz * uz * square[2]
        + 2.0 * (ux * uy * xy + ux * uz * xz + uy * uz * yz)
    )
    speed = ux * ux + uy * uy + uz * uz
    scalar = OMEGA * (zero * (1.0 + 1.5 * speed) - 4.5 * quadratic)
    vec_x = OMEGA * (3.0 * along[0] + 9.0 * (square[0] * ux + xy * uy + xz * uz) - 3.0 * ux * zero)
    vec_y = OMEGA * (3.0 * along[1] + 9.0 * (xy * ux + square[1] * uy + yz * uz) - 3.0 * uy * zero)
    vec_z = OMEGA * (3.0 * along[2] + 9.0 * (xz * ux + yz * uy + square[2] * uz) - 3.0 * uz * zero)
    wall = solid == 1
    for cx in SIGNS:
        base = scalar if cx == 0 else (scalar + vec_x if cx > 0 else scalar - vec_x)
        for cy in SIGNS:
            inner = base if cy == 0 else (base + vec_y if cy > 0 else base - vec_y)
            for cz in SIGNS:
                full = inner if cz == 0 else (inner + vec_z if cz > 0 else inner - vec_z)
                i = number(cx, cy, cz)
                store(i, jnp.where(wall, pull(26 - i), (1.0 - OMEGA) * pull(i) + full))


def pull_plane(tile_of, edges_of, pulled, raw=None):
    lane = lanes()
    for cx in SIGNS:
        low_edge, high_edge, start = edges_of(cx)
        for cy in SIGNS:
            place = start + 3 * (cx + 1) + cy + 1
            for cz in SIGNS:
                i = number(cx, cy, cz)
                source = tile_of(i, cx)
                tile = source
                if cz == -1:
                    edge = pltpu.roll(low_edge, 128 - place, 1)
                    tile = jnp.where(lane == 0, edge, pltpu.roll(source, 1, 1))
                elif cz == 1:
                    edge = pltpu.roll(high_edge, 127 - place, 1)
                    tile = jnp.where(lane == 127, edge, pltpu.roll(source, 127, 1))
                if raw is not None and cx == 1:
                    tile = jnp.where(raw, source, tile)
                pulled[i] = shift_y(tile, cy)


def inner_kernel(step, last, adj, vel, solid, first, second, *rest):
    out, low_out, high_out, made, pulled, sems = rest
    extent_x = adj.shape[1]
    low_edge, high_edge = edges_from(first, second)

    def save(x):
        return pltpu.make_async_copy(made.at[x - 1], out.at[:, x], sems.at[x - 1])

    def plane(x, carry):
        here = pulled.at[lax.rem(x, 2)]
        pull_plane(
            lambda i, cx: adj[i, x + cx],
            lambda cx: (low_edge, high_edge, (x + 1 + cx) * 9),
            here,
        )

        def store(i, tile):
            made[x - 1, i] = tile

        velocity = [vel[a, x] for a in range(3)]
        collide(lambda i: here[i], velocity, solid[0, x], store)
        save(x).start()
        if last:
            return carry
        return pack_columns(lambda i: made[x - 1, i], x, *carry)

    zero = jnp.zeros((16, 128), jnp.float32)
    low_out[...], high_out[...] = lax.fori_loop(1, extent_x - 1, plane, (zero, zero), unroll=2)
    lax.fori_loop(1, extent_x - 1, lambda x, c: (save(x).wait(), c)[1], 0)


def outer_kernel(last, step, adj, vel, solid, first, second, near, two, far, cross, *rest):
    *rest, made, pulled, sems = rest
    low_in, high_in, _, out, *messages = rest
    near, two = (near, two) if last else (two, near)
    extent_x = adj.shape[1]
    edges = edges_from(first, second)
    even = is_even("gx")
    interface = lax.axis_index("gx") == lax.axis_size("gx") - 1

    bottom = lax.axis_index("gx") == 0
    inside = lax.axis_index("gx") < lax.axis_size("gx") - 2

    def one(j):
        return jnp.where(inside, near[j], far[j])

    def below(j):
        return jnp.where(bottom, 0.0, jnp.where(even, two[j], one(j)))

    def above(j):
        tile = jnp.where(even, one(j), two[j])
        return jnp.where(interface, cross[j], tile) if j < 9 else tile

    def plane(n, x, ghost, beyond, raw):
        pull_plane(
            lambda i, cx: beyond(i % 9) if cx == ghost else adj[i, x + cx],
            lambda cx: (
                (beyond(9), pltpu.roll(beyond(9), 64, 1), 0)
                if cx == ghost
                else (*edges, (x + 1 + cx) * 9)
            ),
            pulled.at[n],
            raw,
        )

        def store(i, tile):
            made[n, i] = tile

        velocity = [vel[a, x] for a in range(3)]
        collide(lambda i: pulled[n, i], velocity, solid[0, x], store)
        save = pltpu.make_async_copy(made.at[n], out.at[:, x], sems.at[n])
        save.start()
        return save

    final = extent_x - 1
    saves = [plane(0, 0, -1, below, None), plane(1, final, 1, above, interface)]
    if messages:
        low, high = low_in[...], high_in[...]
        low, high = pack_columns(lambda i: made[0, i], 0, low, high)
        low, high = pack_columns(lambda i: made[1, i], final, low, high)
        write_messages(lambda j: made[1, j], low, high, *messages)
    for save in saves:
        save.wait()


def tile_shape(*lead):
    return jax.ShapeDtypeStruct(lead + (16, 128), jnp.float32)


def in_vmem(n):
    return [pl.BlockSpec(memory_space=pltpu.VMEM)] * n


def in_any(n):
    return [pl.BlockSpec(memory_space=pl.ANY)] * n


def body(sizes, adjoint, saved, solid, band_device, band_cell, band_weight):
    zones, widths, count = sizes
    field = adjoint[0]
    extent_x = field.shape[1]
    axes = ("zone", "gx", "yz")
    params = pltpu.CompilerParams(vmem_limit_bytes=VMEM_LIMIT)

    def send(values, target):
        flat = lambda zone, gx, yz: (zone * widths + gx) * count + yz
        places = itertools.product(range(zones), range(widths), range(count))
        return lax.ppermute(values, axes, [(flat(*here), flat(*target(*here))) for here in places])

    def partner_of(place, shift):
        return place + 1 if (place + shift) % 2 == 0 else place - 1

    def flip(zone, gx, yz):
        return (1 - zone, gx, yz)

    def along_z(shift):
        def target(zone, gx, yz):
            to = partner_of(yz, shift)
            return (zone, gx, to) if 0 <= to < count else flip(zone, gx, yz)

        return target

    def hop_z(hop):
        def target(zone, gx, yz):
            if gx == widths - 1:
                return (zone, gx, (yz + hop) % count)
            return flip(zone, gx, yz)

        return target

    def ends_z(zone, gx, yz):
        if gx == widths - 1 and yz in (0, count - 1):
            return (zone, gx, count - 1 - yz)
        return flip(zone, gx, yz)

    def along_x(shift, taken):
        def target(zone, gx, yz):
            to = partner_of(gx, shift)
            return (zone, to, yz) if 0 <= to < widths and taken(gx) else flip(zone, gx, yz)

        return target

    info = pl.pallas_call(
        info_kernel,
        out_shape=tile_shape(4),
        in_specs=in_vmem(3),
        out_specs=in_vmem(1)[0],
        compiler_params=params,
    )(*[jnp.swapaxes(array[0], 1, 2) for array in (band_device, band_cell, band_weight)])
    messages = (tile_shape(9), tile_shape(10), tile_shape(10))
    field, own, first, second = pl.pallas_call(
        pack_kernel,
        out_shape=(tile_shape(27, extent_x), *messages),
        in_specs=[pl.BlockSpec(memory_space=pltpu.HBM)],
        out_specs=tuple(in_vmem(4)),
        scratch_shapes=[pltpu.SemaphoreType.DMA((extent_x,))],
        compiler_params=params,
    )(pltpu.with_memory_space_constraint(field, pltpu.HBM))
    saved = pltpu.with_memory_space_constraint(saved, pltpu.HBM)
    info = send(info, flip)
    for step in (1, 0):
        last = step == 0
        first = send(first, along_z(1))
        second = send(second, along_z(0))
        others = [send(own, target) for target in (*map(hop_z, range(2, count - 1)), ends_z)]
        carried = () if last else (pltpu.with_memory_space_constraint(solid, pltpu.HBM),)
        *copied, vel = pl.pallas_call(
            lambda *refs: velocity_kernel(step, *refs),
            out_shape=(
                *(jax.ShapeDtypeStruct(array.shape, array.dtype) for array in carried),
                tile_shape(3, extent_x),
            ),
            in_specs=[pl.BlockSpec(memory_space=pltpu.HBM)] * (1 + len(carried)),
            out_specs=tuple(in_vmem(1 + len(carried))),
            scratch_shapes=[
                pltpu.VMEM((extent_x, 27, 16, 128), jnp.float32),
                pltpu.SemaphoreType.DMA((extent_x + 1,)),
            ],
            compiler_params=params,
        )(saved, *carried)
        solid = copied[0] if copied else solid
        two, one = pl.pallas_call(
            side_kernel,
            out_shape=(tile_shape(10),) * 2,
            in_specs=in_vmem(3) + in_any(1),
            out_specs=tuple(in_vmem(2)),
            compiler_params=params,
        )(field, first, second, vel)
        everywhere = lambda gx: True
        two = send(two, along_x(1, everywhere))
        if last:
            near = send(one, along_x(0, lambda gx: gx < widths - 2))
            one = send(one, along_x(0, lambda gx: gx >= widths - 2))
        else:
            near = one = send(one, along_x(0, everywhere))

        def make_planes(kernel, planes, given, new, extra):
            operands = (field, vel, solid, first, second, *given)
            return pl.pallas_call(
                lambda *refs: kernel(step, *refs),
                out_shape=(tile_shape(27, extent_x), *extra),
                in_specs=in_vmem(len(operands)) + in_any(len(new)),
                out_specs=tuple(in_any(1) + in_vmem(len(extra))),
                scratch_shapes=[
                    pltpu.VMEM((planes, 27, 16, 128), jnp.float32),
                    pltpu.VMEM((2, 27, 16, 128), jnp.float32),
                    pltpu.SemaphoreType.DMA((planes,)),
                ],
                input_output_aliases={len(operands): 0} if new else {},
                compiler_params=params,
            )(*operands, *new)

        kernel = lambda step, *refs: inner_kernel(step, last, *refs)
        new, *columns = make_planes(kernel, extent_x - 2, (), (), (tile_shape(),) * 2)
        cross = pl.pallas_call(
            lambda *refs: cross_kernel(count, *refs),
            out_shape=tile_shape(9),
            in_specs=in_vmem(count + 2) + in_any(1),
            out_specs=in_vmem(1)[0],
            compiler_params=params,
        )(own, first, second, *others, info, columns[0])
        cross = send(cross, flip)
        ghosts = (near, two, one) if last else (two, near, one)
        field, *results = make_planes(
            lambda *refs: outer_kernel(last, *refs), 2, (*ghosts, cross, *columns), (new,), () if last else messages
        )
        if not last:
            own, first, second = results
    return field[None]


def solution(mesh):
    sizes = tuple(mesh.shape[axis] for axis in ("zone", "gx", "yz"))
    in_specs = (
        P("zone", None, "gx", None, "yz"),
        P(None, "zone", None, "gx", None, "yz"),
        P("zone", "gx", None, "yz"),
        P("zone", None, "yz", None),
        P("zone", None, "yz", None),
        P("zone", None, "yz", None),
    )
    out_specs = P("zone", None, "gx", None, "yz")
    return jax.shard_map(
        lambda *args: body(sizes, *args),
        mesh=mesh,
        in_specs=in_specs,
        out_specs=out_specs,
        check_vma=False,
    )
```

```python
import itertools

import jax
import jax.numpy as jnp
import numpy as np
from jax import lax
from jax.experimental import pallas as pl
from jax.experimental.pallas import tpu as pltpu
from jax.sharding import PartitionSpec as P

OMEGA = 1.6
VMEM_LIMIT = 20 * 1024 * 1024
SIGNS = (-1, 0, 1)


def number(cx, cy, cz):
    return 9 * (cx + 1) + 3 * (cy + 1) + (cz + 1)


def lanes():
    return lax.broadcasted_iota(jnp.int32, (16, 128), 1)


def shift_y(tile, cy):
    if cy == 0:
        return tile
    row = lax.broadcasted_iota(jnp.int32, tile.shape, 0)
    if cy == 1:
        return jnp.where(row == 15, 0.0, pltpu.roll(tile, 15, 0))
    return jnp.where(row == 0, 0.0, pltpu.roll(tile, 1, 0))


def pack_columns(planes, x, low, high):
    lane = lanes()
    for slot in range(9):
        place = (x + 1) * 9 + slot
        here = lane == place
        low = jnp.where(here, pltpu.roll(planes(3 * slot + 2), place, 1), low)
        high = jnp.where(here, pltpu.roll(planes(3 * slot), place + 1, 1), high)
    return low, high


def is_even(axis):
    return lax.rem(lax.axis_index(axis), 2) == 0


def write_messages(top, low, high, own, first, second):
    even = is_even("yz")
    for j in range(9):
        tile = top(j)
        own[j] = tile
        first[j] = tile
        second[j] = tile
    first[9] = jnp.where(even, low, high)
    second[9] = jnp.where(even, high, low)


def edges_from(first, second):
    even = is_even("yz")
    me, count = lax.axis_index("yz"), lax.axis_size("yz")
    low = jnp.where(me == 0, 0.0, jnp.where(even, first[9], second[9]))
    high = jnp.where(me == count - 1, 0.0, jnp.where(even, second[9], first[9]))
    return low, high


def pack_kernel(adj, field_out, own_out, first_out, second_out, sems):
    extent_x = adj.shape[1]
    copies = [
        pltpu.make_async_copy(adj.at[:, x], field_out.at[:, x], sems.at[x]) for x in range(extent_x)
    ]
    for copy in copies:
        copy.start()
    edges = jnp.zeros((16, 128), jnp.float32), jnp.zeros((16, 128), jnp.float32)
    for x in range(extent_x):
        copies[x].wait()
        edges = pack_columns(lambda i: field_out[i, x], x, *edges)
    write_messages(
        lambda j: field_out[j, extent_x - 1], *edges, own_out, first_out, second_out
    )


def info_kernel(device, cell, weight, out):
    for k in range(2):
        out[k] = (device[:, k] * 128 + cell[:, k]).astype(jnp.float32)
        out[2 + k] = weight[:, k]


def velocity_kernel(step, saved, *rest):
    *carried, out, kept, sems = rest
    extent_x = out.shape[1]
    copies = []
    if carried:
        copies.append(pltpu.make_async_copy(carried[0], carried[1], sems.at[extent_x]))
        copies[0].start()

    def load(x):
        return pltpu.make_async_copy(saved.at[step, 0, :, x], kept.at[x], sems.at[x])

    lax.fori_loop(0, extent_x, lambda x, c: (load(x).start(), c)[1], 0)

    def one(x, carry):
        load(x).wait()
        for a, tile in enumerate(velocity_of(lambda i: kept[x, i])):
            out[a, x] = tile
        return carry

    lax.fori_loop(0, extent_x, one, 0)
    for copy in copies:
        copy.wait()


def side_kernel(adj, first, second, *rest):
    *_, near_out, two_out, far_out = rest
    extent_x = adj.shape[1]
    even = is_even("gx")
    for j in range(9):
        top, bottom = adj[j, extent_x - 1], adj[18 + j, 0]
        near_out[j] = far_out[j] = jnp.where(even, top, bottom)
        two_out[j] = jnp.where(even, bottom, top)
    lane = lanes()
    low, high = edges_from(first, second)
    top, bottom = [
        jnp.where(lane < 64, pltpu.roll(low, 128 - start, 1), pltpu.roll(high, 192 - start, 1))
        for start in (9 * extent_x, 9)
    ]
    near_out[9] = far_out[9] = jnp.where(even, top, bottom)
    two_out[9] = jnp.where(even, bottom, top)


def cross_kernel(count, *refs):
    own, first, second = refs[:3]
    *others, ends = refs[3 : 1 + count]
    info, _, out = refs[1 + count :]
    interface = lax.axis_index("gx") == lax.axis_size("gx") - 1

    @pl.when(interface)
    def _():
        me = lax.axis_index("yz")
        even = is_even("yz")
        at_end = (me == 0) | (me == count - 1)
        rows = (0, 8)
        spots, picks = {}, {}
        for r in rows:
            for k in range(2):
                code = info[k, r : r + 8].astype(jnp.int32)
                ahead = lax.rem(code // 128 - me + count, count)
                spots[r, k] = lax.rem(code, 128)
                turned = jnp.where(even, lax.rem(count - ahead, count), ahead)
                masks = [turned == 1, turned == count - 1]
                masks += [ahead == count - hop for hop in range(2, count - 1)]
                picks[r, k] = masks
        for j in range(9):
            halves = []
            for r in rows:
                total = jnp.zeros((8, 128), jnp.float32)
                for k in range(2):
                    tiles = [ref[j, r : r + 8] for ref in (own, first, second, *others)]
                    tiles[1] = jnp.where(at_end, ends[j, r : r + 8], tiles[1])
                    got = [jnp.take_along_axis(tile, spots[r, k], axis=1) for tile in tiles]
                    picked = got[0]
                    for mask, value in zip(picks[r, k], got[1:]):
                        picked = jnp.where(mask, value, picked)
                    total = total + picked * info[2 + k, r : r + 8]
                halves.append(total)
            out[j] = jnp.concatenate(halves, axis=0)


def velocity_of(saved):
    totals, along_y, along_z = [], [], []
    for cx in SIGNS:
        sums, diffs = [], []
        for cy in SIGNS:
            lo, mid, hi = [saved(number(cx, cy, cz)) for cz in SIGNS]
            sums.append(lo + mid + hi)
            diffs.append(hi - lo)
        totals.append(sums[0] + sums[1] + sums[2])
        along_y.append(sums[2] - sums[0])
        along_z.append(diffs[0] + diffs[1] + diffs[2])
    density = totals[0] + totals[1] + totals[2]
    momentum = (
        totals[2] - totals[0],
        along_y[0] + along_y[1] + along_y[2],
        along_z[0] + along_z[1] + along_z[2],
    )
    return [part / density for part in momentum]


def moments_of(pull):
    rows = []
    for cx in SIGNS:
        plain, first, second = [], [], []
        for cy in SIGNS:
            lo, mid, hi = [pull(cx, cy, cz) for cz in SIGNS]
            both = lo + hi
            plain.append(mid + 0.25 * both)
            first.append(hi - lo)
            second.append(both)
        pair = plain[0] + plain[2]
        rows.append(
            (
                plain[1] + 0.25 * pair,
                plain[2] - plain[0],
                pair,
                first[1] + 0.25 * (first[0] + first[2]),
                first[2] - first[0],
                second[1] + 0.25 * (second[0] + second[2]),
            )
        )
    even = [rows[1][n] + 0.25 * (rows[0][n] + rows[2][n]) for n in range(6)]
    zero = (8.0 / 27.0) * even[0]
    along = (
        (2.0 / 27.0) * (rows[2][0] - rows[0][0]),
        (2.0 / 27.0) * even[1],
        (2.0 / 27.0) * even[3],
    )
    square = (
        (2.0 / 27.0) * (rows[2][0] + rows[0][0]),
        (2.0 / 27.0) * even[2],
        (2.0 / 27.0) * even[5],
    )
    mixed = (
        (1.0 / 54.0) * (rows[2][1] - rows[0][1]),
        (1.0 / 54.0) * (rows[2][3] - rows[0][3]),
        (1.0 / 54.0) * even[4],
    )
    return zero, along, square, mixed


def collide(pull, velocity, solid, store):
    zero, along, square, mixed = moments_of(lambda cx, cy, cz: pull(number(cx, cy, cz)))
    ux, uy, uz = velocity
    xy, xz, yz = mixed
    quadratic = (
        ux * ux * square[0]
        + uy * uy * square[1]
        + uz * uz * square[2]
        + 2.0 * (ux * uy * xy + ux * uz * xz + uy * uz * yz)
    )
    speed = ux * ux + uy * uy + uz * uz
    scalar = OMEGA * (zero * (1.0 + 1.5 * speed) - 4.5 * quadratic)
    vec_x = OMEGA * (3.0 * along[0] + 9.0 * (square[0] * ux + xy * uy + xz * uz) - 3.0 * ux * zero)
    vec_y = OMEGA * (3.0 * along[1] + 9.0 * (xy * ux + square[1] * uy + yz * uz) - 3.0 * uy * zero)
    vec_z = OMEGA * (3.0 * along[2] + 9.0 * (xz * ux + yz * uy + square[2] * uz) - 3.0 * uz * zero)
    wall = solid == 1
    for cx in SIGNS:
        base = scalar if cx == 0 else (scalar + vec_x if cx > 0 else scalar - vec_x)
        for cy in SIGNS:
            inner = base if cy == 0 else (base + vec_y if cy > 0 else base - vec_y)
            for cz in SIGNS:
                full = inner if cz == 0 else (inner + vec_z if cz > 0 else inner - vec_z)
                i = number(cx, cy, cz)
                store(i, jnp.where(wall, pull(26 - i), (1.0 - OMEGA) * pull(i) + full))


def pull_plane(tile_of, edges_of, pulled, raw=None):
    lane = lanes()
    for cx in SIGNS:
        low_edge, high_edge, start = edges_of(cx)
        for cy in SIGNS:
            place = start + 3 * (cx + 1) + cy + 1
            for cz in SIGNS:
                i = number(cx, cy, cz)
                source = tile_of(i, cx)
                tile = source
                if cz == -1:
                    edge = pltpu.roll(low_edge, 128 - place, 1)
                    tile = jnp.where(lane == 0, edge, pltpu.roll(source, 1, 1))
                elif cz == 1:
                    edge = pltpu.roll(high_edge, 127 - place, 1)
                    tile = jnp.where(lane == 127, edge, pltpu.roll(source, 127, 1))
                if raw is not None and cx == 1:
                    tile = jnp.where(raw, source, tile)
                pulled[i] = shift_y(tile, cy)


def inner_kernel(step, last, adj, vel, solid, first, second, *rest):
    out, low_out, high_out, made, pulled, sems = rest
    extent_x = adj.shape[1]
    low_edge, high_edge = edges_from(first, second)

    def save(x):
        return pltpu.make_async_copy(made.at[x - 1], out.at[:, x], sems.at[x - 1])

    def plane(x, carry):
        here = pulled.at[lax.rem(x, 2)]
        pull_plane(
            lambda i, cx: adj[i, x + cx],
            lambda cx: (low_edge, high_edge, (x + 1 + cx) * 9),
            here,
        )

        def store(i, tile):
            made[x - 1, i] = tile

        velocity = [vel[a, x] for a in range(3)]
        collide(lambda i: here[i], velocity, solid[0, x], store)
        save(x).start()
        if last:
            return carry
        return pack_columns(lambda i: made[x - 1, i], x, *carry)

    zero = jnp.zeros((16, 128), jnp.float32)
    low_out[...], high_out[...] = lax.fori_loop(1, extent_x - 1, plane, (zero, zero), unroll=2)
    lax.fori_loop(1, extent_x - 1, lambda x, c: (save(x).wait(), c)[1], 0)


def outer_kernel(step, adj, vel, solid, first, second, near, two, far, cross, *rest):
    *rest, made, pulled, sems = rest
    low_in, high_in, _, out, *messages = rest
    extent_x = adj.shape[1]
    edges = edges_from(first, second)
    even = is_even("gx")
    interface = lax.axis_index("gx") == lax.axis_size("gx") - 1

    bottom = lax.axis_index("gx") == 0
    inside = lax.axis_index("gx") < lax.axis_size("gx") - 2

    def one(j):
        return jnp.where(inside, near[j], far[j])

    def below(j):
        return jnp.where(bottom, 0.0, jnp.where(even, two[j], one(j)))

    def above(j):
        tile = jnp.where(even, one(j), two[j])
        return jnp.where(interface, cross[j], tile) if j < 9 else tile

    def plane(n, x, ghost, beyond, raw):
        pull_plane(
            lambda i, cx: beyond(i % 9) if cx == ghost else adj[i, x + cx],
            lambda cx: (
                (beyond(9), pltpu.roll(beyond(9), 64, 1), 0)
                if cx == ghost
                else (*edges, (x + 1 + cx) * 9)
            ),
            pulled.at[n],
            raw,
        )

        def store(i, tile):
            made[n, i] = tile

        velocity = [vel[a, x] for a in range(3)]
        collide(lambda i: pulled[n, i], velocity, solid[0, x], store)
        save = pltpu.make_async_copy(made.at[n], out.at[:, x], sems.at[n])
        save.start()
        return save

    final = extent_x - 1
    saves = [plane(0, 0, -1, below, None), plane(1, final, 1, above, interface)]
    if messages:
        low, high = low_in[...], high_in[...]
        low, high = pack_columns(lambda i: made[0, i], 0, low, high)
        low, high = pack_columns(lambda i: made[1, i], final, low, high)
        write_messages(lambda j: made[1, j], low, high, *messages)
    for save in saves:
        save.wait()


def tile_shape(*lead):
    return jax.ShapeDtypeStruct(lead + (16, 128), jnp.float32)


def in_vmem(n):
    return [pl.BlockSpec(memory_space=pltpu.VMEM)] * n


def in_any(n):
    return [pl.BlockSpec(memory_space=pl.ANY)] * n


def body(sizes, adjoint, saved, solid, band_device, band_cell, band_weight):
    zones, widths, count = sizes
    field = adjoint[0]
    extent_x = field.shape[1]
    axes = ("zone", "gx", "yz")
    params = pltpu.CompilerParams(vmem_limit_bytes=VMEM_LIMIT)

    def send(values, target):
        flat = lambda zone, gx, yz: (zone * widths + gx) * count + yz
        places = itertools.product(range(zones), range(widths), range(count))
        return lax.ppermute(values, axes, [(flat(*here), flat(*target(*here))) for here in places])

    def partner_of(place, shift):
        return place + 1 if (place + shift) % 2 == 0 else place - 1

    def flip(zone, gx, yz):
        return (1 - zone, gx, yz)

    def along_z(shift):
        def target(zone, gx, yz):
            to = partner_of(yz, shift)
            return (zone, gx, to) if 0 <= to < count else flip(zone, gx, yz)

        return target

    def hop_z(hop):
        def target(zone, gx, yz):
            if gx == widths - 1:
                return (zone, gx, (yz + hop) % count)
            return flip(zone, gx, yz)

        return target

    def ends_z(zone, gx, yz):
        if gx == widths - 1 and yz in (0, count - 1):
            return (zone, gx, count - 1 - yz)
        return flip(zone, gx, yz)

    def along_x(shift, taken):
        def target(zone, gx, yz):
            to = partner_of(gx, shift)
            return (zone, to, yz) if 0 <= to < widths and taken(gx) else flip(zone, gx, yz)

        return target

    info = pl.pallas_call(
        info_kernel,
        out_shape=tile_shape(4),
        in_specs=in_vmem(3),
        out_specs=in_vmem(1)[0],
        compiler_params=params,
    )(*[jnp.swapaxes(array[0], 1, 2) for array in (band_device, band_cell, band_weight)])
    messages = (tile_shape(9), tile_shape(10), tile_shape(10))
    field, own, first, second = pl.pallas_call(
        pack_kernel,
        out_shape=(tile_shape(27, extent_x), *messages),
        in_specs=[pl.BlockSpec(memory_space=pltpu.HBM)],
        out_specs=tuple(in_vmem(4)),
        scratch_shapes=[pltpu.SemaphoreType.DMA((extent_x,))],
        compiler_params=params,
    )(pltpu.with_memory_space_constraint(field, pltpu.HBM))
    saved = pltpu.with_memory_space_constraint(saved, pltpu.HBM)
    info = send(info, flip)
    for step in (1, 0):
        last = step == 0
        swap = last
        first = send(first, along_z(1))
        second = send(second, along_z(0))
        others = [send(own, target) for target in (*map(hop_z, range(2, count - 1)), ends_z)]
        carried = () if last else (pltpu.with_memory_space_constraint(solid, pltpu.HBM),)
        *copied, vel = pl.pallas_call(
            lambda *refs: velocity_kernel(step, *refs),
            out_shape=(
                *(jax.ShapeDtypeStruct(array.shape, array.dtype) for array in carried),
                tile_shape(3, extent_x),
            ),
            in_specs=[pl.BlockSpec(memory_space=pltpu.HBM)] * (1 + len(carried)),
            out_specs=tuple(in_vmem(1 + len(carried))),
            scratch_shapes=[
                pltpu.VMEM((extent_x, 27, 16, 128), jnp.float32),
                pltpu.SemaphoreType.DMA((extent_x + 1,)),
            ],
            compiler_params=params,
        )(saved, *carried)
        solid = copied[0] if copied else solid
        near, two, far = pl.pallas_call(
            side_kernel,
            out_shape=(tile_shape(10),) * 3,
            in_specs=in_vmem(3) + in_any(2),
            out_specs=tuple(in_vmem(3)),
            compiler_params=params,
        )(field, first, second, vel, info)
        near = send(near, along_x(0, lambda gx: gx < widths - 2))
        two = send(two, along_x(1, lambda gx: True))
        far = send(far, along_x(0, lambda gx: gx >= widths - 2))

        def make_planes(kernel, planes, given, new, extra):
            pair = (second, first) if swap else (first, second)
            operands = (field, vel, solid, *pair, *given)

            def run(adj, vel, solid, *refs):
                kernel(step, adj, vel, solid, *(refs[1::-1] if swap else refs[:2]), *refs[2:])

            return pl.pallas_call(
                run,
                out_shape=(tile_shape(27, extent_x), *extra),
                in_specs=in_vmem(len(operands)) + in_any(len(new)),
                out_specs=tuple(in_any(1) + in_vmem(len(extra))),
                scratch_shapes=[
                    pltpu.VMEM((planes, 27, 16, 128), jnp.float32),
                    pltpu.VMEM((2, 27, 16, 128), jnp.float32),
                    pltpu.SemaphoreType.DMA((planes,)),
                ],
                input_output_aliases={len(operands): 0} if new else {},
                compiler_params=params,
            )(*operands, *new)

        kernel = lambda step, *refs: inner_kernel(step, last, *refs)
        new, *columns = make_planes(kernel, extent_x - 2, (), (), (tile_shape(),) * 2)
        cross = pl.pallas_call(
            lambda *refs: cross_kernel(count, *refs),
            out_shape=tile_shape(9),
            in_specs=in_vmem(count + 2) + in_any(1),
            out_specs=in_vmem(1)[0],
            compiler_params=params,
        )(own, first, second, *others, info, columns[0])
        cross = send(cross, flip)
        ghosts = (near, two, far)
        field, *results = make_planes(
            outer_kernel, 2, (*ghosts, cross, *columns), (new,), () if last else messages
        )
        if not last:
            own, first, second = results
    return field[None]


def solution(mesh):
    sizes = tuple(mesh.shape[axis] for axis in ("zone", "gx", "yz"))
    in_specs = (
        P("zone", None, "gx", None, "yz"),
        P(None, "zone", None, "gx", None, "yz"),
        P("zone", "gx", None, "yz"),
        P("zone", None, "yz", None),
        P("zone", None, "yz", None),
        P("zone", None, "yz", None),
    )
    out_specs = P("zone", None, "gx", None, "yz")
    return jax.shard_map(
        lambda *args: body(sizes, *args),
        mesh=mesh,
        in_specs=in_specs,
        out_specs=out_specs,
        check_vma=False,
    )
```

```python
import itertools

import jax
import jax.numpy as jnp
import numpy as np
from jax import lax
from jax.experimental import pallas as pl
from jax.experimental.pallas import tpu as pltpu
from jax.sharding import PartitionSpec as P

OMEGA = 1.6
VMEM_LIMIT = 20 * 1024 * 1024
SIGNS = (-1, 0, 1)


def number(cx, cy, cz):
    return 9 * (cx + 1) + 3 * (cy + 1) + (cz + 1)


def lanes():
    return lax.broadcasted_iota(jnp.int32, (16, 128), 1)


def shift_y(tile, cy):
    if cy == 0:
        return tile
    row = lax.broadcasted_iota(jnp.int32, tile.shape, 0)
    if cy == 1:
        return jnp.where(row == 15, 0.0, pltpu.roll(tile, 15, 0))
    return jnp.where(row == 0, 0.0, pltpu.roll(tile, 1, 0))


def pack_columns(planes, x, low, high):
    lane = lanes()
    for slot in range(9):
        place = (x + 1) * 9 + slot
        here = lane == place
        low = jnp.where(here, pltpu.roll(planes(3 * slot + 2), place, 1), low)
        high = jnp.where(here, pltpu.roll(planes(3 * slot), place + 1, 1), high)
    return low, high


def is_even(axis):
    return lax.rem(lax.axis_index(axis), 2) == 0


def write_messages(top, low, high, own, first, second):
    even = is_even("yz")
    for j in range(9):
        tile = top(j)
        own[j] = tile
        first[j] = tile
        second[j] = tile
    first[9] = jnp.where(even, low, high)
    second[9] = jnp.where(even, high, low)


def edges_from(first, second):
    even = is_even("yz")
    me, count = lax.axis_index("yz"), lax.axis_size("yz")
    low = jnp.where(me == 0, 0.0, jnp.where(even, first[9], second[9]))
    high = jnp.where(me == count - 1, 0.0, jnp.where(even, second[9], first[9]))
    return low, high


def pack_kernel(adj, field_out, own_out, first_out, second_out, sems):
    extent_x = adj.shape[1]
    copies = [
        pltpu.make_async_copy(adj.at[:, x], field_out.at[:, x], sems.at[x]) for x in range(extent_x)
    ]
    for copy in copies:
        copy.start()
    edges = jnp.zeros((16, 128), jnp.float32), jnp.zeros((16, 128), jnp.float32)
    for x in range(extent_x):
        copies[x].wait()
        edges = pack_columns(lambda i: field_out[i, x], x, *edges)
    write_messages(
        lambda j: field_out[j, extent_x - 1], *edges, own_out, first_out, second_out
    )


def info_kernel(device, cell, weight, out):
    for k in range(2):
        out[k] = (device[:, k] * 128 + cell[:, k]).astype(jnp.float32)
        out[2 + k] = weight[:, k]


def velocity_kernel(step, saved, *rest):
    *carried, out, kept, sems = rest
    extent_x = out.shape[1]
    copies = []
    if carried:
        copies.append(pltpu.make_async_copy(carried[0], carried[1], sems.at[extent_x]))
        copies[0].start()

    def load(x):
        return pltpu.make_async_copy(saved.at[step, 0, :, x], kept.at[x], sems.at[x])

    lax.fori_loop(0, extent_x, lambda x, c: (load(x).start(), c)[1], 0)

    def one(x, carry):
        load(x).wait()
        for a, tile in enumerate(velocity_of(lambda i: kept[x, i])):
            out[a, x] = tile
        return carry

    lax.fori_loop(0, extent_x, one, 0)
    for copy in copies:
        copy.wait()


def side_kernel(adj, first, second, *rest):
    *_, two_out, one_out = rest
    extent_x = adj.shape[1]
    even = is_even("gx")
    for j in range(9):
        top, bottom = adj[j, extent_x - 1], adj[18 + j, 0]
        one_out[j] = jnp.where(even, top, bottom)
        two_out[j] = jnp.where(even, bottom, top)
    lane = lanes()
    low, high = edges_from(first, second)
    top, bottom = [
        jnp.where(lane < 64, pltpu.roll(low, 128 - start, 1), pltpu.roll(high, 192 - start, 1))
        for start in (9 * extent_x, 9)
    ]
    one_out[9] = jnp.where(even, top, bottom)
    two_out[9] = jnp.where(even, bottom, top)


def cross_kernel(count, *refs):
    own, first, second = refs[:3]
    *others, ends = refs[3 : 1 + count]
    info, _, out = refs[1 + count :]
    interface = lax.axis_index("gx") == lax.axis_size("gx") - 1

    @pl.when(interface)
    def _():
        me = lax.axis_index("yz")
        even = is_even("yz")
        at_end = (me == 0) | (me == count - 1)
        rows = (0, 8)
        spots, picks = {}, {}
        for r in rows:
            for k in range(2):
                code = info[k, r : r + 8].astype(jnp.int32)
                ahead = lax.rem(code // 128 - me + count, count)
                spots[r, k] = lax.rem(code, 128)
                turned = jnp.where(even, lax.rem(count - ahead, count), ahead)
                masks = [turned == 1, turned == count - 1]
                masks += [ahead == count - hop for hop in range(2, count - 1)]
                picks[r, k] = masks
        for j in range(9):
            halves = []
            for r in rows:
                total = jnp.zeros((8, 128), jnp.float32)
                for k in range(2):
                    tiles = [ref[j, r : r + 8] for ref in (own, first, second, *others)]
                    tiles[1] = jnp.where(at_end, ends[j, r : r + 8], tiles[1])
                    got = [jnp.take_along_axis(tile, spots[r, k], axis=1) for tile in tiles]
                    picked = got[0]
                    for mask, value in zip(picks[r, k], got[1:]):
                        picked = jnp.where(mask, value, picked)
                    total = total + picked * info[2 + k, r : r + 8]
                halves.append(total)
            out[j] = jnp.concatenate(halves, axis=0)


def velocity_of(saved):
    totals, along_y, along_z = [], [], []
    for cx in SIGNS:
        sums, diffs = [], []
        for cy in SIGNS:
            lo, mid, hi = [saved(number(cx, cy, cz)) for cz in SIGNS]
            sums.append(lo + mid + hi)
            diffs.append(hi - lo)
        totals.append(sums[0] + sums[1] + sums[2])
        along_y.append(sums[2] - sums[0])
        along_z.append(diffs[0] + diffs[1] + diffs[2])
    density = totals[0] + totals[1] + totals[2]
    momentum = (
        totals[2] - totals[0],
        along_y[0] + along_y[1] + along_y[2],
        along_z[0] + along_z[1] + along_z[2],
    )
    return [part / density for part in momentum]


def moments_of(pull):
    rows = []
    for cx in SIGNS:
        plain, first, second = [], [], []
        for cy in SIGNS:
            lo, mid, hi = [pull(cx, cy, cz) for cz in SIGNS]
            both = lo + hi
            plain.append(mid + 0.25 * both)
            first.append(hi - lo)
            second.append(both)
        pair = plain[0] + plain[2]
        rows.append(
            (
                plain[1] + 0.25 * pair,
                plain[2] - plain[0],
                pair,
                first[1] + 0.25 * (first[0] + first[2]),
                first[2] - first[0],
                second[1] + 0.25 * (second[0] + second[2]),
            )
        )
    even = [rows[1][n] + 0.25 * (rows[0][n] + rows[2][n]) for n in range(6)]
    zero = (8.0 / 27.0) * even[0]
    along = (
        (2.0 / 27.0) * (rows[2][0] - rows[0][0]),
        (2.0 / 27.0) * even[1],
        (2.0 / 27.0) * even[3],
    )
    square = (
        (2.0 / 27.0) * (rows[2][0] + rows[0][0]),
        (2.0 / 27.0) * even[2],
        (2.0 / 27.0) * even[5],
    )
    mixed = (
        (1.0 / 54.0) * (rows[2][1] - rows[0][1]),
        (1.0 / 54.0) * (rows[2][3] - rows[0][3]),
        (1.0 / 54.0) * even[4],
    )
    return zero, along, square, mixed


def collide(pull, velocity, solid, store):
    zero, along, square, mixed = moments_of(lambda cx, cy, cz: pull(number(cx, cy, cz)))
    ux, uy, uz = velocity
    xy, xz, yz = mixed
    quadratic = (
        ux * ux * square[0]
        + uy * uy * square[1]
        + uz * uz * square[2]
        + 2.0 * (ux * uy * xy + ux * uz * xz + uy * uz * yz)
    )
    speed = ux * ux + uy * uy + uz * uz
    scalar = OMEGA * (zero * (1.0 + 1.5 * speed) - 4.5 * quadratic)
    vec_x = OMEGA * (3.0 * along[0] + 9.0 * (square[0] * ux + xy * uy + xz * uz) - 3.0 * ux * zero)
    vec_y = OMEGA * (3.0 * along[1] + 9.0 * (xy * ux + square[1] * uy + yz * uz) - 3.0 * uy * zero)
    vec_z = OMEGA * (3.0 * along[2] + 9.0 * (xz * ux + yz * uy + square[2] * uz) - 3.0 * uz * zero)
    wall = solid == 1
    for cx in SIGNS:
        base = scalar if cx == 0 else (scalar + vec_x if cx > 0 else scalar - vec_x)
        for cy in SIGNS:
            inner = base if cy == 0 else (base + vec_y if cy > 0 else base - vec_y)
            for cz in SIGNS:
                full = inner if cz == 0 else (inner + vec_z if cz > 0 else inner - vec_z)
                i = number(cx, cy, cz)
                store(i, jnp.where(wall, pull(26 - i), (1.0 - OMEGA) * pull(i) + full))


def pull_plane(tile_of, edges_of, pulled, raw=None):
    lane = lanes()
    for cx in SIGNS:
        low_edge, high_edge, start = edges_of(cx)
        for cy in SIGNS:
            place = start + 3 * (cx + 1) + cy + 1
            for cz in SIGNS:
                i = number(cx, cy, cz)
                source = tile_of(i, cx)
                tile = source
                if cz == -1:
                    edge = pltpu.roll(low_edge, 128 - place, 1)
                    tile = jnp.where(lane == 0, edge, pltpu.roll(source, 1, 1))
                elif cz == 1:
                    edge = pltpu.roll(high_edge, 127 - place, 1)
                    tile = jnp.where(lane == 127, edge, pltpu.roll(source, 127, 1))
                if raw is not None and cx == 1:
                    tile = jnp.where(raw, source, tile)
                pulled[i] = shift_y(tile, cy)


def inner_kernel(step, last, adj, vel, solid, first, second, *rest):
    out, low_out, high_out, made, pulled, sems = rest
    extent_x = adj.shape[1]
    low_edge, high_edge = edges_from(first, second)

    def save(x):
        return pltpu.make_async_copy(made.at[x - 1], out.at[:, x], sems.at[x - 1])

    def plane(x, carry):
        here = pulled.at[lax.rem(x, 2)]
        pull_plane(
            lambda i, cx: adj[i, x + cx],
            lambda cx: (low_edge, high_edge, (x + 1 + cx) * 9),
            here,
        )

        def store(i, tile):
            made[x - 1, i] = tile

        velocity = [vel[a, x] for a in range(3)]
        collide(lambda i: here[i], velocity, solid[0, x], store)
        save(x).start()
        if last:
            return carry
        return pack_columns(lambda i: made[x - 1, i], x, *carry)

    zero = jnp.zeros((16, 128), jnp.float32)
    low_out[...], high_out[...] = lax.fori_loop(1, extent_x - 1, plane, (zero, zero), unroll=2)
    lax.fori_loop(1, extent_x - 1, lambda x, c: (save(x).wait(), c)[1], 0)


def outer_kernel(step, adj, vel, solid, first, second, near, far, two, cross, *rest):
    *rest, made, pulled, sems = rest
    low_in, high_in, _, out, *messages = rest
    extent_x = adj.shape[1]
    edges = edges_from(first, second)
    even = is_even("gx")
    interface = lax.axis_index("gx") == lax.axis_size("gx") - 1

    bottom = lax.axis_index("gx") == 0
    inside = lax.axis_index("gx") < lax.axis_size("gx") - 2

    def one(j):
        return jnp.where(inside, near[j], far[j])

    def below(j):
        return jnp.where(bottom, 0.0, jnp.where(even, two[j], one(j)))

    def above(j):
        tile = jnp.where(even, one(j), two[j])
        return jnp.where(interface, cross[j], tile) if j < 9 else tile

    def plane(n, x, ghost, beyond, raw):
        pull_plane(
            lambda i, cx: beyond(i % 9) if cx == ghost else adj[i, x + cx],
            lambda cx: (
                (beyond(9), pltpu.roll(beyond(9), 64, 1), 0)
                if cx == ghost
                else (*edges, (x + 1 + cx) * 9)
            ),
            pulled.at[n],
            raw,
        )

        def store(i, tile):
            made[n, i] = tile

        velocity = [vel[a, x] for a in range(3)]
        collide(lambda i: pulled[n, i], velocity, solid[0, x], store)
        save = pltpu.make_async_copy(made.at[n], out.at[:, x], sems.at[n])
        save.start()
        return save

    final = extent_x - 1
    saves = [plane(0, 0, -1, below, None), plane(1, final, 1, above, interface)]
    if messages:
        low, high = low_in[...], high_in[...]
        low, high = pack_columns(lambda i: made[0, i], 0, low, high)
        low, high = pack_columns(lambda i: made[1, i], final, low, high)
        write_messages(lambda j: made[1, j], low, high, *messages)
    for save in saves:
        save.wait()


def tile_shape(*lead):
    return jax.ShapeDtypeStruct(lead + (16, 128), jnp.float32)


def in_vmem(n):
    return [pl.BlockSpec(memory_space=pltpu.VMEM)] * n


def in_any(n):
    return [pl.BlockSpec(memory_space=pl.ANY)] * n


def body(sizes, adjoint, saved, solid, band_device, band_cell, band_weight):
    zones, widths, count = sizes
    field = adjoint[0]
    extent_x = field.shape[1]
    axes = ("zone", "gx", "yz")
    params = pltpu.CompilerParams(vmem_limit_bytes=VMEM_LIMIT)

    def send(values, target):
        flat = lambda zone, gx, yz: (zone * widths + gx) * count + yz
        places = itertools.product(range(zones), range(widths), range(count))
        return lax.ppermute(values, axes, [(flat(*here), flat(*target(*here))) for here in places])

    def partner_of(place, shift):
        return place + 1 if (place + shift) % 2 == 0 else place - 1

    def flip(zone, gx, yz):
        return (1 - zone, gx, yz)

    def along_z(shift):
        def target(zone, gx, yz):
            to = partner_of(yz, shift)
            return (zone, gx, to) if 0 <= to < count else flip(zone, gx, yz)

        return target

    def hop_z(hop):
        def target(zone, gx, yz):
            if gx == widths - 1:
                return (zone, gx, (yz + hop) % count)
            return flip(zone, gx, yz)

        return target

    def ends_z(zone, gx, yz):
        if gx == widths - 1 and yz in (0, count - 1):
            return (zone, gx, count - 1 - yz)
        return flip(zone, gx, yz)

    def along_x(shift, taken):
        def target(zone, gx, yz):
            to = partner_of(gx, shift)
            return (zone, to, yz) if 0 <= to < widths and taken(gx) else flip(zone, gx, yz)

        return target

    info = pl.pallas_call(
        info_kernel,
        out_shape=tile_shape(4),
        in_specs=in_vmem(3),
        out_specs=in_vmem(1)[0],
        compiler_params=params,
    )(*[jnp.swapaxes(array[0], 1, 2) for array in (band_device, band_cell, band_weight)])
    messages = (tile_shape(9), tile_shape(10), tile_shape(10))
    field, own, first, second = pl.pallas_call(
        pack_kernel,
        out_shape=(tile_shape(27, extent_x), *messages),
        in_specs=[pl.BlockSpec(memory_space=pltpu.HBM)],
        out_specs=tuple(in_vmem(4)),
        scratch_shapes=[pltpu.SemaphoreType.DMA((extent_x,))],
        compiler_params=params,
    )(pltpu.with_memory_space_constraint(field, pltpu.HBM))
    saved = pltpu.with_memory_space_constraint(saved, pltpu.HBM)
    info = send(info, flip)
    for step in (1, 0):
        last = step == 0
        swap = last
        first = send(first, along_z(1))
        second = send(second, along_z(0))
        others = [send(own, target) for target in (*map(hop_z, range(2, count - 1)), ends_z)]
        carried = () if last else (pltpu.with_memory_space_constraint(solid, pltpu.HBM),)
        *copied, vel = pl.pallas_call(
            lambda *refs: velocity_kernel(step, *refs),
            out_shape=(
                *(jax.ShapeDtypeStruct(array.shape, array.dtype) for array in carried),
                tile_shape(3, extent_x),
            ),
            in_specs=[pl.BlockSpec(memory_space=pltpu.HBM)] * (1 + len(carried)),
            out_specs=tuple(in_vmem(1 + len(carried))),
            scratch_shapes=[
                pltpu.VMEM((extent_x, 27, 16, 128), jnp.float32),
                pltpu.SemaphoreType.DMA((extent_x + 1,)),
            ],
            compiler_params=params,
        )(saved, *carried)
        solid = copied[0] if copied else solid
        two, one = pl.pallas_call(
            side_kernel,
            out_shape=(tile_shape(10),) * 2,
            in_specs=in_vmem(3) + in_any(2),
            out_specs=tuple(in_vmem(2)),
            compiler_params=params,
        )(field, first, second, vel, info)
        near = send(one, along_x(0, lambda gx: gx < widths - 2))
        two = send(two, along_x(1, lambda gx: True))
        one = send(one, along_x(0, lambda gx: gx >= widths - 2))

        def make_planes(kernel, planes, given, new, extra):
            pair = (second, first) if swap else (first, second)
            operands = (field, vel, solid, *pair, *given)

            def run(adj, vel, solid, *refs):
                kernel(step, adj, vel, solid, *(refs[1::-1] if swap else refs[:2]), *refs[2:])

            return pl.pallas_call(
                run,
                out_shape=(tile_shape(27, extent_x), *extra),
                in_specs=in_vmem(len(operands)) + in_any(len(new)),
                out_specs=tuple(in_any(1) + in_vmem(len(extra))),
                scratch_shapes=[
                    pltpu.VMEM((planes, 27, 16, 128), jnp.float32),
                    pltpu.VMEM((2, 27, 16, 128), jnp.float32),
                    pltpu.SemaphoreType.DMA((planes,)),
                ],
                input_output_aliases={len(operands): 0} if new else {},
                compiler_params=params,
            )(*operands, *new)

        kernel = lambda step, *refs: inner_kernel(step, last, *refs)
        new, *columns = make_planes(kernel, extent_x - 2, (), (), (tile_shape(),) * 2)
        cross = pl.pallas_call(
            lambda *refs: cross_kernel(count, *refs),
            out_shape=tile_shape(9),
            in_specs=in_vmem(count + 2) + in_any(1),
            out_specs=in_vmem(1)[0],
            compiler_params=params,
        )(own, first, second, *others, info, columns[0])
        cross = send(cross, flip)
        ghosts = (near, one, two)
        field, *results = make_planes(
            outer_kernel, 2, (*ghosts, cross, *columns), (new,), () if last else messages
        )
        if not last:
            own, first, second = results
    return field[None]


def solution(mesh):
    sizes = tuple(mesh.shape[axis] for axis in ("zone", "gx", "yz"))
    in_specs = (
        P("zone", None, "gx", None, "yz"),
        P(None, "zone", None, "gx", None, "yz"),
        P("zone", "gx", None, "yz"),
        P("zone", None, "yz", None),
        P("zone", None, "yz", None),
        P("zone", None, "yz", None),
    )
    out_specs = P("zone", None, "gx", None, "yz")
    return jax.shard_map(
        lambda *args: body(sizes, *args),
        mesh=mesh,
        in_specs=in_specs,
        out_specs=out_specs,
        check_vma=False,
    )
```

```python
import itertools

import jax
import jax.numpy as jnp
import numpy as np
from jax import lax
from jax.experimental import pallas as pl
from jax.experimental.pallas import tpu as pltpu
from jax.sharding import PartitionSpec as P

OMEGA = 1.6
VMEM_LIMIT = 20 * 1024 * 1024
SIGNS = (-1, 0, 1)


def number(cx, cy, cz):
    return 9 * (cx + 1) + 3 * (cy + 1) + (cz + 1)


def lanes():
    return lax.broadcasted_iota(jnp.int32, (16, 128), 1)


def shift_y(tile, cy):
    if cy == 0:
        return tile
    row = lax.broadcasted_iota(jnp.int32, tile.shape, 0)
    if cy == 1:
        return jnp.where(row == 15, 0.0, pltpu.roll(tile, 15, 0))
    return jnp.where(row == 0, 0.0, pltpu.roll(tile, 1, 0))


def pack_columns(planes, x, low, high):
    lane = lanes()
    for slot in range(9):
        place = (x + 1) * 9 + slot
        here = lane == place
        low = jnp.where(here, pltpu.roll(planes(3 * slot + 2), place, 1), low)
        high = jnp.where(here, pltpu.roll(planes(3 * slot), place + 1, 1), high)
    return low, high


def is_even(axis):
    return lax.rem(lax.axis_index(axis), 2) == 0


def write_messages(top, low, high, own, first, second):
    even = is_even("yz")
    for j in range(9):
        tile = top(j)
        own[j] = tile
        first[j] = tile
        second[j] = tile
    first[9] = jnp.where(even, low, high)
    second[9] = jnp.where(even, high, low)


def edges_from(first, second):
    even = is_even("yz")
    me, count = lax.axis_index("yz"), lax.axis_size("yz")
    low = jnp.where(me == 0, 0.0, jnp.where(even, first[9], second[9]))
    high = jnp.where(me == count - 1, 0.0, jnp.where(even, second[9], first[9]))
    return low, high


def pack_kernel(adj, field_out, own_out, first_out, second_out, sems):
    extent_x = adj.shape[1]
    copies = [
        pltpu.make_async_copy(adj.at[:, x], field_out.at[:, x], sems.at[x]) for x in range(extent_x)
    ]
    for copy in copies:
        copy.start()
    edges = jnp.zeros((16, 128), jnp.float32), jnp.zeros((16, 128), jnp.float32)
    for x in range(extent_x):
        copies[x].wait()
        edges = pack_columns(lambda i: field_out[i, x], x, *edges)
    write_messages(
        lambda j: field_out[j, extent_x - 1], *edges, own_out, first_out, second_out
    )


def info_kernel(device, cell, weight, out):
    for k in range(2):
        out[k] = (device[:, k] * 128 + cell[:, k]).astype(jnp.float32)
        out[2 + k] = weight[:, k]


def velocity_kernel(step, saved, *rest):
    *carried, out, kept, sems = rest
    extent_x = out.shape[1]
    copies = []
    if carried:
        copies.append(pltpu.make_async_copy(carried[0], carried[1], sems.at[extent_x]))
        copies[0].start()

    def load(x):
        return pltpu.make_async_copy(saved.at[step, 0, :, x], kept.at[x], sems.at[x])

    lax.fori_loop(0, extent_x, lambda x, c: (load(x).start(), c)[1], 0)

    def one(x, carry):
        load(x).wait()
        for a, tile in enumerate(velocity_of(lambda i: kept[x, i])):
            out[a, x] = tile
        return carry

    lax.fori_loop(0, extent_x, one, 0)
    for copy in copies:
        copy.wait()


def side_kernel(adj, first, second, *rest):
    *_, near_out, two_out, far_out = rest
    extent_x = adj.shape[1]
    even = is_even("gx")
    for j in range(9):
        top, bottom = adj[j, extent_x - 1], adj[18 + j, 0]
        near_out[j] = far_out[j] = jnp.where(even, top, bottom)
        two_out[j] = jnp.where(even, bottom, top)
    lane = lanes()
    low, high = edges_from(first, second)
    top, bottom = [
        jnp.where(lane < 64, pltpu.roll(low, 128 - start, 1), pltpu.roll(high, 192 - start, 1))
        for start in (9 * extent_x, 9)
    ]
    near_out[9] = far_out[9] = jnp.where(even, top, bottom)
    two_out[9] = jnp.where(even, bottom, top)


def cross_kernel(count, *refs):
    own, first, second = refs[:3]
    *others, ends = refs[3 : 1 + count]
    info, _, out = refs[1 + count :]
    interface = lax.axis_index("gx") == lax.axis_size("gx") - 1

    @pl.when(interface)
    def _():
        me = lax.axis_index("yz")
        even = is_even("yz")
        at_end = (me == 0) | (me == count - 1)
        rows = (0, 8)
        spots, picks = {}, {}
        for r in rows:
            for k in range(2):
                code = info[k, r : r + 8].astype(jnp.int32)
                ahead = lax.rem(code // 128 - me + count, count)
                spots[r, k] = lax.rem(code, 128)
                turned = jnp.where(even, lax.rem(count - ahead, count), ahead)
                masks = [turned == 1, turned == count - 1]
                masks += [ahead == count - hop for hop in range(2, count - 1)]
                picks[r, k] = masks
        for j in range(9):
            halves = []
            for r in rows:
                total = jnp.zeros((8, 128), jnp.float32)
                for k in range(2):
                    tiles = [ref[j, r : r + 8] for ref in (own, first, second, *others)]
                    tiles[1] = jnp.where(at_end, ends[j, r : r + 8], tiles[1])
                    got = [jnp.take_along_axis(tile, spots[r, k], axis=1) for tile in tiles]
                    picked = got[0]
                    for mask, value in zip(picks[r, k], got[1:]):
                        picked = jnp.where(mask, value, picked)
                    total = total + picked * info[2 + k, r : r + 8]
                halves.append(total)
            out[j] = jnp.concatenate(halves, axis=0)


def velocity_of(saved):
    totals, along_y, along_z = [], [], []
    for cx in SIGNS:
        sums, diffs = [], []
        for cy in SIGNS:
            lo, mid, hi = [saved(number(cx, cy, cz)) for cz in SIGNS]
            sums.append(lo + mid + hi)
            diffs.append(hi - lo)
        totals.append(sums[0] + sums[1] + sums[2])
        along_y.append(sums[2] - sums[0])
        along_z.append(diffs[0] + diffs[1] + diffs[2])
    density = totals[0] + totals[1] + totals[2]
    momentum = (
        totals[2] - totals[0],
        along_y[0] + along_y[1] + along_y[2],
        along_z[0] + along_z[1] + along_z[2],
    )
    return [part / density for part in momentum]


def moments_of(pull):
    rows = []
    for cx in SIGNS:
        plain, first, second = [], [], []
        for cy in SIGNS:
            lo, mid, hi = [pull(cx, cy, cz) for cz in SIGNS]
            both = lo + hi
            plain.append(mid + 0.25 * both)
            first.append(hi - lo)
            second.append(both)
        pair = plain[0] + plain[2]
        rows.append(
            (
                plain[1] + 0.25 * pair,
                plain[2] - plain[0],
                pair,
                first[1] + 0.25 * (first[0] + first[2]),
                first[2] - first[0],
                second[1] + 0.25 * (second[0] + second[2]),
            )
        )
    even = [rows[1][n] + 0.25 * (rows[0][n] + rows[2][n]) for n in range(6)]
    zero = (8.0 / 27.0) * even[0]
    along = (
        (2.0 / 27.0) * (rows[2][0] - rows[0][0]),
        (2.0 / 27.0) * even[1],
        (2.0 / 27.0) * even[3],
    )
    square = (
        (2.0 / 27.0) * (rows[2][0] + rows[0][0]),
        (2.0 / 27.0) * even[2],
        (2.0 / 27.0) * even[5],
    )
    mixed = (
        (1.0 / 54.0) * (rows[2][1] - rows[0][1]),
        (1.0 / 54.0) * (rows[2][3] - rows[0][3]),
        (1.0 / 54.0) * even[4],
    )
    return zero, along, square, mixed


def collide(pull, velocity, solid, store):
    zero, along, square, mixed = moments_of(lambda cx, cy, cz: pull(number(cx, cy, cz)))
    ux, uy, uz = velocity
    xy, xz, yz = mixed
    quadratic = (
        ux * ux * square[0]
        + uy * uy * square[1]
        + uz * uz * square[2]
        + 2.0 * (ux * uy * xy + ux * uz * xz + uy * uz * yz)
    )
    speed = ux * ux + uy * uy + uz * uz
    scalar = OMEGA * (zero * (1.0 + 1.5 * speed) - 4.5 * quadratic)
    vec_x = OMEGA * (3.0 * along[0] + 9.0 * (square[0] * ux + xy * uy + xz * uz) - 3.0 * ux * zero)
    vec_y = OMEGA * (3.0 * along[1] + 9.0 * (xy * ux + square[1] * uy + yz * uz) - 3.0 * uy * zero)
    vec_z = OMEGA * (3.0 * along[2] + 9.0 * (xz * ux + yz * uy + square[2] * uz) - 3.0 * uz * zero)
    wall = solid == 1
    for cx in SIGNS:
        base = scalar if cx == 0 else (scalar + vec_x if cx > 0 else scalar - vec_x)
        for cy in SIGNS:
            inner = base if cy == 0 else (base + vec_y if cy > 0 else base - vec_y)
            for cz in SIGNS:
                full = inner if cz == 0 else (inner + vec_z if cz > 0 else inner - vec_z)
                i = number(cx, cy, cz)
                store(i, jnp.where(wall, pull(26 - i), (1.0 - OMEGA) * pull(i) + full))


def pull_plane(tile_of, edges_of, pulled, raw=None):
    lane = lanes()
    for cx in SIGNS:
        low_edge, high_edge, start = edges_of(cx)
        for cy in SIGNS:
            place = start + 3 * (cx + 1) + cy + 1
            for cz in SIGNS:
                i = number(cx, cy, cz)
                source = tile_of(i, cx)
                tile = source
                if cz == -1:
                    edge = pltpu.roll(low_edge, 128 - place, 1)
                    tile = jnp.where(lane == 0, edge, pltpu.roll(source, 1, 1))
                elif cz == 1:
                    edge = pltpu.roll(high_edge, 127 - place, 1)
                    tile = jnp.where(lane == 127, edge, pltpu.roll(source, 127, 1))
                if raw is not None and cx == 1:
                    tile = jnp.where(raw, source, tile)
                pulled[i] = shift_y(tile, cy)


def inner_kernel(step, last, adj, vel, solid, first, second, *rest):
    out, low_out, high_out, made, pulled, sems = rest
    extent_x = adj.shape[1]
    low_edge, high_edge = edges_from(first, second)

    def save(x):
        return pltpu.make_async_copy(made.at[x - 1], out.at[:, x], sems.at[x - 1])

    def plane(x, carry):
        here = pulled.at[lax.rem(x, 2)]
        pull_plane(
            lambda i, cx: adj[i, x + cx],
            lambda cx: (low_edge, high_edge, (x + 1 + cx) * 9),
            here,
        )

        def store(i, tile):
            made[x - 1, i] = tile

        velocity = [vel[a, x] for a in range(3)]
        collide(lambda i: here[i], velocity, solid[0, x], store)
        save(x).start()
        if last:
            return carry
        return pack_columns(lambda i: made[x - 1, i], x, *carry)

    zero = jnp.zeros((16, 128), jnp.float32)
    low_out[...], high_out[...] = lax.fori_loop(1, extent_x - 1, plane, (zero, zero), unroll=2)
    lax.fori_loop(1, extent_x - 1, lambda x, c: (save(x).wait(), c)[1], 0)


def outer_kernel(last, step, adj, vel, solid, first, second, near, two, far, cross, *rest):
    *rest, made, pulled, sems = rest
    low_in, high_in, _, out, *messages = rest
    extent_x = adj.shape[1]
    edges = edges_from(first, second)
    even = is_even("gx")
    interface = lax.axis_index("gx") == lax.axis_size("gx") - 1

    two, far = (far, two) if last else (two, far)
    bottom = lax.axis_index("gx") == 0
    inside = lax.axis_index("gx") < lax.axis_size("gx") - 2

    def one(j):
        return jnp.where(inside, near[j], far[j])

    def below(j):
        return jnp.where(bottom, 0.0, jnp.where(even, two[j], one(j)))

    def above(j):
        tile = jnp.where(even, one(j), two[j])
        return jnp.where(interface, cross[j], tile) if j < 9 else tile

    def plane(n, x, ghost, beyond, raw):
        pull_plane(
            lambda i, cx: beyond(i % 9) if cx == ghost else adj[i, x + cx],
            lambda cx: (
                (beyond(9), pltpu.roll(beyond(9), 64, 1), 0)
                if cx == ghost
                else (*edges, (x + 1 + cx) * 9)
            ),
            pulled.at[n],
            raw,
        )

        def store(i, tile):
            made[n, i] = tile

        velocity = [vel[a, x] for a in range(3)]
        collide(lambda i: pulled[n, i], velocity, solid[0, x], store)
        save = pltpu.make_async_copy(made.at[n], out.at[:, x], sems.at[n])
        save.start()
        return save

    final = extent_x - 1
    saves = [plane(0, 0, -1, below, None), plane(1, final, 1, above, interface)]
    if messages:
        low, high = low_in[...], high_in[...]
        low, high = pack_columns(lambda i: made[0, i], 0, low, high)
        low, high = pack_columns(lambda i: made[1, i], final, low, high)
        write_messages(lambda j: made[1, j], low, high, *messages)
    for save in saves:
        save.wait()


def tile_shape(*lead):
    return jax.ShapeDtypeStruct(lead + (16, 128), jnp.float32)


def in_vmem(n):
    return [pl.BlockSpec(memory_space=pltpu.VMEM)] * n


def in_any(n):
    return [pl.BlockSpec(memory_space=pl.ANY)] * n


def body(sizes, adjoint, saved, solid, band_device, band_cell, band_weight):
    zones, widths, count = sizes
    field = adjoint[0]
    extent_x = field.shape[1]
    axes = ("zone", "gx", "yz")
    params = pltpu.CompilerParams(vmem_limit_bytes=VMEM_LIMIT)

    def send(values, target):
        flat = lambda zone, gx, yz: (zone * widths + gx) * count + yz
        places = itertools.product(range(zones), range(widths), range(count))
        return lax.ppermute(values, axes, [(flat(*here), flat(*target(*here))) for here in places])

    def partner_of(place, shift):
        return place + 1 if (place + shift) % 2 == 0 else place - 1

    def flip(zone, gx, yz):
        return (1 - zone, gx, yz)

    def along_z(shift):
        def target(zone, gx, yz):
            to = partner_of(yz, shift)
            return (zone, gx, to) if 0 <= to < count else flip(zone, gx, yz)

        return target

    def hop_z(hop):
        def target(zone, gx, yz):
            if gx == widths - 1:
                return (zone, gx, (yz + hop) % count)
            return flip(zone, gx, yz)

        return target

    def ends_z(zone, gx, yz):
        if gx == widths - 1 and yz in (0, count - 1):
            return (zone, gx, count - 1 - yz)
        return flip(zone, gx, yz)

    def along_x(shift, taken):
        def target(zone, gx, yz):
            to = partner_of(gx, shift)
            return (zone, to, yz) if 0 <= to < widths and taken(gx) else flip(zone, gx, yz)

        return target

    info = pl.pallas_call(
        info_kernel,
        out_shape=tile_shape(4),
        in_specs=in_vmem(3),
        out_specs=in_vmem(1)[0],
        compiler_params=params,
    )(*[jnp.swapaxes(array[0], 1, 2) for array in (band_device, band_cell, band_weight)])
    messages = (tile_shape(9), tile_shape(10), tile_shape(10))
    field, own, first, second = pl.pallas_call(
        pack_kernel,
        out_shape=(tile_shape(27, extent_x), *messages),
        in_specs=[pl.BlockSpec(memory_space=pltpu.HBM)],
        out_specs=tuple(in_vmem(4)),
        scratch_shapes=[pltpu.SemaphoreType.DMA((extent_x,))],
        compiler_params=params,
    )(pltpu.with_memory_space_constraint(field, pltpu.HBM))
    saved = pltpu.with_memory_space_constraint(saved, pltpu.HBM)
    info = send(info, flip)
    for step in (1, 0):
        last = step == 0
        swap = last
        first = send(first, along_z(1))
        second = send(second, along_z(0))
        others = [send(own, target) for target in (*map(hop_z, range(2, count - 1)), ends_z)]
        carried = () if last else (pltpu.with_memory_space_constraint(solid, pltpu.HBM),)
        *copied, vel = pl.pallas_call(
            lambda *refs: velocity_kernel(step, *refs),
            out_shape=(
                *(jax.ShapeDtypeStruct(array.shape, array.dtype) for array in carried),
                tile_shape(3, extent_x),
            ),
            in_specs=[pl.BlockSpec(memory_space=pltpu.HBM)] * (1 + len(carried)),
            out_specs=tuple(in_vmem(1 + len(carried))),
            scratch_shapes=[
                pltpu.VMEM((extent_x, 27, 16, 128), jnp.float32),
                pltpu.SemaphoreType.DMA((extent_x + 1,)),
            ],
            compiler_params=params,
        )(saved, *carried)
        solid = copied[0] if copied else solid
        near, two, far = pl.pallas_call(
            side_kernel,
            out_shape=(tile_shape(10),) * 3,
            in_specs=in_vmem(3) + in_any(2),
            out_specs=tuple(in_vmem(3)),
            compiler_params=params,
        )(field, first, second, vel, info)
        near = send(near, along_x(0, lambda gx: gx < widths - 2))
        two = send(two, along_x(1, lambda gx: True))
        far = send(far, along_x(0, lambda gx: gx >= widths - 2))

        def make_planes(kernel, planes, given, new, extra):
            pair = (second, first) if swap else (first, second)
            operands = (field, vel, solid, *pair, *given)

            def run(adj, vel, solid, *refs):
                kernel(step, adj, vel, solid, *(refs[1::-1] if swap else refs[:2]), *refs[2:])

            return pl.pallas_call(
                run,
                out_shape=(tile_shape(27, extent_x), *extra),
                in_specs=in_vmem(len(operands)) + in_any(len(new)),
                out_specs=tuple(in_any(1) + in_vmem(len(extra))),
                scratch_shapes=[
                    pltpu.VMEM((planes, 27, 16, 128), jnp.float32),
                    pltpu.VMEM((2, 27, 16, 128), jnp.float32),
                    pltpu.SemaphoreType.DMA((planes,)),
                ],
                input_output_aliases={len(operands): 0} if new else {},
                compiler_params=params,
            )(*operands, *new)

        kernel = lambda step, *refs: inner_kernel(step, last, *refs)
        new, *columns = make_planes(kernel, extent_x - 2, (), (), (tile_shape(),) * 2)
        cross = pl.pallas_call(
            lambda *refs: cross_kernel(count, *refs),
            out_shape=tile_shape(9),
            in_specs=in_vmem(count + 2) + in_any(1),
            out_specs=in_vmem(1)[0],
            compiler_params=params,
        )(own, first, second, *others, info, columns[0])
        cross = send(cross, flip)
        ghosts = (near, far, two) if last else (near, two, far)
        field, *results = make_planes(
            lambda *refs: outer_kernel(last, *refs), 2, (*ghosts, cross, *columns), (new,), () if last else messages
        )
        if not last:
            own, first, second = results
    return field[None]


def solution(mesh):
    sizes = tuple(mesh.shape[axis] for axis in ("zone", "gx", "yz"))
    in_specs = (
        P("zone", None, "gx", None, "yz"),
        P(None, "zone", None, "gx", None, "yz"),
        P("zone", "gx", None, "yz"),
        P("zone", None, "yz", None),
        P("zone", None, "yz", None),
        P("zone", None, "yz", None),
    )
    out_specs = P("zone", None, "gx", None, "yz")
    return jax.shard_map(
        lambda *args: body(sizes, *args),
        mesh=mesh,
        in_specs=in_specs,
        out_specs=out_specs,
        check_vma=False,
    )
```

```python
import itertools

import jax
import jax.numpy as jnp
import numpy as np
from jax import lax
from jax.experimental import pallas as pl
from jax.experimental.pallas import tpu as pltpu
from jax.sharding import PartitionSpec as P

OMEGA = 1.6
VMEM_LIMIT = 20 * 1024 * 1024
SIGNS = (-1, 0, 1)


def number(cx, cy, cz):
    return 9 * (cx + 1) + 3 * (cy + 1) + (cz + 1)


def lanes():
    return lax.broadcasted_iota(jnp.int32, (16, 128), 1)


def shift_y(tile, cy):
    if cy == 0:
        return tile
    row = lax.broadcasted_iota(jnp.int32, tile.shape, 0)
    if cy == 1:
        return jnp.where(row == 15, 0.0, pltpu.roll(tile, 15, 0))
    return jnp.where(row == 0, 0.0, pltpu.roll(tile, 1, 0))


def pack_columns(planes, x, low, high):
    lane = lanes()
    for slot in range(9):
        place = (x + 1) * 9 + slot
        here = lane == place
        low = jnp.where(here, pltpu.roll(planes(3 * slot + 2), place, 1), low)
        high = jnp.where(here, pltpu.roll(planes(3 * slot), place + 1, 1), high)
    return low, high


def is_even(axis):
    return lax.rem(lax.axis_index(axis), 2) == 0


def write_messages(top, low, high, own, first, second):
    even = is_even("yz")
    for j in range(9):
        tile = top(j)
        own[j] = tile
        first[j] = tile
        second[j] = tile
    first[9] = jnp.where(even, low, high)
    second[9] = jnp.where(even, high, low)


def edges_from(first, second):
    even = is_even("yz")
    me, count = lax.axis_index("yz"), lax.axis_size("yz")
    low = jnp.where(me == 0, 0.0, jnp.where(even, first[9], second[9]))
    high = jnp.where(me == count - 1, 0.0, jnp.where(even, second[9], first[9]))
    return low, high


def pack_kernel(adj, field_out, own_out, first_out, second_out, sems):
    extent_x = adj.shape[1]
    copies = [
        pltpu.make_async_copy(adj.at[:, x], field_out.at[:, x], sems.at[x]) for x in range(extent_x)
    ]
    for copy in copies:
        copy.start()
    edges = jnp.zeros((16, 128), jnp.float32), jnp.zeros((16, 128), jnp.float32)
    for x in range(extent_x):
        copies[x].wait()
        edges = pack_columns(lambda i: field_out[i, x], x, *edges)
    write_messages(
        lambda j: field_out[j, extent_x - 1], *edges, own_out, first_out, second_out
    )


def info_kernel(device, cell, weight, out):
    for k in range(2):
        out[k] = (device[:, k] * 128 + cell[:, k]).astype(jnp.float32)
        out[2 + k] = weight[:, k]


def velocity_kernel(step, saved, *rest):
    *carried, out, kept, sems = rest
    extent_x = out.shape[1]
    copies = []
    if carried:
        copies.append(pltpu.make_async_copy(carried[0], carried[1], sems.at[extent_x]))
        copies[0].start()

    def load(x):
        return pltpu.make_async_copy(saved.at[step, 0, :, x], kept.at[x], sems.at[x])

    lax.fori_loop(0, extent_x, lambda x, c: (load(x).start(), c)[1], 0)

    def one(x, carry):
        load(x).wait()
        for a, tile in enumerate(velocity_of(lambda i: kept[x, i])):
            out[a, x] = tile
        return carry

    lax.fori_loop(0, extent_x, one, 0)
    for copy in copies:
        copy.wait()


def side_kernel(adj, first, second, *rest):
    *_, near_out, two_out, far_out = rest
    extent_x = adj.shape[1]
    even = is_even("gx")
    for j in range(9):
        top, bottom = adj[j, extent_x - 1], adj[18 + j, 0]
        near_out[j] = far_out[j] = jnp.where(even, top, bottom)
        two_out[j] = jnp.where(even, bottom, top)
    lane = lanes()
    low, high = edges_from(first, second)
    top, bottom = [
        jnp.where(lane < 64, pltpu.roll(low, 128 - start, 1), pltpu.roll(high, 192 - start, 1))
        for start in (9 * extent_x, 9)
    ]
    near_out[9] = far_out[9] = jnp.where(even, top, bottom)
    two_out[9] = jnp.where(even, bottom, top)


def cross_kernel(count, *refs):
    own, first, second = refs[:3]
    *others, ends = refs[3 : 1 + count]
    info, _, out = refs[1 + count :]
    interface = lax.axis_index("gx") == lax.axis_size("gx") - 1

    @pl.when(interface)
    def _():
        me = lax.axis_index("yz")
        even = is_even("yz")
        at_end = (me == 0) | (me == count - 1)
        rows = (0, 8)
        spots, picks = {}, {}
        for r in rows:
            for k in range(2):
                code = info[k, r : r + 8].astype(jnp.int32)
                ahead = lax.rem(code // 128 - me + count, count)
                spots[r, k] = lax.rem(code, 128)
                turned = jnp.where(even, lax.rem(count - ahead, count), ahead)
                masks = [turned == 1, turned == count - 1]
                masks += [ahead == count - hop for hop in range(2, count - 1)]
                picks[r, k] = masks
        for j in range(9):
            halves = []
            for r in rows:
                total = jnp.zeros((8, 128), jnp.float32)
                for k in range(2):
                    tiles = [ref[j, r : r + 8] for ref in (own, first, second, *others)]
                    tiles[1] = jnp.where(at_end, ends[j, r : r + 8], tiles[1])
                    got = [jnp.take_along_axis(tile, spots[r, k], axis=1) for tile in tiles]
                    picked = got[0]
                    for mask, value in zip(picks[r, k], got[1:]):
                        picked = jnp.where(mask, value, picked)
                    total = total + picked * info[2 + k, r : r + 8]
                halves.append(total)
            out[j] = jnp.concatenate(halves, axis=0)


def velocity_of(saved):
    totals, along_y, along_z = [], [], []
    for cx in SIGNS:
        sums, diffs = [], []
        for cy in SIGNS:
            lo, mid, hi = [saved(number(cx, cy, cz)) for cz in SIGNS]
            sums.append(lo + mid + hi)
            diffs.append(hi - lo)
        totals.append(sums[0] + sums[1] + sums[2])
        along_y.append(sums[2] - sums[0])
        along_z.append(diffs[0] + diffs[1] + diffs[2])
    density = totals[0] + totals[1] + totals[2]
    momentum = (
        totals[2] - totals[0],
        along_y[0] + along_y[1] + along_y[2],
        along_z[0] + along_z[1] + along_z[2],
    )
    return [part / density for part in momentum]


def moments_of(pull):
    rows = []
    for cx in SIGNS:
        plain, first, second = [], [], []
        for cy in SIGNS:
            lo, mid, hi = [pull(cx, cy, cz) for cz in SIGNS]
            both = lo + hi
            plain.append(mid + 0.25 * both)
            first.append(hi - lo)
            second.append(both)
        pair = plain[0] + plain[2]
        rows.append(
            (
                plain[1] + 0.25 * pair,
                plain[2] - plain[0],
                pair,
                first[1] + 0.25 * (first[0] + first[2]),
                first[2] - first[0],
                second[1] + 0.25 * (second[0] + second[2]),
            )
        )
    even = [rows[1][n] + 0.25 * (rows[0][n] + rows[2][n]) for n in range(6)]
    zero = (8.0 / 27.0) * even[0]
    along = (
        (2.0 / 27.0) * (rows[2][0] - rows[0][0]),
        (2.0 / 27.0) * even[1],
        (2.0 / 27.0) * even[3],
    )
    square = (
        (2.0 / 27.0) * (rows[2][0] + rows[0][0]),
        (2.0 / 27.0) * even[2],
        (2.0 / 27.0) * even[5],
    )
    mixed = (
        (1.0 / 54.0) * (rows[2][1] - rows[0][1]),
        (1.0 / 54.0) * (rows[2][3] - rows[0][3]),
        (1.0 / 54.0) * even[4],
    )
    return zero, along, square, mixed


def collide(pull, velocity, solid, store):
    zero, along, square, mixed = moments_of(lambda cx, cy, cz: pull(number(cx, cy, cz)))
    ux, uy, uz = velocity
    xy, xz, yz = mixed
    quadratic = (
        ux * ux * square[0]
        + uy * uy * square[1]
        + uz * uz * square[2]
        + 2.0 * (ux * uy * xy + ux * uz * xz + uy * uz * yz)
    )
    speed = ux * ux + uy * uy + uz * uz
    scalar = OMEGA * (zero * (1.0 + 1.5 * speed) - 4.5 * quadratic)
    vec_x = OMEGA * (3.0 * along[0] + 9.0 * (square[0] * ux + xy * uy + xz * uz) - 3.0 * ux * zero)
    vec_y = OMEGA * (3.0 * along[1] + 9.0 * (xy * ux + square[1] * uy + yz * uz) - 3.0 * uy * zero)
    vec_z = OMEGA * (3.0 * along[2] + 9.0 * (xz * ux + yz * uy + square[2] * uz) - 3.0 * uz * zero)
    wall = solid == 1
    for cx in SIGNS:
        base = scalar if cx == 0 else (scalar + vec_x if cx > 0 else scalar - vec_x)
        for cy in SIGNS:
            inner = base if cy == 0 else (base + vec_y if cy > 0 else base - vec_y)
            for cz in SIGNS:
                full = inner if cz == 0 else (inner + vec_z if cz > 0 else inner - vec_z)
                i = number(cx, cy, cz)
                store(i, jnp.where(wall, pull(26 - i), (1.0 - OMEGA) * pull(i) + full))


def pull_plane(tile_of, edges_of, pulled, raw=None):
    lane = lanes()
    for cx in SIGNS:
        low_edge, high_edge, start = edges_of(cx)
        for cy in SIGNS:
            place = start + 3 * (cx + 1) + cy + 1
            for cz in SIGNS:
                i = number(cx, cy, cz)
                source = tile_of(i, cx)
                tile = source
                if cz == -1:
                    edge = pltpu.roll(low_edge, 128 - place, 1)
                    tile = jnp.where(lane == 0, edge, pltpu.roll(source, 1, 1))
                elif cz == 1:
                    edge = pltpu.roll(high_edge, 127 - place, 1)
                    tile = jnp.where(lane == 127, edge, pltpu.roll(source, 127, 1))
                if raw is not None and cx == 1:
                    tile = jnp.where(raw, source, tile)
                pulled[i] = shift_y(tile, cy)


def inner_kernel(step, last, adj, vel, solid, first, second, *rest):
    out, low_out, high_out, made, pulled, sems = rest
    extent_x = adj.shape[1]
    low_edge, high_edge = edges_from(first, second)

    def save(x):
        return pltpu.make_async_copy(made.at[x - 1], out.at[:, x], sems.at[x - 1])

    def plane(x, carry):
        here = pulled.at[lax.rem(x, 2)]
        pull_plane(
            lambda i, cx: adj[i, x + cx],
            lambda cx: (low_edge, high_edge, (x + 1 + cx) * 9),
            here,
        )

        def store(i, tile):
            made[x - 1, i] = tile

        velocity = [vel[a, x] for a in range(3)]
        collide(lambda i: here[i], velocity, solid[0, x], store)
        save(x).start()
        if last:
            return carry
        return pack_columns(lambda i: made[x - 1, i], x, *carry)

    zero = jnp.zeros((16, 128), jnp.float32)
    low_out[...], high_out[...] = lax.fori_loop(1, extent_x - 1, plane, (zero, zero), unroll=2)
    lax.fori_loop(1, extent_x - 1, lambda x, c: (save(x).wait(), c)[1], 0)


def outer_kernel(step, adj, vel, solid, first, second, near, two, far, cross, *rest):
    *rest, made, pulled, sems = rest
    low_in, high_in, _, out, *messages = rest
    extent_x = adj.shape[1]
    edges = edges_from(first, second)
    even = is_even("gx")
    interface = lax.axis_index("gx") == lax.axis_size("gx") - 1

    bottom = lax.axis_index("gx") == 0
    inside = lax.axis_index("gx") < lax.axis_size("gx") - 2

    def one(j):
        return jnp.where(inside, near[j], far[j])

    def below(j):
        return jnp.where(bottom, 0.0, jnp.where(even, two[j], one(j)))

    def above(j):
        tile = jnp.where(even, one(j), two[j])
        return jnp.where(interface, cross[j], tile) if j < 9 else tile

    def plane(n, x, ghost, beyond, raw):
        pull_plane(
            lambda i, cx: beyond(i % 9) if cx == ghost else adj[i, x + cx],
            lambda cx: (
                (beyond(9), pltpu.roll(beyond(9), 64, 1), 0)
                if cx == ghost
                else (*edges, (x + 1 + cx) * 9)
            ),
            pulled.at[n],
            raw,
        )

        def store(i, tile):
            made[n, i] = tile

        velocity = [vel[a, x] for a in range(3)]
        collide(lambda i: pulled[n, i], velocity, solid[0, x], store)
        save = pltpu.make_async_copy(made.at[n], out.at[:, x], sems.at[n])
        save.start()
        return save

    final = extent_x - 1
    saves = [plane(0, 0, -1, below, None), plane(1, final, 1, above, interface)]
    if messages:
        low, high = low_in[...], high_in[...]
        low, high = pack_columns(lambda i: made[0, i], 0, low, high)
        low, high = pack_columns(lambda i: made[1, i], final, low, high)
        write_messages(lambda j: made[1, j], low, high, *messages)
    for save in saves:
        save.wait()


def tile_shape(*lead):
    return jax.ShapeDtypeStruct(lead + (16, 128), jnp.float32)


def in_vmem(n):
    return [pl.BlockSpec(memory_space=pltpu.VMEM)] * n


def in_any(n):
    return [pl.BlockSpec(memory_space=pl.ANY)] * n


def body(sizes, adjoint, saved, solid, band_device, band_cell, band_weight):
    zones, widths, count = sizes
    field = adjoint[0]
    extent_x = field.shape[1]
    axes = ("zone", "gx", "yz")
    params = pltpu.CompilerParams(vmem_limit_bytes=VMEM_LIMIT)

    def send(values, target):
        flat = lambda zone, gx, yz: (zone * widths + gx) * count + yz
        places = itertools.product(range(zones), range(widths), range(count))
        return lax.ppermute(values, axes, [(flat(*here), flat(*target(*here))) for here in places])

    def partner_of(place, shift):
        return place + 1 if (place + shift) % 2 == 0 else place - 1

    def stay(zone, gx, yz):
        return (zone, gx, yz)

    def flip(zone, gx, yz):
        return (1 - zone, gx, yz) if gx == widths - 1 else (zone, gx, yz)

    def along_z(shift):
        def target(zone, gx, yz):
            to = partner_of(yz, shift)
            return (zone, gx, to) if 0 <= to < count else stay(zone, gx, yz)

        return target

    def hop_z(hop):
        def target(zone, gx, yz):
            if gx == widths - 1:
                return (zone, gx, (yz + hop) % count)
            return stay(zone, gx, yz)

        return target

    def ends_z(zone, gx, yz):
        if gx == widths - 1 and yz in (0, count - 1):
            return (zone, gx, count - 1 - yz)
        return stay(zone, gx, yz)

    def along_x(shift, taken):
        def target(zone, gx, yz):
            to = partner_of(gx, shift)
            return (zone, to, yz) if 0 <= to < widths and taken(gx) else stay(zone, gx, yz)

        return target

    info = pl.pallas_call(
        info_kernel,
        out_shape=tile_shape(4),
        in_specs=in_vmem(3),
        out_specs=in_vmem(1)[0],
        compiler_params=params,
    )(*[jnp.swapaxes(array[0], 1, 2) for array in (band_device, band_cell, band_weight)])
    messages = (tile_shape(9), tile_shape(10), tile_shape(10))
    field, own, first, second = pl.pallas_call(
        pack_kernel,
        out_shape=(tile_shape(27, extent_x), *messages),
        in_specs=[pl.BlockSpec(memory_space=pltpu.HBM)],
        out_specs=tuple(in_vmem(4)),
        scratch_shapes=[pltpu.SemaphoreType.DMA((extent_x,))],
        compiler_params=params,
    )(pltpu.with_memory_space_constraint(field, pltpu.HBM))
    saved = pltpu.with_memory_space_constraint(saved, pltpu.HBM)
    info = send(info, flip)
    for step in (1, 0):
        last = step == 0
        swap = last
        first = send(first, along_z(1))
        second = send(second, along_z(0))
        others = [send(own, target) for target in (*map(hop_z, range(2, count - 1)), ends_z)]
        carried = () if last else (pltpu.with_memory_space_constraint(solid, pltpu.HBM),)
        *copied, vel = pl.pallas_call(
            lambda *refs: velocity_kernel(step, *refs),
            out_shape=(
                *(jax.ShapeDtypeStruct(array.shape, array.dtype) for array in carried),
                tile_shape(3, extent_x),
            ),
            in_specs=[pl.BlockSpec(memory_space=pltpu.HBM)] * (1 + len(carried)),
            out_specs=tuple(in_vmem(1 + len(carried))),
            scratch_shapes=[
                pltpu.VMEM((extent_x, 27, 16, 128), jnp.float32),
                pltpu.SemaphoreType.DMA((extent_x + 1,)),
            ],
            compiler_params=params,
        )(saved, *carried)
        solid = copied[0] if copied else solid
        near, two, far = pl.pallas_call(
            side_kernel,
            out_shape=(tile_shape(10),) * 3,
            in_specs=in_vmem(3) + in_any(2),
            out_specs=tuple(in_vmem(3)),
            compiler_params=params,
        )(field, first, second, vel, info)
        near = send(near, along_x(0, lambda gx: gx < widths - 2))
        two = send(two, along_x(1, lambda gx: True))
        far = send(far, along_x(0, lambda gx: gx >= widths - 2))

        def make_planes(kernel, planes, given, new, extra):
            pair = (second, first) if swap else (first, second)
            operands = (field, vel, solid, *pair, *given)

            def run(adj, vel, solid, *refs):
                kernel(step, adj, vel, solid, *(refs[1::-1] if swap else refs[:2]), *refs[2:])

            return pl.pallas_call(
                run,
                out_shape=(tile_shape(27, extent_x), *extra),
                in_specs=in_vmem(len(operands)) + in_any(len(new)),
                out_specs=tuple(in_any(1) + in_vmem(len(extra))),
                scratch_shapes=[
                    pltpu.VMEM((planes, 27, 16, 128), jnp.float32),
                    pltpu.VMEM((2, 27, 16, 128), jnp.float32),
                    pltpu.SemaphoreType.DMA((planes,)),
                ],
                input_output_aliases={len(operands): 0} if new else {},
                compiler_params=params,
            )(*operands, *new)

        kernel = lambda step, *refs: inner_kernel(step, last, *refs)
        new, *columns = make_planes(kernel, extent_x - 2, (), (), (tile_shape(),) * 2)
        cross = pl.pallas_call(
            lambda *refs: cross_kernel(count, *refs),
            out_shape=tile_shape(9),
            in_specs=in_vmem(count + 2) + in_any(1),
            out_specs=in_vmem(1)[0],
            compiler_params=params,
        )(own, first, second, *others, info, columns[0])
        cross = send(cross, flip)
        ghosts = (near, two, far)
        field, *results = make_planes(
            outer_kernel, 2, (*ghosts, cross, *columns), (new,), () if last else messages
        )
        if not last:
            own, first, second = results
    return field[None]


def solution(mesh):
    sizes = tuple(mesh.shape[axis] for axis in ("zone", "gx", "yz"))
    in_specs = (
        P("zone", None, "gx", None, "yz"),
        P(None, "zone", None, "gx", None, "yz"),
        P("zone", "gx", None, "yz"),
        P("zone", None, "yz", None),
        P("zone", None, "yz", None),
        P("zone", None, "yz", None),
    )
    out_specs = P("zone", None, "gx", None, "yz")
    return jax.shard_map(
        lambda *args: body(sizes, *args),
        mesh=mesh,
        in_specs=in_specs,
        out_specs=out_specs,
        check_vma=False,
    )
```

```python
import itertools

import jax
import jax.numpy as jnp
import numpy as np
from jax import lax
from jax.experimental import pallas as pl
from jax.experimental.pallas import tpu as pltpu
from jax.sharding import PartitionSpec as P

OMEGA = 1.6
VMEM_LIMIT = 20 * 1024 * 1024
SIGNS = (-1, 0, 1)


def number(cx, cy, cz):
    return 9 * (cx + 1) + 3 * (cy + 1) + (cz + 1)


def lanes():
    return lax.broadcasted_iota(jnp.int32, (16, 128), 1)


def shift_y(tile, cy):
    if cy == 0:
        return tile
    row = lax.broadcasted_iota(jnp.int32, tile.shape, 0)
    if cy == 1:
        return jnp.where(row == 15, 0.0, pltpu.roll(tile, 15, 0))
    return jnp.where(row == 0, 0.0, pltpu.roll(tile, 1, 0))


def pack_columns(planes, x, low, high):
    lane = lanes()
    for slot in range(9):
        place = (x + 1) * 9 + slot
        here = lane == place
        low = jnp.where(here, pltpu.roll(planes(3 * slot + 2), place, 1), low)
        high = jnp.where(here, pltpu.roll(planes(3 * slot), place + 1, 1), high)
    return low, high


def is_even(axis):
    return lax.rem(lax.axis_index(axis), 2) == 0


def write_messages(top, low, high, own, first, second):
    even = is_even("yz")
    for j in range(9):
        tile = top(j)
        own[j] = tile
        first[j] = tile
        second[j] = tile
    first[9] = jnp.where(even, low, high)
    second[9] = jnp.where(even, high, low)


def edges_from(first, second):
    even = is_even("yz")
    me, count = lax.axis_index("yz"), lax.axis_size("yz")
    low = jnp.where(me == 0, 0.0, jnp.where(even, first[9], second[9]))
    high = jnp.where(me == count - 1, 0.0, jnp.where(even, second[9], first[9]))
    return low, high


def pack_kernel(adj, field_out, own_out, first_out, second_out, sems):
    extent_x = adj.shape[1]
    copies = [
        pltpu.make_async_copy(adj.at[:, x], field_out.at[:, x], sems.at[x]) for x in range(extent_x)
    ]
    for copy in copies:
        copy.start()
    edges = jnp.zeros((16, 128), jnp.float32), jnp.zeros((16, 128), jnp.float32)
    for x in range(extent_x):
        copies[x].wait()
        edges = pack_columns(lambda i: field_out[i, x], x, *edges)
    write_messages(
        lambda j: field_out[j, extent_x - 1], *edges, own_out, first_out, second_out
    )


def info_kernel(device, cell, weight, out):
    for k in range(2):
        out[k] = (device[:, k] * 128 + cell[:, k]).astype(jnp.float32)
        out[2 + k] = weight[:, k]


def velocity_kernel(step, saved, *rest):
    *carried, out, kept, sems = rest
    extent_x = out.shape[1]
    copies = []
    if carried:
        copies.append(pltpu.make_async_copy(carried[0], carried[1], sems.at[extent_x]))
        copies[0].start()

    def load(x):
        return pltpu.make_async_copy(saved.at[step, 0, :, x], kept.at[x], sems.at[x])

    lax.fori_loop(0, extent_x, lambda x, c: (load(x).start(), c)[1], 0)

    def one(x, carry):
        load(x).wait()
        for a, tile in enumerate(velocity_of(lambda i: kept[x, i])):
            out[a, x] = tile
        return carry

    lax.fori_loop(0, extent_x, one, 0)
    for copy in copies:
        copy.wait()


def side_kernel(adj, first, second, *rest):
    *_, near_out, two_out, far_out = rest
    extent_x = adj.shape[1]
    even = is_even("gx")
    for j in range(9):
        top, bottom = adj[j, extent_x - 1], adj[18 + j, 0]
        near_out[j] = far_out[j] = jnp.where(even, top, bottom)
        two_out[j] = jnp.where(even, bottom, top)
    lane = lanes()
    low, high = edges_from(first, second)
    top, bottom = [
        jnp.where(lane < 64, pltpu.roll(low, 128 - start, 1), pltpu.roll(high, 192 - start, 1))
        for start in (9 * extent_x, 9)
    ]
    near_out[9] = far_out[9] = jnp.where(even, top, bottom)
    two_out[9] = jnp.where(even, bottom, top)


def cross_kernel(count, *refs):
    own, first, second = refs[:3]
    *others, ends = refs[3 : 1 + count]
    info, _, out = refs[1 + count :]
    interface = lax.axis_index("gx") == lax.axis_size("gx") - 1

    @pl.when(interface)
    def _():
        me = lax.axis_index("yz")
        even = is_even("yz")
        at_end = (me == 0) | (me == count - 1)
        rows = (0, 8)
        spots, picks = {}, {}
        for r in rows:
            for k in range(2):
                code = info[k, r : r + 8].astype(jnp.int32)
                ahead = lax.rem(code // 128 - me + count, count)
                spots[r, k] = lax.rem(code, 128)
                turned = jnp.where(even, lax.rem(count - ahead, count), ahead)
                masks = [turned == 1, turned == count - 1]
                masks += [ahead == count - hop for hop in range(2, count - 1)]
                picks[r, k] = masks
        for j in range(9):
            halves = []
            for r in rows:
                total = jnp.zeros((8, 128), jnp.float32)
                for k in range(2):
                    tiles = [ref[j, r : r + 8] for ref in (own, first, second, *others)]
                    tiles[1] = jnp.where(at_end, ends[j, r : r + 8], tiles[1])
                    got = [jnp.take_along_axis(tile, spots[r, k], axis=1) for tile in tiles]
                    picked = got[0]
                    for mask, value in zip(picks[r, k], got[1:]):
                        picked = jnp.where(mask, value, picked)
                    total = total + picked * info[2 + k, r : r + 8]
                halves.append(total)
            out[j] = jnp.concatenate(halves, axis=0)


def velocity_of(saved):
    totals, along_y, along_z = [], [], []
    for cx in SIGNS:
        sums, diffs = [], []
        for cy in SIGNS:
            lo, mid, hi = [saved(number(cx, cy, cz)) for cz in SIGNS]
            sums.append(lo + mid + hi)
            diffs.append(hi - lo)
        totals.append(sums[0] + sums[1] + sums[2])
        along_y.append(sums[2] - sums[0])
        along_z.append(diffs[0] + diffs[1] + diffs[2])
    density = totals[0] + totals[1] + totals[2]
    momentum = (
        totals[2] - totals[0],
        along_y[0] + along_y[1] + along_y[2],
        along_z[0] + along_z[1] + along_z[2],
    )
    return [part / density for part in momentum]


def moments_of(pull):
    rows = []
    for cx in SIGNS:
        plain, first, second = [], [], []
        for cy in SIGNS:
            lo, mid, hi = [pull(cx, cy, cz) for cz in SIGNS]
            both = lo + hi
            plain.append(mid + 0.25 * both)
            first.append(hi - lo)
            second.append(both)
        pair = plain[0] + plain[2]
        rows.append(
            (
                plain[1] + 0.25 * pair,
                plain[2] - plain[0],
                pair,
                first[1] + 0.25 * (first[0] + first[2]),
                first[2] - first[0],
                second[1] + 0.25 * (second[0] + second[2]),
            )
        )
    even = [rows[1][n] + 0.25 * (rows[0][n] + rows[2][n]) for n in range(6)]
    zero = (8.0 / 27.0) * even[0]
    along = (
        (2.0 / 27.0) * (rows[2][0] - rows[0][0]),
        (2.0 / 27.0) * even[1],
        (2.0 / 27.0) * even[3],
    )
    square = (
        (2.0 / 27.0) * (rows[2][0] + rows[0][0]),
        (2.0 / 27.0) * even[2],
        (2.0 / 27.0) * even[5],
    )
    mixed = (
        (1.0 / 54.0) * (rows[2][1] - rows[0][1]),
        (1.0 / 54.0) * (rows[2][3] - rows[0][3]),
        (1.0 / 54.0) * even[4],
    )
    return zero, along, square, mixed


def collide(pull, velocity, solid, store):
    zero, along, square, mixed = moments_of(lambda cx, cy, cz: pull(number(cx, cy, cz)))
    ux, uy, uz = velocity
    xy, xz, yz = mixed
    quadratic = (
        ux * ux * square[0]
        + uy * uy * square[1]
        + uz * uz * square[2]
        + 2.0 * (ux * uy * xy + ux * uz * xz + uy * uz * yz)
    )
    speed = ux * ux + uy * uy + uz * uz
    scalar = OMEGA * (zero * (1.0 + 1.5 * speed) - 4.5 * quadratic)
    vec_x = OMEGA * (3.0 * along[0] + 9.0 * (square[0] * ux + xy * uy + xz * uz) - 3.0 * ux * zero)
    vec_y = OMEGA * (3.0 * along[1] + 9.0 * (xy * ux + square[1] * uy + yz * uz) - 3.0 * uy * zero)
    vec_z = OMEGA * (3.0 * along[2] + 9.0 * (xz * ux + yz * uy + square[2] * uz) - 3.0 * uz * zero)
    wall = solid == 1
    for cx in SIGNS:
        base = scalar if cx == 0 else (scalar + vec_x if cx > 0 else scalar - vec_x)
        for cy in SIGNS:
            inner = base if cy == 0 else (base + vec_y if cy > 0 else base - vec_y)
            for cz in SIGNS:
                full = inner if cz == 0 else (inner + vec_z if cz > 0 else inner - vec_z)
                i = number(cx, cy, cz)
                store(i, jnp.where(wall, pull(26 - i), (1.0 - OMEGA) * pull(i) + full))


def pull_plane(tile_of, edges_of, pulled, raw=None):
    lane = lanes()
    for cx in SIGNS:
        low_edge, high_edge, start = edges_of(cx)
        for cy in SIGNS:
            place = start + 3 * (cx + 1) + cy + 1
            for cz in SIGNS:
                i = number(cx, cy, cz)
                source = tile_of(i, cx)
                tile = source
                if cz == -1:
                    edge = pltpu.roll(low_edge, 128 - place, 1)
                    tile = jnp.where(lane == 0, edge, pltpu.roll(source, 1, 1))
                elif cz == 1:
                    edge = pltpu.roll(high_edge, 127 - place, 1)
                    tile = jnp.where(lane == 127, edge, pltpu.roll(source, 127, 1))
                if raw is not None and cx == 1:
                    tile = jnp.where(raw, source, tile)
                pulled[i] = shift_y(tile, cy)


def inner_kernel(step, last, adj, vel, solid, first, second, *rest):
    out, low_out, high_out, made, pulled, sems = rest
    extent_x = adj.shape[1]
    low_edge, high_edge = edges_from(first, second)

    def save(x):
        return pltpu.make_async_copy(made.at[x - 1], out.at[:, x], sems.at[x - 1])

    def plane(x, carry):
        here = pulled.at[lax.rem(x, 2)]
        pull_plane(
            lambda i, cx: adj[i, x + cx],
            lambda cx: (low_edge, high_edge, (x + 1 + cx) * 9),
            here,
        )

        def store(i, tile):
            made[x - 1, i] = tile

        velocity = [vel[a, x] for a in range(3)]
        collide(lambda i: here[i], velocity, solid[0, x], store)
        save(x).start()
        if last:
            return carry
        return pack_columns(lambda i: made[x - 1, i], x, *carry)

    zero = jnp.zeros((16, 128), jnp.float32)
    low_out[...], high_out[...] = lax.fori_loop(1, extent_x - 1, plane, (zero, zero), unroll=2)
    lax.fori_loop(1, extent_x - 1, lambda x, c: (save(x).wait(), c)[1], 0)


def outer_kernel(step, adj, vel, solid, first, second, near, two, far, cross, *rest):
    *rest, made, pulled, sems = rest
    low_in, high_in, _, out, *messages = rest
    extent_x = adj.shape[1]
    edges = edges_from(first, second)
    even = is_even("gx")
    interface = lax.axis_index("gx") == lax.axis_size("gx") - 1

    bottom = lax.axis_index("gx") == 0
    inside = lax.axis_index("gx") < lax.axis_size("gx") - 2

    def one(j):
        return jnp.where(inside, near[j], far[j])

    def below(j):
        return jnp.where(bottom, 0.0, jnp.where(even, two[j], one(j)))

    def above(j):
        tile = jnp.where(even, one(j), two[j])
        return jnp.where(interface, cross[j], tile) if j < 9 else tile

    def plane(n, x, ghost, beyond, raw):
        pull_plane(
            lambda i, cx: beyond(i % 9) if cx == ghost else adj[i, x + cx],
            lambda cx: (
                (beyond(9), pltpu.roll(beyond(9), 64, 1), 0)
                if cx == ghost
                else (*edges, (x + 1 + cx) * 9)
            ),
            pulled.at[n],
            raw,
        )

        def store(i, tile):
            made[n, i] = tile

        velocity = [vel[a, x] for a in range(3)]
        collide(lambda i: pulled[n, i], velocity, solid[0, x], store)
        save = pltpu.make_async_copy(made.at[n], out.at[:, x], sems.at[n])
        save.start()
        return save

    final = extent_x - 1
    saves = [plane(0, 0, -1, below, None), plane(1, final, 1, above, interface)]
    if messages:
        low, high = low_in[...], high_in[...]
        low, high = pack_columns(lambda i: made[0, i], 0, low, high)
        low, high = pack_columns(lambda i: made[1, i], final, low, high)
        write_messages(lambda j: made[1, j], low, high, *messages)
    for save in saves:
        save.wait()


def tile_shape(*lead):
    return jax.ShapeDtypeStruct(lead + (16, 128), jnp.float32)


def in_vmem(n):
    return [pl.BlockSpec(memory_space=pltpu.VMEM)] * n


def in_any(n):
    return [pl.BlockSpec(memory_space=pl.ANY)] * n


def body(sizes, adjoint, saved, solid, band_device, band_cell, band_weight):
    zones, widths, count = sizes
    field = adjoint[0]
    extent_x = field.shape[1]
    axes = ("zone", "gx", "yz")
    params = pltpu.CompilerParams(vmem_limit_bytes=VMEM_LIMIT)

    def send(values, target):
        flat = lambda zone, gx, yz: (zone * widths + gx) * count + yz
        places = itertools.product(range(zones), range(widths), range(count))
        return lax.ppermute(values, axes, [(flat(*here), flat(*target(*here))) for here in places])

    def partner_of(place, shift):
        return place + 1 if (place + shift) % 2 == 0 else place - 1

    def flip(zone, gx, yz):
        return (1 - zone, gx, yz)

    def along_z(shift):
        def target(zone, gx, yz):
            to = partner_of(yz, shift)
            return (zone, gx, to) if 0 <= to < count else flip(zone, gx, yz)

        return target

    def hop_z(hop):
        def target(zone, gx, yz):
            if gx == widths - 1:
                return (zone, gx, (yz + hop) % count)
            return flip(zone, gx, yz)

        return target

    def ends_z(zone, gx, yz):
        if gx == widths - 1 and yz in (0, count - 1):
            return (zone, gx, count - 1 - yz)
        return flip(zone, gx, yz)

    def along_x(shift, taken):
        def target(zone, gx, yz):
            to = partner_of(gx, shift)
            return (zone, to, yz) if 0 <= to < widths and taken(gx) else flip(zone, gx, yz)

        return target

    info = pl.pallas_call(
        info_kernel,
        out_shape=tile_shape(4),
        in_specs=in_vmem(3),
        out_specs=in_vmem(1)[0],
        compiler_params=params,
    )(*[jnp.swapaxes(array[0], 1, 2) for array in (band_device, band_cell, band_weight)])
    messages = (tile_shape(9), tile_shape(10), tile_shape(10))
    field, own, first, second = pl.pallas_call(
        pack_kernel,
        out_shape=(tile_shape(27, extent_x), *messages),
        in_specs=[pl.BlockSpec(memory_space=pltpu.HBM)],
        out_specs=tuple(in_vmem(4)),
        scratch_shapes=[pltpu.SemaphoreType.DMA((extent_x,))],
        compiler_params=params,
    )(pltpu.with_memory_space_constraint(field, pltpu.HBM))
    saved = pltpu.with_memory_space_constraint(saved, pltpu.HBM)
    info = send(info, flip)
    for step in (1, 0):
        last = step == 0
        swap = last
        first = send(first, along_z(1))
        second = send(second, along_z(0))
        others = [send(own, target) for target in (*map(hop_z, range(2, count - 1)), ends_z)]
        carried = () if last else (pltpu.with_memory_space_constraint(solid, pltpu.HBM),)
        *copied, vel = pl.pallas_call(
            lambda *refs: velocity_kernel(step, *refs),
            out_shape=(
                *(jax.ShapeDtypeStruct(array.shape, array.dtype) for array in carried),
                tile_shape(3, extent_x),
            ),
            in_specs=[pl.BlockSpec(memory_space=pltpu.HBM)] * (1 + len(carried)),
            out_specs=tuple(in_vmem(1 + len(carried))),
            scratch_shapes=[
                pltpu.VMEM((extent_x, 27, 16, 128), jnp.float32),
                pltpu.SemaphoreType.DMA((extent_x + 1,)),
            ],
            compiler_params=params,
        )(saved, *carried)
        solid = copied[0] if copied else solid
        near, two, far = pl.pallas_call(
            side_kernel,
            out_shape=(tile_shape(10),) * 3,
            in_specs=in_vmem(3) + in_any(2),
            out_specs=tuple(in_vmem(3)),
            compiler_params=params,
        )(field, first, second, vel, info)
        near = send(near, along_x(0, lambda gx: gx < widths - 2))
        two = send(two, along_x(1, lambda gx: True))
        far = send(far, along_x(0, lambda gx: gx >= widths - 2))

        def make_planes(kernel, planes, given, new, extra):
            pair = (second, first) if swap else (first, second)
            operands = (field, vel, solid, *pair, *given)

            def run(adj, vel, solid, *refs):
                kernel(step, adj, vel, solid, *(refs[1::-1] if swap else refs[:2]), *refs[2:])

            return pl.pallas_call(
                run,
                out_shape=(tile_shape(27, extent_x), *extra),
                in_specs=in_vmem(len(operands)) + in_any(len(new)),
                out_specs=tuple(in_any(1) + in_vmem(len(extra))),
                scratch_shapes=[
                    pltpu.VMEM((planes, 27, 16, 128), jnp.float32),
                    pltpu.VMEM((2, 27, 16, 128), jnp.float32),
                    pltpu.SemaphoreType.DMA((planes,)),
                ],
                input_output_aliases={len(operands): 0} if new else {},
                compiler_params=params,
            )(*operands, *new)

        kernel = lambda step, *refs: inner_kernel(step, last, *refs)
        new, *columns = make_planes(kernel, extent_x - 2, (), (), (tile_shape(),) * 2)
        cross = pl.pallas_call(
            lambda *refs: cross_kernel(count, *refs),
            out_shape=tile_shape(9),
            in_specs=in_vmem(count + 2) + in_any(1),
            out_specs=in_vmem(1)[0],
            compiler_params=params,
        )(own, first, second, *others, info, vel if last else columns[0])
        cross = send(cross, flip)
        ghosts = (near, two, far)
        field, *results = make_planes(
            outer_kernel, 2, (*ghosts, cross, *columns), (new,), () if last else messages
        )
        if not last:
            own, first, second = results
    return field[None]


def solution(mesh):
    sizes = tuple(mesh.shape[axis] for axis in ("zone", "gx", "yz"))
    in_specs = (
        P("zone", None, "gx", None, "yz"),
        P(None, "zone", None, "gx", None, "yz"),
        P("zone", "gx", None, "yz"),
        P("zone", None, "yz", None),
        P("zone", None, "yz", None),
        P("zone", None, "yz", None),
    )
    out_specs = P("zone", None, "gx", None, "yz")
    return jax.shard_map(
        lambda *args: body(sizes, *args),
        mesh=mesh,
        in_specs=in_specs,
        out_specs=out_specs,
        check_vma=False,
    )
```

```python
import itertools

import jax
import jax.numpy as jnp
import numpy as np
from jax import lax
from jax.experimental import pallas as pl
from jax.experimental.pallas import tpu as pltpu
from jax.sharding import PartitionSpec as P

OMEGA = 1.6
VMEM_LIMIT = 20 * 1024 * 1024
SIGNS = (-1, 0, 1)


def number(cx, cy, cz):
    return 9 * (cx + 1) + 3 * (cy + 1) + (cz + 1)


def lanes():
    return lax.broadcasted_iota(jnp.int32, (16, 128), 1)


def shift_y(tile, cy):
    if cy == 0:
        return tile
    row = lax.broadcasted_iota(jnp.int32, tile.shape, 0)
    if cy == 1:
        return jnp.where(row == 15, 0.0, pltpu.roll(tile, 15, 0))
    return jnp.where(row == 0, 0.0, pltpu.roll(tile, 1, 0))


def pack_columns(planes, x, low, high):
    lane = lanes()
    for slot in range(9):
        place = (x + 1) * 9 + slot
        here = lane == place
        low = jnp.where(here, pltpu.roll(planes(3 * slot + 2), place, 1), low)
        high = jnp.where(here, pltpu.roll(planes(3 * slot), place + 1, 1), high)
    return low, high


def is_even(axis):
    return lax.rem(lax.axis_index(axis), 2) == 0


def write_messages(top, low, high, own, first, second):
    even = is_even("yz")
    for j in range(9):
        tile = top(j)
        own[j] = tile
        first[j] = tile
        second[j] = tile
    first[9] = jnp.where(even, low, high)
    second[9] = jnp.where(even, high, low)


def edges_from(first, second):
    even = is_even("yz")
    me, count = lax.axis_index("yz"), lax.axis_size("yz")
    low = jnp.where(me == 0, 0.0, jnp.where(even, first[9], second[9]))
    high = jnp.where(me == count - 1, 0.0, jnp.where(even, second[9], first[9]))
    return low, high


def pack_kernel(adj, field_out, own_out, first_out, second_out, sems):
    extent_x = adj.shape[1]
    copies = [
        pltpu.make_async_copy(adj.at[:, x], field_out.at[:, x], sems.at[x]) for x in range(extent_x)
    ]
    for copy in copies:
        copy.start()
    edges = jnp.zeros((16, 128), jnp.float32), jnp.zeros((16, 128), jnp.float32)
    for x in range(extent_x):
        copies[x].wait()
        edges = pack_columns(lambda i: field_out[i, x], x, *edges)
    write_messages(
        lambda j: field_out[j, extent_x - 1], *edges, own_out, first_out, second_out
    )


def info_kernel(device, cell, weight, out):
    for k in range(2):
        out[k] = (device[:, k] * 128 + cell[:, k]).astype(jnp.float32)
        out[2 + k] = weight[:, k]


def velocity_kernel(step, saved, *rest):
    *carried, out, kept, sems = rest
    extent_x = out.shape[1]
    copies = []
    if carried:
        copies.append(pltpu.make_async_copy(carried[0], carried[1], sems.at[extent_x]))
        copies[0].start()

    def load(x):
        return pltpu.make_async_copy(saved.at[step, 0, :, x], kept.at[x], sems.at[x])

    lax.fori_loop(0, extent_x, lambda x, c: (load(x).start(), c)[1], 0)

    def one(x, carry):
        load(x).wait()
        for a, tile in enumerate(velocity_of(lambda i: kept[x, i])):
            out[a, x] = tile
        return carry

    lax.fori_loop(0, extent_x, one, 0)
    for copy in copies:
        copy.wait()


def side_kernel(adj, first, second, *rest):
    *_, near_out, two_out, far_out = rest
    extent_x = adj.shape[1]
    even = is_even("gx")
    for j in range(9):
        top, bottom = adj[j, extent_x - 1], adj[18 + j, 0]
        near_out[j] = far_out[j] = jnp.where(even, top, bottom)
        two_out[j] = jnp.where(even, bottom, top)
    lane = lanes()
    low, high = edges_from(first, second)
    top, bottom = [
        jnp.where(lane < 64, pltpu.roll(low, 128 - start, 1), pltpu.roll(high, 192 - start, 1))
        for start in (9 * extent_x, 9)
    ]
    near_out[9] = far_out[9] = jnp.where(even, top, bottom)
    two_out[9] = jnp.where(even, bottom, top)


def cross_kernel(count, *refs):
    own, first, second = refs[:3]
    *others, ends = refs[3 : 1 + count]
    info, _, out = refs[1 + count :]
    interface = lax.axis_index("gx") == lax.axis_size("gx") - 1

    @pl.when(interface)
    def _():
        me = lax.axis_index("yz")
        even = is_even("yz")
        at_end = (me == 0) | (me == count - 1)
        rows = (0, 8)
        spots, picks = {}, {}
        for r in rows:
            for k in range(2):
                code = info[k, r : r + 8].astype(jnp.int32)
                ahead = lax.rem(code // 128 - me + count, count)
                spots[r, k] = lax.rem(code, 128)
                turned = jnp.where(even, lax.rem(count - ahead, count), ahead)
                masks = [turned == 1, turned == count - 1]
                masks += [ahead == count - hop for hop in range(2, count - 1)]
                picks[r, k] = masks
        for j in range(9):
            halves = []
            for r in rows:
                total = jnp.zeros((8, 128), jnp.float32)
                for k in range(2):
                    tiles = [ref[j, r : r + 8] for ref in (own, first, second, *others)]
                    tiles[1] = jnp.where(at_end, ends[j, r : r + 8], tiles[1])
                    got = [jnp.take_along_axis(tile, spots[r, k], axis=1) for tile in tiles]
                    picked = got[0]
                    for mask, value in zip(picks[r, k], got[1:]):
                        picked = jnp.where(mask, value, picked)
                    total = total + picked * info[2 + k, r : r + 8]
                halves.append(total)
            out[j] = jnp.concatenate(halves, axis=0)


def velocity_of(saved):
    totals, along_y, along_z = [], [], []
    for cx in SIGNS:
        sums, diffs = [], []
        for cy in SIGNS:
            lo, mid, hi = [saved(number(cx, cy, cz)) for cz in SIGNS]
            sums.append(lo + mid + hi)
            diffs.append(hi - lo)
        totals.append(sums[0] + sums[1] + sums[2])
        along_y.append(sums[2] - sums[0])
        along_z.append(diffs[0] + diffs[1] + diffs[2])
    density = totals[0] + totals[1] + totals[2]
    momentum = (
        totals[2] - totals[0],
        along_y[0] + along_y[1] + along_y[2],
        along_z[0] + along_z[1] + along_z[2],
    )
    return [part / density for part in momentum]


def moments_of(pull):
    rows = []
    for cx in SIGNS:
        plain, first, second = [], [], []
        for cy in SIGNS:
            lo, mid, hi = [pull(cx, cy, cz) for cz in SIGNS]
            both = lo + hi
            plain.append(mid + 0.25 * both)
            first.append(hi - lo)
            second.append(both)
        pair = plain[0] + plain[2]
        rows.append(
            (
                plain[1] + 0.25 * pair,
                plain[2] - plain[0],
                pair,
                first[1] + 0.25 * (first[0] + first[2]),
                first[2] - first[0],
                second[1] + 0.25 * (second[0] + second[2]),
            )
        )
    even = [rows[1][n] + 0.25 * (rows[0][n] + rows[2][n]) for n in range(6)]
    zero = (8.0 / 27.0) * even[0]
    along = (
        (2.0 / 27.0) * (rows[2][0] - rows[0][0]),
        (2.0 / 27.0) * even[1],
        (2.0 / 27.0) * even[3],
    )
    square = (
        (2.0 / 27.0) * (rows[2][0] + rows[0][0]),
        (2.0 / 27.0) * even[2],
        (2.0 / 27.0) * even[5],
    )
    mixed = (
        (1.0 / 54.0) * (rows[2][1] - rows[0][1]),
        (1.0 / 54.0) * (rows[2][3] - rows[0][3]),
        (1.0 / 54.0) * even[4],
    )
    return zero, along, square, mixed


def collide(pull, velocity, solid, store):
    zero, along, square, mixed = moments_of(lambda cx, cy, cz: pull(number(cx, cy, cz)))
    ux, uy, uz = velocity
    xy, xz, yz = mixed
    quadratic = (
        ux * ux * square[0]
        + uy * uy * square[1]
        + uz * uz * square[2]
        + 2.0 * (ux * uy * xy + ux * uz * xz + uy * uz * yz)
    )
    speed = ux * ux + uy * uy + uz * uz
    scalar = OMEGA * (zero * (1.0 + 1.5 * speed) - 4.5 * quadratic)
    vec_x = OMEGA * (3.0 * along[0] + 9.0 * (square[0] * ux + xy * uy + xz * uz) - 3.0 * ux * zero)
    vec_y = OMEGA * (3.0 * along[1] + 9.0 * (xy * ux + square[1] * uy + yz * uz) - 3.0 * uy * zero)
    vec_z = OMEGA * (3.0 * along[2] + 9.0 * (xz * ux + yz * uy + square[2] * uz) - 3.0 * uz * zero)
    wall = solid == 1
    for cx in SIGNS:
        base = scalar if cx == 0 else (scalar + vec_x if cx > 0 else scalar - vec_x)
        for cy in SIGNS:
            inner = base if cy == 0 else (base + vec_y if cy > 0 else base - vec_y)
            for cz in SIGNS:
                full = inner if cz == 0 else (inner + vec_z if cz > 0 else inner - vec_z)
                i = number(cx, cy, cz)
                store(i, jnp.where(wall, pull(26 - i), (1.0 - OMEGA) * pull(i) + full))


def pull_plane(tile_of, edges_of, pulled, raw=None):
    lane = lanes()
    for cx in SIGNS:
        low_edge, high_edge, start = edges_of(cx)
        for cy in SIGNS:
            place = start + 3 * (cx + 1) + cy + 1
            for cz in SIGNS:
                i = number(cx, cy, cz)
                source = tile_of(i, cx)
                tile = source
                if cz == -1:
                    edge = pltpu.roll(low_edge, 128 - place, 1)
                    tile = jnp.where(lane == 0, edge, pltpu.roll(source, 1, 1))
                elif cz == 1:
                    edge = pltpu.roll(high_edge, 127 - place, 1)
                    tile = jnp.where(lane == 127, edge, pltpu.roll(source, 127, 1))
                if raw is not None and cx == 1:
                    tile = jnp.where(raw, source, tile)
                pulled[i] = shift_y(tile, cy)


def inner_kernel(step, last, adj, vel, solid, first, second, *rest):
    out, low_out, high_out, made, pulled, sems = rest
    extent_x = adj.shape[1]
    low_edge, high_edge = edges_from(first, second)

    def save(x):
        return pltpu.make_async_copy(made.at[x - 1], out.at[:, x], sems.at[x - 1])

    def plane(x, carry):
        here = pulled.at[lax.rem(x, 3)]
        pull_plane(
            lambda i, cx: adj[i, x + cx],
            lambda cx: (low_edge, high_edge, (x + 1 + cx) * 9),
            here,
        )

        def store(i, tile):
            made[x - 1, i] = tile

        velocity = [vel[a, x] for a in range(3)]
        collide(lambda i: here[i], velocity, solid[0, x], store)
        save(x).start()
        if last:
            return carry
        return pack_columns(lambda i: made[x - 1, i], x, *carry)

    zero = jnp.zeros((16, 128), jnp.float32)
    low_out[...], high_out[...] = lax.fori_loop(1, extent_x - 1, plane, (zero, zero), unroll=3)
    lax.fori_loop(1, extent_x - 1, lambda x, c: (save(x).wait(), c)[1], 0)


def outer_kernel(step, adj, vel, solid, first, second, near, two, far, cross, *rest):
    *rest, made, pulled, sems = rest
    low_in, high_in, _, out, *messages = rest
    extent_x = adj.shape[1]
    edges = edges_from(first, second)
    even = is_even("gx")
    interface = lax.axis_index("gx") == lax.axis_size("gx") - 1

    bottom = lax.axis_index("gx") == 0
    inside = lax.axis_index("gx") < lax.axis_size("gx") - 2

    def one(j):
        return jnp.where(inside, near[j], far[j])

    def below(j):
        return jnp.where(bottom, 0.0, jnp.where(even, two[j], one(j)))

    def above(j):
        tile = jnp.where(even, one(j), two[j])
        return jnp.where(interface, cross[j], tile) if j < 9 else tile

    def plane(n, x, ghost, beyond, raw):
        pull_plane(
            lambda i, cx: beyond(i % 9) if cx == ghost else adj[i, x + cx],
            lambda cx: (
                (beyond(9), pltpu.roll(beyond(9), 64, 1), 0)
                if cx == ghost
                else (*edges, (x + 1 + cx) * 9)
            ),
            pulled.at[n],
            raw,
        )

        def store(i, tile):
            made[n, i] = tile

        velocity = [vel[a, x] for a in range(3)]
        collide(lambda i: pulled[n, i], velocity, solid[0, x], store)
        save = pltpu.make_async_copy(made.at[n], out.at[:, x], sems.at[n])
        save.start()
        return save

    final = extent_x - 1
    saves = [plane(0, 0, -1, below, None), plane(1, final, 1, above, interface)]
    if messages:
        low, high = low_in[...], high_in[...]
        low, high = pack_columns(lambda i: made[0, i], 0, low, high)
        low, high = pack_columns(lambda i: made[1, i], final, low, high)
        write_messages(lambda j: made[1, j], low, high, *messages)
    for save in saves:
        save.wait()


def tile_shape(*lead):
    return jax.ShapeDtypeStruct(lead + (16, 128), jnp.float32)


def in_vmem(n):
    return [pl.BlockSpec(memory_space=pltpu.VMEM)] * n


def in_any(n):
    return [pl.BlockSpec(memory_space=pl.ANY)] * n


def body(sizes, adjoint, saved, solid, band_device, band_cell, band_weight):
    zones, widths, count = sizes
    field = adjoint[0]
    extent_x = field.shape[1]
    axes = ("zone", "gx", "yz")
    params = pltpu.CompilerParams(vmem_limit_bytes=VMEM_LIMIT)

    def send(values, target):
        flat = lambda zone, gx, yz: (zone * widths + gx) * count + yz
        places = itertools.product(range(zones), range(widths), range(count))
        return lax.ppermute(values, axes, [(flat(*here), flat(*target(*here))) for here in places])

    def partner_of(place, shift):
        return place + 1 if (place + shift) % 2 == 0 else place - 1

    def flip(zone, gx, yz):
        return (1 - zone, gx, yz)

    def along_z(shift):
        def target(zone, gx, yz):
            to = partner_of(yz, shift)
            return (zone, gx, to) if 0 <= to < count else flip(zone, gx, yz)

        return target

    def hop_z(hop):
        def target(zone, gx, yz):
            if gx == widths - 1:
                return (zone, gx, (yz + hop) % count)
            return flip(zone, gx, yz)

        return target

    def ends_z(zone, gx, yz):
        if gx == widths - 1 and yz in (0, count - 1):
            return (zone, gx, count - 1 - yz)
        return flip(zone, gx, yz)

    def along_x(shift, taken):
        def target(zone, gx, yz):
            to = partner_of(gx, shift)
            return (zone, to, yz) if 0 <= to < widths and taken(gx) else flip(zone, gx, yz)

        return target

    info = pl.pallas_call(
        info_kernel,
        out_shape=tile_shape(4),
        in_specs=in_vmem(3),
        out_specs=in_vmem(1)[0],
        compiler_params=params,
    )(*[jnp.swapaxes(array[0], 1, 2) for array in (band_device, band_cell, band_weight)])
    messages = (tile_shape(9), tile_shape(10), tile_shape(10))
    field, own, first, second = pl.pallas_call(
        pack_kernel,
        out_shape=(tile_shape(27, extent_x), *messages),
        in_specs=[pl.BlockSpec(memory_space=pltpu.HBM)],
        out_specs=tuple(in_vmem(4)),
        scratch_shapes=[pltpu.SemaphoreType.DMA((extent_x,))],
        compiler_params=params,
    )(pltpu.with_memory_space_constraint(field, pltpu.HBM))
    saved = pltpu.with_memory_space_constraint(saved, pltpu.HBM)
    info = send(info, flip)
    for step in (1, 0):
        last = step == 0
        swap = last
        first = send(first, along_z(1))
        second = send(second, along_z(0))
        others = [send(own, target) for target in (*map(hop_z, range(2, count - 1)), ends_z)]
        carried = () if last else (pltpu.with_memory_space_constraint(solid, pltpu.HBM),)
        *copied, vel = pl.pallas_call(
            lambda *refs: velocity_kernel(step, *refs),
            out_shape=(
                *(jax.ShapeDtypeStruct(array.shape, array.dtype) for array in carried),
                tile_shape(3, extent_x),
            ),
            in_specs=[pl.BlockSpec(memory_space=pltpu.HBM)] * (1 + len(carried)),
            out_specs=tuple(in_vmem(1 + len(carried))),
            scratch_shapes=[
                pltpu.VMEM((extent_x, 27, 16, 128), jnp.float32),
                pltpu.SemaphoreType.DMA((extent_x + 1,)),
            ],
            compiler_params=params,
        )(saved, *carried)
        solid = copied[0] if copied else solid
        near, two, far = pl.pallas_call(
            side_kernel,
            out_shape=(tile_shape(10),) * 3,
            in_specs=in_vmem(3) + in_any(2),
            out_specs=tuple(in_vmem(3)),
            compiler_params=params,
        )(field, first, second, vel, info)
        near = send(near, along_x(0, lambda gx: gx < widths - 2))
        two = send(two, along_x(1, lambda gx: True))
        far = send(far, along_x(0, lambda gx: gx >= widths - 2))

        def make_planes(kernel, planes, given, new, extra):
            pair = (second, first) if swap else (first, second)
            operands = (field, vel, solid, *pair, *given)

            def run(adj, vel, solid, *refs):
                kernel(step, adj, vel, solid, *(refs[1::-1] if swap else refs[:2]), *refs[2:])

            return pl.pallas_call(
                run,
                out_shape=(tile_shape(27, extent_x), *extra),
                in_specs=in_vmem(len(operands)) + in_any(len(new)),
                out_specs=tuple(in_any(1) + in_vmem(len(extra))),
                scratch_shapes=[
                    pltpu.VMEM((planes, 27, 16, 128), jnp.float32),
                    pltpu.VMEM((3, 27, 16, 128), jnp.float32),
                    pltpu.SemaphoreType.DMA((planes,)),
                ],
                input_output_aliases={len(operands): 0} if new else {},
                compiler_params=params,
            )(*operands, *new)

        kernel = lambda step, *refs: inner_kernel(step, last, *refs)
        new, *columns = make_planes(kernel, extent_x - 2, (), (), (tile_shape(),) * 2)
        cross = pl.pallas_call(
            lambda *refs: cross_kernel(count, *refs),
            out_shape=tile_shape(9),
            in_specs=in_vmem(count + 2) + in_any(1),
            out_specs=in_vmem(1)[0],
            compiler_params=params,
        )(own, first, second, *others, info, columns[0])
        cross = send(cross, flip)
        ghosts = (near, two, far)
        field, *results = make_planes(
            outer_kernel, 2, (*ghosts, cross, *columns), (new,), () if last else messages
        )
        if not last:
            own, first, second = results
    return field[None]


def solution(mesh):
    sizes = tuple(mesh.shape[axis] for axis in ("zone", "gx", "yz"))
    in_specs = (
        P("zone", None, "gx", None, "yz"),
        P(None, "zone", None, "gx", None, "yz"),
        P("zone", "gx", None, "yz"),
        P("zone", None, "yz", None),
        P("zone", None, "yz", None),
        P("zone", None, "yz", None),
    )
    out_specs = P("zone", None, "gx", None, "yz")
    return jax.shard_map(
        lambda *args: body(sizes, *args),
        mesh=mesh,
        in_specs=in_specs,
        out_specs=out_specs,
        check_vma=False,
    )
```
